512 devices in a mesh: gx: 16 (over y_hi, x, core), gy: 32 (over z, y_lo).
Axes of the slice: x: 4, y: 4 (y_hi: 2, y_lo: 2; y = y_hi * 2 + y_lo), z: 16, core: 2. Of those that a mesh axis runs over, the one named last changes fastest.
Arguments:
- density: float32 [256, 512, 128], P('gx', 'gy'), may hold values from 0.5 to 1.5
- energy: float32 [256, 512, 128], P('gx', 'gy'), may hold values from 1 to 3
- velocity: float32 [3, 256, 512, 128], P(None, 'gx', 'gy'), may hold values from -6 to 6
- mesh_velocity: float32 [3, 256, 512, 128], P(None, 'gx', 'gy'), may hold values from -4 to 4
- density_low: float32 [64, 128, 32], P('gx', 'gy'), may hold values from 0.2 to 0.9
- density_high: float32 [64, 128, 32], P('gx', 'gy'), may hold values from 1.1 to 1.8
- energy_low: float32 [64, 128, 32], P('gx', 'gy'), may hold values from 0.4 to 1.8
- energy_high: float32 [64, 128, 32], P('gx', 'gy'), may hold values from 2.2 to 3.6
Outputs:
- new_density: float32 [256, 512, 128], P('gx', 'gy')
- new_energy: float32 [256, 512, 128], P('gx', 'gy')
- new_velocity: float32 [3, 256, 512, 128], P(None, 'gx', 'gy')
The draws below stay inside these ranges and needn't reach their ends.
All inputs are finite; a program needn't handle non-finite values.
Results may differ from the reference program's by a relative error of at most 0.0003.
Values sent between devices are 32-bit elements; how exact they have to be, the bound alone decides.
A program may use at most 64 MiB of HBM per device.

```python
import math
import jax
import jax.numpy as jnp
import numpy as np
from jax import lax

NZ = 32
NX = 64
NY = 128


def levels(key, dims, shards, smallest, high):
    factor_of = 1.0
    for dim, shards_of in shards:
        draws = jax.random.uniform(jax.random.fold_in(jax.random.fold_in(key, 6), dim), (shards_of,), jnp.float32, smallest / len(shards), high / len(shards))
        factor_of = factor_of * jnp.repeat(jnp.exp(draws), dims[dim] // shards_of).reshape((-1,) + (1,) * (len(dims) - 1 - dim))
    return factor_of


def noise(rng, shape, spread, limit, cuts=(), dtype=jnp.bfloat16):
    entries = jax.random.normal(rng, shape, jnp.float32) * spread
    if len(cuts) > 0:
        entries = levels(rng, shape, cuts, -0.22, 0.18) * entries
    return jnp.clip(entries, min=-limit, max=limit).astype(dtype)


def setup_inputs(seed: int = 0) -> dict:
    streams_of = jax.random.split(jax.random.key(seed), 9)
    return {
        "density": jnp.clip(0.5 + 1.0 * jax.random.uniform(streams_of[0], (4 * NX, 4 * NY, 4 * NZ), jnp.float32) ** levels(streams_of[0], (4 * NX, 4 * NY, 4 * NZ), ((0, 16), (1, 32)), -0.2, 0.2), 0.5, 1.5),
        "energy": jnp.clip(1.0 + 2.0 * jax.random.uniform(streams_of[1], (4 * NX, 4 * NY, 4 * NZ), jnp.float32) ** levels(streams_of[1], (4 * NX, 4 * NY, 4 * NZ), ((0, 16), (1, 32)), -0.2, 0.2), 1.0, 3.0),
        "velocity": noise(streams_of[2], (3, 4 * NX, 4 * NY, 4 * NZ), 1.0, 6.0, ((1, 16), (2, 32)), jnp.float32),
        "mesh_velocity": noise(streams_of[3], (3, 4 * NX, 4 * NY, 4 * NZ), 1.0, 4.0, ((1, 16), (2, 32)), jnp.float32),
        "density_low": jnp.clip(0.2 + 0.7 * jax.random.uniform(streams_of[4], (NX, NY, NZ), jnp.float32) ** levels(streams_of[4], (NX, NY, NZ), ((0, 16), (1, 32)), -0.2, 0.2), 0.2, 0.9),
        "density_high": jnp.clip(1.1 + 0.6999999 * jax.random.uniform(streams_of[5], (NX, NY, NZ), jnp.float32) ** levels(streams_of[5], (NX, NY, NZ), ((0, 16), (1, 32)), -0.2, 0.2), 1.1, 1.8),
        "energy_low": jnp.clip(0.4 + 1.4 * jax.random.uniform(streams_of[6], (NX, NY, NZ), jnp.float32) ** levels(streams_of[6], (NX, NY, NZ), ((0, 16), (1, 32)), -0.2, 0.2), 0.4, 1.8),
        "energy_high": jnp.clip(2.2 + 1.3999999 * jax.random.uniform(streams_of[7], (NX, NY, NZ), jnp.float32) ** levels(streams_of[7], (NX, NY, NZ), ((0, 16), (1, 32)), -0.2, 0.2), 2.2, 3.6),
    }


highest = lax.Precision.HIGHEST
time_step = 0.02
limit_eps = 1e-06

def lagrange_values(node_set, points):
    result = np.ones((len(points), len(node_set)))
    for column in range(len(node_set)):
        for partner in range(len(node_set)):
            if partner != column:
                result[:, column] = result[:, column] * (points - node_set[partner]) / (node_set[column] - node_set[partner])
    return result

def lagrange_slopes(node_set, points):
    node_total = len(node_set)
    result = np.zeros((len(points), node_total))
    for column in range(node_total):
        for skipped in range(node_total):
            if skipped != column:
                factor = np.ones(len(points)) / (node_set[column] - node_set[skipped])
                for partner in range(node_total):
                    if partner != column and partner != skipped:
                        factor = factor * (points - node_set[partner]) / (node_set[column] - node_set[partner])
                result[:, column] = result[:, column] + factor
    return result

def basis_tables():
    gauss_points = np.array([-0.8611363115940526, -0.3399810435848563, 0.3399810435848563, 0.8611363115940526])
    gauss_weights = np.array([0.3478548451374538, 0.6521451548625461, 0.6521451548625461, 0.3478548451374538])
    lobatto_points = np.array([-1.0, -math.sqrt(3.0 / 7.0), 0.0, math.sqrt(3.0 / 7.0), 1.0])
    lobatto_weights = np.array([0.1, 49.0 / 90.0, 32.0 / 45.0, 49.0 / 90.0, 0.1])
    slopes = lagrange_slopes(gauss_points, gauss_points)
    volume = (2.0 / gauss_weights)[:, None] * slopes.T * gauss_weights[None, :]
    trace_low = lagrange_values(gauss_points, np.array([-1.0]))[0]
    trace_high = lagrange_values(gauss_points, np.array([1.0]))[0]
    return {'weights': gauss_weights, 'volume': volume, 'trace_low': trace_low, 'trace_high': trace_high, 'lift_low': 2.0 * trace_low / gauss_weights, 'lift_high': 2.0 * trace_high / gauss_weights, 'to_points': lagrange_values(lobatto_points, gauss_points), 'stiffness': 2.0 * lobatto_weights[:, None] * lagrange_slopes(lobatto_points, lobatto_points), 'lumped': np.array([0.2, lobatto_weights[1], lobatto_weights[2], lobatto_weights[3]])}

def column_tables(lane_count):
    tables = basis_tables()
    zone_total = lane_count // 4
    volume_z = np.zeros((lane_count, lane_count))
    interp_z = np.zeros((lane_count, lane_count))
    pick_z = np.zeros((lane_count, lane_count))
    minus_z = np.zeros((lane_count, lane_count))
    plus_z = np.zeros((lane_count, lane_count))
    stiff_z = np.zeros((lane_count, lane_count))
    average_z = np.zeros((lane_count, lane_count))
    spread_z = np.zeros((zone_total, lane_count))
    for zone_index in range(zone_total):
        offset = 4 * zone_index
        previous = 4 * ((zone_index - 1) % zone_total)
        for within in range(4):
            for source in range(4):
                volume_z[offset + source, offset + within] = tables['volume'][within, source]
                minus_z[previous + source, offset + within] = tables['trace_high'][source]
                plus_z[offset + source, offset + within] = tables['trace_low'][source]
                average_z[offset + source, offset + within] = tables['weights'][source] / 2.0
            pick_z[offset, offset + within] = 1.0
            spread_z[zone_index, offset + within] = 1.0
            for source in range(5):
                interp_z[(offset + source) % lane_count, offset + within] += tables['to_points'][within, source]
        for target in range(5):
            node_index = (offset + target) % lane_count
            for source in range(5):
                stiff_z[(offset + source) % lane_count, node_index] += tables['stiffness'][target, source] / tables['lumped'][node_index % 4]
    result = {'volume_z': volume_z, 'interp_z': interp_z, 'pick_z': pick_z, 'minus_z': minus_z, 'plus_z': plus_z, 'stiff_z': stiff_z, 'average_z': average_z, 'spread_z': spread_z, 'lift_low': np.tile(tables['lift_low'], zone_total), 'lift_high': np.tile(tables['lift_high'], zone_total)}
    return {name_key: jnp.asarray(result[name_key], jnp.float32) for name_key in result}

def split_axis(values, axis_pos, width):
    layout = values.shape
    return values.reshape(layout[:axis_pos] + (layout[axis_pos] // width, width) + layout[axis_pos + 1:])

def merge_axis(values, axis_pos):
    layout = values.shape
    return values.reshape(layout[:axis_pos] + (layout[axis_pos] * layout[axis_pos + 1],) + layout[axis_pos + 2:])

def apply_local(matrix, values, axis_pos):
    letters = 'abcdefgh'[:values.ndim]
    summed = letters[axis_pos]
    output = letters[:axis_pos] + 'q' + letters[axis_pos + 1:]
    return jnp.einsum('q' + summed + ',' + letters + '->' + output, matrix, values, precision=highest)

def zone_traces(fields, axis_pos, vector):
    pieces = split_axis(fields, axis_pos, 4)
    letters = 'abcdefgh'[:pieces.ndim]
    contracted = letters[axis_pos + 1]
    output = letters.replace(contracted, '')
    return jnp.einsum(contracted + ',' + letters + '->' + output, vector, pieces, precision=highest)

def node_windows(extended, axis_pos, zone_count):
    main_part = split_axis(lax.slice_in_dim(extended, 0, 4 * zone_count, axis=axis_pos), axis_pos, 4)
    closing = lax.slice_in_dim(extended, 4, 4 * zone_count + 1, stride=4, axis=axis_pos)
    return jnp.concatenate([main_part, jnp.expand_dims(closing, axis_pos + 1)], axis=axis_pos + 1)

def nodes_to_points(extended, axis_pos, zone_count, to_points):
    return merge_axis(apply_local(to_points, node_windows(extended, axis_pos, zone_count), axis_pos + 1), axis_pos)

def lane_vector(pattern, repeats, axis_pos, array_rank):
    layout = [1] * array_rank
    layout[axis_pos] = len(pattern) * repeats
    return jnp.asarray(np.tile(pattern, repeats).reshape(layout), jnp.float32)

def column_product(values, matrix):
    return jnp.einsum('...m,mn->...n', values, matrix, precision=highest)

def group_extreme(values, extreme):
    lane_index = lax.broadcasted_iota(jnp.int32, values.shape, values.ndim - 1)
    partner = jnp.where(lane_index % 2 == 0, jnp.roll(values, -1, axis=-1), jnp.roll(values, 1, axis=-1))
    paired = extreme(values, partner)
    partner = jnp.where(lane_index // 2 % 2 == 0, jnp.roll(paired, -2, axis=-1), jnp.roll(paired, 2, axis=-1))
    return extreme(paired, partner)

def limit_fields(fields, low_bounds, high_bounds, tables, columns):
    layout = fields.shape
    weights = jnp.asarray(tables['weights'] / 2.0, jnp.float32)
    per_zone = fields.reshape(layout[0], layout[1] // 4, 4, layout[2] // 4, 4, layout[3])
    column_mean = column_product(per_zone, columns['average_z'])
    zone_mean = jnp.einsum('i,j,fxiyjn->fxyn', weights, weights, column_mean, precision=highest)[:, :, None, :, None, :]
    deviation = per_zone - zone_mean
    upper_gap = lax.optimization_barrier(jnp.max(group_extreme(deviation, jnp.maximum), axis=(2, 4), keepdims=True))
    lower_gap = lax.optimization_barrier(jnp.min(group_extreme(deviation, jnp.minimum), axis=(2, 4), keepdims=True))
    ceiling = column_product(high_bounds, columns['spread_z'])[:, :, None, :, None, :]
    floor_value = column_product(low_bounds, columns['spread_z'])[:, :, None, :, None, :]
    allowed = jnp.minimum((ceiling - zone_mean) / (upper_gap + limit_eps), (zone_mean - floor_value) / (limit_eps - lower_gap))
    blend_factor = jnp.clip(allowed, 0.0, 1.0)
    return (zone_mean + blend_factor * deviation).reshape(layout)

def upwind(face_speed, minus_side, plus_side):
    return jnp.maximum(face_speed, 0.0) * minus_side + jnp.minimum(face_speed, 0.0) * plus_side

def sweep_rate(fields, point_speed, flux_low, flux_high, axis_pos, tables):
    volume = jnp.asarray(tables['volume'], jnp.float32)
    local = apply_local(volume, split_axis(point_speed * fields, axis_pos, 4), axis_pos + 1)
    tail = (4,) + (1,) * (fields.ndim - 1 - axis_pos)
    high_lift = jnp.asarray(tables['lift_high'], jnp.float32).reshape(tail)
    low_lift = jnp.asarray(tables['lift_low'], jnp.float32).reshape(tail)
    return merge_axis(local - high_lift * jnp.expand_dims(flux_high, axis_pos + 1) + low_lift * jnp.expand_dims(flux_low, axis_pos + 1), axis_pos)

def column_rate(fields, point_speed, face_speed, columns):
    volume_part = column_product(point_speed * fields, columns['volume_z'])
    flux_low = upwind(face_speed, column_product(fields, columns['minus_z']), column_product(fields, columns['plus_z']))
    flux_high = jnp.roll(flux_low, -4, axis=-1)
    return volume_part - columns['lift_high'] * flux_high + columns['lift_low'] * flux_low

def mesh_fields(wide_mesh, zones_x, zones_y, tables, columns):
    to_points = jnp.asarray(tables['to_points'], jnp.float32)
    across = nodes_to_points(wide_mesh, 1, zones_x, to_points)
    planar = nodes_to_points(across, 2, zones_y, to_points)
    point_speed = column_product(planar, columns['interp_z'])
    face_x = column_product(nodes_to_points(wide_mesh[0][0::4], 1, zones_y, to_points), columns['interp_z'])
    face_y = column_product(nodes_to_points(wide_mesh[1][:, 0::4], 0, zones_x, to_points), columns['interp_z'])
    face_z = column_product(planar[2], columns['pick_z'])
    return (point_speed, face_x, face_y, face_z)

def assemble(main_part, carried, axis_pos):
    leading = lax.index_in_dim(main_part, 0, axis_pos + 1, keepdims=False) + carried
    remainder = lax.slice_in_dim(main_part, 1, 4, axis=axis_pos + 1)
    return merge_axis(jnp.concatenate([jnp.expand_dims(leading, axis_pos + 1), remainder], axis=axis_pos + 1), axis_pos)

def periodic_extend(values, axis_pos):
    return jnp.concatenate([values, lax.slice_in_dim(values, 0, 1, axis=axis_pos)], axis=axis_pos)

def reference_field_rates(fields, mesh_data, tables, columns):
    point_speed, face_x, face_y, face_z = mesh_data
    trace_low = jnp.asarray(tables['trace_low'], jnp.float32)
    trace_high = jnp.asarray(tables['trace_high'], jnp.float32)
    low_x = zone_traces(fields, 1, trace_low)
    high_x = zone_traces(fields, 1, trace_high)
    low_y = zone_traces(fields, 2, trace_low)
    high_y = zone_traces(fields, 2, trace_high)
    flux_low_x = upwind(face_x[:-1], jnp.roll(high_x, 1, axis=1), low_x)
    flux_high_x = jnp.roll(flux_low_x, -1, axis=1)
    flux_low_y = upwind(face_y[:, :-1], jnp.roll(high_y, 1, axis=2), low_y)
    flux_high_y = jnp.roll(flux_low_y, -1, axis=2)
    return sweep_rate(fields, point_speed[0], flux_low_x, flux_high_x, 1, tables) + sweep_rate(fields, point_speed[1], flux_low_y, flux_high_y, 2, tables) + column_rate(fields, point_speed[2], face_z, columns)

def reference_velocity_rate(velocity, mesh_velocity, tables, columns):
    stiffness = jnp.asarray(tables['stiffness'], jnp.float32)
    inverse = 1.0 / tables['lumped']
    total = mesh_velocity[2] * column_product(velocity, columns['stiff_z'])
    for axis_pos, zone_count in ((1, NX), (2, NY)):
        local = apply_local(stiffness, node_windows(periodic_extend(velocity, axis_pos), axis_pos, zone_count), axis_pos + 1)
        carried = jnp.roll(lax.index_in_dim(local, 4, axis_pos + 1, keepdims=False), 1, axis=axis_pos)
        assembled = assemble(local, carried, axis_pos)
        total = total + mesh_velocity[axis_pos - 1] * assembled * lane_vector(inverse, zone_count, axis_pos, 4)
    return -total

def reference(density, energy, velocity, mesh_velocity, density_low, density_high, energy_low, energy_high):
    tables = basis_tables()
    columns = column_tables(4 * NZ)
    fields = jnp.stack([density, energy])
    low_bounds = jnp.stack([density_low, energy_low])
    high_bounds = jnp.stack([density_high, energy_high])
    wide_mesh = periodic_extend(periodic_extend(mesh_velocity, 1), 2)
    mesh_data = mesh_fields(wide_mesh, NX, NY, tables, columns)
    field_rates = reference_field_rates(fields, mesh_data, tables, columns)
    velocity_rate = reference_velocity_rate(velocity, mesh_velocity, tables, columns)
    section_fields = limit_fields(fields + time_step * field_rates, low_bounds, high_bounds, tables, columns)
    section_velocity = velocity + time_step * velocity_rate
    second_rates = reference_field_rates(section_fields, mesh_data, tables, columns)
    second_velocity = reference_velocity_rate(section_velocity, mesh_velocity, tables, columns)
    new_fields = limit_fields(0.5 * fields + 0.5 * (section_fields + time_step * second_rates), low_bounds, high_bounds, tables, columns)
    new_velocity = 0.5 * velocity + 0.5 * (section_velocity + time_step * second_velocity)
    return (new_fields[0], new_fields[1], new_velocity)
```

```python
import functools
import math

import jax
import jax.numpy as jnp
import ml_dtypes
import numpy as np
from jax import lax
from jax.experimental import pallas as pl
from jax.experimental.pallas import tpu as pltpu
from jax.sharding import PartitionSpec as P

MESH = pl.DeviceIdType.MESH
F32 = jnp.float32
BF16 = jnp.bfloat16
time_step = 0.02
limit_eps = 1e-06


def lagrange_values(node_set, points):
    result = np.ones((len(points), len(node_set)))
    for column in range(len(node_set)):
        for partner in range(len(node_set)):
            if partner != column:
                result[:, column] = (
                    result[:, column]
                    * (points - node_set[partner])
                    / (node_set[column] - node_set[partner])
                )
    return result


def lagrange_slopes(node_set, points):
    node_total = len(node_set)
    result = np.zeros((len(points), node_total))
    for column in range(node_total):
        for skipped in range(node_total):
            if skipped != column:
                factor = np.ones(len(points)) / (node_set[column] - node_set[skipped])
                for partner in range(node_total):
                    if partner != column and partner != skipped:
                        factor = (
                            factor
                            * (points - node_set[partner])
                            / (node_set[column] - node_set[partner])
                        )
                result[:, column] = result[:, column] + factor
    return result


def basis_tables():
    gauss_points = np.array(
        [-0.8611363115940526, -0.3399810435848563, 0.3399810435848563, 0.8611363115940526]
    )
    gauss_weights = np.array(
        [0.3478548451374538, 0.6521451548625461, 0.6521451548625461, 0.3478548451374538]
    )
    lobatto_points = np.array([-1.0, -math.sqrt(3.0 / 7.0), 0.0, math.sqrt(3.0 / 7.0), 1.0])
    lobatto_weights = np.array([0.1, 49.0 / 90.0, 32.0 / 45.0, 49.0 / 90.0, 0.1])
    slopes = lagrange_slopes(gauss_points, gauss_points)
    volume = (2.0 / gauss_weights)[:, None] * slopes.T * gauss_weights[None, :]
    trace_low = lagrange_values(gauss_points, np.array([-1.0]))[0]
    trace_high = lagrange_values(gauss_points, np.array([1.0]))[0]
    stiffness = (
        2.0 * lobatto_weights[:, None] * lagrange_slopes(lobatto_points, lobatto_points)
    )
    lumped = np.array([0.2, lobatto_weights[1], lobatto_weights[2], lobatto_weights[3], 0.2])
    return {
        "weights": gauss_weights / 2.0,
        "volume": time_step * volume,
        "trace_low": trace_low,
        "trace_high": trace_high,
        "lift_low": time_step * 2.0 * trace_low / gauss_weights,
        "lift_high": time_step * 2.0 * trace_high / gauss_weights,
        "to_points": lagrange_values(lobatto_points, gauss_points),
        "stiffness": -time_step * stiffness / lumped[:, None],
    }


TABLES = basis_tables()
TABLE = {name: TABLES[name].tolist() for name in TABLES}


def halves(matrix):
    upper = matrix.astype(np.float32).astype(ml_dtypes.bfloat16)
    lower = (matrix - upper.astype(np.float64)).astype(ml_dtypes.bfloat16)
    return upper, lower


def lane_matrices(lanes):
    zones = lanes // 4
    shape = (lanes, lanes)
    volume, lift = np.zeros(shape), np.zeros(shape)
    minus, plus = np.zeros(shape), np.zeros(shape)
    stiff, interp = np.zeros(shape), np.zeros(shape)
    pick, spread = np.zeros(shape), np.zeros(shape)
    for zone in range(zones):
        at = 4 * zone
        before = 4 * ((zone - 1) % zones)
        for within in range(4):
            for source in range(4):
                volume[at + source, at + within] = TABLES["volume"][within, source]
                minus[before + source, at + within] = TABLES["trace_high"][source]
                plus[at + source, at + within] = TABLES["trace_low"][source]
            lift[at, at + within] = TABLES["lift_low"][within]
            lift[at, before + within] = -TABLES["lift_high"][within]
            pick[at, at + within] = 1.0
            spread[zone, at + within] = 1.0
            for source in range(5):
                interp[(at + source) % lanes, at + within] += TABLES["to_points"][within, source]
        for target in range(5):
            for source in range(5):
                stiff[(at + source) % lanes, (at + target) % lanes] += TABLES["stiffness"][
                    target, source
                ]
    minus_h, minus_l = halves(minus)
    plus_h, plus_l = halves(plus)
    stiff_h, stiff_l = halves(stiff)
    interp_h, interp_l = halves(interp)
    pick_h, _ = halves(pick)
    spread_h, _ = halves(spread)
    volume_h, volume_l = halves(volume)
    lift_h, lift_l = halves(lift)
    square = np.concatenate(
        [minus_h, plus_h, minus_l, plus_l, stiff_h, stiff_l, interp_h, interp_l, pick_h, spread_h],
        axis=1,
    )
    tall = np.concatenate(
        [np.concatenate([volume_h, volume_l], 1), np.concatenate([lift_h, lift_l], 1)], axis=0
    )
    return square, tall


def spin(values, steps, axis):
    size = values.shape[axis]
    steps = steps % size
    return values if steps == 0 else pltpu.roll(values, steps, axis)


def rows_of(shape):
    return lax.broadcasted_iota(jnp.int32, shape, len(shape) - 2)


def low_half(shape):
    return rows_of(shape) < 4


def at_zone(shape, zone):
    return rows_of(shape) % 4 == zone


def combine(coefficients, terms):
    total = None
    for factor, term in zip(coefficients, terms):
        part = factor * term
        total = part if total is None else total + part
    return total


def parted(values):
    upper = values.astype(BF16)
    return upper, (values - upper.astype(F32)).astype(BF16)


def product(left, right):
    return jnp.dot(left, right, preferred_element_type=F32)


def by_zone(values):
    return values.reshape((2, 4) + values.shape[1:])


def from_zone(pieces):
    stacked = jnp.stack(pieces, axis=1)
    return stacked.reshape((8,) + stacked.shape[2:])


def pack_x_low(planes):
    mask = low_half((8, 128))
    return [jnp.where(mask, planes[t], spin(planes[t + 1], 4, 0)) for t in (0, 2)]


def pack_x_high(planes):
    mask = low_half((8, 128))
    return [jnp.where(mask, spin(planes[t], 4, 0), planes[t + 1]) for t in (0, 2)]


def unpack_x_high(packed):
    return [spin(packed[0], 4, 0), packed[0], spin(packed[1], 4, 0), packed[1]]


def unpack_x_low(packed):
    return [packed[0], spin(packed[0], 4, 0), packed[1], spin(packed[1], 4, 0)]


def pack_y(values, start):
    parts = by_zone(values)
    shape = (2, 8, 128)
    total = spin(parts[:, 3], 3 - start, 1)
    for place in (2, 1, 0):
        total = jnp.where(at_zone(shape, place), spin(parts[:, place], place - start, 1), total)
    return total


def unpack_y(packed, end):
    return from_zone([spin(packed, end - place, 1) for place in range(4)])


def kernel(
    counts,
    density, energy, velocity, mesh_velocity, density_low, density_high, energy_low, energy_high,
    square_hbm, tall_hbm,
    new_density, new_energy, new_velocity,
    raw_u, raw_v, raw_m, square, tall, bound_in, bound_rows, bounds,
    acc_v, sec_v, acc_f, sec_f, speed, face_x, face_y, face_z, trace_x, trace_y, zoned,
    out_dx, out_ux, out_dy, out_uy, out_corner,
    in_dx, in_ux, in_dy, in_uy, in_corner,
    out_dx2, out_ux2, out_dy2, out_uy2,
    in_dx2, in_ux2, in_dy2, in_uy2,
    load_sem, store_sem, send_sem, recv_sem,
):
    count_x, count_y = counts
    here_x, here_y = lax.axis_index("gx"), lax.axis_index("gy")
    west = lax.rem(here_x + count_x - 1, count_x)
    east = lax.rem(here_x + 1, count_x)
    south = lax.rem(here_y + count_y - 1, count_y)
    north = lax.rem(here_y + 1, count_y)
    to_west, to_east = (west, here_y), (east, here_y)
    to_south, to_north = (here_x, south), (here_x, north)
    to_corner, from_corner = (west, south), (east, north)

    loads = []

    def load(source, target):
        copy = pltpu.make_async_copy(source, target, load_sem.at[len(loads)])
        copy.start()
        loads.append(copy)

    for half in range(2):
        rows, block = pl.ds(16 * half, 16), pl.ds(8 * half, 8)
        load(mesh_velocity.at[:, block], raw_m.at[:, :, rows, :])
        load(velocity.at[:, block], raw_v.at[:, :, rows, :])
        load(density.at[block], raw_u.at[0, :, rows, :])
        load(energy.at[block], raw_u.at[1, :, rows, :])
    load(square_hbm, square)
    load(tall_hbm, tall)
    for index, source in enumerate((density_low, density_high, energy_low, energy_high)):
        load(source, bound_in.at[index])

    barrier = pltpu.get_barrier_semaphore()
    for peer in (to_west, to_east, to_south, to_north, to_corner, from_corner):
        pl.semaphore_signal(barrier, inc=1, device_id=peer, device_id_type=MESH)

    for copy in loads:
        copy.wait()

    full = (8, 8, 128)
    plane = (8, 128)
    low_rows = low_half(plane)
    stiff = TABLE["stiffness"]
    zero = jnp.zeros(plane, F32)

    def field_at(which, j):
        return raw_u[which, :, pl.ds(j, 8, stride=4), :]

    def velocity_at(which, j):
        return raw_v[which, :, pl.ds(j, 8, stride=4), :]

    def mesh_at(which, j):
        return raw_m[which, :, pl.ds(j, 8, stride=4), :]

    def lanes_product(values, column, narrow=1):
        upper, lower = parted(jnp.concatenate([part.reshape(64, 128) for part in values], 0))
        wide = square[:, 128 * column : 128 * (column + 2)]
        both = product(upper, wide)
        total = both[:, :128] + both[:, 128:] + product(lower, wide[:, :128])
        return [total[64 * j : 64 * (j + 1)].reshape(full) for j in range(4)]

    def field_traces(which, values):
        for j in range(4):
            parts = by_zone(values[j])
            places = [parts[:, i] for i in range(4)]
            trace_x[which, 0, j] = combine(TABLE["trace_low"], places)
            trace_x[which, 1, j] = combine(TABLE["trace_high"], places)
        trace_y[which, 0] = combine(TABLE["trace_low"], values)
        trace_y[which, 1] = combine(TABLE["trace_high"], values)

    def put_pair(target, item, pair):
        target[item, 0] = pair[0]
        target[item, 1] = pair[1]

    def pack_field(which, item, buffers):
        west_to, east_to, south_to, north_to = buffers
        put_pair(west_to, item, pack_x_low([trace_x[which, 0, j, 0] for j in range(4)]))
        put_pair(east_to, item, pack_x_high([trace_x[which, 1, j, 1] for j in range(4)]))
        south_to[item] = pack_y(trace_y[which, 0], 0)
        north_to[item] = pack_y(trace_y[which, 1], 3)

    def pack_velocity(values, item, buffers):
        west_to, east_to, south_to, north_to = buffers
        put_pair(west_to, item, pack_x_low([values[j][0] for j in range(4)]))
        closing = [
            combine(stiff[4][:4], [values[j][4 + i] for i in range(4)]) for j in range(4)
        ]
        put_pair(east_to, item, pack_x_high(closing))
        south_to[item] = pack_y(values[0], 0)
        north_to[item] = pack_y(combine(stiff[4][:4], values), 3)

    buffers_a = (out_dx, out_ux, out_dy, out_uy)
    for which in range(3):
        pack_velocity([velocity_at(which, j) for j in range(4)], 2 + which, buffers_a)
    for which in range(2):
        field_traces(which, [field_at(which, j) for j in range(4)])
        pack_field(which, which, buffers_a)
    corner = zero
    for item in range(4):
        values = [mesh_at(min(item, 2), j) for j in range(4)]
        if item < 3:
            values = lanes_product(values, 6)
        else:
            upper, lower = parted(jnp.concatenate([v.reshape(64, 128) for v in values], 0))
            picker = square[:, 128 * 8 : 128 * 9]
            total = product(upper, picker) + product(lower, picker)
            values = [total[64 * j : 64 * (j + 1)].reshape(full) for j in range(4)]
        for j in range(4):
            zoned[item, j] = values[j]
        put_pair(out_dx, 5 + item, pack_x_low([values[j][0] for j in range(4)]))
        out_dy[5 + item] = pack_y(values[0], 0)
        corner = jnp.where(rows_of(plane) == item, spin(values[0][0], item, 0), corner)
    out_corner[...] = corner

    pl.semaphore_wait(barrier, 6)
    copies = []

    def send(source, target, peer):
        copy = pltpu.make_async_remote_copy(
            src_ref=source, dst_ref=target,
            send_sem=send_sem.at[len(copies)], recv_sem=recv_sem.at[len(copies)],
            device_id=peer, device_id_type=MESH,
        )
        copy.start()
        copies.append(copy)
        return copy

    first = [
        send(out_dx, in_dx, to_west),
        send(out_ux, in_ux, to_east),
        send(out_dy, in_dy, to_south),
        send(out_uy, in_uy, to_north),
        send(out_corner, in_corner, to_corner),
    ]

    bound_rows[...] = jnp.zeros((4, 2, 8, 128), F32)
    for index in range(4):
        for zone in range(4):
            bound_rows[index, zone % 2, pl.ds(4 * (zone // 2), 4), pl.ds(0, 32)] = bound_in[
                index, zone
            ]
    values = bound_rows[...].reshape(64, 128)
    spreader = square[:, 128 * 9 : 128 * 10]
    upper = values.astype(BF16)
    rest = values - upper.astype(F32)
    middle = rest.astype(BF16)
    lowest = (rest - middle.astype(F32)).astype(BF16)
    values = product(upper, spreader) + (product(middle, spreader) + product(lowest, spreader))
    bounds[...] = values.reshape(4, 2, 8, 128)

    def velocity_before(which, values, base, scale):
        along_z = lanes_product(values, 4)
        closing = combine(stiff[4][:4], values)
        after = jnp.where(at_zone(full, 3), 0.0, spin(values[0], 7, 1))
        carried = jnp.where(at_zone(full, 0), 0.0, spin(closing, 1, 1))
        for j in range(4):
            parts = by_zone(values[j])
            places = [parts[:, i] for i in range(4)]
            ending = combine(stiff[4][:4], places)
            next_plane = jnp.stack(
                [parts[1, 0], jnp.where(low_rows, spin(parts[0, 0], 4, 0), 0.0)]
            )
            last_end = jnp.stack([jnp.where(low_rows, 0.0, spin(ending[1], 4, 0)), ending[0]])
            sums = []
            for a in range(4):
                factors = list(stiff[a])
                if a == 0:
                    factors[0] += stiff[4][4]
                total = combine(factors, places + [next_plane])
                sums.append(total + last_end if a == 0 else total)
            along_x = from_zone(sums)
            factors = list(stiff[j])
            if j == 0:
                factors[0] += stiff[4][4]
            along_y = combine(factors, values + [after])
            if j == 0:
                along_y = along_y + carried
            rate = (
                mesh_at(0, j) * along_x + mesh_at(1, j) * along_y + mesh_at(2, j) * along_z[j]
            )
            acc_v[which, j] = base(j) + (rate if scale == 1.0 else scale * rate)

    def velocity_after(which, scale, item, buffers):
        from_east, from_west, from_north, from_south = buffers
        later = unpack_x_high([from_east[item, 0], from_east[item, 1]])
        earlier = unpack_x_low([from_west[item, 0], from_west[item, 1]])
        above = jnp.where(at_zone(full, 3), unpack_y(from_north[item], 3), 0.0)
        below = jnp.where(at_zone(full, 0), unpack_y(from_south[item], 0), 0.0)
        done = []
        for j in range(4):
            ahead = jnp.where(low_rows, 0.0, later[j])
            behind = jnp.where(low_rows, earlier[j], 0.0)
            extra_x = jnp.stack(
                [scale * behind, zero, zero, zero]
                + [(scale * stiff[a][4]) * ahead for a in range(4)]
            )
            extra_y = (scale * stiff[j][4]) * above
            if j == 0:
                extra_y = extra_y + scale * below
            done.append(acc_v[which, j] + mesh_at(0, j) * extra_x + mesh_at(1, j) * extra_y)
        return done

    def mesh_points():
        points = TABLE["to_points"]
        for item in range(4):
            values = [zoned[item, j] for j in range(4)]
            later = unpack_x_high([in_dx[5 + item, 0], in_dx[5 + item, 1]])
            later = [
                jnp.where(low_rows, spin(values[j][0], 4, 0), later[j]) for j in range(4)
            ]
            above = jnp.where(
                at_zone(full, 3), unpack_y(in_dy[5 + item], 3), spin(values[0], 7, 1)
            )
            rows = rows_of(plane)
            far = jnp.where(rows == 3, spin(above[0], 4, 0), spin(later[0], 7, 0))
            far = jnp.where(rows == 7, spin(in_corner[...], 7 - item, 0), far)
            values = values + [above]
            later = later + [far]
            across = []
            for b in range(5):
                parts = by_zone(values[b])
                places = [parts[:, a] for a in range(4)]
                places.append(jnp.stack([parts[1, 0], later[b]]))
                across.append(from_zone([combine(points[i], places) for i in range(4)]))
            for j in range(4):
                result = combine(points[j], across)
                if item < 3:
                    speed[item, j] = result
                else:
                    face_z[j] = result
                if item == 0:
                    for q in range(3):
                        edge = [later[b] if q == 2 else values[b][4 * q] for b in range(5)]
                        face_x[q, j] = combine(points[j], edge)
            if item == 1:
                face_y[0] = across[0]
                face_y[1] = across[4]

    def upwind(face, minus_side, plus_side):
        return jnp.maximum(face, 0.0) * minus_side + jnp.minimum(face, 0.0) * plus_side

    def field_before(which, values, base, scale):
        upper, lower = parted(jnp.concatenate([part.reshape(64, 128) for part in values], 0))
        wide = square[:, 0:256]
        sides = product(upper, wide) + product(lower, wide) + product(upper, square[:, 256:512])
        flux = [
            upwind(
                face_z[j],
                sides[64 * j : 64 * (j + 1), :128].reshape(full),
                sides[64 * j : 64 * (j + 1), 128:].reshape(full),
            ).reshape(64, 128)
            for j in range(4)
        ]
        moved = [(speed[2, j] * values[j]).reshape(64, 128) for j in range(4)]
        both = jnp.concatenate([jnp.concatenate(moved, 0), jnp.concatenate(flux, 0)], 1)
        upper, lower = parted(both)
        sums = product(upper, tall[...])
        along_z = sums[:, :128] + sums[:, 128:] + product(lower, tall[:, :128])
        moved = [speed[1, j] * values[j] for j in range(4)]
        for j in range(4):
            parts = by_zone(speed[0, j] * values[j])
            places = [parts[:, i] for i in range(4)]
            along_x = from_zone([combine(TABLE["volume"][i], places) for i in range(4)])
            along_y = combine(TABLE["volume"][j], moved)
            rate = along_x + along_y + along_z[64 * j : 64 * (j + 1)].reshape(full)
            acc_f[which, j] = base(j) + (rate if scale == 1.0 else scale * rate)

    def in_group(values, join):
        lane = lax.broadcasted_iota(jnp.int32, values.shape, 2)
        partner = jnp.where(lane % 2 == 0, spin(values, 127, 2), spin(values, 1, 2))
        values = join(values, partner)
        partner = jnp.where(lane // 2 % 2 == 0, spin(values, 126, 2), spin(values, 2, 2))
        return join(values, partner)

    def limited(which, values):
        weights = TABLE["weights"]
        across = by_zone(combine(weights, values))
        mean = combine(weights, [across[:, i] for i in range(4)])
        lane = lax.broadcasted_iota(jnp.int32, (2, 8, 128), 2) % 4
        middle = (lane == 1) | (lane == 2)
        mean = in_group(mean * jnp.where(middle, weights[1], weights[0]), jnp.add)
        top = functools.reduce(jnp.maximum, values)
        bottom = functools.reduce(jnp.minimum, values)
        top, bottom = by_zone(top), by_zone(bottom)
        top = functools.reduce(jnp.maximum, [top[:, i] for i in range(4)])
        bottom = functools.reduce(jnp.minimum, [bottom[:, i] for i in range(4)])
        rise = in_group(top, jnp.maximum) - mean
        fall = in_group(bottom, jnp.minimum) - mean
        low, high = bounds[2 * which], bounds[2 * which + 1]
        theta = jnp.minimum(
            (high - mean) / (rise + limit_eps), (mean - low) / (limit_eps - fall)
        )
        theta = jnp.clip(theta, 0.0, 1.0)
        result = []
        for j in range(4):
            parts = by_zone(values[j])
            result.append(
                from_zone([mean + theta * (parts[:, i] - mean) for i in range(4)])
            )
        return result

    def field_after(which, scale, item, buffers):
        from_east, from_west, from_north, from_south = buffers
        later = unpack_x_high([from_east[item, 0], from_east[item, 1]])
        earlier = unpack_x_low([from_west[item, 0], from_west[item, 1]])
        low_lift = [scale * factor for factor in TABLE["lift_low"]]
        high_lift = [-scale * factor for factor in TABLE["lift_high"]]
        low, high = trace_y[which, 0], trace_y[which, 1]
        before = jnp.where(at_zone(full, 0), unpack_y(from_south[item], 0), spin(high, 1, 1))
        after = jnp.where(at_zone(full, 3), unpack_y(from_north[item], 3), spin(low, 7, 1))
        lower_y = upwind(face_y[0], before, low)
        upper_y = upwind(face_y[1], high, after)
        values = []
        for j in range(4):
            low, high = trace_x[which, 0, j], trace_x[which, 1, j]
            before = jnp.where(low_rows, earlier[j], spin(high[1], 4, 0))
            after = jnp.where(low_rows, spin(low[0], 4, 0), later[j])
            flux = [
                upwind(face_x[0, j], before, low[0]),
                upwind(face_x[1, j], high[0], low[1]),
                upwind(face_x[2, j], high[1], after),
            ]
            lower_x, upper_x = jnp.stack(flux[:2]), jnp.stack(flux[1:])
            lift = from_zone(
                [low_lift[i] * lower_x + high_lift[i] * upper_x for i in range(4)]
            )
            values.append(
                acc_f[which, j] + lift + (low_lift[j] * lower_y + high_lift[j] * upper_y)
            )
        return limited(which, values)

    for which in range(3):
        values = [velocity_at(which, j) for j in range(4)]
        velocity_before(which, values, lambda j: values[j], 1.0)
    for copy in first:
        copy.wait_recv()
    arrived_a = (in_dx, in_ux, in_dy, in_uy)
    buffers_b = (out_dx2, out_ux2, out_dy2, out_uy2)
    targets_b = (in_dx2, in_ux2, in_dy2, in_uy2)
    peers = (to_west, to_east, to_south, to_north)
    for which in range(3):
        values = velocity_after(which, 1.0, 2 + which, arrived_a)
        for j in range(4):
            sec_v[which, j] = values[j]
        pack_velocity(values, 2 + which, buffers_b)
    second_v = [
        send(source.at[pl.ds(2, 3)], target.at[pl.ds(2, 3)], peer)
        for source, target, peer in zip(buffers_b, targets_b, peers)
    ]
    mesh_points()
    for which in range(2):
        values = [field_at(which, j) for j in range(4)]
        field_before(which, values, lambda j: values[j], 1.0)
        values = field_after(which, 1.0, which, arrived_a)
        for j in range(4):
            sec_f[which, j] = values[j]
        field_traces(which, values)
        pack_field(which, which, buffers_b)
    second_f = [
        send(source.at[pl.ds(0, 2)], target.at[pl.ds(0, 2)], peer)
        for source, target, peer in zip(buffers_b, targets_b, peers)
    ]

    for which in range(3):
        values = [sec_v[which, j] for j in range(4)]
        velocity_before(
            which, values, lambda j: 0.5 * velocity_at(which, j) + 0.5 * values[j], 0.5
        )
    for which in range(2):
        values = [sec_f[which, j] for j in range(4)]
        field_before(which, values, lambda j: 0.5 * field_at(which, j) + 0.5 * values[j], 0.5)
    stores = []

    def store(source, target):
        copy = pltpu.make_async_copy(source, target, store_sem.at[len(stores)])
        copy.start()
        stores.append(copy)

    arrived_b = (in_dx2, in_ux2, in_dy2, in_uy2)
    for copy in second_v:
        copy.wait_recv()
    for which in range(3):
        values = velocity_after(which, 0.5, 2 + which, arrived_b)
        for j in range(4):
            raw_v[which, :, pl.ds(j, 8, stride=4), :] = values[j]
    for half in range(2):
        rows, block = pl.ds(16 * half, 16), pl.ds(8 * half, 8)
        store(raw_v.at[:, :, rows, :], new_velocity.at[:, block])
    for copy in second_f:
        copy.wait_recv()
    for which, target in enumerate((new_density, new_energy)):
        values = field_after(which, 0.5, which, arrived_b)
        for j in range(4):
            raw_u[which, :, pl.ds(j, 8, stride=4), :] = values[j]
        for half in range(2):
            rows, block = pl.ds(16 * half, 16), pl.ds(8 * half, 8)
            store(raw_u.at[which, :, rows, :], target.at[block])
    for copy in copies:
        copy.wait_send()
    for copy in stores:
        copy.wait()


def solution(mesh):
    counts = (mesh.shape["gx"], mesh.shape["gy"])
    square, tall = lane_matrices(128)

    def on_device(*arguments):
        items_a, items_v = 9, 5
        vmem = lambda *shape: pltpu.VMEM(shape, F32)
        scratch = [
            vmem(2, 8, 32, 128), vmem(3, 8, 32, 128), vmem(3, 8, 32, 128),
            pltpu.VMEM(square.shape, BF16), pltpu.VMEM(tall.shape, BF16),
            vmem(4, 4, 4, 32), vmem(4, 2, 8, 128), vmem(4, 2, 8, 128),
            vmem(3, 4, 8, 8, 128), vmem(3, 4, 8, 8, 128),
            vmem(2, 4, 8, 8, 128), vmem(2, 4, 8, 8, 128),
            vmem(3, 4, 8, 8, 128), vmem(3, 4, 8, 128), vmem(2, 8, 8, 128), vmem(4, 8, 8, 128),
            vmem(2, 2, 4, 2, 8, 128), vmem(2, 2, 8, 8, 128), vmem(4, 4, 8, 8, 128),
        ]
        sides = [vmem(items, 2, 8, 128) for items in (items_a, items_v, items_a, items_v)]
        scratch += sides + [vmem(8, 128)] + sides + [vmem(8, 128)]
        scratch += [vmem(items_v, 2, 8, 128)] * 8
        scratch += [
            pltpu.SemaphoreType.DMA((14,)),
            pltpu.SemaphoreType.DMA((6,)),
            pltpu.SemaphoreType.DMA((13,)),
            pltpu.SemaphoreType.DMA((13,)),
        ]
        outputs = [arguments[0], arguments[1], arguments[2]]
        return pl.pallas_call(
            functools.partial(kernel, counts),
            out_shape=[jax.ShapeDtypeStruct(value.shape, F32) for value in outputs],
            in_specs=[pl.BlockSpec(memory_space=pl.ANY)] * 10,
            out_specs=[pl.BlockSpec(memory_space=pl.ANY)] * 3,
            scratch_shapes=scratch,
            compiler_params=pltpu.CompilerParams(
                collective_id=0, has_side_effects=True, vmem_limit_bytes=48 * 1024 * 1024
            ),
        )(*arguments, jnp.asarray(square), jnp.asarray(tall))

    fields, vectors = P("gx", "gy", None), P(None, "gx", "gy", None)
    return jax.shard_map(
        on_device,
        mesh=mesh,
        in_specs=(fields, fields, vectors, vectors, fields, fields, fields, fields),
        out_specs=(fields, fields, vectors),
        check_vma=False,
    )
```

```python
import functools
import math

import jax
import jax.numpy as jnp
import numpy as np
from jax import lax
from jax.experimental import pallas as pl
from jax.experimental.pallas import tpu as pltpu
from jax.sharding import PartitionSpec as P

MESH = pl.DeviceIdType.MESH
F32 = jnp.float32
BF16 = jnp.bfloat16
time_step = 0.02
limit_eps = 1e-06


def lagrange_values(node_set, points):
    result = np.ones((len(points), len(node_set)))
    for column in range(len(node_set)):
        for partner in range(len(node_set)):
            if partner != column:
                result[:, column] = (
                    result[:, column]
                    * (points - node_set[partner])
                    / (node_set[column] - node_set[partner])
                )
    return result


def lagrange_slopes(node_set, points):
    node_total = len(node_set)
    result = np.zeros((len(points), node_total))
    for column in range(node_total):
        for skipped in range(node_total):
            if skipped != column:
                factor = np.ones(len(points)) / (node_set[column] - node_set[skipped])
                for partner in range(node_total):
                    if partner != column and partner != skipped:
                        factor = (
                            factor
                            * (points - node_set[partner])
                            / (node_set[column] - node_set[partner])
                        )
                result[:, column] = result[:, column] + factor
    return result


def basis_tables():
    gauss_points = np.array(
        [-0.8611363115940526, -0.3399810435848563, 0.3399810435848563, 0.8611363115940526]
    )
    gauss_weights = np.array(
        [0.3478548451374538, 0.6521451548625461, 0.6521451548625461, 0.3478548451374538]
    )
    lobatto_points = np.array([-1.0, -math.sqrt(3.0 / 7.0), 0.0, math.sqrt(3.0 / 7.0), 1.0])
    lobatto_weights = np.array([0.1, 49.0 / 90.0, 32.0 / 45.0, 49.0 / 90.0, 0.1])
    slopes = lagrange_slopes(gauss_points, gauss_points)
    volume = (2.0 / gauss_weights)[:, None] * slopes.T * gauss_weights[None, :]
    trace_low = lagrange_values(gauss_points, np.array([-1.0]))[0]
    trace_high = lagrange_values(gauss_points, np.array([1.0]))[0]
    stiffness = (
        2.0 * lobatto_weights[:, None] * lagrange_slopes(lobatto_points, lobatto_points)
    )
    lumped = np.array([0.2, lobatto_weights[1], lobatto_weights[2], lobatto_weights[3], 0.2])
    return {
        "weights": gauss_weights / 2.0,
        "volume": time_step * volume,
        "trace_low": trace_low,
        "trace_high": trace_high,
        "lift_low": time_step * 2.0 * trace_low / gauss_weights,
        "lift_high": time_step * 2.0 * trace_high / gauss_weights,
        "to_points": lagrange_values(lobatto_points, gauss_points),
        "stiffness": -time_step * stiffness / lumped[:, None],
    }


TABLES = basis_tables()
TABLE = {name: TABLES[name].tolist() for name in TABLES}


def lane_matrices(lanes):
    zones = lanes // 4
    shape = (lanes, lanes)
    volume, lift = np.zeros(shape), np.zeros(shape)
    minus, plus = np.zeros(shape), np.zeros(shape)
    stiff, interp = np.zeros(shape), np.zeros(shape)
    pick, spread = np.zeros(shape), np.zeros(shape)
    for zone in range(zones):
        at = 4 * zone
        before = 4 * ((zone - 1) % zones)
        for within in range(4):
            for source in range(4):
                volume[at + source, at + within] = TABLES["volume"][within, source]
                minus[before + source, at + within] = TABLES["trace_high"][source]
                plus[at + source, at + within] = TABLES["trace_low"][source]
            lift[at, at + within] = TABLES["lift_low"][within]
            lift[at, before + within] = -TABLES["lift_high"][within]
            pick[at, at + within] = 1.0
            spread[zone, at + within] = 1.0
            for source in range(5):
                interp[(at + source) % lanes, at + within] += TABLES["to_points"][within, source]
        for target in range(5):
            for source in range(5):
                stiff[(at + source) % lanes, (at + target) % lanes] += TABLES["stiffness"][
                    target, source
                ]
    square = np.concatenate([minus, plus, stiff, interp, pick, spread], axis=1)
    tall = np.concatenate([volume, lift], axis=0)
    return square.astype(np.float32), tall.astype(np.float32)


def spin(values, steps, axis):
    size = values.shape[axis]
    steps = steps % size
    return values if steps == 0 else pltpu.roll(values, steps, axis)


def rows_of(shape):
    return lax.broadcasted_iota(jnp.int32, shape, len(shape) - 2)


def low_half(shape):
    return rows_of(shape) < 4


def at_zone(shape, zone):
    return rows_of(shape) % 4 == zone


def combine(coefficients, terms):
    total = None
    for factor, term in zip(coefficients, terms):
        part = factor * term
        total = part if total is None else total + part
    return total


def parted(values):
    upper = values.astype(BF16)
    return upper, (values - upper.astype(F32)).astype(BF16)


def product(left, right):
    return jnp.dot(left, right, preferred_element_type=F32)


def by_zone(values):
    return values.reshape((2, 4) + values.shape[1:])


def from_zone(pieces):
    stacked = jnp.stack(pieces, axis=1)
    return stacked.reshape((8,) + stacked.shape[2:])


def pack_x_low(planes):
    mask = low_half((8, 128))
    return [jnp.where(mask, planes[t], spin(planes[t + 1], 4, 0)) for t in (0, 2)]


def pack_x_high(planes):
    mask = low_half((8, 128))
    return [jnp.where(mask, spin(planes[t], 4, 0), planes[t + 1]) for t in (0, 2)]


def unpack_x_high(packed):
    return [spin(packed[0], 4, 0), packed[0], spin(packed[1], 4, 0), packed[1]]


def unpack_x_low(packed):
    return [packed[0], spin(packed[0], 4, 0), packed[1], spin(packed[1], 4, 0)]


def pack_y(values, start):
    parts = by_zone(values)
    shape = (2, 8, 128)
    total = spin(parts[:, 3], 3 - start, 1)
    for place in (2, 1, 0):
        total = jnp.where(at_zone(shape, place), spin(parts[:, place], place - start, 1), total)
    return total


def unpack_y(packed, end):
    return from_zone([spin(packed, end - place, 1) for place in range(4)])


def kernel(
    counts,
    density, energy, velocity, mesh_velocity, density_low, density_high, energy_low, energy_high,
    square_hbm, tall_hbm,
    results,
    raw_u, raw_v, raw_m, square_in, tall_in, square, tall, bound_in, bound_rows, bounds,
    acc_v, sec_v, acc_f, sec_f, speed, face_x, face_y, face_z, trace_x, trace_y, zoned,
    out_dx, out_ux, out_dy, out_uy, in_dx, in_ux, in_dy, in_uy, out_corner, in_corner,
    out_vx, out_wx, out_vy, out_wy, in_vx, in_wx, in_vy, in_wy,
    out_dx2, out_ux2, out_dy2, out_uy2, in_dx2, in_ux2, in_dy2, in_uy2,
    out_vx2, out_wx2, out_vy2, out_wy2, in_vx2, in_wx2, in_vy2, in_wy2,
    done, load_sem, store_sem, send_sem, recv_sem,
):
    count_x, count_y = counts
    here_x, here_y = lax.axis_index("gx"), lax.axis_index("gy")
    west = lax.rem(here_x + count_x - 1, count_x)
    east = lax.rem(here_x + 1, count_x)
    south = lax.rem(here_y + count_y - 1, count_y)
    north = lax.rem(here_y + 1, count_y)
    to_west, to_east = (west, here_y), (east, here_y)
    to_south, to_north = (here_x, south), (here_x, north)
    to_corner, from_corner = (west, south), (east, north)

    loads = {}

    def load(name, source, target):
        copy = pltpu.make_async_copy(source, target, load_sem.at[sum(map(len, loads.values()))])
        copy.start()
        loads.setdefault(name, []).append(copy)

    def loaded(name):
        for copy in loads[name]:
            copy.wait()

    places = [(pl.ds(16 * half, 16), pl.ds(8 * half, 8)) for half in range(2)]
    for rows, block in places:
        load("mesh", mesh_velocity.at[:, block], raw_m.at[:, :, rows, :])
    load("tables", square_hbm, square_in)
    for rows, block in places:
        load("fields", density.at[block], raw_u.at[0, :, rows, :])
        load("fields", energy.at[block], raw_u.at[1, :, rows, :])
    for rows, block in places:
        load("velocity", velocity.at[:, block], raw_v.at[:, :, rows, :])
    load("tall", tall_hbm, tall_in)
    for index, source in enumerate((density_low, density_high, energy_low, energy_high)):
        load("bounds", source, bound_in.at[index])

    barrier = pltpu.get_barrier_semaphore()
    for peer in (to_west, to_east, to_south, to_north, to_corner, from_corner):
        pl.semaphore_signal(barrier, inc=1, device_id=peer, device_id_type=MESH)

    loaded("tables")
    for column, target, gap in ((0, 0, 2), (1, 1, 2), (2, 4, 1), (3, 6, 1), (4, 8, 0), (5, 9, 0)):
        upper, lower = parted(square_in[:, 128 * column : 128 * (column + 1)])
        square[:, 128 * target : 128 * (target + 1)] = upper
        if gap:
            square[:, 128 * (target + gap) : 128 * (target + gap + 1)] = lower

    full = (8, 8, 128)
    plane = (8, 128)
    low_rows = low_half(plane)
    stiff = TABLE["stiffness"]
    zero = jnp.zeros(plane, F32)

    def field_at(which, j):
        return raw_u[which, :, pl.ds(j, 8, stride=4), :]

    def velocity_at(which, j):
        return raw_v[which, :, pl.ds(j, 8, stride=4), :]

    def mesh_at(which, j):
        return raw_m[which, :, pl.ds(j, 8, stride=4), :]

    def lanes_product(values, column, narrow=1):
        upper, lower = parted(jnp.concatenate([part.reshape(64, 128) for part in values], 0))
        wide = square[:, 128 * column : 128 * (column + 2)]
        both = product(upper, wide)
        total = both[:, :128] + both[:, 128:] + product(lower, wide[:, :128])
        return [total[64 * j : 64 * (j + 1)].reshape(full) for j in range(4)]

    def field_traces(which, values):
        for j in range(4):
            parts = by_zone(values[j])
            places = [parts[:, i] for i in range(4)]
            trace_x[which, 0, j] = combine(TABLE["trace_low"], places)
            trace_x[which, 1, j] = combine(TABLE["trace_high"], places)
        trace_y[which, 0] = combine(TABLE["trace_low"], values)
        trace_y[which, 1] = combine(TABLE["trace_high"], values)

    def put_pair(target, item, pair):
        target[item, 0] = pair[0]
        target[item, 1] = pair[1]

    def pack_field(which, item, buffers):
        west_to, east_to, south_to, north_to = buffers
        put_pair(west_to, item, pack_x_low([trace_x[which, 0, j, 0] for j in range(4)]))
        put_pair(east_to, item, pack_x_high([trace_x[which, 1, j, 1] for j in range(4)]))
        south_to[item] = pack_y(trace_y[which, 0], 0)
        north_to[item] = pack_y(trace_y[which, 1], 3)

    def pack_velocity(values, item, buffers):
        west_to, east_to, south_to, north_to = buffers
        put_pair(west_to, item, pack_x_low([values[j][0] for j in range(4)]))
        closing = [
            combine(stiff[4][:4], [values[j][4 + i] for i in range(4)]) for j in range(4)
        ]
        put_pair(east_to, item, pack_x_high(closing))
        south_to[item] = pack_y(values[0], 0)
        north_to[item] = pack_y(combine(stiff[4][:4], values), 3)

    loaded("mesh")
    corner = zero
    for item in range(4):
        values = [mesh_at(min(item, 2), j) for j in range(4)]
        if item < 3:
            values = lanes_product(values, 6)
        else:
            upper, lower = parted(jnp.concatenate([v.reshape(64, 128) for v in values], 0))
            picker = square[:, 128 * 8 : 128 * 9]
            total = product(upper, picker) + product(lower, picker)
            values = [total[64 * j : 64 * (j + 1)].reshape(full) for j in range(4)]
        for j in range(4):
            zoned[item, j] = values[j]
        put_pair(out_dx, 2 + item, pack_x_low([values[j][0] for j in range(4)]))
        out_dy[2 + item] = pack_y(values[0], 0)
        corner = jnp.where(rows_of(plane) == item, spin(values[0][0], item, 0), corner)
    out_corner[...] = corner
    loaded("fields")
    for which in range(2):
        field_traces(which, [field_at(which, j) for j in range(4)])
        pack_field(which, which, (out_dx, out_ux, out_dy, out_uy))

    pl.semaphore_wait(barrier, 6)
    copies = []
    peers = (to_west, to_east, to_south, to_north)

    def send(source, target, peer):
        copy = pltpu.make_async_remote_copy(
            src_ref=source, dst_ref=target,
            send_sem=send_sem.at[len(copies)], recv_sem=recv_sem.at[len(copies)],
            device_id=peer, device_id_type=MESH,
        )
        copy.start()
        copies.append(copy)
        return copy

    def send_all(sources, targets):
        return [send(*triple) for triple in zip(sources, targets, peers)]

    arrived_a, arrived_b = (in_dx, in_ux, in_dy, in_uy), (in_dx2, in_ux2, in_dy2, in_uy2)
    leaving_a, leaving_b = (out_dx, out_ux, out_dy, out_uy), (out_dx2, out_ux2, out_dy2, out_uy2)
    arrived_c, arrived_d = (in_vx, in_wx, in_vy, in_wy), (in_vx2, in_wx2, in_vy2, in_wy2)
    leaving_c, leaving_d = (out_vx, out_wx, out_vy, out_wy), (out_vx2, out_wx2, out_vy2, out_wy2)
    first = send_all(leaving_a, arrived_a) + [send(out_corner, in_corner, to_corner)]
    loaded("velocity")
    for which in range(3):
        pack_velocity([velocity_at(which, j) for j in range(4)], which, leaving_c)
    first_v = send_all(leaving_c, arrived_c)

    loaded("tall")
    upper, lower = parted(tall_in[...])
    tall[:, :128] = upper
    tall[:, 128:] = lower
    loaded("bounds")
    bound_rows[...] = jnp.zeros((4, 2, 8, 128), F32)
    for index in range(4):
        for zone in range(4):
            bound_rows[index, zone % 2, pl.ds(4 * (zone // 2), 4), pl.ds(0, 32)] = bound_in[
                index, zone
            ]
    values = bound_rows[...].reshape(64, 128)
    spreader = square[:, 128 * 9 : 128 * 10]
    upper = values.astype(BF16)
    rest = values - upper.astype(F32)
    middle = rest.astype(BF16)
    lowest = (rest - middle.astype(F32)).astype(BF16)
    values = product(upper, spreader) + (product(middle, spreader) + product(lowest, spreader))
    bounds[...] = values.reshape(4, 2, 8, 128)

    def velocity_before(which, values, base, scale):
        along_z = lanes_product(values, 4)
        closing = combine(stiff[4][:4], values)
        after = jnp.where(at_zone(full, 3), 0.0, spin(values[0], 7, 1))
        carried = jnp.where(at_zone(full, 0), 0.0, spin(closing, 1, 1))
        for j in range(4):
            parts = by_zone(values[j])
            places = [parts[:, i] for i in range(4)]
            ending = combine(stiff[4][:4], places)
            next_plane = jnp.stack(
                [parts[1, 0], jnp.where(low_rows, spin(parts[0, 0], 4, 0), 0.0)]
            )
            last_end = jnp.stack([jnp.where(low_rows, 0.0, spin(ending[1], 4, 0)), ending[0]])
            sums = []
            for a in range(4):
                factors = list(stiff[a])
                if a == 0:
                    factors[0] += stiff[4][4]
                total = combine(factors, places + [next_plane])
                sums.append(total + last_end if a == 0 else total)
            along_x = from_zone(sums)
            factors = list(stiff[j])
            if j == 0:
                factors[0] += stiff[4][4]
            along_y = combine(factors, values + [after])
            if j == 0:
                along_y = along_y + carried
            rate = (
                mesh_at(0, j) * along_x + mesh_at(1, j) * along_y + mesh_at(2, j) * along_z[j]
            )
            acc_v[which, j] = base(j) + (rate if scale == 1.0 else scale * rate)

    def velocity_after(which, scale, item, buffers):
        from_east, from_west, from_north, from_south = buffers
        later = unpack_x_high([from_east[item, 0], from_east[item, 1]])
        earlier = unpack_x_low([from_west[item, 0], from_west[item, 1]])
        above = jnp.where(at_zone(full, 3), unpack_y(from_north[item], 3), 0.0)
        below = jnp.where(at_zone(full, 0), unpack_y(from_south[item], 0), 0.0)
        done = []
        for j in range(4):
            ahead = jnp.where(low_rows, 0.0, later[j])
            behind = jnp.where(low_rows, earlier[j], 0.0)
            extra_x = jnp.stack(
                [scale * behind, zero, zero, zero]
                + [(scale * stiff[a][4]) * ahead for a in range(4)]
            )
            extra_y = (scale * stiff[j][4]) * above
            if j == 0:
                extra_y = extra_y + scale * below
            done.append(acc_v[which, j] + mesh_at(0, j) * extra_x + mesh_at(1, j) * extra_y)
        return done

    points = TABLE["to_points"]

    def mesh_before(item):
        values = [zoned[item, j] for j in range(4)]
        across = []
        for b in range(4):
            parts = by_zone(values[b])
            places = [parts[:, a] for a in range(4)]
            inner = jnp.where(low_rows, spin(parts[0, 0], 4, 0), 0.0)
            places.append(jnp.stack([parts[1, 0], inner]))
            across.append(from_zone([combine(points[i], places) for i in range(4)]))
        last = at_zone(full, 3)
        across.append(jnp.where(last, 0.0, spin(across[0], 7, 1)))
        for j in range(4):
            result = combine(points[j], across)
            if item < 3:
                speed[item, j] = result
            else:
                face_z[j] = result
        if item == 0:
            for q in range(2):
                edge = [values[b][4 * q] for b in range(4)]
                edge.append(jnp.where(at_zone(plane, 3), 0.0, spin(edge[0], 7, 0)))
                for j in range(4):
                    face_x[q, j] = combine(points[j], edge)
        if item == 1:
            face_y[0] = across[0]
            face_y[1] = across[4]

    def mesh_after(item):
        rows = rows_of(plane)
        later = unpack_x_high([in_dx[2 + item, 0], in_dx[2 + item, 1]])
        later = [jnp.where(low_rows, 0.0, value) for value in later]
        far = jnp.where(at_zone(plane, 3), 0.0, spin(later[0], 7, 0))
        far = jnp.where(rows == 7, spin(in_corner[...], 7 - item, 0), far)
        later.append(jnp.where(low_rows, 0.0, far))
        above = jnp.where(at_zone(full, 3), unpack_y(in_dy[2 + item], 3), 0.0)
        parts = by_zone(above)
        places = [parts[:, a] for a in range(4)]
        places.append(
            jnp.stack([parts[1, 0], jnp.where(low_rows, spin(parts[0, 0], 4, 0), 0.0)])
        )
        across = from_zone([combine(points[i], places) for i in range(4)])
        edge = [combine(points[j], later) for j in range(4)]
        for j in range(4):
            extra = points[j][4] * across
            extra = jnp.concatenate(
                [extra[:4], jnp.stack([extra[4 + i] + points[i][4] * edge[j] for i in range(4)])]
            )
            if item < 3:
                speed[item, j] += extra
            else:
                face_z[j] += extra
        if item == 0:
            for j in range(4):
                lowest = face_x[0, j] + points[j][4] * above[0]
                face_x[0, j] = lowest
                face_x[1, j] += points[j][4] * above[4]
                face_x[2, j] = jnp.where(low_rows, spin(lowest, 4, 0), edge[j])
        if item == 1:
            for side, halo, plain in ((0, later[0], None), (1, later[4], across)):
                for x in range(8):
                    if x < 4 and plain is None:
                        continue
                    value = face_y[side, x]
                    if plain is not None:
                        value = value + plain[x]
                    if x >= 4:
                        value = value + points[x - 4][4] * halo
                    face_y[side, x] = value

    def upwind(face, minus_side, plus_side):
        return jnp.maximum(face, 0.0) * minus_side + jnp.minimum(face, 0.0) * plus_side

    def field_before(which, values, base, scale):
        upper, lower = parted(jnp.concatenate([part.reshape(64, 128) for part in values], 0))
        wide = square[:, 0:256]
        sides = product(upper, wide) + product(lower, wide) + product(upper, square[:, 256:512])
        flux = [
            upwind(
                face_z[j],
                sides[64 * j : 64 * (j + 1), :128].reshape(full),
                sides[64 * j : 64 * (j + 1), 128:].reshape(full),
            ).reshape(64, 128)
            for j in range(4)
        ]
        moved = [(speed[2, j] * values[j]).reshape(64, 128) for j in range(4)]
        both = jnp.concatenate([jnp.concatenate(moved, 0), jnp.concatenate(flux, 0)], 1)
        upper, lower = parted(both)
        sums = product(upper, tall[...])
        along_z = sums[:, :128] + sums[:, 128:] + product(lower, tall[:, :128])
        moved = [speed[1, j] * values[j] for j in range(4)]
        for j in range(4):
            parts = by_zone(speed[0, j] * values[j])
            places = [parts[:, i] for i in range(4)]
            along_x = from_zone([combine(TABLE["volume"][i], places) for i in range(4)])
            along_y = combine(TABLE["volume"][j], moved)
            rate = along_x + along_y + along_z[64 * j : 64 * (j + 1)].reshape(full)
            acc_f[which, j] = base(j) + (rate if scale == 1.0 else scale * rate)

    def in_group(values, join):
        lane = lax.broadcasted_iota(jnp.int32, values.shape, 2)
        partner = jnp.where(lane % 2 == 0, spin(values, 127, 2), spin(values, 1, 2))
        values = join(values, partner)
        partner = jnp.where(lane // 2 % 2 == 0, spin(values, 126, 2), spin(values, 2, 2))
        return join(values, partner)

    def limited(which, values):
        weights = TABLE["weights"]
        across = by_zone(combine(weights, values))
        mean = combine(weights, [across[:, i] for i in range(4)])
        lane = lax.broadcasted_iota(jnp.int32, (2, 8, 128), 2) % 4
        middle = (lane == 1) | (lane == 2)
        mean = in_group(mean * jnp.where(middle, weights[1], weights[0]), jnp.add)
        top = functools.reduce(jnp.maximum, values)
        bottom = functools.reduce(jnp.minimum, values)
        top, bottom = by_zone(top), by_zone(bottom)
        top = functools.reduce(jnp.maximum, [top[:, i] for i in range(4)])
        bottom = functools.reduce(jnp.minimum, [bottom[:, i] for i in range(4)])
        rise = in_group(top, jnp.maximum) - mean
        fall = in_group(bottom, jnp.minimum) - mean
        low, high = bounds[2 * which], bounds[2 * which + 1]
        theta = jnp.minimum(
            (high - mean) / (rise + limit_eps), (mean - low) / (limit_eps - fall)
        )
        theta = jnp.clip(theta, 0.0, 1.0)
        result = []
        for j in range(4):
            parts = by_zone(values[j])
            result.append(
                from_zone([mean + theta * (parts[:, i] - mean) for i in range(4)])
            )
        return result

    def field_after(which, scale, item, buffers):
        from_east, from_west, from_north, from_south = buffers
        later = unpack_x_high([from_east[item, 0], from_east[item, 1]])
        earlier = unpack_x_low([from_west[item, 0], from_west[item, 1]])
        low_lift = [scale * factor for factor in TABLE["lift_low"]]
        high_lift = [-scale * factor for factor in TABLE["lift_high"]]
        low, high = trace_y[which, 0], trace_y[which, 1]
        before = jnp.where(at_zone(full, 0), unpack_y(from_south[item], 0), spin(high, 1, 1))
        after = jnp.where(at_zone(full, 3), unpack_y(from_north[item], 3), spin(low, 7, 1))
        lower_y = upwind(face_y[0], before, low)
        upper_y = upwind(face_y[1], high, after)
        values = []
        for j in range(4):
            low, high = trace_x[which, 0, j], trace_x[which, 1, j]
            before = jnp.where(low_rows, earlier[j], spin(high[1], 4, 0))
            after = jnp.where(low_rows, spin(low[0], 4, 0), later[j])
            flux = [
                upwind(face_x[0, j], before, low[0]),
                upwind(face_x[1, j], high[0], low[1]),
                upwind(face_x[2, j], high[1], after),
            ]
            lower_x, upper_x = jnp.stack(flux[:2]), jnp.stack(flux[1:])
            lift = from_zone(
                [low_lift[i] * lower_x + high_lift[i] * upper_x for i in range(4)]
            )
            values.append(
                acc_f[which, j] + lift + (low_lift[j] * lower_y + high_lift[j] * upper_y)
            )
        return limited(which, values)

    for item in range(4):
        mesh_before(item)
    for which in range(3):
        values = [velocity_at(which, j) for j in range(4)]
        velocity_before(which, values, lambda j: values[j], 1.0)
    for copy in first:
        copy.wait_recv()
    for item in range(4):
        mesh_after(item)
    for which in range(2):
        values = [field_at(which, j) for j in range(4)]
        field_before(which, values, lambda j: values[j], 1.0)
        values = field_after(which, 1.0, which, arrived_a)
        for j in range(4):
            sec_f[which, j] = values[j]
        field_traces(which, values)
        pack_field(which, which, leaving_b)
    second = send_all(leaving_b, arrived_b)
    for copy in first_v:
        copy.wait_recv()
    for which in range(3):
        values = velocity_after(which, 1.0, which, arrived_c)
        for j in range(4):
            sec_v[which, j] = values[j]
        pack_velocity(values, which, leaving_d)
    second_v = send_all(leaving_d, arrived_d)

    for which in range(2):
        values = [sec_f[which, j] for j in range(4)]
        field_before(which, values, lambda j: 0.5 * field_at(which, j) + 0.5 * values[j], 0.5)
    for which in range(3):
        values = [sec_v[which, j] for j in range(4)]
        velocity_before(
            which, values, lambda j: 0.5 * velocity_at(which, j) + 0.5 * values[j], 0.5
        )
    stores = []

    def store(source, target):
        copy = pltpu.make_async_copy(source, target, store_sem.at[len(stores)])
        copy.start()
        stores.append(copy)

    for copy in second:
        copy.wait_recv()
    for which in range(2):
        values = field_after(which, 0.5, which, arrived_b)
        for j in range(4):
            done[which, :, pl.ds(j, 8, stride=4), :] = values[j]
        store(done.at[which], results.at[which])
    for copy in second_v:
        copy.wait_recv()
    for which in range(3):
        values = velocity_after(which, 0.5, which, arrived_d)
        for j in range(4):
            done[2 + which, :, pl.ds(j, 8, stride=4), :] = values[j]
        store(done.at[2 + which], results.at[2 + which])
    for copy in copies:
        copy.wait_send()
    for copy in stores:
        copy.wait()


def unfold(results, new_density, new_energy, new_velocity, store_sem):
    copies = []
    for half in range(2):
        rows, block = pl.ds(16 * half, 16), pl.ds(8 * half, 8)
        for source, target in (
            (results.at[0, :, rows, :], new_density.at[block]),
            (results.at[1, :, rows, :], new_energy.at[block]),
            (results.at[pl.ds(2, 3), :, rows, :], new_velocity.at[:, block]),
        ):
            copy = pltpu.make_async_copy(source, target, store_sem.at[len(copies)])
            copy.start()
            copies.append(copy)
    for copy in copies:
        copy.wait()


def solution(mesh):
    counts = (mesh.shape["gx"], mesh.shape["gy"])
    square, tall = lane_matrices(128)

    def on_device(*arguments):
        vmem = lambda *shape: pltpu.VMEM(shape, F32)
        scratch = [
            vmem(2, 8, 32, 128), vmem(3, 8, 32, 128), vmem(3, 8, 32, 128),
            vmem(*square.shape), vmem(*tall.shape),
            pltpu.VMEM((128, 1280), BF16), pltpu.VMEM((256, 256), BF16),
            vmem(4, 4, 4, 32), vmem(4, 2, 8, 128), vmem(4, 2, 8, 128),
            vmem(3, 4, 8, 8, 128), vmem(3, 4, 8, 8, 128),
            vmem(2, 4, 8, 8, 128), vmem(2, 4, 8, 8, 128),
            vmem(3, 4, 8, 8, 128), vmem(3, 4, 8, 128), vmem(2, 8, 8, 128), vmem(4, 8, 8, 128),
            vmem(2, 2, 4, 2, 8, 128), vmem(2, 2, 8, 8, 128), vmem(4, 4, 8, 8, 128),
        ]
        sides = [vmem(items, 2, 8, 128) for items in (6, 2, 6, 2)]
        scratch += sides + sides + [vmem(8, 128)] * 2
        for items in (3, 2, 3):
            scratch += [vmem(items, 2, 8, 128)] * 8
        scratch += [
            vmem(5, 8, 32, 128),
            pltpu.SemaphoreType.DMA((14,)),
            pltpu.SemaphoreType.DMA((5,)),
            pltpu.SemaphoreType.DMA((17,)),
            pltpu.SemaphoreType.DMA((17,)),
        ]
        results = pl.pallas_call(
            functools.partial(kernel, counts),
            out_shape=jax.ShapeDtypeStruct((5, 8, 32, 128), F32),
            in_specs=[pl.BlockSpec(memory_space=pltpu.HBM)] * 10,
            out_specs=pl.BlockSpec(memory_space=pltpu.HBM),
            scratch_shapes=scratch,
            compiler_params=pltpu.CompilerParams(
                collective_id=0, has_side_effects=True, vmem_limit_bytes=56 * 1024 * 1024
            ),
        )(*arguments, jnp.asarray(square), jnp.asarray(tall))
        return pl.pallas_call(
            unfold,
            out_shape=[jax.ShapeDtypeStruct(value.shape, F32) for value in arguments[:3]],
            in_specs=[pl.BlockSpec(memory_space=pltpu.HBM)],
            out_specs=[pl.BlockSpec(memory_space=pltpu.HBM)] * 3,
            scratch_shapes=[pltpu.SemaphoreType.DMA((6,))],
            compiler_params=pltpu.CompilerParams(vmem_limit_bytes=56 * 1024 * 1024),
        )(results)

    fields, vectors = P("gx", "gy", None), P(None, "gx", "gy", None)
    return jax.shard_map(
        on_device,
        mesh=mesh,
        in_specs=(fields, fields, vectors, vectors, fields, fields, fields, fields),
        out_specs=(fields, fields, vectors),
        check_vma=False,
    )
```

```python
import functools
import math

import jax
import jax.numpy as jnp
import numpy as np
from jax import lax
from jax.experimental import pallas as pl
from jax.experimental.pallas import tpu as pltpu
from jax.sharding import PartitionSpec as P

MESH = pl.DeviceIdType.MESH
F32 = jnp.float32
BF16 = jnp.bfloat16
time_step = 0.02
limit_eps = 1e-06


def lagrange_values(node_set, points):
    result = np.ones((len(points), len(node_set)))
    for column in range(len(node_set)):
        for partner in range(len(node_set)):
            if partner != column:
                result[:, column] = (
                    result[:, column]
                    * (points - node_set[partner])
                    / (node_set[column] - node_set[partner])
                )
    return result


def lagrange_slopes(node_set, points):
    node_total = len(node_set)
    result = np.zeros((len(points), node_total))
    for column in range(node_total):
        for skipped in range(node_total):
            if skipped != column:
                factor = np.ones(len(points)) / (node_set[column] - node_set[skipped])
                for partner in range(node_total):
                    if partner != column and partner != skipped:
                        factor = (
                            factor
                            * (points - node_set[partner])
                            / (node_set[column] - node_set[partner])
                        )
                result[:, column] = result[:, column] + factor
    return result


def basis_tables():
    gauss_points = np.array(
        [-0.8611363115940526, -0.3399810435848563, 0.3399810435848563, 0.8611363115940526]
    )
    gauss_weights = np.array(
        [0.3478548451374538, 0.6521451548625461, 0.6521451548625461, 0.3478548451374538]
    )
    lobatto_points = np.array([-1.0, -math.sqrt(3.0 / 7.0), 0.0, math.sqrt(3.0 / 7.0), 1.0])
    lobatto_weights = np.array([0.1, 49.0 / 90.0, 32.0 / 45.0, 49.0 / 90.0, 0.1])
    slopes = lagrange_slopes(gauss_points, gauss_points)
    volume = (2.0 / gauss_weights)[:, None] * slopes.T * gauss_weights[None, :]
    trace_low = lagrange_values(gauss_points, np.array([-1.0]))[0]
    trace_high = lagrange_values(gauss_points, np.array([1.0]))[0]
    stiffness = (
        2.0 * lobatto_weights[:, None] * lagrange_slopes(lobatto_points, lobatto_points)
    )
    lumped = np.array([0.2, lobatto_weights[1], lobatto_weights[2], lobatto_weights[3], 0.2])
    return {
        "weights": gauss_weights / 2.0,
        "volume": time_step * volume,
        "trace_low": trace_low,
        "trace_high": trace_high,
        "lift_low": time_step * 2.0 * trace_low / gauss_weights,
        "lift_high": time_step * 2.0 * trace_high / gauss_weights,
        "to_points": lagrange_values(lobatto_points, gauss_points),
        "stiffness": -time_step * stiffness / lumped[:, None],
    }


TABLES = basis_tables()
TABLE = {name: TABLES[name].tolist() for name in TABLES}


def lane_matrices(lanes):
    zones = lanes // 4
    shape = (lanes, lanes)
    volume, lift = np.zeros(shape), np.zeros(shape)
    minus, plus = np.zeros(shape), np.zeros(shape)
    stiff, interp = np.zeros(shape), np.zeros(shape)
    pick, spread = np.zeros(shape), np.zeros(shape)
    for zone in range(zones):
        at = 4 * zone
        before = 4 * ((zone - 1) % zones)
        for within in range(4):
            for source in range(4):
                volume[at + source, at + within] = TABLES["volume"][within, source]
                minus[before + source, at + within] = TABLES["trace_high"][source]
                plus[at + source, at + within] = TABLES["trace_low"][source]
            lift[at, at + within] = TABLES["lift_low"][within]
            lift[at, before + within] = -TABLES["lift_high"][within]
            pick[at, at + within] = 1.0
            spread[zone, at + within] = 1.0
            for source in range(5):
                interp[(at + source) % lanes, at + within] += TABLES["to_points"][within, source]
        for target in range(5):
            for source in range(5):
                stiff[(at + source) % lanes, (at + target) % lanes] += TABLES["stiffness"][
                    target, source
                ]
    square = np.concatenate([minus, plus, stiff, interp, pick, spread], axis=1)
    tall = np.concatenate([volume, lift], axis=0)
    return square.astype(np.float32), tall.astype(np.float32)


def spin(values, steps, axis):
    size = values.shape[axis]
    steps = steps % size
    return values if steps == 0 else pltpu.roll(values, steps, axis)


def rows_of(shape):
    return lax.broadcasted_iota(jnp.int32, shape, len(shape) - 2)


def low_half(shape):
    return rows_of(shape) < 4


def at_zone(shape, zone):
    return rows_of(shape) % 4 == zone


def combine(coefficients, terms):
    total = None
    for factor, term in zip(coefficients, terms):
        part = factor * term
        total = part if total is None else total + part
    return total


def parted(values):
    upper = values.astype(BF16)
    return upper, (values - upper.astype(F32)).astype(BF16)


def product(left, right):
    return jnp.dot(left, right, preferred_element_type=F32)


def by_zone(values):
    return values.reshape((2, 4) + values.shape[1:])


def from_zone(pieces):
    stacked = jnp.stack(pieces, axis=1)
    return stacked.reshape((8,) + stacked.shape[2:])


def pack_x_low(planes):
    mask = low_half((8, 128))
    return [jnp.where(mask, planes[t], spin(planes[t + 1], 4, 0)) for t in (0, 2)]


def pack_x_high(planes):
    mask = low_half((8, 128))
    return [jnp.where(mask, spin(planes[t], 4, 0), planes[t + 1]) for t in (0, 2)]


def unpack_x_high(packed):
    return [spin(packed[0], 4, 0), packed[0], spin(packed[1], 4, 0), packed[1]]


def unpack_x_low(packed):
    return [packed[0], spin(packed[0], 4, 0), packed[1], spin(packed[1], 4, 0)]


def pack_y(values, start):
    parts = by_zone(values)
    shape = (2, 8, 128)
    total = spin(parts[:, 3], 3 - start, 1)
    for place in (2, 1, 0):
        total = jnp.where(at_zone(shape, place), spin(parts[:, place], place - start, 1), total)
    return total


def unpack_y(packed, end):
    return from_zone([spin(packed, end - place, 1) for place in range(4)])


def kernel(
    counts,
    density, energy, velocity, mesh_velocity, density_low, density_high, energy_low, energy_high,
    square_hbm, tall_hbm,
    results,
    raw_u, raw_v, raw_m, square_in, tall_in, square, tall, bound_in, bound_rows, bounds,
    acc_v, sec_v, acc_f, sec_f, speed, face_x, face_y, face_z, trace_x, trace_y, zoned,
    out_dx, out_ux, out_dy, out_uy, in_dx, in_ux, in_dy, in_uy, out_corner, in_corner,
    out_vx, out_wx, out_vy, out_wy, in_vx, in_wx, in_vy, in_wy,
    out_dx2, out_ux2, out_dy2, out_uy2, in_dx2, in_ux2, in_dy2, in_uy2,
    out_vx2, out_wx2, out_vy2, out_wy2, in_vx2, in_wx2, in_vy2, in_wy2,
    load_sem, send_sem, recv_sem,
):
    count_x, count_y = counts
    here_x, here_y = lax.axis_index("gx"), lax.axis_index("gy")
    west = lax.rem(here_x + count_x - 1, count_x)
    east = lax.rem(here_x + 1, count_x)
    south = lax.rem(here_y + count_y - 1, count_y)
    north = lax.rem(here_y + 1, count_y)
    to_west, to_east = (west, here_y), (east, here_y)
    to_south, to_north = (here_x, south), (here_x, north)
    to_corner, from_corner = (west, south), (east, north)

    loads = {}

    def load(name, source, target):
        copy = pltpu.make_async_copy(source, target, load_sem.at[sum(map(len, loads.values()))])
        copy.start()
        loads.setdefault(name, []).append(copy)

    def loaded(name):
        for copy in loads[name]:
            copy.wait()

    places = [(pl.ds(16 * half, 16), pl.ds(8 * half, 8)) for half in range(2)]
    for rows, block in places:
        load("mesh", mesh_velocity.at[:, block], raw_m.at[:, :, rows, :])
    load("tables", square_hbm, square_in)
    for rows, block in places:
        load("fields", density.at[block], raw_u.at[0, :, rows, :])
        load("fields", energy.at[block], raw_u.at[1, :, rows, :])
    for rows, block in places:
        load("velocity", velocity.at[:, block], raw_v.at[:, :, rows, :])
    load("tall", tall_hbm, tall_in)
    for index, source in enumerate((density_low, density_high, energy_low, energy_high)):
        load("bounds", source, bound_in.at[index])

    barrier = pltpu.get_barrier_semaphore()
    for peer in (to_west, to_east, to_south, to_north, to_corner, from_corner):
        pl.semaphore_signal(barrier, inc=1, device_id=peer, device_id_type=MESH)

    loaded("tables")
    for column, target, gap in ((0, 0, 2), (1, 1, 2), (2, 4, 1), (3, 6, 1), (4, 8, 0), (5, 9, 0)):
        upper, lower = parted(square_in[:, 128 * column : 128 * (column + 1)])
        square[:, 128 * target : 128 * (target + 1)] = upper
        if gap:
            square[:, 128 * (target + gap) : 128 * (target + gap + 1)] = lower

    full = (8, 8, 128)
    plane = (8, 128)
    low_rows = low_half(plane)
    stiff = TABLE["stiffness"]
    zero = jnp.zeros(plane, F32)

    def field_at(which, j):
        return raw_u[which, :, pl.ds(j, 8, stride=4), :]

    def velocity_at(which, j):
        return raw_v[which, :, pl.ds(j, 8, stride=4), :]

    def mesh_at(which, j):
        return raw_m[which, :, pl.ds(j, 8, stride=4), :]

    def lanes_product(values, column, narrow=1):
        upper, lower = parted(jnp.concatenate([part.reshape(64, 128) for part in values], 0))
        wide = square[:, 128 * column : 128 * (column + 2)]
        both = product(upper, wide)
        total = both[:, :128] + both[:, 128:] + product(lower, wide[:, :128])
        return [total[64 * j : 64 * (j + 1)].reshape(full) for j in range(4)]

    def field_traces(which, values):
        for j in range(4):
            parts = by_zone(values[j])
            places = [parts[:, i] for i in range(4)]
            trace_x[which, 0, j] = combine(TABLE["trace_low"], places)
            trace_x[which, 1, j] = combine(TABLE["trace_high"], places)
        trace_y[which, 0] = combine(TABLE["trace_low"], values)
        trace_y[which, 1] = combine(TABLE["trace_high"], values)

    def put_pair(target, item, pair):
        target[item, 0] = pair[0]
        target[item, 1] = pair[1]

    def pack_field(which, item, buffers):
        west_to, east_to, south_to, north_to = buffers
        put_pair(west_to, item, pack_x_low([trace_x[which, 0, j, 0] for j in range(4)]))
        put_pair(east_to, item, pack_x_high([trace_x[which, 1, j, 1] for j in range(4)]))
        south_to[item] = pack_y(trace_y[which, 0], 0)
        north_to[item] = pack_y(trace_y[which, 1], 3)

    def pack_velocity(values, item, buffers):
        west_to, east_to, south_to, north_to = buffers
        put_pair(west_to, item, pack_x_low([values[j][0] for j in range(4)]))
        closing = [
            combine(stiff[4][:4], [values[j][4 + i] for i in range(4)]) for j in range(4)
        ]
        put_pair(east_to, item, pack_x_high(closing))
        south_to[item] = pack_y(values[0], 0)
        north_to[item] = pack_y(combine(stiff[4][:4], values), 3)

    loaded("mesh")
    corner = zero
    for item in range(4):
        values = [mesh_at(min(item, 2), j) for j in range(4)]
        if item < 3:
            values = lanes_product(values, 6)
        else:
            upper, lower = parted(jnp.concatenate([v.reshape(64, 128) for v in values], 0))
            picker = square[:, 128 * 8 : 128 * 9]
            total = product(upper, picker) + product(lower, picker)
            values = [total[64 * j : 64 * (j + 1)].reshape(full) for j in range(4)]
        for j in range(4):
            zoned[item, j] = values[j]
        put_pair(out_dx, 2 + item, pack_x_low([values[j][0] for j in range(4)]))
        out_dy[2 + item] = pack_y(values[0], 0)
        corner = jnp.where(rows_of(plane) == item, spin(values[0][0], item, 0), corner)
    out_corner[...] = corner
    loaded("fields")
    for which in range(2):
        field_traces(which, [field_at(which, j) for j in range(4)])
        pack_field(which, which, (out_dx, out_ux, out_dy, out_uy))

    pl.semaphore_wait(barrier, 6)
    copies = []
    peers = (to_west, to_east, to_south, to_north)

    def send(source, target, peer):
        copy = pltpu.make_async_remote_copy(
            src_ref=source, dst_ref=target,
            send_sem=send_sem.at[len(copies)], recv_sem=recv_sem.at[len(copies)],
            device_id=peer, device_id_type=MESH,
        )
        copy.start()
        copies.append(copy)
        return copy

    def send_all(sources, targets):
        return [send(*triple) for triple in zip(sources, targets, peers)]

    arrived_a, arrived_b = (in_dx, in_ux, in_dy, in_uy), (in_dx2, in_ux2, in_dy2, in_uy2)
    leaving_a, leaving_b = (out_dx, out_ux, out_dy, out_uy), (out_dx2, out_ux2, out_dy2, out_uy2)
    arrived_c, arrived_d = (in_vx, in_wx, in_vy, in_wy), (in_vx2, in_wx2, in_vy2, in_wy2)
    leaving_c, leaving_d = (out_vx, out_wx, out_vy, out_wy), (out_vx2, out_wx2, out_vy2, out_wy2)
    first = send_all(leaving_a, arrived_a) + [send(out_corner, in_corner, to_corner)]
    loaded("velocity")
    for which in range(3):
        pack_velocity([velocity_at(which, j) for j in range(4)], which, leaving_c)
    first_v = send_all(leaving_c, arrived_c)

    loaded("tall")
    upper, lower = parted(tall_in[...])
    tall[:, :128] = upper
    tall[:, 128:] = lower
    loaded("bounds")
    bound_rows[...] = jnp.zeros((4, 2, 8, 128), F32)
    for index in range(4):
        for zone in range(4):
            bound_rows[index, zone % 2, pl.ds(4 * (zone // 2), 4), pl.ds(0, 32)] = bound_in[
                index, zone
            ]
    values = bound_rows[...].reshape(64, 128)
    spreader = square[:, 128 * 9 : 128 * 10]
    upper = values.astype(BF16)
    rest = values - upper.astype(F32)
    middle = rest.astype(BF16)
    lowest = (rest - middle.astype(F32)).astype(BF16)
    values = product(upper, spreader) + (product(middle, spreader) + product(lowest, spreader))
    bounds[...] = values.reshape(4, 2, 8, 128)

    def velocity_before(which, values, base, scale):
        along_z = lanes_product(values, 4)
        closing = combine(stiff[4][:4], values)
        after = jnp.where(at_zone(full, 3), 0.0, spin(values[0], 7, 1))
        carried = jnp.where(at_zone(full, 0), 0.0, spin(closing, 1, 1))
        for j in range(4):
            parts = by_zone(values[j])
            places = [parts[:, i] for i in range(4)]
            ending = combine(stiff[4][:4], places)
            next_plane = jnp.stack(
                [parts[1, 0], jnp.where(low_rows, spin(parts[0, 0], 4, 0), 0.0)]
            )
            last_end = jnp.stack([jnp.where(low_rows, 0.0, spin(ending[1], 4, 0)), ending[0]])
            sums = []
            for a in range(4):
                factors = list(stiff[a])
                if a == 0:
                    factors[0] += stiff[4][4]
                total = combine(factors, places + [next_plane])
                sums.append(total + last_end if a == 0 else total)
            along_x = from_zone(sums)
            factors = list(stiff[j])
            if j == 0:
                factors[0] += stiff[4][4]
            along_y = combine(factors, values + [after])
            if j == 0:
                along_y = along_y + carried
            rate = (
                mesh_at(0, j) * along_x + mesh_at(1, j) * along_y + mesh_at(2, j) * along_z[j]
            )
            acc_v[which, j] = base(j) + (rate if scale == 1.0 else scale * rate)

    def velocity_after(which, scale, item, buffers):
        from_east, from_west, from_north, from_south = buffers
        later = unpack_x_high([from_east[item, 0], from_east[item, 1]])
        earlier = unpack_x_low([from_west[item, 0], from_west[item, 1]])
        above = jnp.where(at_zone(full, 3), unpack_y(from_north[item], 3), 0.0)
        below = jnp.where(at_zone(full, 0), unpack_y(from_south[item], 0), 0.0)
        done = []
        for j in range(4):
            ahead = jnp.where(low_rows, 0.0, later[j])
            behind = jnp.where(low_rows, earlier[j], 0.0)
            extra_x = jnp.stack(
                [scale * behind, zero, zero, zero]
                + [(scale * stiff[a][4]) * ahead for a in range(4)]
            )
            extra_y = (scale * stiff[j][4]) * above
            if j == 0:
                extra_y = extra_y + scale * below
            done.append(acc_v[which, j] + mesh_at(0, j) * extra_x + mesh_at(1, j) * extra_y)
        return done

    points = TABLE["to_points"]

    def mesh_before(item):
        values = [zoned[item, j] for j in range(4)]
        across = []
        for b in range(4):
            parts = by_zone(values[b])
            places = [parts[:, a] for a in range(4)]
            inner = jnp.where(low_rows, spin(parts[0, 0], 4, 0), 0.0)
            places.append(jnp.stack([parts[1, 0], inner]))
            across.append(from_zone([combine(points[i], places) for i in range(4)]))
        last = at_zone(full, 3)
        across.append(jnp.where(last, 0.0, spin(across[0], 7, 1)))
        for j in range(4):
            result = combine(points[j], across)
            if item < 3:
                speed[item, j] = result
            else:
                face_z[j] = result
        if item == 0:
            for q in range(2):
                edge = [values[b][4 * q] for b in range(4)]
                edge.append(jnp.where(at_zone(plane, 3), 0.0, spin(edge[0], 7, 0)))
                for j in range(4):
                    face_x[q, j] = combine(points[j], edge)
        if item == 1:
            face_y[0] = across[0]
            face_y[1] = across[4]

    def mesh_after(item):
        rows = rows_of(plane)
        later = unpack_x_high([in_dx[2 + item, 0], in_dx[2 + item, 1]])
        later = [jnp.where(low_rows, 0.0, value) for value in later]
        far = jnp.where(at_zone(plane, 3), 0.0, spin(later[0], 7, 0))
        far = jnp.where(rows == 7, spin(in_corner[...], 7 - item, 0), far)
        later.append(jnp.where(low_rows, 0.0, far))
        above = jnp.where(at_zone(full, 3), unpack_y(in_dy[2 + item], 3), 0.0)
        parts = by_zone(above)
        places = [parts[:, a] for a in range(4)]
        places.append(
            jnp.stack([parts[1, 0], jnp.where(low_rows, spin(parts[0, 0], 4, 0), 0.0)])
        )
        across = from_zone([combine(points[i], places) for i in range(4)])
        edge = [combine(points[j], later) for j in range(4)]
        for j in range(4):
            extra = points[j][4] * across
            extra = jnp.concatenate(
                [extra[:4], jnp.stack([extra[4 + i] + points[i][4] * edge[j] for i in range(4)])]
            )
            if item < 3:
                speed[item, j] += extra
            else:
                face_z[j] += extra
        if item == 0:
            for j in range(4):
                lowest = face_x[0, j] + points[j][4] * above[0]
                face_x[0, j] = lowest
                face_x[1, j] += points[j][4] * above[4]
                face_x[2, j] = jnp.where(low_rows, spin(lowest, 4, 0), edge[j])
        if item == 1:
            for side, halo, plain in ((0, later[0], None), (1, later[4], across)):
                for x in range(8):
                    if x < 4 and plain is None:
                        continue
                    value = face_y[side, x]
                    if plain is not None:
                        value = value + plain[x]
                    if x >= 4:
                        value = value + points[x - 4][4] * halo
                    face_y[side, x] = value

    def upwind(face, minus_side, plus_side):
        return jnp.maximum(face, 0.0) * minus_side + jnp.minimum(face, 0.0) * plus_side

    def field_before(which, values, base, scale):
        upper, lower = parted(jnp.concatenate([part.reshape(64, 128) for part in values], 0))
        wide = square[:, 0:256]
        sides = product(upper, wide) + product(lower, wide) + product(upper, square[:, 256:512])
        flux = [
            upwind(
                face_z[j],
                sides[64 * j : 64 * (j + 1), :128].reshape(full),
                sides[64 * j : 64 * (j + 1), 128:].reshape(full),
            ).reshape(64, 128)
            for j in range(4)
        ]
        moved = [(speed[2, j] * values[j]).reshape(64, 128) for j in range(4)]
        both = jnp.concatenate([jnp.concatenate(moved, 0), jnp.concatenate(flux, 0)], 1)
        upper, lower = parted(both)
        sums = product(upper, tall[...])
        along_z = sums[:, :128] + sums[:, 128:] + product(lower, tall[:, :128])
        moved = [speed[1, j] * values[j] for j in range(4)]
        for j in range(4):
            parts = by_zone(speed[0, j] * values[j])
            places = [parts[:, i] for i in range(4)]
            along_x = from_zone([combine(TABLE["volume"][i], places) for i in range(4)])
            along_y = combine(TABLE["volume"][j], moved)
            rate = along_x + along_y + along_z[64 * j : 64 * (j + 1)].reshape(full)
            acc_f[which, j] = base(j) + (rate if scale == 1.0 else scale * rate)

    def in_group(values, join):
        lane = lax.broadcasted_iota(jnp.int32, values.shape, 2)
        partner = jnp.where(lane % 2 == 0, spin(values, 127, 2), spin(values, 1, 2))
        values = join(values, partner)
        partner = jnp.where(lane // 2 % 2 == 0, spin(values, 126, 2), spin(values, 2, 2))
        return join(values, partner)

    def limited(which, values):
        weights = TABLE["weights"]
        across = by_zone(combine(weights, values))
        mean = combine(weights, [across[:, i] for i in range(4)])
        lane = lax.broadcasted_iota(jnp.int32, (2, 8, 128), 2) % 4
        middle = (lane == 1) | (lane == 2)
        mean = in_group(mean * jnp.where(middle, weights[1], weights[0]), jnp.add)
        top = functools.reduce(jnp.maximum, values)
        bottom = functools.reduce(jnp.minimum, values)
        top, bottom = by_zone(top), by_zone(bottom)
        top = functools.reduce(jnp.maximum, [top[:, i] for i in range(4)])
        bottom = functools.reduce(jnp.minimum, [bottom[:, i] for i in range(4)])
        rise = in_group(top, jnp.maximum) - mean
        fall = in_group(bottom, jnp.minimum) - mean
        low, high = bounds[2 * which], bounds[2 * which + 1]
        theta = jnp.minimum(
            (high - mean) / (rise + limit_eps), (mean - low) / (limit_eps - fall)
        )
        theta = jnp.clip(theta, 0.0, 1.0)
        result = []
        for j in range(4):
            parts = by_zone(values[j])
            result.append(
                from_zone([mean + theta * (parts[:, i] - mean) for i in range(4)])
            )
        return result

    def field_after(which, scale, item, buffers):
        from_east, from_west, from_north, from_south = buffers
        later = unpack_x_high([from_east[item, 0], from_east[item, 1]])
        earlier = unpack_x_low([from_west[item, 0], from_west[item, 1]])
        low_lift = [scale * factor for factor in TABLE["lift_low"]]
        high_lift = [-scale * factor for factor in TABLE["lift_high"]]
        low, high = trace_y[which, 0], trace_y[which, 1]
        before = jnp.where(at_zone(full, 0), unpack_y(from_south[item], 0), spin(high, 1, 1))
        after = jnp.where(at_zone(full, 3), unpack_y(from_north[item], 3), spin(low, 7, 1))
        lower_y = upwind(face_y[0], before, low)
        upper_y = upwind(face_y[1], high, after)
        values = []
        for j in range(4):
            low, high = trace_x[which, 0, j], trace_x[which, 1, j]
            before = jnp.where(low_rows, earlier[j], spin(high[1], 4, 0))
            after = jnp.where(low_rows, spin(low[0], 4, 0), later[j])
            flux = [
                upwind(face_x[0, j], before, low[0]),
                upwind(face_x[1, j], high[0], low[1]),
                upwind(face_x[2, j], high[1], after),
            ]
            lower_x, upper_x = jnp.stack(flux[:2]), jnp.stack(flux[1:])
            lift = from_zone(
                [low_lift[i] * lower_x + high_lift[i] * upper_x for i in range(4)]
            )
            values.append(
                acc_f[which, j] + lift + (low_lift[j] * lower_y + high_lift[j] * upper_y)
            )
        return limited(which, values)

    for item in range(4):
        mesh_before(item)
    for which in range(3):
        values = [velocity_at(which, j) for j in range(4)]
        velocity_before(which, values, lambda j: values[j], 1.0)
    for copy in first:
        copy.wait_recv()
    for item in range(4):
        mesh_after(item)
    for which in range(2):
        values = [field_at(which, j) for j in range(4)]
        field_before(which, values, lambda j: values[j], 1.0)
        values = field_after(which, 1.0, which, arrived_a)
        for j in range(4):
            sec_f[which, j] = values[j]
        field_traces(which, values)
        pack_field(which, which, leaving_b)
    second = send_all(leaving_b, arrived_b)
    for copy in first_v:
        copy.wait_recv()
    for which in range(3):
        values = velocity_after(which, 1.0, which, arrived_c)
        for j in range(4):
            sec_v[which, j] = values[j]
        pack_velocity(values, which, leaving_d)
    second_v = send_all(leaving_d, arrived_d)

    for which in range(2):
        values = [sec_f[which, j] for j in range(4)]
        field_before(which, values, lambda j: 0.5 * field_at(which, j) + 0.5 * values[j], 0.5)
    for which in range(3):
        values = [sec_v[which, j] for j in range(4)]
        velocity_before(
            which, values, lambda j: 0.5 * velocity_at(which, j) + 0.5 * values[j], 0.5
        )
    for copy in second:
        copy.wait_recv()
    for which in range(2):
        values = field_after(which, 0.5, which, arrived_b)
        for j in range(4):
            results[which, :, pl.ds(j, 8, stride=4), :] = values[j]
    for copy in second_v:
        copy.wait_recv()
    for which in range(3):
        values = velocity_after(which, 0.5, which, arrived_d)
        for j in range(4):
            results[2 + which, :, pl.ds(j, 8, stride=4), :] = values[j]
    for copy in copies:
        copy.wait_send()


def unfold(results, new_density, new_energy, new_velocity, store_sem):
    copies = []
    for half in range(2):
        rows, block = pl.ds(16 * half, 16), pl.ds(8 * half, 8)
        for source, target in (
            (results.at[0, :, rows, :], new_density.at[block]),
            (results.at[1, :, rows, :], new_energy.at[block]),
            (results.at[pl.ds(2, 3), :, rows, :], new_velocity.at[:, block]),
        ):
            copy = pltpu.make_async_copy(source, target, store_sem.at[len(copies)])
            copy.start()
            copies.append(copy)
    for copy in copies:
        copy.wait()


def solution(mesh):
    counts = (mesh.shape["gx"], mesh.shape["gy"])
    square, tall = lane_matrices(128)

    def on_device(*arguments):
        vmem = lambda *shape: pltpu.VMEM(shape, F32)
        scratch = [
            vmem(2, 8, 32, 128), vmem(3, 8, 32, 128), vmem(3, 8, 32, 128),
            vmem(*square.shape), vmem(*tall.shape),
            pltpu.VMEM((128, 1280), BF16), pltpu.VMEM((256, 256), BF16),
            vmem(4, 4, 4, 32), vmem(4, 2, 8, 128), vmem(4, 2, 8, 128),
            vmem(3, 4, 8, 8, 128), vmem(3, 4, 8, 8, 128),
            vmem(2, 4, 8, 8, 128), vmem(2, 4, 8, 8, 128),
            vmem(3, 4, 8, 8, 128), vmem(3, 4, 8, 128), vmem(2, 8, 8, 128), vmem(4, 8, 8, 128),
            vmem(2, 2, 4, 2, 8, 128), vmem(2, 2, 8, 8, 128), vmem(4, 4, 8, 8, 128),
        ]
        sides = [vmem(items, 2, 8, 128) for items in (6, 2, 6, 2)]
        scratch += sides + sides + [vmem(8, 128)] * 2
        for items in (3, 2, 3):
            scratch += [vmem(items, 2, 8, 128)] * 8
        scratch += [
            pltpu.SemaphoreType.DMA((14,)),
            pltpu.SemaphoreType.DMA((17,)),
            pltpu.SemaphoreType.DMA((17,)),
        ]
        operands = [
            pltpu.with_memory_space_constraint(value, pltpu.HBM)
            for value in (*arguments, jnp.asarray(square), jnp.asarray(tall))
        ]
        results = pl.pallas_call(
            functools.partial(kernel, counts),
            out_shape=pltpu.VMEM((5, 8, 32, 128), F32),
            in_specs=[pl.BlockSpec(memory_space=pltpu.HBM)] * 10,
            out_specs=pl.BlockSpec(memory_space=pltpu.VMEM),
            scratch_shapes=scratch,
            compiler_params=pltpu.CompilerParams(
                collective_id=0, has_side_effects=True, vmem_limit_bytes=32 * 1024 * 1024
            ),
        )(*operands)
        return pl.pallas_call(
            unfold,
            out_shape=[jax.ShapeDtypeStruct(value.shape, F32) for value in arguments[:3]],
            in_specs=[pl.BlockSpec(memory_space=pltpu.VMEM)],
            out_specs=[pl.BlockSpec(memory_space=pltpu.HBM)] * 3,
            scratch_shapes=[pltpu.SemaphoreType.DMA((6,))],
            compiler_params=pltpu.CompilerParams(vmem_limit_bytes=32 * 1024 * 1024),
        )(results)

    fields, vectors = P("gx", "gy", None), P(None, "gx", "gy", None)
    return jax.shard_map(
        on_device,
        mesh=mesh,
        in_specs=(fields, fields, vectors, vectors, fields, fields, fields, fields),
        out_specs=(fields, fields, vectors),
        check_vma=False,
    )
```

```python
import functools
import math

import jax
import jax.numpy as jnp
import numpy as np
from jax import lax
from jax.experimental import pallas as pl
from jax.experimental.pallas import tpu as pltpu
from jax.sharding import PartitionSpec as P

MESH = pl.DeviceIdType.MESH
F32 = jnp.float32
BF16 = jnp.bfloat16
time_step = 0.02
limit_eps = 1e-06


def lagrange_values(node_set, points):
    result = np.ones((len(points), len(node_set)))
    for column in range(len(node_set)):
        for partner in range(len(node_set)):
            if partner != column:
                result[:, column] = (
                    result[:, column]
                    * (points - node_set[partner])
                    / (node_set[column] - node_set[partner])
                )
    return result


def lagrange_slopes(node_set, points):
    node_total = len(node_set)
    result = np.zeros((len(points), node_total))
    for column in range(node_total):
        for skipped in range(node_total):
            if skipped != column:
                factor = np.ones(len(points)) / (node_set[column] - node_set[skipped])
                for partner in range(node_total):
                    if partner != column and partner != skipped:
                        factor = (
                            factor
                            * (points - node_set[partner])
                            / (node_set[column] - node_set[partner])
                        )
                result[:, column] = result[:, column] + factor
    return result


def basis_tables():
    gauss_points = np.array(
        [-0.8611363115940526, -0.3399810435848563, 0.3399810435848563, 0.8611363115940526]
    )
    gauss_weights = np.array(
        [0.3478548451374538, 0.6521451548625461, 0.6521451548625461, 0.3478548451374538]
    )
    lobatto_points = np.array([-1.0, -math.sqrt(3.0 / 7.0), 0.0, math.sqrt(3.0 / 7.0), 1.0])
    lobatto_weights = np.array([0.1, 49.0 / 90.0, 32.0 / 45.0, 49.0 / 90.0, 0.1])
    slopes = lagrange_slopes(gauss_points, gauss_points)
    volume = (2.0 / gauss_weights)[:, None] * slopes.T * gauss_weights[None, :]
    trace_low = lagrange_values(gauss_points, np.array([-1.0]))[0]
    trace_high = lagrange_values(gauss_points, np.array([1.0]))[0]
    stiffness = (
        2.0 * lobatto_weights[:, None] * lagrange_slopes(lobatto_points, lobatto_points)
    )
    lumped = np.array([0.2, lobatto_weights[1], lobatto_weights[2], lobatto_weights[3], 0.2])
    return {
        "weights": gauss_weights / 2.0,
        "volume": time_step * volume,
        "trace_low": trace_low,
        "trace_high": trace_high,
        "lift_low": time_step * 2.0 * trace_low / gauss_weights,
        "lift_high": time_step * 2.0 * trace_high / gauss_weights,
        "to_points": lagrange_values(lobatto_points, gauss_points),
        "stiffness": -time_step * stiffness / lumped[:, None],
    }


TABLES = basis_tables()
TABLE = {name: TABLES[name].tolist() for name in TABLES}


def lane_matrices(lanes):
    zones = lanes // 4
    shape = (lanes, lanes)
    volume, lift = np.zeros(shape), np.zeros(shape)
    minus, plus = np.zeros(shape), np.zeros(shape)
    stiff, interp = np.zeros(shape), np.zeros(shape)
    pick, spread = np.zeros(shape), np.zeros(shape)
    for zone in range(zones):
        at = 4 * zone
        before = 4 * ((zone - 1) % zones)
        for within in range(4):
            for source in range(4):
                volume[at + source, at + within] = TABLES["volume"][within, source]
                minus[before + source, at + within] = TABLES["trace_high"][source]
                plus[at + source, at + within] = TABLES["trace_low"][source]
            lift[at, at + within] = TABLES["lift_low"][within]
            lift[at, before + within] = -TABLES["lift_high"][within]
            pick[at, at + within] = 1.0
            spread[zone, at + within] = 1.0
            for source in range(5):
                interp[(at + source) % lanes, at + within] += TABLES["to_points"][within, source]
        for target in range(5):
            for source in range(5):
                stiff[(at + source) % lanes, (at + target) % lanes] += TABLES["stiffness"][
                    target, source
                ]
    square = np.concatenate([minus, plus, stiff, interp, pick, spread], axis=1)
    tall = np.concatenate([volume, lift], axis=0)
    return square.astype(np.float32), tall.astype(np.float32)


def spin(values, steps, axis):
    size = values.shape[axis]
    steps = steps % size
    return values if steps == 0 else pltpu.roll(values, steps, axis)


def rows_of(shape):
    return lax.broadcasted_iota(jnp.int32, shape, len(shape) - 2)


def low_half(shape):
    return rows_of(shape) < 4


def at_zone(shape, zone):
    return rows_of(shape) % 4 == zone


def combine(coefficients, terms):
    total = None
    for factor, term in zip(coefficients, terms):
        part = factor * term
        total = part if total is None else total + part
    return total


def parted(values):
    upper = values.astype(BF16)
    return upper, (values - upper.astype(F32)).astype(BF16)


def product(left, right):
    return jnp.dot(left, right, preferred_element_type=F32)


def by_zone(values):
    return values.reshape((2, 4) + values.shape[1:])


def from_zone(pieces):
    stacked = jnp.stack(pieces, axis=1)
    return stacked.reshape((8,) + stacked.shape[2:])


def pack_x_low(planes):
    mask = low_half((8, 128))
    return [jnp.where(mask, planes[t], spin(planes[t + 1], 4, 0)) for t in (0, 2)]


def pack_x_high(planes):
    mask = low_half((8, 128))
    return [jnp.where(mask, spin(planes[t], 4, 0), planes[t + 1]) for t in (0, 2)]


def unpack_x_high(packed):
    return [spin(packed[0], 4, 0), packed[0], spin(packed[1], 4, 0), packed[1]]


def unpack_x_low(packed):
    return [packed[0], spin(packed[0], 4, 0), packed[1], spin(packed[1], 4, 0)]


def pack_y(values, start):
    parts = by_zone(values)
    shape = (2, 8, 128)
    total = spin(parts[:, 3], 3 - start, 1)
    for place in (2, 1, 0):
        total = jnp.where(at_zone(shape, place), spin(parts[:, place], place - start, 1), total)
    return total


def unpack_y(packed, end):
    return from_zone([spin(packed, end - place, 1) for place in range(4)])


def kernel(
    counts,
    density, energy, velocity, mesh_velocity, density_low, density_high, energy_low, energy_high,
    square_hbm, tall_hbm,
    results,
    raw_u, raw_v, raw_m, square_in, tall_in, square, tall, bound_in, bound_rows, bounds,
    acc_v, sec_v, acc_f, sec_f, speed, face_x, face_y, face_z, trace_x, trace_y, zoned,
    out_dx, out_ux, out_dy, out_uy, in_dx, in_ux, in_dy, in_uy, out_corner, in_corner,
    out_vx, out_wx, out_vy, out_wy, in_vx, in_wx, in_vy, in_wy,
    out_dx2, out_ux2, out_dy2, out_uy2, in_dx2, in_ux2, in_dy2, in_uy2,
    out_vx2, out_wx2, out_vy2, out_wy2, in_vx2, in_wx2, in_vy2, in_wy2,
    load_sem, send_sem, recv_sem,
):
    count_x, count_y = counts
    here_x, here_y = lax.axis_index("gx"), lax.axis_index("gy")
    west = lax.rem(here_x + count_x - 1, count_x)
    east = lax.rem(here_x + 1, count_x)
    south = lax.rem(here_y + count_y - 1, count_y)
    north = lax.rem(here_y + 1, count_y)
    to_west, to_east = (west, here_y), (east, here_y)
    to_south, to_north = (here_x, south), (here_x, north)
    to_corner, from_corner = (west, south), (east, north)

    loads = {}

    def load(name, source, target):
        copy = pltpu.make_async_copy(source, target, load_sem.at[sum(map(len, loads.values()))])
        copy.start()
        loads.setdefault(name, []).append(copy)

    def loaded(name):
        for copy in loads[name]:
            copy.wait()

    places = [(pl.ds(16 * half, 16), pl.ds(8 * half, 8)) for half in range(2)]
    for rows, block in places:
        load("mesh", mesh_velocity.at[:, block], raw_m.at[:, :, rows, :])
    load("tables", square_hbm, square_in)
    for rows, block in places:
        load("fields", density.at[block], raw_u.at[0, :, rows, :])
        load("fields", energy.at[block], raw_u.at[1, :, rows, :])
    for rows, block in places:
        load("velocity", velocity.at[:, block], raw_v.at[:, :, rows, :])
    load("tall", tall_hbm, tall_in)
    for index, source in enumerate((density_low, density_high, energy_low, energy_high)):
        load("bounds", source, bound_in.at[index])

    barrier = pltpu.get_barrier_semaphore()
    for peer in (to_west, to_east, to_south, to_north, to_corner, from_corner):
        pl.semaphore_signal(barrier, inc=1, device_id=peer, device_id_type=MESH)

    loaded("tables")
    for column, target, gap in ((0, 0, 2), (1, 1, 2), (2, 4, 1), (3, 6, 1), (4, 8, 0), (5, 9, 0)):
        upper, lower = parted(square_in[:, 128 * column : 128 * (column + 1)])
        square[:, 128 * target : 128 * (target + 1)] = upper
        if gap:
            square[:, 128 * (target + gap) : 128 * (target + gap + 1)] = lower

    full = (8, 8, 128)
    plane = (8, 128)
    low_rows = low_half(plane)
    stiff = TABLE["stiffness"]
    zero = jnp.zeros(plane, F32)

    def field_at(which, j):
        return raw_u[which, :, pl.ds(j, 8, stride=4), :]

    def velocity_at(which, j):
        return raw_v[which, :, pl.ds(j, 8, stride=4), :]

    def mesh_at(which, j):
        return raw_m[which, :, pl.ds(j, 8, stride=4), :]

    def lanes_product(values, column, narrow=1):
        upper, lower = parted(jnp.concatenate([part.reshape(64, 128) for part in values], 0))
        wide = square[:, 128 * column : 128 * (column + 2)]
        both = product(upper, wide)
        total = both[:, :128] + both[:, 128:] + product(lower, wide[:, :128])
        return [total[64 * j : 64 * (j + 1)].reshape(full) for j in range(4)]

    def field_traces(which, values):
        for j in range(4):
            parts = by_zone(values[j])
            places = [parts[:, i] for i in range(4)]
            trace_x[which, 0, j] = combine(TABLE["trace_low"], places)
            trace_x[which, 1, j] = combine(TABLE["trace_high"], places)
        trace_y[which, 0] = combine(TABLE["trace_low"], values)
        trace_y[which, 1] = combine(TABLE["trace_high"], values)

    def put_pair(target, item, pair):
        target[item, 0] = pair[0]
        target[item, 1] = pair[1]

    def pack_field(which, item, buffers):
        west_to, east_to, south_to, north_to = buffers
        put_pair(west_to, item, pack_x_low([trace_x[which, 0, j, 0] for j in range(4)]))
        put_pair(east_to, item, pack_x_high([trace_x[which, 1, j, 1] for j in range(4)]))
        south_to[item] = pack_y(trace_y[which, 0], 0)
        north_to[item] = pack_y(trace_y[which, 1], 3)

    def pack_velocity(values, item, buffers):
        west_to, east_to, south_to, north_to = buffers
        put_pair(west_to, item, pack_x_low([values[j][0] for j in range(4)]))
        closing = [
            combine(stiff[4][:4], [values[j][4 + i] for i in range(4)]) for j in range(4)
        ]
        put_pair(east_to, item, pack_x_high(closing))
        south_to[item] = pack_y(values[0], 0)
        north_to[item] = pack_y(combine(stiff[4][:4], values), 3)

    loaded("mesh")
    corner = zero
    for item in range(4):
        values = [mesh_at(min(item, 2), j) for j in range(4)]
        if item < 3:
            values = lanes_product(values, 6)
        else:
            upper, lower = parted(jnp.concatenate([v.reshape(64, 128) for v in values], 0))
            picker = square[:, 128 * 8 : 128 * 9]
            total = product(upper, picker) + product(lower, picker)
            values = [total[64 * j : 64 * (j + 1)].reshape(full) for j in range(4)]
        for j in range(4):
            zoned[item, j] = values[j]
        put_pair(out_dx, 2 + item, pack_x_low([values[j][0] for j in range(4)]))
        out_dy[2 + item] = pack_y(values[0], 0)
        corner = jnp.where(rows_of(plane) == item, spin(values[0][0], item, 0), corner)
    out_corner[...] = corner
    loaded("fields")

    @pl.loop(0, 2)
    def _(which):
        field_traces(which, [field_at(which, j) for j in range(4)])
        pack_field(which, which, (out_dx, out_ux, out_dy, out_uy))

    pl.semaphore_wait(barrier, 6)
    copies = []
    peers = (to_west, to_east, to_south, to_north)

    def send(source, target, peer):
        copy = pltpu.make_async_remote_copy(
            src_ref=source, dst_ref=target,
            send_sem=send_sem.at[len(copies)], recv_sem=recv_sem.at[len(copies)],
            device_id=peer, device_id_type=MESH,
        )
        copy.start()
        copies.append(copy)
        return copy

    def send_all(sources, targets):
        return [send(*triple) for triple in zip(sources, targets, peers)]

    arrived_a, arrived_b = (in_dx, in_ux, in_dy, in_uy), (in_dx2, in_ux2, in_dy2, in_uy2)
    leaving_a, leaving_b = (out_dx, out_ux, out_dy, out_uy), (out_dx2, out_ux2, out_dy2, out_uy2)
    arrived_c, arrived_d = (in_vx, in_wx, in_vy, in_wy), (in_vx2, in_wx2, in_vy2, in_wy2)
    leaving_c, leaving_d = (out_vx, out_wx, out_vy, out_wy), (out_vx2, out_wx2, out_vy2, out_wy2)
    first = send_all(leaving_a, arrived_a) + [send(out_corner, in_corner, to_corner)]
    loaded("velocity")

    @pl.loop(0, 3)
    def _(which):
        pack_velocity([velocity_at(which, j) for j in range(4)], which, leaving_c)

    first_v = send_all(leaving_c, arrived_c)

    loaded("tall")
    upper, lower = parted(tall_in[...])
    tall[:, :128] = upper
    tall[:, 128:] = lower
    loaded("bounds")
    bound_rows[...] = jnp.zeros((4, 2, 8, 128), F32)
    for index in range(4):
        for zone in range(4):
            bound_rows[index, zone % 2, pl.ds(4 * (zone // 2), 4), pl.ds(0, 32)] = bound_in[
                index, zone
            ]
    values = bound_rows[...].reshape(64, 128)
    spreader = square[:, 128 * 9 : 128 * 10]
    upper = values.astype(BF16)
    rest = values - upper.astype(F32)
    middle = rest.astype(BF16)
    lowest = (rest - middle.astype(F32)).astype(BF16)
    values = product(upper, spreader) + (product(middle, spreader) + product(lowest, spreader))
    bounds[...] = values.reshape(4, 2, 8, 128)

    def velocity_before(which, values, base, scale):
        along_z = lanes_product(values, 4)
        closing = combine(stiff[4][:4], values)
        after = jnp.where(at_zone(full, 3), 0.0, spin(values[0], 7, 1))
        carried = jnp.where(at_zone(full, 0), 0.0, spin(closing, 1, 1))
        for j in range(4):
            parts = by_zone(values[j])
            places = [parts[:, i] for i in range(4)]
            ending = combine(stiff[4][:4], places)
            next_plane = jnp.stack(
                [parts[1, 0], jnp.where(low_rows, spin(parts[0, 0], 4, 0), 0.0)]
            )
            last_end = jnp.stack([jnp.where(low_rows, 0.0, spin(ending[1], 4, 0)), ending[0]])
            sums = []
            for a in range(4):
                factors = list(stiff[a])
                if a == 0:
                    factors[0] += stiff[4][4]
                total = combine(factors, places + [next_plane])
                sums.append(total + last_end if a == 0 else total)
            along_x = from_zone(sums)
            factors = list(stiff[j])
            if j == 0:
                factors[0] += stiff[4][4]
            along_y = combine(factors, values + [after])
            if j == 0:
                along_y = along_y + carried
            rate = (
                mesh_at(0, j) * along_x + mesh_at(1, j) * along_y + mesh_at(2, j) * along_z[j]
            )
            acc_v[which, j] = base(j) + (rate if scale == 1.0 else scale * rate)

    def velocity_after(which, scale, item, buffers):
        from_east, from_west, from_north, from_south = buffers
        later = unpack_x_high([from_east[item, 0], from_east[item, 1]])
        earlier = unpack_x_low([from_west[item, 0], from_west[item, 1]])
        above = jnp.where(at_zone(full, 3), unpack_y(from_north[item], 3), 0.0)
        below = jnp.where(at_zone(full, 0), unpack_y(from_south[item], 0), 0.0)
        done = []
        for j in range(4):
            ahead = jnp.where(low_rows, 0.0, later[j])
            behind = jnp.where(low_rows, earlier[j], 0.0)
            extra_x = jnp.stack(
                [scale * behind, zero, zero, zero]
                + [(scale * stiff[a][4]) * ahead for a in range(4)]
            )
            extra_y = (scale * stiff[j][4]) * above
            if j == 0:
                extra_y = extra_y + scale * below
            done.append(acc_v[which, j] + mesh_at(0, j) * extra_x + mesh_at(1, j) * extra_y)
        return done

    points = TABLE["to_points"]

    def mesh_before(item):
        values = [zoned[item, j] for j in range(4)]
        across = []
        for b in range(4):
            parts = by_zone(values[b])
            places = [parts[:, a] for a in range(4)]
            inner = jnp.where(low_rows, spin(parts[0, 0], 4, 0), 0.0)
            places.append(jnp.stack([parts[1, 0], inner]))
            across.append(from_zone([combine(points[i], places) for i in range(4)]))
        last = at_zone(full, 3)
        across.append(jnp.where(last, 0.0, spin(across[0], 7, 1)))
        for j in range(4):
            result = combine(points[j], across)
            if item < 3:
                speed[item, j] = result
            else:
                face_z[j] = result
        if item == 0:
            for q in range(2):
                edge = [values[b][4 * q] for b in range(4)]
                edge.append(jnp.where(at_zone(plane, 3), 0.0, spin(edge[0], 7, 0)))
                for j in range(4):
                    face_x[q, j] = combine(points[j], edge)
        if item == 1:
            face_y[0] = across[0]
            face_y[1] = across[4]

    def mesh_after(item):
        rows = rows_of(plane)
        later = unpack_x_high([in_dx[2 + item, 0], in_dx[2 + item, 1]])
        later = [jnp.where(low_rows, 0.0, value) for value in later]
        far = jnp.where(at_zone(plane, 3), 0.0, spin(later[0], 7, 0))
        far = jnp.where(rows == 7, spin(in_corner[...], 7 - item, 0), far)
        later.append(jnp.where(low_rows, 0.0, far))
        above = jnp.where(at_zone(full, 3), unpack_y(in_dy[2 + item], 3), 0.0)
        parts = by_zone(above)
        places = [parts[:, a] for a in range(4)]
        places.append(
            jnp.stack([parts[1, 0], jnp.where(low_rows, spin(parts[0, 0], 4, 0), 0.0)])
        )
        across = from_zone([combine(points[i], places) for i in range(4)])
        edge = [combine(points[j], later) for j in range(4)]
        for j in range(4):
            extra = points[j][4] * across
            extra = jnp.concatenate(
                [extra[:4], jnp.stack([extra[4 + i] + points[i][4] * edge[j] for i in range(4)])]
            )
            if item < 3:
                speed[item, j] += extra
            else:
                face_z[j] += extra
        if item == 0:
            for j in range(4):
                lowest = face_x[0, j] + points[j][4] * above[0]
                face_x[0, j] = lowest
                face_x[1, j] += points[j][4] * above[4]
                face_x[2, j] = jnp.where(low_rows, spin(lowest, 4, 0), edge[j])
        if item == 1:
            for side, halo, plain in ((0, later[0], None), (1, later[4], across)):
                for x in range(8):
                    if x < 4 and plain is None:
                        continue
                    value = face_y[side, x]
                    if plain is not None:
                        value = value + plain[x]
                    if x >= 4:
                        value = value + points[x - 4][4] * halo
                    face_y[side, x] = value

    def upwind(face, minus_side, plus_side):
        return jnp.maximum(face, 0.0) * minus_side + jnp.minimum(face, 0.0) * plus_side

    def field_before(which, values, base, scale):
        upper, lower = parted(jnp.concatenate([part.reshape(64, 128) for part in values], 0))
        wide = square[:, 0:256]
        sides = product(upper, wide) + product(lower, wide) + product(upper, square[:, 256:512])
        flux = [
            upwind(
                face_z[j],
                sides[64 * j : 64 * (j + 1), :128].reshape(full),
                sides[64 * j : 64 * (j + 1), 128:].reshape(full),
            ).reshape(64, 128)
            for j in range(4)
        ]
        moved = [(speed[2, j] * values[j]).reshape(64, 128) for j in range(4)]
        both = jnp.concatenate([jnp.concatenate(moved, 0), jnp.concatenate(flux, 0)], 1)
        upper, lower = parted(both)
        sums = product(upper, tall[...])
        along_z = sums[:, :128] + sums[:, 128:] + product(lower, tall[:, :128])
        moved = [speed[1, j] * values[j] for j in range(4)]
        for j in range(4):
            parts = by_zone(speed[0, j] * values[j])
            places = [parts[:, i] for i in range(4)]
            along_x = from_zone([combine(TABLE["volume"][i], places) for i in range(4)])
            along_y = combine(TABLE["volume"][j], moved)
            rate = along_x + along_y + along_z[64 * j : 64 * (j + 1)].reshape(full)
            acc_f[which, j] = base(j) + (rate if scale == 1.0 else scale * rate)

    def in_group(values, join):
        lane = lax.broadcasted_iota(jnp.int32, values.shape, 2)
        partner = jnp.where(lane % 2 == 0, spin(values, 127, 2), spin(values, 1, 2))
        values = join(values, partner)
        partner = jnp.where(lane // 2 % 2 == 0, spin(values, 126, 2), spin(values, 2, 2))
        return join(values, partner)

    def limited(which, values):
        weights = TABLE["weights"]
        across = by_zone(combine(weights, values))
        mean = combine(weights, [across[:, i] for i in range(4)])
        lane = lax.broadcasted_iota(jnp.int32, (2, 8, 128), 2) % 4
        middle = (lane == 1) | (lane == 2)
        mean = in_group(mean * jnp.where(middle, weights[1], weights[0]), jnp.add)
        top = functools.reduce(jnp.maximum, values)
        bottom = functools.reduce(jnp.minimum, values)
        top, bottom = by_zone(top), by_zone(bottom)
        top = functools.reduce(jnp.maximum, [top[:, i] for i in range(4)])
        bottom = functools.reduce(jnp.minimum, [bottom[:, i] for i in range(4)])
        rise = in_group(top, jnp.maximum) - mean
        fall = in_group(bottom, jnp.minimum) - mean
        low, high = bounds[2 * which], bounds[2 * which + 1]
        theta = jnp.minimum(
            (high - mean) / (rise + limit_eps), (mean - low) / (limit_eps - fall)
        )
        theta = jnp.clip(theta, 0.0, 1.0)
        result = []
        for j in range(4):
            parts = by_zone(values[j])
            result.append(
                from_zone([mean + theta * (parts[:, i] - mean) for i in range(4)])
            )
        return result

    def field_after(which, scale, item, buffers):
        from_east, from_west, from_north, from_south = buffers
        later = unpack_x_high([from_east[item, 0], from_east[item, 1]])
        earlier = unpack_x_low([from_west[item, 0], from_west[item, 1]])
        low_lift = [scale * factor for factor in TABLE["lift_low"]]
        high_lift = [-scale * factor for factor in TABLE["lift_high"]]
        low, high = trace_y[which, 0], trace_y[which, 1]
        before = jnp.where(at_zone(full, 0), unpack_y(from_south[item], 0), spin(high, 1, 1))
        after = jnp.where(at_zone(full, 3), unpack_y(from_north[item], 3), spin(low, 7, 1))
        lower_y = upwind(face_y[0], before, low)
        upper_y = upwind(face_y[1], high, after)
        values = []
        for j in range(4):
            low, high = trace_x[which, 0, j], trace_x[which, 1, j]
            before = jnp.where(low_rows, earlier[j], spin(high[1], 4, 0))
            after = jnp.where(low_rows, spin(low[0], 4, 0), later[j])
            flux = [
                upwind(face_x[0, j], before, low[0]),
                upwind(face_x[1, j], high[0], low[1]),
                upwind(face_x[2, j], high[1], after),
            ]
            lower_x, upper_x = jnp.stack(flux[:2]), jnp.stack(flux[1:])
            lift = from_zone(
                [low_lift[i] * lower_x + high_lift[i] * upper_x for i in range(4)]
            )
            values.append(
                acc_f[which, j] + lift + (low_lift[j] * lower_y + high_lift[j] * upper_y)
            )
        return limited(which, values)

    for item in range(4):
        mesh_before(item)

    @pl.loop(0, 3)
    def _(which):
        values = [velocity_at(which, j) for j in range(4)]
        velocity_before(which, values, lambda j: values[j], 1.0)

    for copy in first:
        copy.wait_recv()
    for item in range(4):
        mesh_after(item)

    @pl.loop(0, 2)
    def _(which):
        values = [field_at(which, j) for j in range(4)]
        field_before(which, values, lambda j: values[j], 1.0)
        values = field_after(which, 1.0, which, arrived_a)
        for j in range(4):
            sec_f[which, j] = values[j]
        field_traces(which, values)
        pack_field(which, which, leaving_b)

    second = send_all(leaving_b, arrived_b)
    for copy in first_v:
        copy.wait_recv()

    @pl.loop(0, 3)
    def _(which):
        values = velocity_after(which, 1.0, which, arrived_c)
        for j in range(4):
            sec_v[which, j] = values[j]
        pack_velocity(values, which, leaving_d)

    second_v = send_all(leaving_d, arrived_d)

    @pl.loop(0, 2)
    def _(which):
        values = [sec_f[which, j] for j in range(4)]
        field_before(which, values, lambda j: 0.5 * field_at(which, j) + 0.5 * values[j], 0.5)

    @pl.loop(0, 3)
    def _(which):
        values = [sec_v[which, j] for j in range(4)]
        velocity_before(
            which, values, lambda j: 0.5 * velocity_at(which, j) + 0.5 * values[j], 0.5
        )

    for copy in second:
        copy.wait_recv()

    @pl.loop(0, 2)
    def _(which):
        values = field_after(which, 0.5, which, arrived_b)
        for j in range(4):
            results[which, :, pl.ds(j, 8, stride=4), :] = values[j]

    for copy in second_v:
        copy.wait_recv()

    @pl.loop(0, 3)
    def _(which):
        values = velocity_after(which, 0.5, which, arrived_d)
        for j in range(4):
            results[2 + which, :, pl.ds(j, 8, stride=4), :] = values[j]

    for copy in copies:
        copy.wait_send()


def unfold(results, new_density, new_energy, new_velocity, store_sem):
    copies = []
    for half in range(2):
        rows, block = pl.ds(16 * half, 16), pl.ds(8 * half, 8)
        for source, target in (
            (results.at[0, :, rows, :], new_density.at[block]),
            (results.at[1, :, rows, :], new_energy.at[block]),
            (results.at[pl.ds(2, 3), :, rows, :], new_velocity.at[:, block]),
        ):
            copy = pltpu.make_async_copy(source, target, store_sem.at[len(copies)])
            copy.start()
            copies.append(copy)
    for copy in copies:
        copy.wait()


def solution(mesh):
    counts = (mesh.shape["gx"], mesh.shape["gy"])
    square, tall = lane_matrices(128)

    def on_device(*arguments):
        vmem = lambda *shape: pltpu.VMEM(shape, F32)
        scratch = [
            vmem(2, 8, 32, 128), vmem(3, 8, 32, 128), vmem(3, 8, 32, 128),
            vmem(*square.shape), vmem(*tall.shape),
            pltpu.VMEM((128, 1280), BF16), pltpu.VMEM((256, 256), BF16),
            vmem(4, 4, 4, 32), vmem(4, 2, 8, 128), vmem(4, 2, 8, 128),
            vmem(3, 4, 8, 8, 128), vmem(3, 4, 8, 8, 128),
            vmem(2, 4, 8, 8, 128), vmem(2, 4, 8, 8, 128),
            vmem(3, 4, 8, 8, 128), vmem(3, 4, 8, 128), vmem(2, 8, 8, 128), vmem(4, 8, 8, 128),
            vmem(2, 2, 4, 2, 8, 128), vmem(2, 2, 8, 8, 128), vmem(4, 4, 8, 8, 128),
        ]
        sides = [vmem(items, 2, 8, 128) for items in (6, 2, 6, 2)]
        scratch += sides + sides + [vmem(8, 128)] * 2
        for items in (3, 2, 3):
            scratch += [vmem(items, 2, 8, 128)] * 8
        scratch += [
            pltpu.SemaphoreType.DMA((14,)),
            pltpu.SemaphoreType.DMA((17,)),
            pltpu.SemaphoreType.DMA((17,)),
        ]
        operands = [
            pltpu.with_memory_space_constraint(value, pltpu.HBM)
            for value in (*arguments, jnp.asarray(square), jnp.asarray(tall))
        ]
        results = pl.pallas_call(
            functools.partial(kernel, counts),
            out_shape=pltpu.VMEM((5, 8, 32, 128), F32),
            in_specs=[pl.BlockSpec(memory_space=pltpu.HBM)] * 10,
            out_specs=pl.BlockSpec(memory_space=pltpu.VMEM),
            scratch_shapes=scratch,
            compiler_params=pltpu.CompilerParams(
                collective_id=0, has_side_effects=True, vmem_limit_bytes=32 * 1024 * 1024
            ),
        )(*operands)
        return pl.pallas_call(
            unfold,
            out_shape=[jax.ShapeDtypeStruct(value.shape, F32) for value in arguments[:3]],
            in_specs=[pl.BlockSpec(memory_space=pltpu.VMEM)],
            out_specs=[pl.BlockSpec(memory_space=pltpu.HBM)] * 3,
            scratch_shapes=[pltpu.SemaphoreType.DMA((6,))],
            compiler_params=pltpu.CompilerParams(vmem_limit_bytes=32 * 1024 * 1024),
        )(results)

    fields, vectors = P("gx", "gy", None), P(None, "gx", "gy", None)
    return jax.shard_map(
        on_device,
        mesh=mesh,
        in_specs=(fields, fields, vectors, vectors, fields, fields, fields, fields),
        out_specs=(fields, fields, vectors),
        check_vma=False,
    )
```

```python
import functools
import math

import jax
import jax.numpy as jnp
import numpy as np
from jax import lax
from jax.experimental import pallas as pl
from jax.experimental.pallas import tpu as pltpu
from jax.sharding import PartitionSpec as P

MESH = pl.DeviceIdType.MESH
F32 = jnp.float32
BF16 = jnp.bfloat16
time_step = 0.02
limit_eps = 1e-06


def lagrange_values(node_set, points):
    result = np.ones((len(points), len(node_set)))
    for column in range(len(node_set)):
        for partner in range(len(node_set)):
            if partner != column:
                result[:, column] = (
                    result[:, column]
                    * (points - node_set[partner])
                    / (node_set[column] - node_set[partner])
                )
    return result


def lagrange_slopes(node_set, points):
    node_total = len(node_set)
    result = np.zeros((len(points), node_total))
    for column in range(node_total):
        for skipped in range(node_total):
            if skipped != column:
                factor = np.ones(len(points)) / (node_set[column] - node_set[skipped])
                for partner in range(node_total):
                    if partner != column and partner != skipped:
                        factor = (
                            factor
                            * (points - node_set[partner])
                            / (node_set[column] - node_set[partner])
                        )
                result[:, column] = result[:, column] + factor
    return result


def basis_tables():
    gauss_points = np.array(
        [-0.8611363115940526, -0.3399810435848563, 0.3399810435848563, 0.8611363115940526]
    )
    gauss_weights = np.array(
        [0.3478548451374538, 0.6521451548625461, 0.6521451548625461, 0.3478548451374538]
    )
    lobatto_points = np.array([-1.0, -math.sqrt(3.0 / 7.0), 0.0, math.sqrt(3.0 / 7.0), 1.0])
    lobatto_weights = np.array([0.1, 49.0 / 90.0, 32.0 / 45.0, 49.0 / 90.0, 0.1])
    slopes = lagrange_slopes(gauss_points, gauss_points)
    volume = (2.0 / gauss_weights)[:, None] * slopes.T * gauss_weights[None, :]
    trace_low = lagrange_values(gauss_points, np.array([-1.0]))[0]
    trace_high = lagrange_values(gauss_points, np.array([1.0]))[0]
    stiffness = (
        2.0 * lobatto_weights[:, None] * lagrange_slopes(lobatto_points, lobatto_points)
    )
    lumped = np.array([0.2, lobatto_weights[1], lobatto_weights[2], lobatto_weights[3], 0.2])
    return {
        "weights": gauss_weights / 2.0,
        "volume": time_step * volume,
        "trace_low": trace_low,
        "trace_high": trace_high,
        "lift_low": time_step * 2.0 * trace_low / gauss_weights,
        "lift_high": time_step * 2.0 * trace_high / gauss_weights,
        "to_points": lagrange_values(lobatto_points, gauss_points),
        "stiffness": -time_step * stiffness / lumped[:, None],
    }


TABLES = basis_tables()
TABLE = {name: TABLES[name].tolist() for name in TABLES}


def lane_matrices(lanes):
    zones = lanes // 4
    shape = (lanes, lanes)
    volume, lift = np.zeros(shape), np.zeros(shape)
    minus, plus = np.zeros(shape), np.zeros(shape)
    stiff, interp = np.zeros(shape), np.zeros(shape)
    pick, spread = np.zeros(shape), np.zeros(shape)
    for zone in range(zones):
        at = 4 * zone
        before = 4 * ((zone - 1) % zones)
        for within in range(4):
            for source in range(4):
                volume[at + source, at + within] = TABLES["volume"][within, source]
                minus[before + source, at + within] = TABLES["trace_high"][source]
                plus[at + source, at + within] = TABLES["trace_low"][source]
            lift[at, at + within] = TABLES["lift_low"][within]
            lift[at, before + within] = -TABLES["lift_high"][within]
            pick[at, at + within] = 1.0
            spread[zone, at + within] = 1.0
            for source in range(5):
                interp[(at + source) % lanes, at + within] += TABLES["to_points"][within, source]
        for target in range(5):
            for source in range(5):
                stiff[(at + source) % lanes, (at + target) % lanes] += TABLES["stiffness"][
                    target, source
                ]
    square = np.concatenate([minus, plus, stiff, interp, pick, spread], axis=1)
    tall = np.concatenate([volume, lift], axis=0)
    return square.astype(np.float32), tall.astype(np.float32)


def spin(values, steps, axis):
    size = values.shape[axis]
    steps = steps % size
    return values if steps == 0 else pltpu.roll(values, steps, axis)


def rows_of(shape):
    return lax.broadcasted_iota(jnp.int32, shape, len(shape) - 2)


def low_half(shape):
    return rows_of(shape) < 4


def at_zone(shape, zone):
    return rows_of(shape) % 4 == zone


def combine(coefficients, terms):
    total = None
    for factor, term in zip(coefficients, terms):
        part = factor * term
        total = part if total is None else total + part
    return total


def parted(values):
    upper = values.astype(BF16)
    return upper, (values - upper.astype(F32)).astype(BF16)


def product(left, right):
    return jnp.dot(left, right, preferred_element_type=F32)


def by_zone(values):
    return values.reshape((2, 4) + values.shape[1:])


def from_zone(pieces):
    stacked = jnp.stack(pieces, axis=1)
    return stacked.reshape((8,) + stacked.shape[2:])


def pack_x_low(planes):
    mask = low_half((8, 128))
    return [jnp.where(mask, planes[t], spin(planes[t + 1], 4, 0)) for t in (0, 2)]


def pack_x_high(planes):
    mask = low_half((8, 128))
    return [jnp.where(mask, spin(planes[t], 4, 0), planes[t + 1]) for t in (0, 2)]


def unpack_x_high(packed):
    return [spin(packed[0], 4, 0), packed[0], spin(packed[1], 4, 0), packed[1]]


def unpack_x_low(packed):
    return [packed[0], spin(packed[0], 4, 0), packed[1], spin(packed[1], 4, 0)]


def pack_y(values, start):
    parts = by_zone(values)
    shape = (2, 8, 128)
    total = spin(parts[:, 3], 3 - start, 1)
    for place in (2, 1, 0):
        total = jnp.where(at_zone(shape, place), spin(parts[:, place], place - start, 1), total)
    return total


def unpack_y(packed, end):
    return from_zone([spin(packed, end - place, 1) for place in range(4)])


def kernel(
    counts,
    density, energy, velocity, mesh_velocity, density_low, density_high, energy_low, energy_high,
    square_hbm, tall_hbm,
    results,
    raw_u, raw_v, raw_m, square_in, tall_in, square, tall, bound_in, bound_rows, bounds,
    acc_v, sec_v, acc_f, sec_f, speed, face_x, face_y, face_z, trace_x, trace_y, halo_x, halo_y, halo_corner,
    out_dx, out_ux, out_dy, out_uy, in_dx, in_ux, in_dy, in_uy,
    out_my, in_mx, in_my, out_corner, in_corner,
    out_vx, out_wx, out_vy, out_wy, in_vx, in_wx, in_vy, in_wy,
    out_dx2, out_ux2, out_dy2, out_uy2, in_dx2, in_ux2, in_dy2, in_uy2,
    out_vx2, out_wx2, out_vy2, out_wy2, in_vx2, in_wx2, in_vy2, in_wy2,
    load_sem, send_sem, recv_sem,
):
    count_x, count_y = counts
    here_x, here_y = lax.axis_index("gx"), lax.axis_index("gy")
    west = lax.rem(here_x + count_x - 1, count_x)
    east = lax.rem(here_x + 1, count_x)
    south = lax.rem(here_y + count_y - 1, count_y)
    north = lax.rem(here_y + 1, count_y)
    to_west, to_east = (west, here_y), (east, here_y)
    to_south, to_north = (here_x, south), (here_x, north)
    to_corner, from_corner = (west, south), (east, north)

    loads = {}

    def load(name, source, target):
        copy = pltpu.make_async_copy(source, target, load_sem.at[sum(map(len, loads.values()))])
        copy.start()
        loads.setdefault(name, []).append(copy)

    def loaded(name):
        for copy in loads[name]:
            copy.wait()

    places = [(pl.ds(16 * half, 16), pl.ds(8 * half, 8)) for half in range(2)]
    for rows, block in places:
        load("mesh", mesh_velocity.at[:, block], raw_m.at[:, :, rows, :])
    load("tables", square_hbm, square_in)
    for rows, block in places:
        load("fields", density.at[block], raw_u.at[0, :, rows, :])
        load("fields", energy.at[block], raw_u.at[1, :, rows, :])
    for rows, block in places:
        load("velocity", velocity.at[:, block], raw_v.at[:, :, rows, :])
    load("tall", tall_hbm, tall_in)
    for index, source in enumerate((density_low, density_high, energy_low, energy_high)):
        load("bounds", source, bound_in.at[index])

    barrier = pltpu.get_barrier_semaphore()
    for peer in (to_west, to_east, to_south, to_north, to_corner, from_corner):
        pl.semaphore_signal(barrier, inc=1, device_id=peer, device_id_type=MESH)

    full = (8, 8, 128)
    plane = (8, 128)
    low_rows = low_half(plane)
    stiff = TABLE["stiffness"]
    zero = jnp.zeros(plane, F32)

    def field_at(which, j):
        return raw_u[which, :, pl.ds(j, 8, stride=4), :]

    def velocity_at(which, j):
        return raw_v[which, :, pl.ds(j, 8, stride=4), :]

    def mesh_at(which, j):
        return raw_m[which, :, pl.ds(j, 8, stride=4), :]

    def lanes_product(values, column, narrow=1):
        upper, lower = parted(jnp.concatenate([part.reshape(64, 128) for part in values], 0))
        wide = square[:, 128 * column : 128 * (column + 2)]
        both = product(upper, wide)
        total = both[:, :128] + both[:, 128:] + product(lower, wide[:, :128])
        return [total[64 * j : 64 * (j + 1)].reshape(full) for j in range(4)]

    def field_traces(which, values):
        for j in range(4):
            parts = by_zone(values[j])
            places = [parts[:, i] for i in range(4)]
            trace_x[which, 0, j] = combine(TABLE["trace_low"], places)
            trace_x[which, 1, j] = combine(TABLE["trace_high"], places)
        trace_y[which, 0] = combine(TABLE["trace_low"], values)
        trace_y[which, 1] = combine(TABLE["trace_high"], values)

    def put_pair(target, item, pair):
        target[item, 0] = pair[0]
        target[item, 1] = pair[1]

    def pack_field(which, item, buffers):
        west_to, east_to, south_to, north_to = buffers
        put_pair(west_to, item, pack_x_low([trace_x[which, 0, j, 0] for j in range(4)]))
        put_pair(east_to, item, pack_x_high([trace_x[which, 1, j, 1] for j in range(4)]))
        south_to[item] = pack_y(trace_y[which, 0], 0)
        north_to[item] = pack_y(trace_y[which, 1], 3)

    def pack_velocity(values, item, buffers):
        west_to, east_to, south_to, north_to = buffers
        put_pair(west_to, item, pack_x_low([values[j][0] for j in range(4)]))
        closing = [
            combine(stiff[4][:4], [values[j][4 + i] for i in range(4)]) for j in range(4)
        ]
        put_pair(east_to, item, pack_x_high(closing))
        south_to[item] = pack_y(values[0], 0)
        north_to[item] = pack_y(combine(stiff[4][:4], values), 3)

    loaded("mesh")
    corner = zero
    for which in range(3):
        values = mesh_at(which, 0)
        out_my[which] = pack_y(values, 0)
        corner = jnp.where(rows_of(plane) == which, spin(values[0], which, 0), corner)
    out_corner[...] = corner

    pl.semaphore_wait(barrier, 6)
    copies = []
    peers = (to_west, to_east, to_south, to_north)

    def send(source, target, peer):
        copy = pltpu.make_async_remote_copy(
            src_ref=source, dst_ref=target,
            send_sem=send_sem.at[len(copies)], recv_sem=recv_sem.at[len(copies)],
            device_id=peer, device_id_type=MESH,
        )
        copy.start()
        copies.append(copy)
        return copy

    def send_all(sources, targets):
        return [send(*triple) for triple in zip(sources, targets, peers)]

    arrived_a, arrived_b = (in_dx, in_ux, in_dy, in_uy), (in_dx2, in_ux2, in_dy2, in_uy2)
    leaving_a, leaving_b = (out_dx, out_ux, out_dy, out_uy), (out_dx2, out_ux2, out_dy2, out_uy2)
    arrived_c, arrived_d = (in_vx, in_wx, in_vy, in_wy), (in_vx2, in_wx2, in_vy2, in_wy2)
    leaving_c, leaving_d = (out_vx, out_wx, out_vy, out_wy), (out_vx2, out_wx2, out_vy2, out_wy2)
    first_m = [
        send(raw_m.at[:, 0, pl.ds(0, 16), :], in_mx, to_west),
        send(out_my, in_my, to_south),
        send(out_corner, in_corner, to_corner),
    ]
    loaded("fields")
    for which in range(2):
        field_traces(which, [field_at(which, j) for j in range(4)])
        pack_field(which, which, leaving_a)
    first = send_all(leaving_a, arrived_a)
    loaded("velocity")
    for which in range(3):
        pack_velocity([velocity_at(which, j) for j in range(4)], which, leaving_c)
    first_v = send_all(leaving_c, arrived_c)

    loaded("tables")
    for column, target, gap in ((0, 0, 2), (1, 1, 2), (2, 4, 1), (3, 6, 1), (4, 8, 0), (5, 9, 0)):
        upper, lower = parted(square_in[:, 128 * column : 128 * (column + 1)])
        square[:, 128 * target : 128 * (target + 1)] = upper
        if gap:
            square[:, 128 * (target + gap) : 128 * (target + gap + 1)] = lower

    loaded("tall")
    upper, lower = parted(tall_in[...])
    tall[:, :128] = upper
    tall[:, 128:] = lower
    loaded("bounds")
    bound_rows[...] = jnp.zeros((4, 2, 8, 128), F32)
    for index in range(4):
        for zone in range(4):
            bound_rows[index, zone % 2, pl.ds(4 * (zone // 2), 4), pl.ds(0, 32)] = bound_in[
                index, zone
            ]
    values = bound_rows[...].reshape(64, 128)
    spreader = square[:, 128 * 9 : 128 * 10]
    upper = values.astype(BF16)
    rest = values - upper.astype(F32)
    middle = rest.astype(BF16)
    lowest = (rest - middle.astype(F32)).astype(BF16)
    values = product(upper, spreader) + (product(middle, spreader) + product(lowest, spreader))
    bounds[...] = values.reshape(4, 2, 8, 128)

    def velocity_before(which, values, base, scale):
        along_z = lanes_product(values, 4)
        closing = combine(stiff[4][:4], values)
        after = jnp.where(at_zone(full, 3), 0.0, spin(values[0], 7, 1))
        carried = jnp.where(at_zone(full, 0), 0.0, spin(closing, 1, 1))
        for j in range(4):
            parts = by_zone(values[j])
            places = [parts[:, i] for i in range(4)]
            ending = combine(stiff[4][:4], places)
            next_plane = jnp.stack(
                [parts[1, 0], jnp.where(low_rows, spin(parts[0, 0], 4, 0), 0.0)]
            )
            last_end = jnp.stack([jnp.where(low_rows, 0.0, spin(ending[1], 4, 0)), ending[0]])
            sums = []
            for a in range(4):
                factors = list(stiff[a])
                if a == 0:
                    factors[0] += stiff[4][4]
                total = combine(factors, places + [next_plane])
                sums.append(total + last_end if a == 0 else total)
            along_x = from_zone(sums)
            factors = list(stiff[j])
            if j == 0:
                factors[0] += stiff[4][4]
            along_y = combine(factors, values + [after])
            if j == 0:
                along_y = along_y + carried
            rate = (
                mesh_at(0, j) * along_x + mesh_at(1, j) * along_y + mesh_at(2, j) * along_z[j]
            )
            acc_v[which, j] = base(j) + (rate if scale == 1.0 else scale * rate)

    def velocity_after(which, scale, item, buffers):
        from_east, from_west, from_north, from_south = buffers
        later = unpack_x_high([from_east[item, 0], from_east[item, 1]])
        earlier = unpack_x_low([from_west[item, 0], from_west[item, 1]])
        above = jnp.where(at_zone(full, 3), unpack_y(from_north[item], 3), 0.0)
        below = jnp.where(at_zone(full, 0), unpack_y(from_south[item], 0), 0.0)
        done = []
        for j in range(4):
            ahead = jnp.where(low_rows, 0.0, later[j])
            behind = jnp.where(low_rows, earlier[j], 0.0)
            extra_x = jnp.stack(
                [scale * behind, zero, zero, zero]
                + [(scale * stiff[a][4]) * ahead for a in range(4)]
            )
            extra_y = (scale * stiff[j][4]) * above
            if j == 0:
                extra_y = extra_y + scale * below
            done.append(acc_v[which, j] + mesh_at(0, j) * extra_x + mesh_at(1, j) * extra_y)
        return done

    points = TABLE["to_points"]

    def picked(values):
        upper, lower = parted(values)
        picker = square[:, 128 * 8 : 128 * 9]
        return product(upper, picker) + product(lower, picker)

    def mesh_before(item):
        values = [mesh_at(min(item, 2), j) for j in range(4)]
        if item < 3:
            values = lanes_product(values, 6)
        else:
            total = picked(jnp.concatenate([v.reshape(64, 128) for v in values], 0))
            values = [total[64 * j : 64 * (j + 1)].reshape(full) for j in range(4)]
        across = []
        for b in range(4):
            parts = by_zone(values[b])
            places = [parts[:, a] for a in range(4)]
            inner = jnp.where(low_rows, spin(parts[0, 0], 4, 0), 0.0)
            places.append(jnp.stack([parts[1, 0], inner]))
            across.append(from_zone([combine(points[i], places) for i in range(4)]))
        last = at_zone(full, 3)
        across.append(jnp.where(last, 0.0, spin(across[0], 7, 1)))
        for j in range(4):
            result = combine(points[j], across)
            if item < 3:
                speed[item, j] = result
            else:
                face_z[j] = result
        if item == 0:
            for q in range(2):
                edge = [values[b][4 * q] for b in range(4)]
                edge.append(jnp.where(at_zone(plane, 3), 0.0, spin(edge[0], 7, 0)))
                for j in range(4):
                    face_x[q, j] = combine(points[j], edge)
        if item == 1:
            face_y[0] = across[0]
            face_y[1] = across[4]

    def mesh_halo():
        values = jnp.concatenate(
            [in_mx[...].reshape(48, 128), in_my[...].reshape(48, 128), in_corner[...], zero], 0
        )
        upper, lower = parted(values)
        wide = square[:, 128 * 6 : 128 * 8]
        both = product(upper, wide)
        both = both[:, :128] + both[:, 128:] + product(lower, wide[:, :128])
        extra = picked(values)
        for item in range(4):
            which, source = min(item, 2), both if item < 3 else extra
            rows = source[16 * which : 16 * (which + 1)]
            halo_x[item, pl.ds(0, 16)] = rows
            halo_x[item, pl.ds(16, 16)] = rows
            halo_y[item] = source[48 + 16 * which : 64 + 16 * which].reshape(2, 8, 128)
            halo_corner[item] = spin(source[96:104], 7 - which, 0)

    def mesh_after(item):
        rows = rows_of(plane)
        later = [
            jnp.where(low_rows, 0.0, halo_x[item, pl.ds(j, 8, stride=4), :]) for j in range(4)
        ]
        far = jnp.where(at_zone(plane, 3), 0.0, spin(later[0], 7, 0))
        far = jnp.where(rows == 7, halo_corner[item], far)
        later.append(jnp.where(low_rows, 0.0, far))
        above = jnp.where(at_zone(full, 3), unpack_y(halo_y[item], 3), 0.0)
        parts = by_zone(above)
        places = [parts[:, a] for a in range(4)]
        places.append(
            jnp.stack([parts[1, 0], jnp.where(low_rows, spin(parts[0, 0], 4, 0), 0.0)])
        )
        across = from_zone([combine(points[i], places) for i in range(4)])
        edge = [combine(points[j], later) for j in range(4)]
        for j in range(4):
            extra = points[j][4] * across
            extra = jnp.concatenate(
                [extra[:4], jnp.stack([extra[4 + i] + points[i][4] * edge[j] for i in range(4)])]
            )
            if item < 3:
                speed[item, j] += extra
            else:
                face_z[j] += extra
        if item == 0:
            for j in range(4):
                lowest = face_x[0, j] + points[j][4] * above[0]
                face_x[0, j] = lowest
                face_x[1, j] += points[j][4] * above[4]
                face_x[2, j] = jnp.where(low_rows, spin(lowest, 4, 0), edge[j])
        if item == 1:
            for side, halo, plain in ((0, later[0], None), (1, later[4], across)):
                for x in range(8):
                    if x < 4 and plain is None:
                        continue
                    value = face_y[side, x]
                    if plain is not None:
                        value = value + plain[x]
                    if x >= 4:
                        value = value + points[x - 4][4] * halo
                    face_y[side, x] = value

    def upwind(face, minus_side, plus_side):
        return jnp.maximum(face, 0.0) * minus_side + jnp.minimum(face, 0.0) * plus_side

    def field_before(which, values, base, scale):
        upper, lower = parted(jnp.concatenate([part.reshape(64, 128) for part in values], 0))
        wide = square[:, 0:256]
        sides = product(upper, wide) + product(lower, wide) + product(upper, square[:, 256:512])
        flux = [
            upwind(
                face_z[j],
                sides[64 * j : 64 * (j + 1), :128].reshape(full),
                sides[64 * j : 64 * (j + 1), 128:].reshape(full),
            ).reshape(64, 128)
            for j in range(4)
        ]
        moved = [(speed[2, j] * values[j]).reshape(64, 128) for j in range(4)]
        both = jnp.concatenate([jnp.concatenate(moved, 0), jnp.concatenate(flux, 0)], 1)
        upper, lower = parted(both)
        sums = product(upper, tall[...])
        along_z = sums[:, :128] + sums[:, 128:] + product(lower, tall[:, :128])
        moved = [speed[1, j] * values[j] for j in range(4)]
        for j in range(4):
            parts = by_zone(speed[0, j] * values[j])
            places = [parts[:, i] for i in range(4)]
            along_x = from_zone([combine(TABLE["volume"][i], places) for i in range(4)])
            along_y = combine(TABLE["volume"][j], moved)
            rate = along_x + along_y + along_z[64 * j : 64 * (j + 1)].reshape(full)
            acc_f[which, j] = base(j) + (rate if scale == 1.0 else scale * rate)

    def in_group(values, join):
        lane = lax.broadcasted_iota(jnp.int32, values.shape, 2)
        partner = jnp.where(lane % 2 == 0, spin(values, 127, 2), spin(values, 1, 2))
        values = join(values, partner)
        partner = jnp.where(lane // 2 % 2 == 0, spin(values, 126, 2), spin(values, 2, 2))
        return join(values, partner)

    def limited(which, values):
        weights = TABLE["weights"]
        across = by_zone(combine(weights, values))
        mean = combine(weights, [across[:, i] for i in range(4)])
        lane = lax.broadcasted_iota(jnp.int32, (2, 8, 128), 2) % 4
        middle = (lane == 1) | (lane == 2)
        mean = in_group(mean * jnp.where(middle, weights[1], weights[0]), jnp.add)
        top = functools.reduce(jnp.maximum, values)
        bottom = functools.reduce(jnp.minimum, values)
        top, bottom = by_zone(top), by_zone(bottom)
        top = functools.reduce(jnp.maximum, [top[:, i] for i in range(4)])
        bottom = functools.reduce(jnp.minimum, [bottom[:, i] for i in range(4)])
        rise = in_group(top, jnp.maximum) - mean
        fall = in_group(bottom, jnp.minimum) - mean
        low, high = bounds[2 * which], bounds[2 * which + 1]
        theta = jnp.minimum(
            (high - mean) / (rise + limit_eps), (mean - low) / (limit_eps - fall)
        )
        theta = jnp.clip(theta, 0.0, 1.0)
        result = []
        for j in range(4):
            parts = by_zone(values[j])
            result.append(
                from_zone([mean + theta * (parts[:, i] - mean) for i in range(4)])
            )
        return result

    def field_after(which, scale, item, buffers):
        from_east, from_west, from_north, from_south = buffers
        later = unpack_x_high([from_east[item, 0], from_east[item, 1]])
        earlier = unpack_x_low([from_west[item, 0], from_west[item, 1]])
        low_lift = [scale * factor for factor in TABLE["lift_low"]]
        high_lift = [-scale * factor for factor in TABLE["lift_high"]]
        low, high = trace_y[which, 0], trace_y[which, 1]
        before = jnp.where(at_zone(full, 0), unpack_y(from_south[item], 0), spin(high, 1, 1))
        after = jnp.where(at_zone(full, 3), unpack_y(from_north[item], 3), spin(low, 7, 1))
        lower_y = upwind(face_y[0], before, low)
        upper_y = upwind(face_y[1], high, after)
        values = []
        for j in range(4):
            low, high = trace_x[which, 0, j], trace_x[which, 1, j]
            before = jnp.where(low_rows, earlier[j], spin(high[1], 4, 0))
            after = jnp.where(low_rows, spin(low[0], 4, 0), later[j])
            flux = [
                upwind(face_x[0, j], before, low[0]),
                upwind(face_x[1, j], high[0], low[1]),
                upwind(face_x[2, j], high[1], after),
            ]
            lower_x, upper_x = jnp.stack(flux[:2]), jnp.stack(flux[1:])
            lift = from_zone(
                [low_lift[i] * lower_x + high_lift[i] * upper_x for i in range(4)]
            )
            values.append(
                acc_f[which, j] + lift + (low_lift[j] * lower_y + high_lift[j] * upper_y)
            )
        return limited(which, values)

    for item in range(4):
        mesh_before(item)
    for which in range(3):
        values = [velocity_at(which, j) for j in range(4)]
        velocity_before(which, values, lambda j: values[j], 1.0)
    for copy in first_m:
        copy.wait_recv()
    mesh_halo()
    for item in range(4):
        mesh_after(item)
    for which in range(2):
        values = [field_at(which, j) for j in range(4)]
        field_before(which, values, lambda j: values[j], 1.0)
    for copy in first:
        copy.wait_recv()
    second = []
    for which in range(2):
        values = field_after(which, 1.0, which, arrived_a)
        for j in range(4):
            sec_f[which, j] = values[j]
        field_traces(which, values)
        pack_field(which, which, leaving_b)
        second.append(
            send_all([ref.at[which] for ref in leaving_b], [ref.at[which] for ref in arrived_b])
        )
    for copy in first_v:
        copy.wait_recv()
    for which in range(3):
        values = velocity_after(which, 1.0, which, arrived_c)
        for j in range(4):
            sec_v[which, j] = values[j]
        pack_velocity(values, which, leaving_d)
    second_v = send_all(leaving_d, arrived_d)

    for which in range(2):
        values = [sec_f[which, j] for j in range(4)]
        field_before(which, values, lambda j: 0.5 * field_at(which, j) + 0.5 * values[j], 0.5)
    for which in range(3):
        values = [sec_v[which, j] for j in range(4)]
        velocity_before(
            which, values, lambda j: 0.5 * velocity_at(which, j) + 0.5 * values[j], 0.5
        )
    for which in range(2):
        for copy in second[which]:
            copy.wait_recv()
        values = field_after(which, 0.5, which, arrived_b)
        for j in range(4):
            results[which, :, pl.ds(j, 8, stride=4), :] = values[j]
    for copy in second_v:
        copy.wait_recv()
    for which in range(3):
        values = velocity_after(which, 0.5, which, arrived_d)
        for j in range(4):
            results[2 + which, :, pl.ds(j, 8, stride=4), :] = values[j]
    for copy in copies:
        copy.wait_send()


def unfold(results, new_density, new_energy, new_velocity, store_sem):
    copies = []
    for half in range(2):
        rows, block = pl.ds(16 * half, 16), pl.ds(8 * half, 8)
        for source, target in (
            (results.at[0, :, rows, :], new_density.at[block]),
            (results.at[1, :, rows, :], new_energy.at[block]),
            (results.at[pl.ds(2, 3), :, rows, :], new_velocity.at[:, block]),
        ):
            copy = pltpu.make_async_copy(source, target, store_sem.at[len(copies)])
            copy.start()
            copies.append(copy)
    for copy in copies:
        copy.wait()


def solution(mesh):
    counts = (mesh.shape["gx"], mesh.shape["gy"])
    square, tall = lane_matrices(128)

    def on_device(*arguments):
        vmem = lambda *shape: pltpu.VMEM(shape, F32)
        scratch = [
            vmem(2, 8, 32, 128), vmem(3, 8, 32, 128), vmem(3, 8, 32, 128),
            vmem(*square.shape), vmem(*tall.shape),
            pltpu.VMEM((128, 1280), BF16), pltpu.VMEM((256, 256), BF16),
            vmem(4, 4, 4, 32), vmem(4, 2, 8, 128), vmem(4, 2, 8, 128),
            vmem(3, 4, 8, 8, 128), vmem(3, 4, 8, 8, 128),
            vmem(2, 4, 8, 8, 128), vmem(2, 4, 8, 8, 128),
            vmem(3, 4, 8, 8, 128), vmem(3, 4, 8, 128), vmem(2, 8, 8, 128), vmem(4, 8, 8, 128),
            vmem(2, 2, 4, 2, 8, 128), vmem(2, 2, 8, 8, 128),
            vmem(4, 32, 128), vmem(4, 2, 8, 128), vmem(4, 8, 128),
        ]
        scratch += [vmem(2, 2, 8, 128)] * 8
        scratch += [vmem(3, 2, 8, 128), vmem(3, 16, 128), vmem(3, 2, 8, 128)] + [vmem(8, 128)] * 2
        for items in (3, 2, 3):
            scratch += [vmem(items, 2, 8, 128)] * 8
        scratch += [
            pltpu.SemaphoreType.DMA((14,)),
            pltpu.SemaphoreType.DMA((23,)),
            pltpu.SemaphoreType.DMA((23,)),
        ]
        operands = [
            pltpu.with_memory_space_constraint(value, pltpu.HBM)
            for value in (*arguments, jnp.asarray(square), jnp.asarray(tall))
        ]
        results = pl.pallas_call(
            functools.partial(kernel, counts),
            out_shape=pltpu.VMEM((5, 8, 32, 128), F32),
            in_specs=[pl.BlockSpec(memory_space=pltpu.HBM)] * 10,
            out_specs=pl.BlockSpec(memory_space=pltpu.VMEM),
            scratch_shapes=scratch,
            compiler_params=pltpu.CompilerParams(
                collective_id=0, has_side_effects=True, vmem_limit_bytes=32 * 1024 * 1024
            ),
        )(*operands)
        return pl.pallas_call(
            unfold,
            out_shape=[jax.ShapeDtypeStruct(value.shape, F32) for value in arguments[:3]],
            in_specs=[pl.BlockSpec(memory_space=pltpu.VMEM)],
            out_specs=[pl.BlockSpec(memory_space=pltpu.HBM)] * 3,
            scratch_shapes=[pltpu.SemaphoreType.DMA((6,))],
            compiler_params=pltpu.CompilerParams(vmem_limit_bytes=32 * 1024 * 1024),
        )(results)

    fields, vectors = P("gx", "gy", None), P(None, "gx", "gy", None)
    return jax.shard_map(
        on_device,
        mesh=mesh,
        in_specs=(fields, fields, vectors, vectors, fields, fields, fields, fields),
        out_specs=(fields, fields, vectors),
        check_vma=False,
    )
```

```python
import functools
import math

import jax
import jax.numpy as jnp
import numpy as np
from jax import lax
from jax.experimental import pallas as pl
from jax.experimental.pallas import tpu as pltpu
from jax.sharding import PartitionSpec as P

MESH = pl.DeviceIdType.MESH
F32 = jnp.float32
BF16 = jnp.bfloat16
time_step = 0.02
limit_eps = 1e-06


def lagrange_values(node_set, points):
    result = np.ones((len(points), len(node_set)))
    for column in range(len(node_set)):
        for partner in range(len(node_set)):
            if partner != column:
                result[:, column] = (
                    result[:, column]
                    * (points - node_set[partner])
                    / (node_set[column] - node_set[partner])
                )
    return result


def lagrange_slopes(node_set, points):
    node_total = len(node_set)
    result = np.zeros((len(points), node_total))
    for column in range(node_total):
        for skipped in range(node_total):
            if skipped != column:
                factor = np.ones(len(points)) / (node_set[column] - node_set[skipped])
                for partner in range(node_total):
                    if partner != column and partner != skipped:
                        factor = (
                            factor
                            * (points - node_set[partner])
                            / (node_set[column] - node_set[partner])
                        )
                result[:, column] = result[:, column] + factor
    return result


def basis_tables():
    gauss_points = np.array(
        [-0.8611363115940526, -0.3399810435848563, 0.3399810435848563, 0.8611363115940526]
    )
    gauss_weights = np.array(
        [0.3478548451374538, 0.6521451548625461, 0.6521451548625461, 0.3478548451374538]
    )
    lobatto_points = np.array([-1.0, -math.sqrt(3.0 / 7.0), 0.0, math.sqrt(3.0 / 7.0), 1.0])
    lobatto_weights = np.array([0.1, 49.0 / 90.0, 32.0 / 45.0, 49.0 / 90.0, 0.1])
    slopes = lagrange_slopes(gauss_points, gauss_points)
    volume = (2.0 / gauss_weights)[:, None] * slopes.T * gauss_weights[None, :]
    trace_low = lagrange_values(gauss_points, np.array([-1.0]))[0]
    trace_high = lagrange_values(gauss_points, np.array([1.0]))[0]
    stiffness = (
        2.0 * lobatto_weights[:, None] * lagrange_slopes(lobatto_points, lobatto_points)
    )
    lumped = np.array([0.2, lobatto_weights[1], lobatto_weights[2], lobatto_weights[3], 0.2])
    return {
        "weights": gauss_weights / 2.0,
        "volume": time_step * volume,
        "trace_low": trace_low,
        "trace_high": trace_high,
        "lift_low": time_step * 2.0 * trace_low / gauss_weights,
        "lift_high": time_step * 2.0 * trace_high / gauss_weights,
        "to_points": lagrange_values(lobatto_points, gauss_points),
        "stiffness": -time_step * stiffness / lumped[:, None],
    }


TABLES = basis_tables()
TABLE = {name: TABLES[name].tolist() for name in TABLES}


def lane_matrices(lanes):
    zones = lanes // 4
    shape = (lanes, lanes)
    volume, lift = np.zeros(shape), np.zeros(shape)
    minus, plus = np.zeros(shape), np.zeros(shape)
    stiff, interp = np.zeros(shape), np.zeros(shape)
    pick, spread = np.zeros(shape), np.zeros(shape)
    for zone in range(zones):
        at = 4 * zone
        before = 4 * ((zone - 1) % zones)
        for within in range(4):
            for source in range(4):
                volume[at + source, at + within] = TABLES["volume"][within, source]
                minus[before + source, at + within] = TABLES["trace_high"][source]
                plus[at + source, at + within] = TABLES["trace_low"][source]
            lift[at, at + within] = TABLES["lift_low"][within]
            lift[at, before + within] = -TABLES["lift_high"][within]
            pick[at, at + within] = 1.0
            spread[zone, at + within] = 1.0
            for source in range(5):
                interp[(at + source) % lanes, at + within] += TABLES["to_points"][within, source]
        for target in range(5):
            for source in range(5):
                stiff[(at + source) % lanes, (at + target) % lanes] += TABLES["stiffness"][
                    target, source
                ]
    square = np.concatenate([minus, plus, stiff, interp, pick, spread], axis=1)
    tall = np.concatenate([volume, lift], axis=0)
    return square.astype(np.float32), tall.astype(np.float32)


def spin(values, steps, axis):
    size = values.shape[axis]
    steps = steps % size
    return values if steps == 0 else pltpu.roll(values, steps, axis)


def rows_of(shape):
    return lax.broadcasted_iota(jnp.int32, shape, len(shape) - 2)


def low_half(shape):
    return rows_of(shape) < 4


def at_zone(shape, zone):
    return rows_of(shape) % 4 == zone


def combine(coefficients, terms):
    total = None
    for factor, term in zip(coefficients, terms):
        part = factor * term
        total = part if total is None else total + part
    return total


def parted(values):
    upper = values.astype(BF16)
    return upper, (values - upper.astype(F32)).astype(BF16)


def product(left, right):
    return jnp.dot(left, right, preferred_element_type=F32)


def mirrored(matrix):
    size = len(matrix[0])
    middle = size // 2
    even = [[(row[c] + row[size - 1 - c]) / 2 for c in range(middle)] for row in matrix]
    odd = [[(row[c] - row[size - 1 - c]) / 2 for c in range(middle)] for row in matrix]
    centre = [row[middle] for row in matrix] if size % 2 else None
    return even, odd, centre


def pairs_of(values):
    size = len(values)
    sums = [values[c] + values[size - 1 - c] for c in range(size // 2)]
    gaps = [values[c] - values[size - 1 - c] for c in range(size // 2)]
    return sums, gaps


def slopes_of(matrix, values):
    even, odd, centre = mirrored(matrix)
    sums, gaps = pairs_of(values)
    size = len(matrix)
    result = [None] * size
    for a in range(size // 2):
        factors, terms = list(even[a]), list(sums)
        if centre is not None:
            factors.append(centre[a])
            terms.append(values[size // 2])
        outer, inner = combine(factors, terms), combine(odd[a], gaps)
        result[a], result[size - 1 - a] = inner + outer, inner - outer
    if size % 2:
        result[size // 2] = combine(odd[size // 2], gaps)
    return result


def points_of(matrix, values):
    even, odd, centre = mirrored(matrix)
    sums, gaps = pairs_of(values)
    result = [None] * 4
    for i in range(2):
        outer = combine(even[i] + [centre[i]], sums + [values[2]])
        inner = combine(odd[i], gaps)
        result[i], result[3 - i] = outer + inner, outer - inner
    return result


def traces_of(values):
    sums, gaps = pairs_of(values)
    even, odd, _ = mirrored([TABLE["trace_low"]])
    outer, inner = combine(even[0], sums), combine(odd[0], gaps)
    return outer + inner, outer - inner


def lifts_of(lower, upper):
    even, odd, _ = mirrored([TABLE["lift_low"]])
    gap, both = lower - upper, lower + upper
    result = [None] * 4
    for i in range(2):
        outer, inner = even[0][i] * gap, odd[0][i] * both
        result[i], result[3 - i] = outer + inner, outer - inner
    return result


def turned(pieces):
    return [jnp.stack([pieces[j][i] for j in range(4)]) for i in range(4)]


def pack_x_low(planes):
    mask = low_half((8, 128))
    return [jnp.where(mask, planes[t], spin(planes[t + 1], 4, 0)) for t in (0, 2)]


def pack_x_high(planes):
    mask = low_half((8, 128))
    return [jnp.where(mask, spin(planes[t], 4, 0), planes[t + 1]) for t in (0, 2)]


def unpack_x_high(packed):
    return [spin(packed[0], 4, 0), packed[0], spin(packed[1], 4, 0), packed[1]]


def unpack_x_low(packed):
    return [packed[0], spin(packed[0], 4, 0), packed[1], spin(packed[1], 4, 0)]


def pack_y(values, start):
    shape = (8, 128)
    packed = []
    for half in range(2):
        total = spin(values[4 * half + 3], 3 - start, 0)
        for place in (2, 1, 0):
            moved = spin(values[4 * half + place], place - start, 0)
            total = jnp.where(at_zone(shape, place), moved, total)
        packed.append(total)
    return packed


def unpack_y(packed, end):
    return jnp.stack([spin(packed, end - place, 0) for place in range(4)])


def kernel(
    counts,
    density, energy, velocity, mesh_velocity, density_low, density_high, energy_low, energy_high,
    square_hbm, tall_hbm,
    results,
    raw_u, raw_v, raw_m, square_in, tall_in, square, ends, picker, tall, bound_in, bound_rows,
    bounds, work_u, work_v, work_m,
    acc_v, sec_v, acc_f, sec_f, speed, face_x, face_y, trace_x, trace_y, ends_z,
    halo_x, halo_y, halo_corner,
    out_dx, out_ux, out_dy, out_uy, in_dx, in_ux, in_dy, in_uy,
    out_my, in_mx, in_my, out_corner, in_corner,
    out_vx, out_wx, out_vy, out_wy, in_vx, in_wx, in_vy, in_wy,
    out_dx2, out_ux2, out_dy2, out_uy2, in_dx2, in_ux2, in_dy2, in_uy2,
    out_vx2, out_wx2, out_vy2, out_wy2, in_vx2, in_wx2, in_vy2, in_wy2,
    load_sem, send_sem, recv_sem,
):
    count_x, count_y = counts
    here_x, here_y = lax.axis_index("gx"), lax.axis_index("gy")
    west = lax.rem(here_x + count_x - 1, count_x)
    east = lax.rem(here_x + 1, count_x)
    south = lax.rem(here_y + count_y - 1, count_y)
    north = lax.rem(here_y + 1, count_y)
    to_west, to_east = (west, here_y), (east, here_y)
    to_south, to_north = (here_x, south), (here_x, north)
    to_corner, from_corner = (west, south), (east, north)

    loads = {}

    def load(name, source, target):
        copy = pltpu.make_async_copy(source, target, load_sem.at[sum(map(len, loads.values()))])
        copy.start()
        loads.setdefault(name, []).append(copy)

    def loaded(name):
        for copy in loads[name]:
            copy.wait()

    places = [(pl.ds(16 * half, 16), pl.ds(8 * half, 8)) for half in range(2)]
    for rows, block in places:
        load("mesh", mesh_velocity.at[:, block], raw_m.at[:, :, rows, :])
    load("tables", square_hbm, square_in)
    for rows, block in places:
        load("fields", density.at[block], raw_u.at[0, :, rows, :])
        load("fields", energy.at[block], raw_u.at[1, :, rows, :])
    for rows, block in places:
        load("velocity", velocity.at[:, block], raw_v.at[:, :, rows, :])
    load("tall", tall_hbm, tall_in)
    for index, source in enumerate((density_low, density_high, energy_low, energy_high)):
        load("bounds", source, bound_in.at[index])

    barrier = pltpu.get_barrier_semaphore()
    for peer in (to_west, to_east, to_south, to_north, to_corner, from_corner):
        pl.semaphore_signal(barrier, inc=1, device_id=peer, device_id_type=MESH)

    quad, plane = (4, 8, 128), (8, 128)
    low_rows, low_quad = low_half(plane), low_half(quad)
    first_zone, last_zone = at_zone(quad, 0), at_zone(quad, 3)
    stiff, points = TABLE["stiffness"], TABLE["to_points"]
    zero = jnp.zeros(plane, F32)

    def arrange(source, target, which):
        for j in range(4):
            target[which, :, j] = source[which, :, pl.ds(j, 8, stride=4), :]

    def put_pair(target, item, pair):
        target[item, 0] = pair[0]
        target[item, 1] = pair[1]

    def sided(values):
        upper, lower = parted(values)
        return upper, jnp.concatenate([upper, lower], 1)

    def lanes_product(values, column):
        _, pair = sided(values)
        both = product(pair, square[:, 256 * column : 256 * (column + 1)])
        return both[:, :128] + both[:, 128:]

    def picked(values):
        return product(sided(values)[1], picker[...])

    def field_traces(which, source):
        for half in range(2):
            chunk = pl.ds(4 * half, 4)
            low, high = traces_of([source[which, 4 * half + i] for i in range(4)])
            trace_x[which, 0, half], trace_x[which, 1, half] = low, high
            low, high = traces_of([source[which, chunk, j] for j in range(4)])
            trace_y[which, 0, chunk], trace_y[which, 1, chunk] = low, high

    def pack_field(which, item, buffers):
        west_to, east_to, south_to, north_to = buffers
        put_pair(west_to, item, pack_x_low(trace_x[which, 0, 0]))
        put_pair(east_to, item, pack_x_high(trace_x[which, 1, 1]))
        put_pair(south_to, item, pack_y(trace_y[which, 0], 0))
        put_pair(north_to, item, pack_y(trace_y[which, 1], 3))

    def pack_velocity(source, item, buffers):
        west_to, east_to, south_to, north_to = buffers
        put_pair(west_to, item, pack_x_low(source[item, 0]))
        closing = combine(stiff[4][:4], [source[item, 4 + a] for a in range(4)])
        put_pair(east_to, item, pack_x_high(closing))
        put_pair(south_to, item, pack_y(source[item, :, 0], 0))
        closing = combine(stiff[4][:4], [source[item, :, j] for j in range(4)])
        put_pair(north_to, item, pack_y(closing, 3))

    loaded("mesh")
    corner = zero
    for which in range(3):
        values = raw_m[which, :, pl.ds(0, 8, stride=4), :]
        put_pair(out_my, which, pack_y(values, 0))
        corner = jnp.where(rows_of(plane) == which, spin(values[0], which, 0), corner)
    out_corner[...] = corner

    pl.semaphore_wait(barrier, 6)
    copies = []
    peers = (to_west, to_east, to_south, to_north)

    def send(source, target, peer):
        copy = pltpu.make_async_remote_copy(
            src_ref=source, dst_ref=target,
            send_sem=send_sem.at[len(copies)], recv_sem=recv_sem.at[len(copies)],
            device_id=peer, device_id_type=MESH,
        )
        copy.start()
        copies.append(copy)
        return copy

    def send_all(sources, targets):
        return [send(*triple) for triple in zip(sources, targets, peers)]

    arrived_a, arrived_b = (in_dx, in_ux, in_dy, in_uy), (in_dx2, in_ux2, in_dy2, in_uy2)
    leaving_a, leaving_b = (out_dx, out_ux, out_dy, out_uy), (out_dx2, out_ux2, out_dy2, out_uy2)
    arrived_c, arrived_d = (in_vx, in_wx, in_vy, in_wy), (in_vx2, in_wx2, in_vy2, in_wy2)
    leaving_c, leaving_d = (out_vx, out_wx, out_vy, out_wy), (out_vx2, out_wx2, out_vy2, out_wy2)
    first_m = [
        send(raw_m.at[:, 0, pl.ds(0, 16), :], in_mx, to_west),
        send(out_my, in_my, to_south),
        send(out_corner, in_corner, to_corner),
    ]
    loaded("fields")
    for which in range(2):
        arrange(raw_u, work_u, which)
        field_traces(which, work_u)
        pack_field(which, which, leaving_a)
    first = send_all(leaving_a, arrived_a)
    loaded("velocity")
    for which in range(3):
        arrange(raw_v, work_v, which)
        pack_velocity(work_v, which, leaving_c)
    first_v = send_all(leaving_c, arrived_c)

    loaded("tables")
    minus, plus, stiff_z, interp_z, pick_z, spread_z = (
        square_in[:, 128 * column : 128 * (column + 1)] for column in range(6)
    )
    for column, table in enumerate((stiff_z, interp_z)):
        upper, lower = parted(table)
        at = 256 * column
        square[:128, at : at + 128] = upper
        square[128:, at : at + 128] = upper
        square[:128, at + 128 : at + 256] = lower
        square[128:, at + 128 : at + 256] = jnp.zeros((128, 128), BF16)
    for column, table in enumerate((minus, plus)):
        upper, lower = parted(table)
        at = 128 * column
        ends[:128, at : at + 128] = upper
        ends[128:256, at : at + 128] = upper
        ends[256:, at : at + 128] = lower
    picker[:128] = pick_z.astype(BF16)
    picker[128:] = pick_z.astype(BF16)
    loaded("tall")
    upper, lower = parted(tall_in[...])
    tall[:, :128] = upper
    tall[:, 128:] = lower

    loaded("bounds")
    bound_rows[...] = jnp.zeros((4, 2, 8, 128), F32)
    for index in range(4):
        for zone in range(4):
            bound_rows[index, zone % 2, pl.ds(4 * (zone // 2), 4), pl.ds(0, 32)] = bound_in[
                index, zone
            ]
    values = bound_rows[...].reshape(64, 128)
    spreader = spread_z.astype(BF16)
    upper = values.astype(BF16)
    rest = values - upper.astype(F32)
    middle = rest.astype(BF16)
    lowest = (rest - middle.astype(F32)).astype(BF16)
    values = product(upper, spreader) + (product(middle, spreader) + product(lowest, spreader))
    bounds[...] = values.reshape(4, 2, 8, 128)

    def velocity_before(which, source, base):
        along_z = lanes_product(source[which].reshape(256, 128), 0).reshape(8, 4, 8, 128)
        own = stiff[4][4]
        opening = source[which, 0]
        inner = jnp.where(low_quad, spin(opening, 4, 1), 0.0)
        last_end = combine(stiff[4], [source[which, 4 + a] for a in range(4)] + [inner])
        carried = jnp.where(low_quad, own * opening, spin(last_end, 4, 1))
        for half in range(2):
            chunk = pl.ds(4 * half, 4)
            ahead = source[which, 4] if half == 0 else inner
            along_x = slopes_of(stiff, [source[which, 4 * half + a] for a in range(4)] + [ahead])
            along_x[0] = along_x[0] + carried
            carried = along_x[4]
            lines = [source[which, chunk, j] for j in range(4)]
            ahead = jnp.where(last_zone, 0.0, spin(lines[0], 7, 1))
            along_y = slopes_of(stiff, lines + [ahead])
            along_y[0] = along_y[0] + jnp.where(first_zone, own * lines[0], spin(along_y[4], 1, 1))
            along_y = turned(along_y[:4])
            for a in range(4):
                x = 4 * half + a
                acc_v[which, x] = base(x) + (
                    work_m[0, x] * along_x[a]
                    + work_m[1, x] * along_y[a]
                    + work_m[2, x] * along_z[x]
                )

    def velocity_after(which, put, arrived):
        from_east, from_west, from_north, from_south = arrived
        later = jnp.stack(unpack_x_high([from_east[which, 0], from_east[which, 1]]))
        earlier = jnp.stack(unpack_x_low([from_west[which, 0], from_west[which, 1]]))
        later = jnp.where(low_quad, 0.0, later)
        earlier = jnp.where(low_quad, earlier, 0.0)
        for half in range(2):
            above = jnp.where(last_zone, unpack_y(from_north[which, half], 3), 0.0)
            below = jnp.where(first_zone, unpack_y(from_south[which, half], 0), 0.0)
            extra_y = [stiff[j][4] * above for j in range(4)]
            extra_y[0] = extra_y[0] + below
            extra_y = turned(extra_y)
            for a in range(4):
                x = 4 * half + a
                value = acc_v[which, x] + work_m[1, x] * extra_y[a]
                if half == 1:
                    value = value + work_m[0, x] * (stiff[a][4] * later)
                elif a == 0:
                    value = value + work_m[0, x] * earlier
                put(x, value)

    def mesh_before(item):
        values = work_m[min(item, 2)].reshape(256, 128)
        values = lanes_product(values, 1) if item < 3 else picked(values)
        values = values.reshape(8, 4, 8, 128)
        inner = jnp.where(low_quad, spin(values[0], 4, 1), 0.0)
        for half in range(2):
            chunk = pl.ds(4 * half, 4)
            ahead = values[4] if half == 0 else inner
            across = points_of(points, [values[4 * half + a] for a in range(4)] + [ahead])
            across = turned(across)
            ahead = jnp.where(last_zone, 0.0, spin(across[0], 7, 1))
            for j, result in enumerate(points_of(points, across + [ahead])):
                speed[item, chunk, j] = result
            if item == 0:
                edge = values[4 * half]
                ahead = jnp.where(at_zone(plane, 3), 0.0, spin(edge[0], 7, 0))
                edge = points_of(points, [edge[j] for j in range(4)] + [ahead])
                face_x[half] = jnp.stack(edge)
            if item == 1:
                face_y[0, chunk] = across[0]
                face_y[1, chunk] = ahead

    def mesh_halo():
        values = jnp.concatenate(
            [in_mx[...].reshape(48, 128), in_my[...].reshape(48, 128), in_corner[...], zero], 0
        )
        both, extra = lanes_product(values, 1), picked(values)
        for item in range(4):
            which, source = min(item, 2), both if item < 3 else extra
            rows = source[16 * which : 16 * (which + 1)]
            halo_x[item, pl.ds(0, 16)] = rows
            halo_x[item, pl.ds(16, 16)] = rows
            halo_y[item] = source[48 + 16 * which : 64 + 16 * which].reshape(2, 8, 128)
            halo_corner[item] = spin(source[96:104], 7 - which, 0)

    def mesh_after(item):
        rows = rows_of(plane)
        later = [
            jnp.where(low_rows, 0.0, halo_x[item, pl.ds(j, 8, stride=4), :]) for j in range(4)
        ]
        far = jnp.where(at_zone(plane, 3), 0.0, spin(later[0], 7, 0))
        far = jnp.where(rows == 7, halo_corner[item], far)
        later.append(jnp.where(low_rows, 0.0, far))
        edge = jnp.stack(points_of(points, later))
        above = [
            jnp.where(last_zone, unpack_y(halo_y[item, half], 3), 0.0) for half in range(2)
        ]
        inner = jnp.where(low_rows, spin(above[0][0], 4, 0), 0.0)
        for half in range(2):
            ahead = above[1][0] if half == 0 else inner
            across = points_of(points, [above[half][a] for a in range(4)] + [ahead])
            for i in range(4):
                x = 4 * half + i
                extra = jnp.stack([points[j][4] * across[i] for j in range(4)])
                if half == 1:
                    extra = extra + points[i][4] * edge
                speed[item, x] += extra
                if item == 1:
                    upper = face_y[1, x] + across[i]
                    if half == 1:
                        upper = upper + points[i][4] * later[4]
                        face_y[0, x] += points[i][4] * later[0]
                    face_y[1, x] = upper
            if item == 0:
                face_x[half] += jnp.stack([points[j][4] * above[half][0] for j in range(4)])
        if item == 0:
            face_x[2] = jnp.where(low_quad, spin(face_x[0], 4, 1), edge)

    def upwind(face, minus_side, plus_side):
        return jnp.maximum(face, 0.0) * minus_side + jnp.minimum(face, 0.0) * plus_side

    def field_ends(which, source):
        upper, pair = sided(source[which].reshape(256, 128))
        sides = product(pair, ends[:256]) + product(upper, ends[256:])
        ends_z[which, 0] = sides[:, :128]
        ends_z[which, 1] = sides[:, 128:]

    def field_before(which, source, base):
        values = source[which].reshape(256, 128)
        flux = upwind(speed[3].reshape(256, 128), ends_z[which, 0], ends_z[which, 1])
        moved = speed[2].reshape(256, 128) * values
        upper, lower = parted(jnp.concatenate([moved, flux], 1))
        sums = product(upper, tall[...])
        along_z = sums[:, :128] + sums[:, 128:] + product(lower, tall[:, :128])
        along_z = along_z.reshape(8, 4, 8, 128)
        for half in range(2):
            chunk = pl.ds(4 * half, 4)
            places = [4 * half + i for i in range(4)]
            along_x = slopes_of(TABLE["volume"], [speed[0, x] * source[which, x] for x in places])
            along_y = slopes_of(
                TABLE["volume"],
                [speed[1, chunk, j] * source[which, chunk, j] for j in range(4)],
            )
            along_y = turned(along_y)
            for i, x in enumerate(places):
                acc_f[which, x] = base(x) + ((along_x[i] + along_y[i]) + along_z[x])

    def in_group(values, join):
        lane = lax.broadcasted_iota(jnp.int32, plane, 1)
        partner = jnp.where(lane % 2 == 0, spin(values, 127, 1), spin(values, 1, 1))
        values = join(values, partner)
        partner = jnp.where(lane // 2 % 2 == 0, spin(values, 126, 1), spin(values, 2, 1))
        return join(values, partner)

    def over_zone(values, join):
        total = functools.reduce(join, values)
        return functools.reduce(join, [total[j] for j in range(4)])

    def limited(which, half, values):
        weights = TABLE["weights"]
        mean = combine(weights, values)
        mean = combine(weights, [mean[j] for j in range(4)])
        lane = lax.broadcasted_iota(jnp.int32, plane, 1) % 4
        middle = (lane == 1) | (lane == 2)
        mean = in_group(mean * jnp.where(middle, weights[1], weights[0]), jnp.add)
        rise = in_group(over_zone(values, jnp.maximum), jnp.maximum) - mean
        fall = in_group(over_zone(values, jnp.minimum), jnp.minimum) - mean
        low, high = bounds[2 * which, half], bounds[2 * which + 1, half]
        theta = jnp.minimum(
            (high - mean) / (rise + limit_eps), (mean - low) / (limit_eps - fall)
        )
        theta = jnp.clip(theta, 0.0, 1.0)
        return [mean + theta * (value - mean) for value in values]

    def field_after(which, scale, put, arrived):
        from_east, from_west, from_north, from_south = arrived
        later = jnp.stack(unpack_x_high([from_east[which, 0], from_east[which, 1]]))
        earlier = jnp.stack(unpack_x_low([from_west[which, 0], from_west[which, 1]]))
        low, high = trace_x[which, 0], trace_x[which, 1]
        flux = [
            upwind(face_x[0], jnp.where(low_quad, earlier, spin(high[1], 4, 1)), low[0]),
            upwind(face_x[1], high[0], low[1]),
            upwind(face_x[2], high[1], jnp.where(low_quad, spin(low[0], 4, 1), later)),
        ]
        for half in range(2):
            chunk = pl.ds(4 * half, 4)
            low, high = trace_y[which, 0, chunk], trace_y[which, 1, chunk]
            before = jnp.where(first_zone, unpack_y(from_south[which, half], 0), spin(high, 1, 1))
            after = jnp.where(last_zone, unpack_y(from_north[which, half], 3), spin(low, 7, 1))
            lift_y = turned(
                lifts_of(
                    upwind(face_y[0, chunk], before, low), upwind(face_y[1, chunk], high, after)
                )
            )
            lift_x = lifts_of(flux[half], flux[half + 1])
            values = [
                acc_f[which, 4 * half + i] + (lift_x[i] + lift_y[i]) for i in range(4)
            ]
            if scale != 1.0:
                values = [scale * value for value in values]
            values = limited(which, half, values)
            for i in range(4):
                put(4 * half + i, values[i])

    for which in range(3):
        arrange(raw_m, work_m, which)
    for item in range(4):
        mesh_before(item)
    for which in range(2):
        field_ends(which, work_u)
    for which in range(3):
        velocity_before(which, work_v, lambda x: work_v[which, x])
    for copy in first_m:
        copy.wait_recv()
    mesh_halo()
    for item in range(4):
        mesh_after(item)
    for which in range(2):
        field_before(which, work_u, lambda x: work_u[which, x])
    for copy in first:
        copy.wait_recv()

    def keep_field(x, value):
        sec_f[which, x] = value

    def keep_velocity(x, value):
        sec_v[which, x] = value

    second = []
    for which in range(2):
        field_after(which, 1.0, keep_field, arrived_a)
        field_traces(which, sec_f)
        pack_field(which, which, leaving_b)
        second.append(
            send_all([ref.at[which] for ref in leaving_b], [ref.at[which] for ref in arrived_b])
        )
    for copy in first_v:
        copy.wait_recv()
    for which in range(3):
        velocity_after(which, keep_velocity, arrived_c)
        pack_velocity(sec_v, which, leaving_d)
    second_v = send_all(leaving_d, arrived_d)

    for which in range(2):
        field_ends(which, sec_f)
    for which in range(2):
        field_before(which, sec_f, lambda x: work_u[which, x] + sec_f[which, x])
    for which in range(3):
        velocity_before(which, sec_v, lambda x: work_v[which, x] + sec_v[which, x])

    def finish_field(x, value):
        for j in range(4):
            results[which, x, pl.ds(j, 8, stride=4), :] = value[j]

    def finish_velocity(x, value):
        for j in range(4):
            results[2 + which, x, pl.ds(j, 8, stride=4), :] = 0.5 * value[j]

    for which in range(2):
        for copy in second[which]:
            copy.wait_recv()
        field_after(which, 0.5, finish_field, arrived_b)
    for copy in second_v:
        copy.wait_recv()
    for which in range(3):
        velocity_after(which, finish_velocity, arrived_d)
    for copy in copies:
        copy.wait_send()


def unfold(results, new_density, new_energy, new_velocity, store_sem):
    copies = []
    for half in range(2):
        rows, block = pl.ds(16 * half, 16), pl.ds(8 * half, 8)
        for source, target in (
            (results.at[0, :, rows, :], new_density.at[block]),
            (results.at[1, :, rows, :], new_energy.at[block]),
            (results.at[pl.ds(2, 3), :, rows, :], new_velocity.at[:, block]),
        ):
            copy = pltpu.make_async_copy(source, target, store_sem.at[len(copies)])
            copy.start()
            copies.append(copy)
    for copy in copies:
        copy.wait()


def solution(mesh):
    counts = (mesh.shape["gx"], mesh.shape["gy"])
    square, tall = lane_matrices(128)

    def on_device(*arguments):
        vmem = lambda *shape: pltpu.VMEM(shape, F32)
        scratch = [
            vmem(2, 8, 32, 128), vmem(3, 8, 32, 128), vmem(3, 8, 32, 128),
            vmem(*square.shape), vmem(*tall.shape),
            pltpu.VMEM((256, 512), BF16), pltpu.VMEM((384, 256), BF16),
            pltpu.VMEM((256, 128), BF16), pltpu.VMEM((256, 256), BF16),
            vmem(4, 4, 4, 32), vmem(4, 2, 8, 128), vmem(4, 2, 8, 128),
            vmem(2, 8, 4, 8, 128), vmem(3, 8, 4, 8, 128), vmem(3, 8, 4, 8, 128),
            vmem(3, 8, 4, 8, 128), vmem(3, 8, 4, 8, 128),
            vmem(2, 8, 4, 8, 128), vmem(2, 8, 4, 8, 128),
            vmem(4, 8, 4, 8, 128), vmem(3, 4, 8, 128), vmem(2, 8, 8, 128),
            vmem(2, 2, 2, 4, 8, 128), vmem(2, 2, 8, 8, 128), vmem(2, 2, 256, 128),
            vmem(4, 32, 128), vmem(4, 2, 8, 128), vmem(4, 8, 128),
        ]
        scratch += [vmem(2, 2, 8, 128)] * 8
        scratch += [vmem(3, 2, 8, 128), vmem(3, 16, 128), vmem(3, 2, 8, 128)] + [vmem(8, 128)] * 2
        for items in (3, 2, 3):
            scratch += [vmem(items, 2, 8, 128)] * 8
        scratch += [
            pltpu.SemaphoreType.DMA((14,)),
            pltpu.SemaphoreType.DMA((23,)),
            pltpu.SemaphoreType.DMA((23,)),
        ]
        operands = [
            pltpu.with_memory_space_constraint(value, pltpu.HBM)
            for value in (*arguments, jnp.asarray(square), jnp.asarray(tall))
        ]
        results = pl.pallas_call(
            functools.partial(kernel, counts),
            out_shape=pltpu.VMEM((5, 8, 32, 128), F32),
            in_specs=[pl.BlockSpec(memory_space=pltpu.HBM)] * 10,
            out_specs=pl.BlockSpec(memory_space=pltpu.VMEM),
            scratch_shapes=scratch,
            compiler_params=pltpu.CompilerParams(
                collective_id=0, has_side_effects=True, vmem_limit_bytes=32 * 1024 * 1024
            ),
        )(*operands)
        return pl.pallas_call(
            unfold,
            out_shape=[jax.ShapeDtypeStruct(value.shape, F32) for value in arguments[:3]],
            in_specs=[pl.BlockSpec(memory_space=pltpu.VMEM)],
            out_specs=[pl.BlockSpec(memory_space=pltpu.HBM)] * 3,
            scratch_shapes=[pltpu.SemaphoreType.DMA((6,))],
            compiler_params=pltpu.CompilerParams(vmem_limit_bytes=32 * 1024 * 1024),
        )(results)

    fields, vectors = P("gx", "gy", None), P(None, "gx", "gy", None)
    return jax.shard_map(
        on_device,
        mesh=mesh,
        in_specs=(fields, fields, vectors, vectors, fields, fields, fields, fields),
        out_specs=(fields, fields, vectors),
        check_vma=False,
    )
```

```python
import functools
import math

import jax
import jax.numpy as jnp
import numpy as np
from jax import lax
from jax.experimental import pallas as pl
from jax.experimental.pallas import tpu as pltpu
from jax.sharding import PartitionSpec as P

MESH = pl.DeviceIdType.MESH
F32 = jnp.float32
BF16 = jnp.bfloat16
time_step = 0.02
limit_eps = 1e-06


def lagrange_values(node_set, points):
    result = np.ones((len(points), len(node_set)))
    for column in range(len(node_set)):
        for partner in range(len(node_set)):
            if partner != column:
                result[:, column] = (
                    result[:, column]
                    * (points - node_set[partner])
                    / (node_set[column] - node_set[partner])
                )
    return result


def lagrange_slopes(node_set, points):
    node_total = len(node_set)
    result = np.zeros((len(points), node_total))
    for column in range(node_total):
        for skipped in range(node_total):
            if skipped != column:
                factor = np.ones(len(points)) / (node_set[column] - node_set[skipped])
                for partner in range(node_total):
                    if partner != column and partner != skipped:
                        factor = (
                            factor
                            * (points - node_set[partner])
                            / (node_set[column] - node_set[partner])
                        )
                result[:, column] = result[:, column] + factor
    return result


def basis_tables():
    gauss_points = np.array(
        [-0.8611363115940526, -0.3399810435848563, 0.3399810435848563, 0.8611363115940526]
    )
    gauss_weights = np.array(
        [0.3478548451374538, 0.6521451548625461, 0.6521451548625461, 0.3478548451374538]
    )
    lobatto_points = np.array([-1.0, -math.sqrt(3.0 / 7.0), 0.0, math.sqrt(3.0 / 7.0), 1.0])
    lobatto_weights = np.array([0.1, 49.0 / 90.0, 32.0 / 45.0, 49.0 / 90.0, 0.1])
    slopes = lagrange_slopes(gauss_points, gauss_points)
    volume = (2.0 / gauss_weights)[:, None] * slopes.T * gauss_weights[None, :]
    trace_low = lagrange_values(gauss_points, np.array([-1.0]))[0]
    trace_high = lagrange_values(gauss_points, np.array([1.0]))[0]
    stiffness = (
        2.0 * lobatto_weights[:, None] * lagrange_slopes(lobatto_points, lobatto_points)
    )
    lumped = np.array([0.2, lobatto_weights[1], lobatto_weights[2], lobatto_weights[3], 0.2])
    return {
        "weights": gauss_weights / 2.0,
        "volume": time_step * volume,
        "trace_low": trace_low,
        "trace_high": trace_high,
        "lift_low": time_step * 2.0 * trace_low / gauss_weights,
        "lift_high": time_step * 2.0 * trace_high / gauss_weights,
        "to_points": lagrange_values(lobatto_points, gauss_points),
        "stiffness": -time_step * stiffness / lumped[:, None],
    }


TABLES = basis_tables()
TABLE = {name: TABLES[name].tolist() for name in TABLES}


def lane_matrices(lanes):
    zones = lanes // 4
    shape = (lanes, lanes)
    volume, lift = np.zeros(shape), np.zeros(shape)
    minus, plus = np.zeros(shape), np.zeros(shape)
    stiff, interp = np.zeros(shape), np.zeros(shape)
    pick, spread = np.zeros(shape), np.zeros(shape)
    for zone in range(zones):
        at = 4 * zone
        before = 4 * ((zone - 1) % zones)
        for within in range(4):
            for source in range(4):
                volume[at + source, at + within] = TABLES["volume"][within, source]
                minus[before + source, at + within] = TABLES["trace_high"][source]
                plus[at + source, at + within] = TABLES["trace_low"][source]
            lift[at, at + within] = TABLES["lift_low"][within]
            lift[at, before + within] = -TABLES["lift_high"][within]
            pick[at, at + within] = 1.0
            spread[zone, at + within] = 1.0
            for source in range(5):
                interp[(at + source) % lanes, at + within] += TABLES["to_points"][within, source]
        for target in range(5):
            for source in range(5):
                stiff[(at + source) % lanes, (at + target) % lanes] += TABLES["stiffness"][
                    target, source
                ]
    matrices = [minus, plus, stiff, interp, pick, spread, volume, lift]
    return np.concatenate(matrices, axis=1).astype(np.float32)


def spin(values, steps, axis):
    size = values.shape[axis]
    steps = steps % size
    return values if steps == 0 else pltpu.roll(values, steps, axis)


def rows_of(shape):
    return lax.broadcasted_iota(jnp.int32, shape, len(shape) - 2)


def low_half(shape):
    return rows_of(shape) < 4


def at_zone(shape, zone):
    return rows_of(shape) % 4 == zone


def combine(coefficients, terms):
    total = None
    for factor, term in zip(coefficients, terms):
        part = factor * term
        total = part if total is None else total + part
    return total


def parted(values):
    upper = values.astype(BF16)
    return upper, (values - upper.astype(F32)).astype(BF16)


def product(left, right):
    return jnp.dot(left, right, preferred_element_type=F32)


def mirrored(matrix):
    size = len(matrix[0])
    middle = size // 2
    even = [[(row[c] + row[size - 1 - c]) / 2 for c in range(middle)] for row in matrix]
    odd = [[(row[c] - row[size - 1 - c]) / 2 for c in range(middle)] for row in matrix]
    centre = [row[middle] for row in matrix] if size % 2 else None
    return even, odd, centre


def pairs_of(values):
    size = len(values)
    sums = [values[c] + values[size - 1 - c] for c in range(size // 2)]
    gaps = [values[c] - values[size - 1 - c] for c in range(size // 2)]
    return sums, gaps


def slopes_of(matrix, values):
    even, odd, centre = mirrored(matrix)
    sums, gaps = pairs_of(values)
    size = len(matrix)
    result = [None] * size
    for a in range(size // 2):
        factors, terms = list(even[a]), list(sums)
        if centre is not None:
            factors.append(centre[a])
            terms.append(values[size // 2])
        outer, inner = combine(factors, terms), combine(odd[a], gaps)
        result[a], result[size - 1 - a] = inner + outer, inner - outer
    if size % 2:
        result[size // 2] = combine(odd[size // 2], gaps)
    return result


def points_of(matrix, values):
    even, odd, centre = mirrored(matrix)
    sums, gaps = pairs_of(values)
    result = [None] * 4
    for i in range(2):
        outer = combine(even[i] + [centre[i]], sums + [values[2]])
        inner = combine(odd[i], gaps)
        result[i], result[3 - i] = outer + inner, outer - inner
    return result


def traces_of(values):
    sums, gaps = pairs_of(values)
    even, odd, _ = mirrored([TABLE["trace_low"]])
    outer, inner = combine(even[0], sums), combine(odd[0], gaps)
    return outer + inner, outer - inner


def lifts_of(lower, upper):
    even, odd, _ = mirrored([TABLE["lift_low"]])
    gap, both = lower - upper, lower + upper
    result = [None] * 4
    for i in range(2):
        outer, inner = even[0][i] * gap, odd[0][i] * both
        result[i], result[3 - i] = outer + inner, outer - inner
    return result


def turned(pieces):
    return [jnp.stack([pieces[j][i] for j in range(4)]) for i in range(4)]


def pack_x_low(planes):
    mask = low_half((8, 128))
    return [jnp.where(mask, planes[t], spin(planes[t + 1], 4, 0)) for t in (0, 2)]


def pack_x_high(planes):
    mask = low_half((8, 128))
    return [jnp.where(mask, spin(planes[t], 4, 0), planes[t + 1]) for t in (0, 2)]


def unpack_x_high(packed):
    return [spin(packed[0], 4, 0), packed[0], spin(packed[1], 4, 0), packed[1]]


def unpack_x_low(packed):
    return [packed[0], spin(packed[0], 4, 0), packed[1], spin(packed[1], 4, 0)]


def pack_y(values, start):
    shape = (8, 128)
    packed = []
    for half in range(2):
        total = spin(values[4 * half + 3], 3 - start, 0)
        for place in (2, 1, 0):
            moved = spin(values[4 * half + place], place - start, 0)
            total = jnp.where(at_zone(shape, place), moved, total)
        packed.append(total)
    return packed


def unpack_y(packed, end):
    return jnp.stack([spin(packed, end - place, 0) for place in range(4)])


def kernel(
    counts,
    density, energy, velocity, mesh_velocity, density_low, density_high, energy_low, energy_high,
    tables_hbm,
    results,
    raw_u, raw_v, raw_m, tables, square, ends, picker, tall, bound_in, bound_rows,
    bounds, work_u, work_v, work_m,
    acc_v, sec_v, acc_f, sec_f, speed, face_x, face_y, trace_x, trace_y, ends_z,
    halo_x, halo_y, halo_corner,
    out_dx, out_ux, out_dy, out_uy, in_dx, in_ux, in_dy, in_uy,
    out_corner, in_corner,
    out_dx2, out_ux2, out_dy2, out_uy2, in_dx2, in_ux2, in_dy2, in_uy2,
    load_sem, send_sem, recv_sem,
):
    count_x, count_y = counts
    here_x, here_y = lax.axis_index("gx"), lax.axis_index("gy")
    west = lax.rem(here_x + count_x - 1, count_x)
    east = lax.rem(here_x + 1, count_x)
    south = lax.rem(here_y + count_y - 1, count_y)
    north = lax.rem(here_y + 1, count_y)
    to_west, to_east = (west, here_y), (east, here_y)
    to_south, to_north = (here_x, south), (here_x, north)
    to_corner, from_corner = (west, south), (east, north)

    loads = {}

    def load(name, source, target):
        copy = pltpu.make_async_copy(source, target, load_sem.at[sum(map(len, loads.values()))])
        copy.start()
        loads.setdefault(name, []).append(copy)

    def loaded(name):
        for copy in loads[name]:
            copy.wait()

    places = [(pl.ds(16 * half, 16), pl.ds(8 * half, 8)) for half in range(2)]
    for rows, block in places:
        load("mesh", mesh_velocity.at[:, block], raw_m.at[:, :, rows, :])
        load("velocity", velocity.at[:, block], raw_v.at[:, :, rows, :])
    for rows, block in places:
        load("fields", density.at[block], raw_u.at[0, :, rows, :])
        load("fields", energy.at[block], raw_u.at[1, :, rows, :])

    barrier = pltpu.get_barrier_semaphore()
    for peer in (to_west, to_east, to_south, to_north, to_corner, from_corner):
        pl.semaphore_signal(barrier, inc=1, device_id=peer, device_id_type=MESH)
    load("tables", tables_hbm, tables)
    for index, source in enumerate((density_low, density_high, energy_low, energy_high)):
        load("bounds", source, bound_in.at[index])

    quad, plane = (4, 8, 128), (8, 128)
    low_rows, low_quad = low_half(plane), low_half(quad)
    first_zone, last_zone = at_zone(quad, 0), at_zone(quad, 3)
    stiff, points = TABLE["stiffness"], TABLE["to_points"]
    zero = jnp.zeros(plane, F32)

    def arrange(source, target, which):
        for j in range(4):
            target[which, :, j] = source[which, :, pl.ds(j, 8, stride=4), :]

    def put_pair(target, item, pair):
        target[item, 0] = pair[0]
        target[item, 1] = pair[1]

    def sided(values):
        upper, lower = parted(values)
        return upper, jnp.concatenate([upper, lower], 1)

    def lanes_product(values, column):
        _, pair = sided(values)
        both = product(pair, square[:, 256 * column : 256 * (column + 1)])
        return both[:, :128] + both[:, 128:]

    def picked(values):
        return product(sided(values)[1], picker[...])

    def field_traces(which, source):
        for half in range(2):
            chunk = pl.ds(4 * half, 4)
            low, high = traces_of([source[which, 4 * half + i] for i in range(4)])
            trace_x[which, 0, half], trace_x[which, 1, half] = low, high
            low, high = traces_of([source[which, chunk, j] for j in range(4)])
            trace_y[which, 0, chunk], trace_y[which, 1, chunk] = low, high

    def pack_field(which, item, buffers):
        west_to, east_to, south_to, north_to = buffers
        put_pair(west_to, item, pack_x_low(trace_x[which, 0, 0]))
        put_pair(east_to, item, pack_x_high(trace_x[which, 1, 1]))
        put_pair(south_to, item, pack_y(trace_y[which, 0], 0))
        put_pair(north_to, item, pack_y(trace_y[which, 1], 3))

    def pack_velocity(source, which, offset, buffers):
        item = offset + which
        west_to, east_to, south_to, north_to = buffers
        put_pair(west_to, item, pack_x_low(source[which, 0]))
        closing = combine(stiff[4][:4], [source[which, 4 + a] for a in range(4)])
        put_pair(east_to, item, pack_x_high(closing))
        put_pair(south_to, item, pack_y(source[which, :, 0], 0))
        closing = combine(stiff[4][:4], [source[which, :, j] for j in range(4)])
        put_pair(north_to, item, pack_y(closing, 3))

    leaving_a, leaving_b = (out_dx, out_ux, out_dy, out_uy), (out_dx2, out_ux2, out_dy2, out_uy2)
    arrived_a, arrived_b = (in_dx, in_ux, in_dy, in_uy), (in_dx2, in_ux2, in_dy2, in_uy2)
    loaded("mesh")
    corner = zero
    for which in range(3):
        values = raw_m[which, :, pl.ds(0, 8, stride=4), :]
        put_pair(out_dy, 5 + which, pack_y(values, 0))
        corner = jnp.where(rows_of(plane) == which, spin(values[0], which, 0), corner)
        values = [raw_m[which, 0, pl.ds(j, 8, stride=4), :] for j in range(4)]
        put_pair(out_dx, 5 + which, pack_x_low(values))
    out_corner[...] = corner
    loaded("velocity")
    for which in range(3):
        arrange(raw_v, work_v, which)
        pack_velocity(work_v, which, 2, leaving_a)
    loaded("fields")
    for which in range(2):
        arrange(raw_u, work_u, which)
        field_traces(which, work_u)
        pack_field(which, which, leaving_a)

    pl.semaphore_wait(barrier, 6)
    copies = []
    peers = (to_west, to_east, to_south, to_north)

    def send(source, target, peer):
        copy = pltpu.make_async_remote_copy(
            src_ref=source, dst_ref=target,
            send_sem=send_sem.at[len(copies)], recv_sem=recv_sem.at[len(copies)],
            device_id=peer, device_id_type=MESH,
        )
        copy.start()
        copies.append(copy)
        return copy

    def send_all(sources, targets):
        return [send(*triple) for triple in zip(sources, targets, peers)]

    first = send_all(leaving_a, arrived_a) + [send(out_corner, in_corner, to_corner)]

    loaded("tables")
    minus, plus, stiff_z, interp_z, pick_z, spread_z, volume_z, lift_z = (
        tables[:, 128 * column : 128 * (column + 1)] for column in range(8)
    )
    for column, table in enumerate((stiff_z, interp_z)):
        upper, lower = parted(table)
        at = 256 * column
        square[:128, at : at + 128] = upper
        square[128:, at : at + 128] = upper
        square[:128, at + 128 : at + 256] = lower
        square[128:, at + 128 : at + 256] = jnp.zeros((128, 128), BF16)
    for column, table in enumerate((minus, plus)):
        upper, lower = parted(table)
        at = 128 * column
        ends[:128, at : at + 128] = upper
        ends[128:256, at : at + 128] = upper
        ends[256:, at : at + 128] = lower
    picker[:128] = pick_z.astype(BF16)
    picker[128:] = pick_z.astype(BF16)
    for row, table in enumerate((volume_z, lift_z)):
        upper, lower = parted(table)
        tall[128 * row : 128 * (row + 1), :128] = upper
        tall[128 * row : 128 * (row + 1), 128:] = lower

    loaded("bounds")
    bound_rows[...] = jnp.zeros((4, 2, 8, 128), F32)
    for index in range(4):
        for zone in range(4):
            bound_rows[index, zone % 2, pl.ds(4 * (zone // 2), 4), pl.ds(0, 32)] = bound_in[
                index, zone
            ]
    values = bound_rows[...].reshape(64, 128)
    spreader = spread_z.astype(BF16)
    upper = values.astype(BF16)
    rest = values - upper.astype(F32)
    middle = rest.astype(BF16)
    lowest = (rest - middle.astype(F32)).astype(BF16)
    values = product(upper, spreader) + (product(middle, spreader) + product(lowest, spreader))
    bounds[...] = values.reshape(4, 2, 8, 128)

    def velocity_before(which, source, base):
        along_z = lanes_product(source[which].reshape(256, 128), 0).reshape(8, 4, 8, 128)
        own = stiff[4][4]
        opening = source[which, 0]
        inner = jnp.where(low_quad, spin(opening, 4, 1), 0.0)
        last_end = combine(stiff[4], [source[which, 4 + a] for a in range(4)] + [inner])
        carried = jnp.where(low_quad, own * opening, spin(last_end, 4, 1))
        for half in range(2):
            chunk = pl.ds(4 * half, 4)
            ahead = source[which, 4] if half == 0 else inner
            along_x = slopes_of(stiff, [source[which, 4 * half + a] for a in range(4)] + [ahead])
            along_x[0] = along_x[0] + carried
            carried = along_x[4]
            lines = [source[which, chunk, j] for j in range(4)]
            ahead = jnp.where(last_zone, 0.0, spin(lines[0], 7, 1))
            along_y = slopes_of(stiff, lines + [ahead])
            along_y[0] = along_y[0] + jnp.where(first_zone, own * lines[0], spin(along_y[4], 1, 1))
            along_y = turned(along_y[:4])
            for a in range(4):
                x = 4 * half + a
                acc_v[which, x] = base(x) + (
                    work_m[0, x] * along_x[a]
                    + work_m[1, x] * along_y[a]
                    + work_m[2, x] * along_z[x]
                )

    def velocity_after(which, put, arrived):
        from_east, from_west, from_north, from_south = arrived
        later = jnp.stack(unpack_x_high([from_east[2 + which, 0], from_east[2 + which, 1]]))
        earlier = jnp.stack(unpack_x_low([from_west[2 + which, 0], from_west[2 + which, 1]]))
        later = jnp.where(low_quad, 0.0, later)
        earlier = jnp.where(low_quad, earlier, 0.0)
        for half in range(2):
            above = jnp.where(last_zone, unpack_y(from_north[2 + which, half], 3), 0.0)
            below = jnp.where(first_zone, unpack_y(from_south[2 + which, half], 0), 0.0)
            extra_y = [stiff[j][4] * above for j in range(4)]
            extra_y[0] = extra_y[0] + below
            extra_y = turned(extra_y)
            for a in range(4):
                x = 4 * half + a
                value = acc_v[which, x] + work_m[1, x] * extra_y[a]
                if half == 1:
                    value = value + work_m[0, x] * (stiff[a][4] * later)
                elif a == 0:
                    value = value + work_m[0, x] * earlier
                put(x, value)

    def mesh_before(item):
        values = work_m[min(item, 2)].reshape(256, 128)
        values = lanes_product(values, 1) if item < 3 else picked(values)
        values = values.reshape(8, 4, 8, 128)
        inner = jnp.where(low_quad, spin(values[0], 4, 1), 0.0)
        for half in range(2):
            chunk = pl.ds(4 * half, 4)
            ahead = values[4] if half == 0 else inner
            across = points_of(points, [values[4 * half + a] for a in range(4)] + [ahead])
            across = turned(across)
            ahead = jnp.where(last_zone, 0.0, spin(across[0], 7, 1))
            for j, result in enumerate(points_of(points, across + [ahead])):
                speed[item, chunk, j] = result
            if item == 0:
                edge = values[4 * half]
                ahead = jnp.where(at_zone(plane, 3), 0.0, spin(edge[0], 7, 0))
                edge = points_of(points, [edge[j] for j in range(4)] + [ahead])
                face_x[half] = jnp.stack(edge)
            if item == 1:
                face_y[0, chunk] = across[0]
                face_y[1, chunk] = ahead

    def mesh_halo():
        values = jnp.concatenate(
            [in_dx[5:8].reshape(48, 128), in_dy[5:8].reshape(48, 128), in_corner[...], zero], 0
        )
        both, extra = lanes_product(values, 1), picked(values)
        for item in range(4):
            which, source = min(item, 2), both if item < 3 else extra
            halo_x[item] = source[16 * which : 16 * (which + 1)].reshape(2, 8, 128)
            halo_y[item] = source[48 + 16 * which : 64 + 16 * which].reshape(2, 8, 128)
            halo_corner[item] = spin(source[96:104], 7 - which, 0)

    def mesh_after(item):
        rows = rows_of(plane)
        later = unpack_x_high([halo_x[item, 0], halo_x[item, 1]])
        later = [jnp.where(low_rows, 0.0, value) for value in later]
        far = jnp.where(at_zone(plane, 3), 0.0, spin(later[0], 7, 0))
        far = jnp.where(rows == 7, halo_corner[item], far)
        later.append(jnp.where(low_rows, 0.0, far))
        edge = jnp.stack(points_of(points, later))
        above = [
            jnp.where(last_zone, unpack_y(halo_y[item, half], 3), 0.0) for half in range(2)
        ]
        inner = jnp.where(low_rows, spin(above[0][0], 4, 0), 0.0)
        for half in range(2):
            ahead = above[1][0] if half == 0 else inner
            across = points_of(points, [above[half][a] for a in range(4)] + [ahead])
            for i in range(4):
                x = 4 * half + i
                extra = jnp.stack([points[j][4] * across[i] for j in range(4)])
                if half == 1:
                    extra = extra + points[i][4] * edge
                speed[item, x] += extra
                if item == 1:
                    upper = face_y[1, x] + across[i]
                    if half == 1:
                        upper = upper + points[i][4] * later[4]
                        face_y[0, x] += points[i][4] * later[0]
                    face_y[1, x] = upper
            if item == 0:
                face_x[half] += jnp.stack([points[j][4] * above[half][0] for j in range(4)])
        if item == 0:
            face_x[2] = jnp.where(low_quad, spin(face_x[0], 4, 1), edge)

    def upwind(face, minus_side, plus_side):
        return jnp.maximum(face, 0.0) * minus_side + jnp.minimum(face, 0.0) * plus_side

    def field_ends(which, source):
        upper, pair = sided(source[which].reshape(256, 128))
        sides = product(pair, ends[:256]) + product(upper, ends[256:])
        ends_z[which, 0] = sides[:, :128]
        ends_z[which, 1] = sides[:, 128:]

    def field_before(which, source, base):
        values = source[which].reshape(256, 128)
        flux = upwind(speed[3].reshape(256, 128), ends_z[which, 0], ends_z[which, 1])
        moved = speed[2].reshape(256, 128) * values
        upper, lower = parted(jnp.concatenate([moved, flux], 1))
        sums = product(upper, tall[...])
        along_z = sums[:, :128] + sums[:, 128:] + product(lower, tall[:, :128])
        along_z = along_z.reshape(8, 4, 8, 128)
        for half in range(2):
            chunk = pl.ds(4 * half, 4)
            places = [4 * half + i for i in range(4)]
            along_x = slopes_of(TABLE["volume"], [speed[0, x] * source[which, x] for x in places])
            along_y = slopes_of(
                TABLE["volume"],
                [speed[1, chunk, j] * source[which, chunk, j] for j in range(4)],
            )
            along_y = turned(along_y)
            for i, x in enumerate(places):
                acc_f[which, x] = base(x) + ((along_x[i] + along_y[i]) + along_z[x])

    def in_group(values, join):
        lane = lax.broadcasted_iota(jnp.int32, plane, 1)
        partner = jnp.where(lane % 2 == 0, spin(values, 127, 1), spin(values, 1, 1))
        values = join(values, partner)
        partner = jnp.where(lane // 2 % 2 == 0, spin(values, 126, 1), spin(values, 2, 1))
        return join(values, partner)

    def over_zone(values, join):
        total = functools.reduce(join, values)
        return functools.reduce(join, [total[j] for j in range(4)])

    def limited(which, half, values):
        weights = TABLE["weights"]
        mean = combine(weights, values)
        mean = combine(weights, [mean[j] for j in range(4)])
        lane = lax.broadcasted_iota(jnp.int32, plane, 1) % 4
        middle = (lane == 1) | (lane == 2)
        mean = in_group(mean * jnp.where(middle, weights[1], weights[0]), jnp.add)
        rise = in_group(over_zone(values, jnp.maximum), jnp.maximum) - mean
        fall = in_group(over_zone(values, jnp.minimum), jnp.minimum) - mean
        low, high = bounds[2 * which, half], bounds[2 * which + 1, half]
        theta = jnp.minimum(
            (high - mean) / (rise + limit_eps), (mean - low) / (limit_eps - fall)
        )
        theta = jnp.clip(theta, 0.0, 1.0)
        return [mean + theta * (value - mean) for value in values]

    def field_after(which, scale, put, arrived):
        from_east, from_west, from_north, from_south = arrived
        later = jnp.stack(unpack_x_high([from_east[which, 0], from_east[which, 1]]))
        earlier = jnp.stack(unpack_x_low([from_west[which, 0], from_west[which, 1]]))
        low, high = trace_x[which, 0], trace_x[which, 1]
        flux = [
            upwind(face_x[0], jnp.where(low_quad, earlier, spin(high[1], 4, 1)), low[0]),
            upwind(face_x[1], high[0], low[1]),
            upwind(face_x[2], high[1], jnp.where(low_quad, spin(low[0], 4, 1), later)),
        ]
        for half in range(2):
            chunk = pl.ds(4 * half, 4)
            low, high = trace_y[which, 0, chunk], trace_y[which, 1, chunk]
            before = jnp.where(first_zone, unpack_y(from_south[which, half], 0), spin(high, 1, 1))
            after = jnp.where(last_zone, unpack_y(from_north[which, half], 3), spin(low, 7, 1))
            lift_y = turned(
                lifts_of(
                    upwind(face_y[0, chunk], before, low), upwind(face_y[1, chunk], high, after)
                )
            )
            lift_x = lifts_of(flux[half], flux[half + 1])
            values = [
                acc_f[which, 4 * half + i] + (lift_x[i] + lift_y[i]) for i in range(4)
            ]
            if scale != 1.0:
                values = [scale * value for value in values]
            values = limited(which, half, values)
            for i in range(4):
                put(4 * half + i, values[i])

    for which in range(3):
        arrange(raw_m, work_m, which)
    for item in range(4):
        mesh_before(item)
    for which in range(2):
        field_ends(which, work_u)
    for which in range(3):
        velocity_before(which, work_v, lambda x: work_v[which, x])
    for copy in first:
        copy.wait_recv()

    def keep_field(x, value):
        sec_f[which, x] = value

    def keep_velocity(x, value):
        sec_v[which, x] = value

    def send_part(part):
        return send_all([ref.at[part] for ref in leaving_b], [ref.at[part] for ref in arrived_b])

    for which in range(3):
        velocity_after(which, keep_velocity, arrived_a)
        pack_velocity(sec_v, which, 2, leaving_b)
    second_v = send_part(pl.ds(2, 3))
    mesh_halo()
    for item in range(4):
        mesh_after(item)
    for which in range(2):
        field_before(which, work_u, lambda x: work_u[which, x])
    for which in range(2):
        field_after(which, 1.0, keep_field, arrived_a)
        field_traces(which, sec_f)
        pack_field(which, which, leaving_b)
    second = send_part(pl.ds(0, 2))

    for which in range(3):
        velocity_before(which, sec_v, lambda x: work_v[which, x] + sec_v[which, x])
    for which in range(2):
        field_ends(which, sec_f)
    for which in range(2):
        field_before(which, sec_f, lambda x: work_u[which, x] + sec_f[which, x])

    def finish_field(x, value):
        for j in range(4):
            results[which, x, pl.ds(j, 8, stride=4), :] = value[j]

    def finish_velocity(x, value):
        for j in range(4):
            results[2 + which, x, pl.ds(j, 8, stride=4), :] = 0.5 * value[j]

    for copy in second_v:
        copy.wait_recv()
    for which in range(3):
        velocity_after(which, finish_velocity, arrived_b)
    for copy in second:
        copy.wait_recv()
    for which in range(2):
        field_after(which, 0.5, finish_field, arrived_b)
    for copy in copies:
        copy.wait_send()


def unfold(results, new_density, new_energy, new_velocity, store_sem):
    copies = []
    for half in range(2):
        rows, block = pl.ds(16 * half, 16), pl.ds(8 * half, 8)
        for source, target in (
            (results.at[0, :, rows, :], new_density.at[block]),
            (results.at[1, :, rows, :], new_energy.at[block]),
            (results.at[pl.ds(2, 3), :, rows, :], new_velocity.at[:, block]),
        ):
            copy = pltpu.make_async_copy(source, target, store_sem.at[len(copies)])
            copy.start()
            copies.append(copy)
    for copy in copies:
        copy.wait()


def solution(mesh):
    counts = (mesh.shape["gx"], mesh.shape["gy"])
    matrices = lane_matrices(128)

    def on_device(*arguments):
        vmem = lambda *shape: pltpu.VMEM(shape, F32)
        scratch = [
            vmem(2, 8, 32, 128), vmem(3, 8, 32, 128), vmem(3, 8, 32, 128),
            vmem(*matrices.shape),
            pltpu.VMEM((256, 512), BF16), pltpu.VMEM((384, 256), BF16),
            pltpu.VMEM((256, 128), BF16), pltpu.VMEM((256, 256), BF16),
            vmem(4, 4, 4, 32), vmem(4, 2, 8, 128), vmem(4, 2, 8, 128),
            vmem(2, 8, 4, 8, 128), vmem(3, 8, 4, 8, 128), vmem(3, 8, 4, 8, 128),
            vmem(3, 8, 4, 8, 128), vmem(3, 8, 4, 8, 128),
            vmem(2, 8, 4, 8, 128), vmem(2, 8, 4, 8, 128),
            vmem(4, 8, 4, 8, 128), vmem(3, 4, 8, 128), vmem(2, 8, 8, 128),
            vmem(2, 2, 2, 4, 8, 128), vmem(2, 2, 8, 8, 128), vmem(2, 2, 256, 128),
            vmem(4, 2, 8, 128), vmem(4, 2, 8, 128), vmem(4, 8, 128),
        ]
        sides = [vmem(items, 2, 8, 128) for items in (8, 5, 8, 5)]
        scratch += sides + sides + [vmem(8, 128)] * 2 + [vmem(5, 2, 8, 128)] * 8
        scratch += [
            pltpu.SemaphoreType.DMA((13,)),
            pltpu.SemaphoreType.DMA((13,)),
            pltpu.SemaphoreType.DMA((13,)),
        ]
        operands = [
            pltpu.with_memory_space_constraint(value, pltpu.HBM)
            for value in (*arguments, jnp.asarray(matrices))
        ]
        results = pl.pallas_call(
            functools.partial(kernel, counts),
            out_shape=pltpu.VMEM((5, 8, 32, 128), F32),
            in_specs=[pl.BlockSpec(memory_space=pltpu.HBM)] * 9,
            out_specs=pl.BlockSpec(memory_space=pltpu.VMEM),
            scratch_shapes=scratch,
            compiler_params=pltpu.CompilerParams(
                collective_id=0, has_side_effects=True, vmem_limit_bytes=32 * 1024 * 1024
            ),
        )(*operands)
        return pl.pallas_call(
            unfold,
            out_shape=[jax.ShapeDtypeStruct(value.shape, F32) for value in arguments[:3]],
            in_specs=[pl.BlockSpec(memory_space=pltpu.VMEM)],
            out_specs=[pl.BlockSpec(memory_space=pltpu.HBM)] * 3,
            scratch_shapes=[pltpu.SemaphoreType.DMA((6,))],
            compiler_params=pltpu.CompilerParams(vmem_limit_bytes=32 * 1024 * 1024),
        )(results)

    fields, vectors = P("gx", "gy", None), P(None, "gx", "gy", None)
    return jax.shard_map(
        on_device,
        mesh=mesh,
        in_specs=(fields, fields, vectors, vectors, fields, fields, fields, fields),
        out_specs=(fields, fields, vectors),
        check_vma=False,
    )
```

```python
import functools
import math

import jax
import jax.numpy as jnp
import numpy as np
from jax import lax
from jax.experimental import pallas as pl
from jax.experimental.pallas import tpu as pltpu
from jax.sharding import PartitionSpec as P

MESH = pl.DeviceIdType.MESH
F32 = jnp.float32
BF16 = jnp.bfloat16
time_step = 0.02
limit_eps = 1e-06


def lagrange_values(node_set, points):
    result = np.ones((len(points), len(node_set)))
    for column in range(len(node_set)):
        for partner in range(len(node_set)):
            if partner != column:
                result[:, column] = (
                    result[:, column]
                    * (points - node_set[partner])
                    / (node_set[column] - node_set[partner])
                )
    return result


def lagrange_slopes(node_set, points):
    node_total = len(node_set)
    result = np.zeros((len(points), node_total))
    for column in range(node_total):
        for skipped in range(node_total):
            if skipped != column:
                factor = np.ones(len(points)) / (node_set[column] - node_set[skipped])
                for partner in range(node_total):
                    if partner != column and partner != skipped:
                        factor = (
                            factor
                            * (points - node_set[partner])
                            / (node_set[column] - node_set[partner])
                        )
                result[:, column] = result[:, column] + factor
    return result


def basis_tables():
    gauss_points = np.array(
        [-0.8611363115940526, -0.3399810435848563, 0.3399810435848563, 0.8611363115940526]
    )
    gauss_weights = np.array(
        [0.3478548451374538, 0.6521451548625461, 0.6521451548625461, 0.3478548451374538]
    )
    lobatto_points = np.array([-1.0, -math.sqrt(3.0 / 7.0), 0.0, math.sqrt(3.0 / 7.0), 1.0])
    lobatto_weights = np.array([0.1, 49.0 / 90.0, 32.0 / 45.0, 49.0 / 90.0, 0.1])
    slopes = lagrange_slopes(gauss_points, gauss_points)
    volume = (2.0 / gauss_weights)[:, None] * slopes.T * gauss_weights[None, :]
    trace_low = lagrange_values(gauss_points, np.array([-1.0]))[0]
    trace_high = lagrange_values(gauss_points, np.array([1.0]))[0]
    stiffness = (
        2.0 * lobatto_weights[:, None] * lagrange_slopes(lobatto_points, lobatto_points)
    )
    lumped = np.array([0.2, lobatto_weights[1], lobatto_weights[2], lobatto_weights[3], 0.2])
    return {
        "weights": gauss_weights / 2.0,
        "volume": time_step * volume,
        "trace_low": trace_low,
        "trace_high": trace_high,
        "lift_low": time_step * 2.0 * trace_low / gauss_weights,
        "lift_high": time_step * 2.0 * trace_high / gauss_weights,
        "to_points": lagrange_values(lobatto_points, gauss_points),
        "stiffness": -time_step * stiffness / lumped[:, None],
    }


TABLES = basis_tables()
TABLE = {name: TABLES[name].tolist() for name in TABLES}


def lane_matrices(lanes):
    zones = lanes // 4
    shape = (lanes, lanes)
    volume, lift = np.zeros(shape), np.zeros(shape)
    minus, plus = np.zeros(shape), np.zeros(shape)
    stiff, interp = np.zeros(shape), np.zeros(shape)
    pick, spread = np.zeros(shape), np.zeros(shape)
    for zone in range(zones):
        at = 4 * zone
        before = 4 * ((zone - 1) % zones)
        for within in range(4):
            for source in range(4):
                volume[at + source, at + within] = TABLES["volume"][within, source]
                minus[before + source, at + within] = TABLES["trace_high"][source]
                plus[at + source, at + within] = TABLES["trace_low"][source]
            lift[at, at + within] = TABLES["lift_low"][within]
            lift[at, before + within] = -TABLES["lift_high"][within]
            pick[at, at + within] = 1.0
            spread[zone, at + within] = 1.0
            for source in range(5):
                interp[(at + source) % lanes, at + within] += TABLES["to_points"][within, source]
        for target in range(5):
            for source in range(5):
                stiff[(at + source) % lanes, (at + target) % lanes] += TABLES["stiffness"][
                    target, source
                ]
    matrices = [minus, plus, stiff, interp, pick, spread, volume, lift]
    return np.concatenate(matrices, axis=1).astype(np.float32)


def spin(values, steps, axis):
    size = values.shape[axis]
    steps = steps % size
    return values if steps == 0 else pltpu.roll(values, steps, axis)


def rows_of(shape):
    return lax.broadcasted_iota(jnp.int32, shape, len(shape) - 2)


def low_half(shape):
    return rows_of(shape) < 4


def at_zone(shape, zone):
    return rows_of(shape) % 4 == zone


def combine(coefficients, terms):
    total = None
    for factor, term in zip(coefficients, terms):
        part = factor * term
        total = part if total is None else total + part
    return total


def parted(values):
    upper = values.astype(BF16)
    return upper, (values - upper.astype(F32)).astype(BF16)


def product(left, right):
    return jnp.dot(left, right, preferred_element_type=F32)


def mirrored(matrix):
    size = len(matrix[0])
    middle = size // 2
    even = [[(row[c] + row[size - 1 - c]) / 2 for c in range(middle)] for row in matrix]
    odd = [[(row[c] - row[size - 1 - c]) / 2 for c in range(middle)] for row in matrix]
    centre = [row[middle] for row in matrix] if size % 2 else None
    return even, odd, centre


def pairs_of(values):
    size = len(values)
    sums = [values[c] + values[size - 1 - c] for c in range(size // 2)]
    gaps = [values[c] - values[size - 1 - c] for c in range(size // 2)]
    return sums, gaps


def slopes_of(matrix, values):
    even, odd, centre = mirrored(matrix)
    sums, gaps = pairs_of(values)
    size = len(matrix)
    result = [None] * size
    for a in range(size // 2):
        factors, terms = list(even[a]), list(sums)
        if centre is not None:
            factors.append(centre[a])
            terms.append(values[size // 2])
        outer, inner = combine(factors, terms), combine(odd[a], gaps)
        result[a], result[size - 1 - a] = inner + outer, inner - outer
    if size % 2:
        result[size // 2] = combine(odd[size // 2], gaps)
    return result


def points_of(matrix, values):
    even, odd, centre = mirrored(matrix)
    sums, gaps = pairs_of(values)
    result = [None] * 4
    for i in range(2):
        outer = combine(even[i] + [centre[i]], sums + [values[2]])
        inner = combine(odd[i], gaps)
        result[i], result[3 - i] = outer + inner, outer - inner
    return result


def traces_of(values):
    sums, gaps = pairs_of(values)
    even, odd, _ = mirrored([TABLE["trace_low"]])
    outer, inner = combine(even[0], sums), combine(odd[0], gaps)
    return outer + inner, outer - inner


def lifts_of(lower, upper):
    even, odd, _ = mirrored([TABLE["lift_low"]])
    gap, both = lower - upper, lower + upper
    result = [None] * 4
    for i in range(2):
        outer, inner = even[0][i] * gap, odd[0][i] * both
        result[i], result[3 - i] = outer + inner, outer - inner
    return result


def turned(pieces):
    return [jnp.stack([pieces[j][i] for j in range(4)]) for i in range(4)]


def pack_x_low(planes):
    mask = low_half((8, 128))
    return [jnp.where(mask, planes[t], spin(planes[t + 1], 4, 0)) for t in (0, 2)]


def pack_x_high(planes):
    mask = low_half((8, 128))
    return [jnp.where(mask, spin(planes[t], 4, 0), planes[t + 1]) for t in (0, 2)]


def unpack_x_high(packed):
    return [spin(packed[0], 4, 0), packed[0], spin(packed[1], 4, 0), packed[1]]


def unpack_x_low(packed):
    return [packed[0], spin(packed[0], 4, 0), packed[1], spin(packed[1], 4, 0)]


def pack_y(values, start):
    shape = (8, 128)
    packed = []
    for half in range(2):
        total = spin(values[4 * half + 3], 3 - start, 0)
        for place in (2, 1, 0):
            moved = spin(values[4 * half + place], place - start, 0)
            total = jnp.where(at_zone(shape, place), moved, total)
        packed.append(total)
    return packed


def unpack_y(packed, end):
    return jnp.stack([spin(packed, end - place, 0) for place in range(4)])


def kernel(
    counts,
    density, energy, velocity, mesh_velocity, density_low, density_high, energy_low, energy_high,
    tables_hbm,
    results,
    raw_u, raw_v, raw_m, tables, square, ends, picker, tall, bound_in, bound_rows,
    bounds, work_u, work_v, work_m,
    acc_v, sec_v, acc_f, sec_f, speed, face_x, face_y, trace_x, trace_y, ends_z,
    halo_x, halo_y, halo_corner,
    out_dx, out_ux, out_dy, out_uy, in_dx, in_ux, in_dy, in_uy,
    out_corner, in_corner,
    out_dx2, out_ux2, out_dy2, out_uy2, in_dx2, in_ux2, in_dy2, in_uy2,
    load_sem, send_sem, recv_sem,
):
    count_x, count_y = counts
    here_x, here_y = lax.axis_index("gx"), lax.axis_index("gy")
    west = lax.rem(here_x + count_x - 1, count_x)
    east = lax.rem(here_x + 1, count_x)
    south = lax.rem(here_y + count_y - 1, count_y)
    north = lax.rem(here_y + 1, count_y)
    to_west, to_east = (west, here_y), (east, here_y)
    to_south, to_north = (here_x, south), (here_x, north)
    to_corner, from_corner = (west, south), (east, north)

    barrier = pltpu.get_barrier_semaphore()
    for peer in (to_west, to_east, to_south, to_north, to_corner, from_corner):
        pl.semaphore_signal(barrier, inc=1, device_id=peer, device_id_type=MESH)

    loads = {}

    def load(name, source, target):
        copy = pltpu.make_async_copy(source, target, load_sem.at[sum(map(len, loads.values()))])
        copy.start()
        loads.setdefault(name, []).append(copy)

    def loaded(name):
        for copy in loads[name]:
            copy.wait()

    places = [(pl.ds(16 * half, 16), pl.ds(8 * half, 8)) for half in range(2)]
    for rows, block in places:
        load("velocity", velocity.at[:, block], raw_v.at[:, :, rows, :])
        load("fields", density.at[block], raw_u.at[0, :, rows, :])
        load("fields", energy.at[block], raw_u.at[1, :, rows, :])
    for rows, block in places:
        load("mesh", mesh_velocity.at[:, block], raw_m.at[:, :, rows, :])

    load("tables", tables_hbm, tables)
    for index, source in enumerate((density_low, density_high, energy_low, energy_high)):
        load("bounds", source, bound_in.at[index])

    quad, plane = (4, 8, 128), (8, 128)
    low_rows, low_quad = low_half(plane), low_half(quad)
    first_zone, last_zone = at_zone(quad, 0), at_zone(quad, 3)
    stiff, points = TABLE["stiffness"], TABLE["to_points"]
    zero = jnp.zeros(plane, F32)

    def arrange(source, target, which, half):
        chunk = pl.ds(4 * half, 4)
        for j in range(4):
            target[which, chunk, j] = source[which, chunk, pl.ds(j, 8, stride=4), :]

    def put_pair(target, item, pair):
        target[item, 0] = pair[0]
        target[item, 1] = pair[1]

    def sided(values):
        upper, lower = parted(values)
        return upper, jnp.concatenate([upper, lower], 1)

    def lanes_product(values, column):
        _, pair = sided(values)
        both = product(pair, square[:, 256 * column : 256 * (column + 1)])
        return both[:, :128] + both[:, 128:]

    def picked(values):
        return product(sided(values)[1], picker[...])

    def traces_along_x(section, which, source, half):
        low, high = traces_of([source[which, 4 * half + i] for i in range(4)])
        trace_x[section, which, 0, half], trace_x[section, which, 1, half] = low, high

    def traces_along_y(which, source, half):
        chunk = pl.ds(4 * half, 4)
        low, high = traces_of([source[which, chunk, j] for j in range(4)])
        trace_y[which, 0, chunk], trace_y[which, 1, chunk] = low, high

    def pack_east(section, fields, vectors, target):
        for which in range(3):
            closing = combine(stiff[4][:4], [vectors[which, 4 + a] for a in range(4)])
            put_pair(target, 2 + which, pack_x_high(closing))
        for which in range(2):
            traces_along_x(section, which, fields, 1)
            put_pair(target, which, pack_x_high(trace_x[section, which, 1, 1]))

    def pack_west(section, fields, vectors, target):
        for which in range(3):
            put_pair(target, 2 + which, pack_x_low(vectors[which, 0]))
        for which in range(2):
            traces_along_x(section, which, fields, 0)
            put_pair(target, which, pack_x_low(trace_x[section, which, 0, 0]))

    def pack_south_north(fields, vectors, south_to, north_to):
        for which in range(2):
            for half in range(2):
                traces_along_y(which, fields, half)
            put_pair(south_to, which, pack_y(trace_y[which, 0], 0))
            put_pair(north_to, which, pack_y(trace_y[which, 1], 3))
        for which in range(3):
            put_pair(south_to, 2 + which, pack_y(vectors[which, :, 0], 0))
            closing = combine(stiff[4][:4], [vectors[which, :, j] for j in range(4)])
            put_pair(north_to, 2 + which, pack_y(closing, 3))

    loaded("velocity")
    loaded("fields")
    for half in (1, 0):
        for which in range(3):
            arrange(raw_v, work_v, which, half)
        for which in range(2):
            arrange(raw_u, work_u, which, half)
    pack_east(0, work_u, work_v, out_ux)
    pack_west(0, work_u, work_v, out_dx)
    loaded("mesh")
    for which in range(3):
        values = [raw_m[which, 0, pl.ds(j, 8, stride=4), :] for j in range(4)]
        put_pair(out_dx, 5 + which, pack_x_low(values))

    pl.semaphore_wait(barrier, 6)
    copies = []

    def send(source, target, peer):
        copy = pltpu.make_async_remote_copy(
            src_ref=source, dst_ref=target,
            send_sem=send_sem.at[len(copies)], recv_sem=recv_sem.at[len(copies)],
            device_id=peer, device_id_type=MESH,
        )
        copy.start()
        copies.append(copy)
        return copy

    first_ux = send(out_ux, in_ux, to_east)
    first = [send(out_dx, in_dx, to_west)]
    pack_south_north(work_u, work_v, out_dy, out_uy)
    corner = zero
    for which in range(3):
        values = raw_m[which, :, pl.ds(0, 8, stride=4), :]
        put_pair(out_dy, 5 + which, pack_y(values, 0))
        corner = jnp.where(rows_of(plane) == which, spin(values[0], which, 0), corner)
    out_corner[...] = corner
    first += [
        send(out_corner, in_corner, to_corner),
        send(out_dy, in_dy, to_south),
        send(out_uy, in_uy, to_north),
    ]
    arrived_a, arrived_b = (in_dx, in_ux, in_dy, in_uy), (in_dx2, in_ux2, in_dy2, in_uy2)

    loaded("tables")
    minus, plus, stiff_z, interp_z, pick_z, spread_z, volume_z, lift_z = (
        tables[:, 128 * column : 128 * (column + 1)] for column in range(8)
    )
    for column, table in enumerate((stiff_z, interp_z)):
        upper, lower = parted(table)
        at = 256 * column
        square[:128, at : at + 128] = upper
        square[128:, at : at + 128] = upper
        square[:128, at + 128 : at + 256] = lower
        square[128:, at + 128 : at + 256] = jnp.zeros((128, 128), BF16)
    for column, table in enumerate((minus, plus)):
        upper, lower = parted(table)
        at = 128 * column
        ends[:128, at : at + 128] = upper
        ends[128:256, at : at + 128] = upper
        ends[256:, at : at + 128] = lower
    picker[:128] = pick_z.astype(BF16)
    picker[128:] = pick_z.astype(BF16)
    for row, table in enumerate((volume_z, lift_z)):
        upper, lower = parted(table)
        tall[128 * row : 128 * (row + 1), :128] = upper
        tall[128 * row : 128 * (row + 1), 128:] = lower

    loaded("bounds")
    bound_rows[...] = jnp.zeros((4, 2, 8, 128), F32)
    for index in range(4):
        for zone in range(4):
            bound_rows[index, zone % 2, pl.ds(4 * (zone // 2), 4), pl.ds(0, 32)] = bound_in[
                index, zone
            ]
    values = bound_rows[...].reshape(64, 128)
    spreader = spread_z.astype(BF16)
    upper = values.astype(BF16)
    rest = values - upper.astype(F32)
    middle = rest.astype(BF16)
    lowest = (rest - middle.astype(F32)).astype(BF16)
    values = product(upper, spreader) + (product(middle, spreader) + product(lowest, spreader))
    bounds[...] = values.reshape(4, 2, 8, 128)

    def velocity_before(which, source, base):
        along_z = lanes_product(source[which].reshape(256, 128), 0).reshape(8, 4, 8, 128)
        own = stiff[4][4]
        opening = source[which, 0]
        inner = jnp.where(low_quad, spin(opening, 4, 1), 0.0)
        last_end = combine(stiff[4], [source[which, 4 + a] for a in range(4)] + [inner])
        carried = jnp.where(low_quad, own * opening, spin(last_end, 4, 1))
        for half in range(2):
            chunk = pl.ds(4 * half, 4)
            ahead = source[which, 4] if half == 0 else inner
            along_x = slopes_of(stiff, [source[which, 4 * half + a] for a in range(4)] + [ahead])
            along_x[0] = along_x[0] + carried
            carried = along_x[4]
            lines = [source[which, chunk, j] for j in range(4)]
            ahead = jnp.where(last_zone, 0.0, spin(lines[0], 7, 1))
            along_y = slopes_of(stiff, lines + [ahead])
            along_y[0] = along_y[0] + jnp.where(first_zone, own * lines[0], spin(along_y[4], 1, 1))
            along_y = turned(along_y[:4])
            for a in range(4):
                x = 4 * half + a
                acc_v[which, x] = base(x) + (
                    work_m[0, x] * along_x[a]
                    + work_m[1, x] * along_y[a]
                    + work_m[2, x] * along_z[x]
                )

    def velocity_after(which, half, put, arrived):
        from_east, from_west, from_north, from_south = arrived
        item = 2 + which
        above = jnp.where(last_zone, unpack_y(from_north[item, half], 3), 0.0)
        below = jnp.where(first_zone, unpack_y(from_south[item, half], 0), 0.0)
        extra_y = [stiff[j][4] * above for j in range(4)]
        extra_y[0] = extra_y[0] + below
        extra_y = turned(extra_y)
        if half == 1:
            later = jnp.stack(unpack_x_high([from_east[item, 0], from_east[item, 1]]))
            later = jnp.where(low_quad, 0.0, later)
        else:
            earlier = jnp.stack(unpack_x_low([from_west[item, 0], from_west[item, 1]]))
            earlier = jnp.where(low_quad, earlier, 0.0)
        for a in range(4):
            x = 4 * half + a
            value = acc_v[which, x] + work_m[1, x] * extra_y[a]
            if half == 1:
                value = value + work_m[0, x] * (stiff[a][4] * later)
            elif a == 0:
                value = value + work_m[0, x] * earlier
            put(x, value)

    def mesh_before(item):
        values = work_m[min(item, 2)].reshape(256, 128)
        values = lanes_product(values, 1) if item < 3 else picked(values)
        values = values.reshape(8, 4, 8, 128)
        inner = jnp.where(low_quad, spin(values[0], 4, 1), 0.0)
        for half in range(2):
            chunk = pl.ds(4 * half, 4)
            ahead = values[4] if half == 0 else inner
            across = points_of(points, [values[4 * half + a] for a in range(4)] + [ahead])
            across = turned(across)
            ahead = jnp.where(last_zone, 0.0, spin(across[0], 7, 1))
            for j, result in enumerate(points_of(points, across + [ahead])):
                speed[item, chunk, j] = result
            if item == 0:
                edge = values[4 * half]
                ahead = jnp.where(at_zone(plane, 3), 0.0, spin(edge[0], 7, 0))
                edge = points_of(points, [edge[j] for j in range(4)] + [ahead])
                face_x[half] = jnp.stack(edge)
            if item == 1:
                face_y[0, chunk] = across[0]
                face_y[1, chunk] = ahead

    def mesh_halo():
        values = jnp.concatenate(
            [in_dx[5:8].reshape(48, 128), in_dy[5:8].reshape(48, 128), in_corner[...], zero], 0
        )
        both, extra = lanes_product(values, 1), picked(values)
        for item in range(4):
            which, source = min(item, 2), both if item < 3 else extra
            halo_x[item] = source[16 * which : 16 * (which + 1)].reshape(2, 8, 128)
            halo_y[item] = source[48 + 16 * which : 64 + 16 * which].reshape(2, 8, 128)
            halo_corner[item] = spin(source[96:104], 7 - which, 0)

    def mesh_after(item, half):
        rows = rows_of(plane)
        above = jnp.where(last_zone, unpack_y(halo_y[item, half], 3), 0.0)
        if half == 1:
            first_above = jnp.where(at_zone(plane, 3), spin(halo_y[item, 0], 3, 0), 0.0)
            ahead = jnp.where(low_rows, spin(first_above, 4, 0), 0.0)
            later = unpack_x_high([halo_x[item, 0], halo_x[item, 1]])
            later = [jnp.where(low_rows, 0.0, value) for value in later]
            far = jnp.where(at_zone(plane, 3), 0.0, spin(later[0], 7, 0))
            far = jnp.where(rows == 7, halo_corner[item], far)
            later.append(jnp.where(low_rows, 0.0, far))
            edge = jnp.stack(points_of(points, later))
        else:
            ahead = jnp.where(at_zone(plane, 3), spin(halo_y[item, 1], 3, 0), 0.0)
        across = points_of(points, [above[a] for a in range(4)] + [ahead])
        for i in range(4):
            x = 4 * half + i
            extra = jnp.stack([points[j][4] * across[i] for j in range(4)])
            if half == 1:
                extra = extra + points[i][4] * edge
            speed[item, x] += extra
            if item == 1:
                upper = face_y[1, x] + across[i]
                if half == 1:
                    upper = upper + points[i][4] * later[4]
                    face_y[0, x] += points[i][4] * later[0]
                face_y[1, x] = upper
        if item == 0:
            face_x[half] += jnp.stack([points[j][4] * above[0] for j in range(4)])
            if half == 1:
                lowest = face_x[0] + jnp.stack([points[j][4] * first_above for j in range(4)])
                face_x[2] = jnp.where(low_quad, spin(lowest, 4, 1), edge)

    def upwind(face, minus_side, plus_side):
        return jnp.maximum(face, 0.0) * minus_side + jnp.minimum(face, 0.0) * plus_side

    def field_ends(which, source):
        upper, pair = sided(source[which].reshape(256, 128))
        sides = product(pair, ends[:256]) + product(upper, ends[256:])
        ends_z[which, 0] = sides[:, :128]
        ends_z[which, 1] = sides[:, 128:]

    def field_before(which, half, source, base):
        chunk, rows = pl.ds(4 * half, 4), pl.ds(128 * half, 128)
        values = source[which, chunk].reshape(128, 128)
        flux = upwind(
            speed[3, chunk].reshape(128, 128), ends_z[which, 0, rows], ends_z[which, 1, rows]
        )
        moved = speed[2, chunk].reshape(128, 128) * values
        upper, lower = parted(jnp.concatenate([moved, flux], 1))
        sums = product(upper, tall[...])
        along_z = sums[:, :128] + sums[:, 128:] + product(lower, tall[:, :128])
        along_z = along_z.reshape(4, 4, 8, 128)
        places = [4 * half + i for i in range(4)]
        along_x = slopes_of(TABLE["volume"], [speed[0, x] * source[which, x] for x in places])
        along_y = slopes_of(
            TABLE["volume"],
            [speed[1, chunk, j] * source[which, chunk, j] for j in range(4)],
        )
        along_y = turned(along_y)
        for i, x in enumerate(places):
            acc_f[which, x] = base(x) + ((along_x[i] + along_y[i]) + along_z[i])

    def in_group(values, join):
        lane = lax.broadcasted_iota(jnp.int32, plane, 1)
        partner = jnp.where(lane % 2 == 0, spin(values, 127, 1), spin(values, 1, 1))
        values = join(values, partner)
        partner = jnp.where(lane // 2 % 2 == 0, spin(values, 126, 1), spin(values, 2, 1))
        return join(values, partner)

    def over_zone(values, join):
        total = functools.reduce(join, values)
        return functools.reduce(join, [total[j] for j in range(4)])

    def limited(which, half, values):
        weights = TABLE["weights"]
        mean = combine(weights, values)
        mean = combine(weights, [mean[j] for j in range(4)])
        lane = lax.broadcasted_iota(jnp.int32, plane, 1) % 4
        middle = (lane == 1) | (lane == 2)
        mean = in_group(mean * jnp.where(middle, weights[1], weights[0]), jnp.add)
        rise = in_group(over_zone(values, jnp.maximum), jnp.maximum) - mean
        fall = in_group(over_zone(values, jnp.minimum), jnp.minimum) - mean
        low, high = bounds[2 * which, half], bounds[2 * which + 1, half]
        theta = jnp.minimum(
            (high - mean) / (rise + limit_eps), (mean - low) / (limit_eps - fall)
        )
        theta = jnp.clip(theta, 0.0, 1.0)
        return [mean + theta * (value - mean) for value in values]

    def field_after(section, which, half, put, arrived):
        from_east, from_west, from_north, from_south = arrived
        low, high = trace_x[section, which, 0], trace_x[section, which, 1]
        flux = [None, upwind(face_x[1], high[0], low[1]), None]
        if half == 1:
            later = jnp.stack(unpack_x_high([from_east[which, 0], from_east[which, 1]]))
            later = jnp.where(low_quad, spin(low[0], 4, 1), later)
            flux[2] = upwind(face_x[2], high[1], later)
        else:
            earlier = jnp.stack(unpack_x_low([from_west[which, 0], from_west[which, 1]]))
            earlier = jnp.where(low_quad, earlier, spin(high[1], 4, 1))
            flux[0] = upwind(face_x[0], earlier, low[0])
        chunk = pl.ds(4 * half, 4)
        low, high = trace_y[which, 0, chunk], trace_y[which, 1, chunk]
        before = jnp.where(first_zone, unpack_y(from_south[which, half], 0), spin(high, 1, 1))
        after = jnp.where(last_zone, unpack_y(from_north[which, half], 3), spin(low, 7, 1))
        lift_y = turned(
            lifts_of(upwind(face_y[0, chunk], before, low), upwind(face_y[1, chunk], high, after))
        )
        lift_x = lifts_of(flux[half], flux[half + 1])
        values = [acc_f[which, 4 * half + i] + (lift_x[i] + lift_y[i]) for i in range(4)]
        if section == 1:
            values = [0.5 * value for value in values]
        values = limited(which, half, values)
        for i in range(4):
            put(4 * half + i, values[i])

    for which in range(3):
        for half in range(2):
            arrange(raw_m, work_m, which, half)
    for item in range(4):
        mesh_before(item)
    for which in range(2):
        field_ends(which, work_u)
    for which in range(3):
        velocity_before(which, work_v, lambda x: work_v[which, x])

    def keep_field(x, value):
        sec_f[which, x] = value

    def keep_velocity(x, value):
        sec_v[which, x] = value

    def finish_field(x, value):
        for j in range(4):
            results[which, x, pl.ds(j, 8, stride=4), :] = value[j]

    def finish_velocity(x, value):
        for j in range(4):
            results[2 + which, x, pl.ds(j, 8, stride=4), :] = 0.5 * value[j]

    for copy in first:
        copy.wait_recv()
    mesh_halo()
    for half in (1, 0):
        if half == 0:
            first_ux.wait_recv()
        for item in range(4):
            mesh_after(item, half)
        for which in range(2):
            field_before(which, half, work_u, lambda x: work_u[which, x])
        for which in range(3):
            velocity_after(which, half, keep_velocity, arrived_a)
        for which in range(2):
            field_after(0, which, half, keep_field, arrived_a)
        if half == 1:
            pack_east(1, sec_f, sec_v, out_ux2)
            second_ux = send(out_ux2, in_ux2, to_east)
    pack_west(1, sec_f, sec_v, out_dx2)
    second = [send(out_dx2, in_dx2, to_west)]
    pack_south_north(sec_f, sec_v, out_dy2, out_uy2)
    second += [send(out_dy2, in_dy2, to_south), send(out_uy2, in_uy2, to_north)]

    for which in range(3):
        velocity_before(which, sec_v, lambda x: work_v[which, x] + sec_v[which, x])
    for which in range(2):
        field_ends(which, sec_f)
    for which in range(2):
        for half in range(2):
            field_before(which, half, sec_f, lambda x: work_u[which, x] + sec_f[which, x])
    for copy in second:
        copy.wait_recv()
    for half in (1, 0):
        if half == 0:
            second_ux.wait_recv()
        for which in range(3):
            velocity_after(which, half, finish_velocity, arrived_b)
        for which in range(2):
            field_after(1, which, half, finish_field, arrived_b)
    for copy in copies:
        copy.wait_send()


def unfold(results, new_density, new_energy, new_velocity, store_sem):
    copies = []
    for half in range(2):
        rows, block = pl.ds(16 * half, 16), pl.ds(8 * half, 8)
        for source, target in (
            (results.at[0, :, rows, :], new_density.at[block]),
            (results.at[1, :, rows, :], new_energy.at[block]),
            (results.at[pl.ds(2, 3), :, rows, :], new_velocity.at[:, block]),
        ):
            copy = pltpu.make_async_copy(source, target, store_sem.at[len(copies)])
            copy.start()
            copies.append(copy)
    for copy in copies:
        copy.wait()


def solution(mesh):
    counts = (mesh.shape["gx"], mesh.shape["gy"])
    matrices = lane_matrices(128)

    def on_device(*arguments):
        vmem = lambda *shape: pltpu.VMEM(shape, F32)
        scratch = [
            vmem(2, 8, 32, 128), vmem(3, 8, 32, 128), vmem(3, 8, 32, 128),
            vmem(*matrices.shape),
            pltpu.VMEM((256, 512), BF16), pltpu.VMEM((384, 256), BF16),
            pltpu.VMEM((256, 128), BF16), pltpu.VMEM((256, 256), BF16),
            vmem(4, 4, 4, 32), vmem(4, 2, 8, 128), vmem(4, 2, 8, 128),
            vmem(2, 8, 4, 8, 128), vmem(3, 8, 4, 8, 128), vmem(3, 8, 4, 8, 128),
            vmem(3, 8, 4, 8, 128), vmem(3, 8, 4, 8, 128),
            vmem(2, 8, 4, 8, 128), vmem(2, 8, 4, 8, 128),
            vmem(4, 8, 4, 8, 128), vmem(3, 4, 8, 128), vmem(2, 8, 8, 128),
            vmem(2, 2, 2, 2, 4, 8, 128), vmem(2, 2, 8, 8, 128), vmem(2, 2, 256, 128),
            vmem(4, 2, 8, 128), vmem(4, 2, 8, 128), vmem(4, 8, 128),
        ]
        sides = [vmem(items, 2, 8, 128) for items in (8, 5, 8, 5)]
        scratch += sides + sides + [vmem(8, 128)] * 2 + [vmem(5, 2, 8, 128)] * 8
        scratch += [
            pltpu.SemaphoreType.DMA((13,)),
            pltpu.SemaphoreType.DMA((13,)),
            pltpu.SemaphoreType.DMA((13,)),
        ]
        operands = [
            pltpu.with_memory_space_constraint(value, pltpu.HBM)
            for value in (*arguments, jnp.asarray(matrices))
        ]
        results = pl.pallas_call(
            functools.partial(kernel, counts),
            out_shape=pltpu.VMEM((5, 8, 32, 128), F32),
            in_specs=[pl.BlockSpec(memory_space=pltpu.HBM)] * 9,
            out_specs=pl.BlockSpec(memory_space=pltpu.VMEM),
            scratch_shapes=scratch,
            compiler_params=pltpu.CompilerParams(
                collective_id=0, has_side_effects=True, vmem_limit_bytes=32 * 1024 * 1024
            ),
        )(*operands)
        return pl.pallas_call(
            unfold,
            out_shape=[jax.ShapeDtypeStruct(value.shape, F32) for value in arguments[:3]],
            in_specs=[pl.BlockSpec(memory_space=pltpu.VMEM)],
            out_specs=[pl.BlockSpec(memory_space=pltpu.HBM)] * 3,
            scratch_shapes=[pltpu.SemaphoreType.DMA((6,))],
            compiler_params=pltpu.CompilerParams(vmem_limit_bytes=32 * 1024 * 1024),
        )(results)

    fields, vectors = P("gx", "gy", None), P(None, "gx", "gy", None)
    return jax.shard_map(
        on_device,
        mesh=mesh,
        in_specs=(fields, fields, vectors, vectors, fields, fields, fields, fields),
        out_specs=(fields, fields, vectors),
        check_vma=False,
    )
```

```python
import functools
import math

import jax
import jax.numpy as jnp
import numpy as np
from jax import lax
from jax.experimental import pallas as pl
from jax.experimental.pallas import tpu as pltpu
from jax.sharding import PartitionSpec as P

MESH = pl.DeviceIdType.MESH
F32 = jnp.float32
BF16 = jnp.bfloat16
time_step = 0.02
limit_eps = 1e-06


def lagrange_values(node_set, points):
    result = np.ones((len(points), len(node_set)))
    for column in range(len(node_set)):
        for partner in range(len(node_set)):
            if partner != column:
                result[:, column] = (
                    result[:, column]
                    * (points - node_set[partner])
                    / (node_set[column] - node_set[partner])
                )
    return result


def lagrange_slopes(node_set, points):
    node_total = len(node_set)
    result = np.zeros((len(points), node_total))
    for column in range(node_total):
        for skipped in range(node_total):
            if skipped != column:
                factor = np.ones(len(points)) / (node_set[column] - node_set[skipped])
                for partner in range(node_total):
                    if partner != column and partner != skipped:
                        factor = (
                            factor
                            * (points - node_set[partner])
                            / (node_set[column] - node_set[partner])
                        )
                result[:, column] = result[:, column] + factor
    return result


def basis_tables():
    gauss_points = np.array(
        [-0.8611363115940526, -0.3399810435848563, 0.3399810435848563, 0.8611363115940526]
    )
    gauss_weights = np.array(
        [0.3478548451374538, 0.6521451548625461, 0.6521451548625461, 0.3478548451374538]
    )
    lobatto_points = np.array([-1.0, -math.sqrt(3.0 / 7.0), 0.0, math.sqrt(3.0 / 7.0), 1.0])
    lobatto_weights = np.array([0.1, 49.0 / 90.0, 32.0 / 45.0, 49.0 / 90.0, 0.1])
    slopes = lagrange_slopes(gauss_points, gauss_points)
    volume = (2.0 / gauss_weights)[:, None] * slopes.T * gauss_weights[None, :]
    trace_low = lagrange_values(gauss_points, np.array([-1.0]))[0]
    trace_high = lagrange_values(gauss_points, np.array([1.0]))[0]
    stiffness = (
        2.0 * lobatto_weights[:, None] * lagrange_slopes(lobatto_points, lobatto_points)
    )
    lumped = np.array([0.2, lobatto_weights[1], lobatto_weights[2], lobatto_weights[3], 0.2])
    return {
        "weights": gauss_weights / 2.0,
        "volume": time_step * volume,
        "trace_low": trace_low,
        "trace_high": trace_high,
        "lift_low": time_step * 2.0 * trace_low / gauss_weights,
        "lift_high": time_step * 2.0 * trace_high / gauss_weights,
        "to_points": lagrange_values(lobatto_points, gauss_points),
        "stiffness": -time_step * stiffness / lumped[:, None],
    }


TABLES = basis_tables()
TABLE = {name: TABLES[name].tolist() for name in TABLES}


def lane_matrices(lanes):
    zones = lanes // 4
    shape = (lanes, lanes)
    volume, lift = np.zeros(shape), np.zeros(shape)
    minus, plus = np.zeros(shape), np.zeros(shape)
    stiff, interp = np.zeros(shape), np.zeros(shape)
    pick, spread = np.zeros(shape), np.zeros(shape)
    for zone in range(zones):
        at = 4 * zone
        before = 4 * ((zone - 1) % zones)
        for within in range(4):
            for source in range(4):
                volume[at + source, at + within] = TABLES["volume"][within, source]
                minus[before + source, at + within] = TABLES["trace_high"][source]
                plus[at + source, at + within] = TABLES["trace_low"][source]
            lift[at, at + within] = TABLES["lift_low"][within]
            lift[at, before + within] = -TABLES["lift_high"][within]
            pick[at, at + within] = 1.0
            spread[zone, at + within] = 1.0
            for source in range(5):
                interp[(at + source) % lanes, at + within] += TABLES["to_points"][within, source]
        for target in range(5):
            for source in range(5):
                stiff[(at + source) % lanes, (at + target) % lanes] += TABLES["stiffness"][
                    target, source
                ]
    matrices = [minus, plus, stiff, interp, pick, spread, volume, lift]
    return np.concatenate(matrices, axis=1).astype(np.float32)


def spin(values, steps, axis):
    size = values.shape[axis]
    steps = steps % size
    return values if steps == 0 else pltpu.roll(values, steps, axis)


def rows_of(shape):
    return lax.broadcasted_iota(jnp.int32, shape, len(shape) - 2)


def low_half(shape):
    return rows_of(shape) < 4


def at_zone(shape, zone):
    return rows_of(shape) % 4 == zone


def combine(coefficients, terms):
    total = None
    for factor, term in zip(coefficients, terms):
        part = factor * term
        total = part if total is None else total + part
    return total


def parted(values):
    upper = values.astype(BF16)
    return upper, (values - upper.astype(F32)).astype(BF16)


def product(left, right):
    return jnp.dot(left, right, preferred_element_type=F32)


def mirrored(matrix):
    size = len(matrix[0])
    middle = size // 2
    even = [[(row[c] + row[size - 1 - c]) / 2 for c in range(middle)] for row in matrix]
    odd = [[(row[c] - row[size - 1 - c]) / 2 for c in range(middle)] for row in matrix]
    centre = [row[middle] for row in matrix] if size % 2 else None
    return even, odd, centre


def pairs_of(values):
    size = len(values)
    sums = [values[c] + values[size - 1 - c] for c in range(size // 2)]
    gaps = [values[c] - values[size - 1 - c] for c in range(size // 2)]
    return sums, gaps


def slopes_of(matrix, values):
    even, odd, centre = mirrored(matrix)
    sums, gaps = pairs_of(values)
    size = len(matrix)
    result = [None] * size
    for a in range(size // 2):
        factors, terms = list(even[a]), list(sums)
        if centre is not None:
            factors.append(centre[a])
            terms.append(values[size // 2])
        outer, inner = combine(factors, terms), combine(odd[a], gaps)
        result[a], result[size - 1 - a] = inner + outer, inner - outer
    if size % 2:
        result[size // 2] = combine(odd[size // 2], gaps)
    return result


def points_of(matrix, values):
    even, odd, centre = mirrored(matrix)
    sums, gaps = pairs_of(values)
    result = [None] * 4
    for i in range(2):
        outer = combine(even[i] + [centre[i]], sums + [values[2]])
        inner = combine(odd[i], gaps)
        result[i], result[3 - i] = outer + inner, outer - inner
    return result


def traces_of(values):
    sums, gaps = pairs_of(values)
    even, odd, _ = mirrored([TABLE["trace_low"]])
    outer, inner = combine(even[0], sums), combine(odd[0], gaps)
    return outer + inner, outer - inner


def lifts_of(lower, upper):
    even, odd, _ = mirrored([TABLE["lift_low"]])
    gap, both = lower - upper, lower + upper
    result = [None] * 4
    for i in range(2):
        outer, inner = even[0][i] * gap, odd[0][i] * both
        result[i], result[3 - i] = outer + inner, outer - inner
    return result


def turned(pieces):
    return [jnp.stack([pieces[j][i] for j in range(4)]) for i in range(4)]


def pack_x_low(planes):
    mask = low_half((8, 128))
    return [jnp.where(mask, planes[t], spin(planes[t + 1], 4, 0)) for t in (0, 2)]


def pack_x_high(planes):
    mask = low_half((8, 128))
    return [jnp.where(mask, spin(planes[t], 4, 0), planes[t + 1]) for t in (0, 2)]


def unpack_x_high(packed):
    return [spin(packed[0], 4, 0), packed[0], spin(packed[1], 4, 0), packed[1]]


def unpack_x_low(packed):
    return [packed[0], spin(packed[0], 4, 0), packed[1], spin(packed[1], 4, 0)]


def pack_y(values, start):
    shape = (8, 128)
    packed = []
    for half in range(2):
        total = spin(values[4 * half + 3], 3 - start, 0)
        for place in (2, 1, 0):
            moved = spin(values[4 * half + place], place - start, 0)
            total = jnp.where(at_zone(shape, place), moved, total)
        packed.append(total)
    return packed


def unpack_y(packed, end):
    return jnp.stack([spin(packed, end - place, 0) for place in range(4)])


def kernel(
    counts,
    density, energy, velocity, mesh_velocity, density_low, density_high, energy_low, energy_high,
    tables_hbm,
    results,
    raw_u, raw_v, raw_m, tables, square, ends, picker, tall, bound_in, bound_rows,
    bounds, work_u, work_v, work_m,
    acc_v, sec_v, acc_f, sec_f, speed, face_x, face_y, trace_x, trace_y, ends_z,
    halo_x, halo_y, halo_corner,
    out_dx, out_ux, out_dy, out_uy, in_dx, in_ux, in_dy, in_uy,
    out_my, in_mx, in_my, out_corner, in_corner,
    out_vx, out_wx, out_vy, out_wy, in_vx, in_wx, in_vy, in_wy,
    out_dx2, out_ux2, out_dy2, out_uy2, in_dx2, in_ux2, in_dy2, in_uy2,
    out_vx2, out_wx2, out_vy2, out_wy2, in_vx2, in_wx2, in_vy2, in_wy2,
    load_sem, send_sem, recv_sem,
):
    count_x, count_y = counts
    here_x, here_y = lax.axis_index("gx"), lax.axis_index("gy")
    west = lax.rem(here_x + count_x - 1, count_x)
    east = lax.rem(here_x + 1, count_x)
    south = lax.rem(here_y + count_y - 1, count_y)
    north = lax.rem(here_y + 1, count_y)
    to_west, to_east = (west, here_y), (east, here_y)
    to_south, to_north = (here_x, south), (here_x, north)
    to_corner, from_corner = (west, south), (east, north)

    barrier = pltpu.get_barrier_semaphore()
    for peer in (to_west, to_east, to_south, to_north, to_corner, from_corner):
        pl.semaphore_signal(barrier, inc=1, device_id=peer, device_id_type=MESH)

    loads = {}

    def load(name, source, target):
        copy = pltpu.make_async_copy(source, target, load_sem.at[sum(map(len, loads.values()))])
        copy.start()
        loads.setdefault(name, []).append(copy)

    def loaded(name):
        for copy in loads[name]:
            copy.wait()

    places = [(pl.ds(16 * half, 16), pl.ds(8 * half, 8)) for half in range(2)]
    for rows, block in places:
        load("mesh", mesh_velocity.at[:, block], raw_m.at[:, :, rows, :])
    for rows, block in places:
        load("velocity", velocity.at[:, block], raw_v.at[:, :, rows, :])
    for rows, block in places:
        load("fields", density.at[block], raw_u.at[0, :, rows, :])
        load("fields", energy.at[block], raw_u.at[1, :, rows, :])
    load("tables", tables_hbm, tables)
    for index, source in enumerate((density_low, density_high, energy_low, energy_high)):
        load("bounds", source, bound_in.at[index])

    quad, plane = (4, 8, 128), (8, 128)
    low_rows, low_quad = low_half(plane), low_half(quad)
    first_zone, last_zone = at_zone(quad, 0), at_zone(quad, 3)
    stiff, points = TABLE["stiffness"], TABLE["to_points"]
    zero = jnp.zeros(plane, F32)

    def arrange(source, target, which):
        for j in range(4):
            target[which, :, j] = source[which, :, pl.ds(j, 8, stride=4), :]

    def put_pair(target, item, pair):
        target[item, 0] = pair[0]
        target[item, 1] = pair[1]

    def sided(values):
        upper, lower = parted(values)
        return upper, jnp.concatenate([upper, lower], 1)

    def lanes_product(values, column):
        _, pair = sided(values)
        both = product(pair, square[:, 256 * column : 256 * (column + 1)])
        return both[:, :128] + both[:, 128:]

    def picked(values):
        return product(sided(values)[1], picker[...])

    def field_traces(which, source):
        for half in range(2):
            chunk = pl.ds(4 * half, 4)
            low, high = traces_of([source[which, 4 * half + i] for i in range(4)])
            trace_x[which, 0, half], trace_x[which, 1, half] = low, high
            low, high = traces_of([source[which, chunk, j] for j in range(4)])
            trace_y[which, 0, chunk], trace_y[which, 1, chunk] = low, high

    def pack_field(which, item, buffers):
        west_to, east_to, south_to, north_to = buffers
        put_pair(west_to, item, pack_x_low(trace_x[which, 0, 0]))
        put_pair(east_to, item, pack_x_high(trace_x[which, 1, 1]))
        put_pair(south_to, item, pack_y(trace_y[which, 0], 0))
        put_pair(north_to, item, pack_y(trace_y[which, 1], 3))

    def pack_velocity(source, item, buffers):
        west_to, east_to, south_to, north_to = buffers
        put_pair(west_to, item, pack_x_low(source[item, 0]))
        closing = combine(stiff[4][:4], [source[item, 4 + a] for a in range(4)])
        put_pair(east_to, item, pack_x_high(closing))
        put_pair(south_to, item, pack_y(source[item, :, 0], 0))
        closing = combine(stiff[4][:4], [source[item, :, j] for j in range(4)])
        put_pair(north_to, item, pack_y(closing, 3))

    loaded("mesh")
    corner = zero
    for which in range(3):
        values = raw_m[which, :, pl.ds(0, 8, stride=4), :]
        put_pair(out_my, which, pack_y(values, 0))
        corner = jnp.where(rows_of(plane) == which, spin(values[0], which, 0), corner)
    out_corner[...] = corner

    pl.semaphore_wait(barrier, 6)
    copies = []
    peers = (to_west, to_east, to_south, to_north)

    def send(source, target, peer):
        copy = pltpu.make_async_remote_copy(
            src_ref=source, dst_ref=target,
            send_sem=send_sem.at[len(copies)], recv_sem=recv_sem.at[len(copies)],
            device_id=peer, device_id_type=MESH,
        )
        copy.start()
        copies.append(copy)
        return copy

    def send_all(sources, targets):
        return [send(*triple) for triple in zip(sources, targets, peers)]

    arrived_a, arrived_b = (in_dx, in_ux, in_dy, in_uy), (in_dx2, in_ux2, in_dy2, in_uy2)
    leaving_a, leaving_b = (out_dx, out_ux, out_dy, out_uy), (out_dx2, out_ux2, out_dy2, out_uy2)
    arrived_c, arrived_d = (in_vx, in_wx, in_vy, in_wy), (in_vx2, in_wx2, in_vy2, in_wy2)
    leaving_c, leaving_d = (out_vx, out_wx, out_vy, out_wy), (out_vx2, out_wx2, out_vy2, out_wy2)
    first_m = [
        send(raw_m.at[:, 0, pl.ds(0, 16), :], in_mx, to_west),
        send(out_my, in_my, to_south),
        send(out_corner, in_corner, to_corner),
    ]
    loaded("velocity")
    for which in range(3):
        arrange(raw_v, work_v, which)
        pack_velocity(work_v, which, leaving_c)
    first_v = send_all(leaving_c, arrived_c)
    loaded("fields")
    for which in range(2):
        arrange(raw_u, work_u, which)
        field_traces(which, work_u)
        pack_field(which, which, leaving_a)
    first = send_all(leaving_a, arrived_a)

    loaded("tables")
    minus, plus, stiff_z, interp_z, pick_z, spread_z, volume_z, lift_z = (
        tables[:, 128 * column : 128 * (column + 1)] for column in range(8)
    )
    for column, table in enumerate((stiff_z, interp_z)):
        upper, lower = parted(table)
        at = 256 * column
        square[:128, at : at + 128] = upper
        square[128:, at : at + 128] = upper
        square[:128, at + 128 : at + 256] = lower
        square[128:, at + 128 : at + 256] = jnp.zeros((128, 128), BF16)
    for column, table in enumerate((minus, plus)):
        upper, lower = parted(table)
        at = 128 * column
        ends[:128, at : at + 128] = upper
        ends[128:256, at : at + 128] = upper
        ends[256:, at : at + 128] = lower
    picker[:128] = pick_z.astype(BF16)
    picker[128:] = pick_z.astype(BF16)
    for row, table in enumerate((volume_z, lift_z)):
        upper, lower = parted(table)
        tall[128 * row : 128 * (row + 1), :128] = upper
        tall[128 * row : 128 * (row + 1), 128:] = lower

    loaded("bounds")
    bound_rows[...] = jnp.zeros((4, 2, 8, 128), F32)
    for index in range(4):
        for zone in range(4):
            bound_rows[index, zone % 2, pl.ds(4 * (zone // 2), 4), pl.ds(0, 32)] = bound_in[
                index, zone
            ]
    values = bound_rows[...].reshape(64, 128)
    spreader = spread_z.astype(BF16)
    upper = values.astype(BF16)
    rest = values - upper.astype(F32)
    middle = rest.astype(BF16)
    lowest = (rest - middle.astype(F32)).astype(BF16)
    values = product(upper, spreader) + (product(middle, spreader) + product(lowest, spreader))
    bounds[...] = values.reshape(4, 2, 8, 128)

    def velocity_before(which, source, base):
        along_z = lanes_product(source[which].reshape(256, 128), 0).reshape(8, 4, 8, 128)
        own = stiff[4][4]
        opening = source[which, 0]
        inner = jnp.where(low_quad, spin(opening, 4, 1), 0.0)
        last_end = combine(stiff[4], [source[which, 4 + a] for a in range(4)] + [inner])
        carried = jnp.where(low_quad, own * opening, spin(last_end, 4, 1))
        for half in range(2):
            chunk = pl.ds(4 * half, 4)
            ahead = source[which, 4] if half == 0 else inner
            along_x = slopes_of(stiff, [source[which, 4 * half + a] for a in range(4)] + [ahead])
            along_x[0] = along_x[0] + carried
            carried = along_x[4]
            lines = [source[which, chunk, j] for j in range(4)]
            ahead = jnp.where(last_zone, 0.0, spin(lines[0], 7, 1))
            along_y = slopes_of(stiff, lines + [ahead])
            along_y[0] = along_y[0] + jnp.where(first_zone, own * lines[0], spin(along_y[4], 1, 1))
            along_y = turned(along_y[:4])
            for a in range(4):
                x = 4 * half + a
                acc_v[which, x] = base(x) + (
                    work_m[0, x] * along_x[a]
                    + work_m[1, x] * along_y[a]
                    + work_m[2, x] * along_z[x]
                )

    def velocity_after(which, put, arrived):
        from_east, from_west, from_north, from_south = arrived
        later = jnp.stack(unpack_x_high([from_east[which, 0], from_east[which, 1]]))
        earlier = jnp.stack(unpack_x_low([from_west[which, 0], from_west[which, 1]]))
        later = jnp.where(low_quad, 0.0, later)
        earlier = jnp.where(low_quad, earlier, 0.0)
        for half in range(2):
            above = jnp.where(last_zone, unpack_y(from_north[which, half], 3), 0.0)
            below = jnp.where(first_zone, unpack_y(from_south[which, half], 0), 0.0)
            extra_y = [stiff[j][4] * above for j in range(4)]
            extra_y[0] = extra_y[0] + below
            extra_y = turned(extra_y)
            for a in range(4):
                x = 4 * half + a
                value = acc_v[which, x] + work_m[1, x] * extra_y[a]
                if half == 1:
                    value = value + work_m[0, x] * (stiff[a][4] * later)
                elif a == 0:
                    value = value + work_m[0, x] * earlier
                put(x, value)

    def mesh_before(item):
        values = work_m[min(item, 2)].reshape(256, 128)
        values = lanes_product(values, 1) if item < 3 else picked(values)
        values = values.reshape(8, 4, 8, 128)
        inner = jnp.where(low_quad, spin(values[0], 4, 1), 0.0)
        for half in range(2):
            chunk = pl.ds(4 * half, 4)
            ahead = values[4] if half == 0 else inner
            across = points_of(points, [values[4 * half + a] for a in range(4)] + [ahead])
            across = turned(across)
            ahead = jnp.where(last_zone, 0.0, spin(across[0], 7, 1))
            for j, result in enumerate(points_of(points, across + [ahead])):
                speed[item, chunk, j] = result
            if item == 0:
                edge = values[4 * half]
                ahead = jnp.where(at_zone(plane, 3), 0.0, spin(edge[0], 7, 0))
                edge = points_of(points, [edge[j] for j in range(4)] + [ahead])
                face_x[half] = jnp.stack(edge)
            if item == 1:
                face_y[0, chunk] = across[0]
                face_y[1, chunk] = ahead

    def mesh_halo():
        values = jnp.concatenate(
            [in_mx[...].reshape(48, 128), in_my[...].reshape(48, 128), in_corner[...], zero], 0
        )
        both, extra = lanes_product(values, 1), picked(values)
        for item in range(4):
            which, source = min(item, 2), both if item < 3 else extra
            rows = source[16 * which : 16 * (which + 1)]
            halo_x[item, pl.ds(0, 16)] = rows
            halo_x[item, pl.ds(16, 16)] = rows
            halo_y[item] = source[48 + 16 * which : 64 + 16 * which].reshape(2, 8, 128)
            halo_corner[item] = spin(source[96:104], 7 - which, 0)

    def mesh_after(item):
        rows = rows_of(plane)
        later = [
            jnp.where(low_rows, 0.0, halo_x[item, pl.ds(j, 8, stride=4), :]) for j in range(4)
        ]
        far = jnp.where(at_zone(plane, 3), 0.0, spin(later[0], 7, 0))
        far = jnp.where(rows == 7, halo_corner[item], far)
        later.append(jnp.where(low_rows, 0.0, far))
        edge = jnp.stack(points_of(points, later))
        above = [
            jnp.where(last_zone, unpack_y(halo_y[item, half], 3), 0.0) for half in range(2)
        ]
        inner = jnp.where(low_rows, spin(above[0][0], 4, 0), 0.0)
        for half in range(2):
            ahead = above[1][0] if half == 0 else inner
            across = points_of(points, [above[half][a] for a in range(4)] + [ahead])
            for i in range(4):
                x = 4 * half + i
                extra = jnp.stack([points[j][4] * across[i] for j in range(4)])
                if half == 1:
                    extra = extra + points[i][4] * edge
                speed[item, x] += extra
                if item == 1:
                    upper = face_y[1, x] + across[i]
                    if half == 1:
                        upper = upper + points[i][4] * later[4]
                        face_y[0, x] += points[i][4] * later[0]
                    face_y[1, x] = upper
            if item == 0:
                face_x[half] += jnp.stack([points[j][4] * above[half][0] for j in range(4)])
        if item == 0:
            face_x[2] = jnp.where(low_quad, spin(face_x[0], 4, 1), edge)

    def upwind(face, minus_side, plus_side):
        return jnp.maximum(face, 0.0) * minus_side + jnp.minimum(face, 0.0) * plus_side

    def field_ends(which, source):
        upper, pair = sided(source[which].reshape(256, 128))
        sides = product(pair, ends[:256]) + product(upper, ends[256:])
        ends_z[which, 0] = sides[:, :128]
        ends_z[which, 1] = sides[:, 128:]

    def field_before(which, source, base):
        values = source[which].reshape(256, 128)
        flux = upwind(speed[3].reshape(256, 128), ends_z[which, 0], ends_z[which, 1])
        moved = speed[2].reshape(256, 128) * values
        upper, lower = parted(jnp.concatenate([moved, flux], 1))
        sums = product(upper, tall[...])
        along_z = sums[:, :128] + sums[:, 128:] + product(lower, tall[:, :128])
        along_z = along_z.reshape(8, 4, 8, 128)
        for half in range(2):
            chunk = pl.ds(4 * half, 4)
            places = [4 * half + i for i in range(4)]
            along_x = slopes_of(TABLE["volume"], [speed[0, x] * source[which, x] for x in places])
            along_y = slopes_of(
                TABLE["volume"],
                [speed[1, chunk, j] * source[which, chunk, j] for j in range(4)],
            )
            along_y = turned(along_y)
            for i, x in enumerate(places):
                acc_f[which, x] = base(x) + ((along_x[i] + along_y[i]) + along_z[x])

    def in_group(values, join):
        lane = lax.broadcasted_iota(jnp.int32, plane, 1)
        partner = jnp.where(lane % 2 == 0, spin(values, 127, 1), spin(values, 1, 1))
        values = join(values, partner)
        partner = jnp.where(lane // 2 % 2 == 0, spin(values, 126, 1), spin(values, 2, 1))
        return join(values, partner)

    def over_zone(values, join):
        total = functools.reduce(join, values)
        return functools.reduce(join, [total[j] for j in range(4)])

    def limited(which, half, values):
        weights = TABLE["weights"]
        mean = combine(weights, values)
        mean = combine(weights, [mean[j] for j in range(4)])
        lane = lax.broadcasted_iota(jnp.int32, plane, 1) % 4
        middle = (lane == 1) | (lane == 2)
        mean = in_group(mean * jnp.where(middle, weights[1], weights[0]), jnp.add)
        rise = in_group(over_zone(values, jnp.maximum), jnp.maximum) - mean
        fall = in_group(over_zone(values, jnp.minimum), jnp.minimum) - mean
        low, high = bounds[2 * which, half], bounds[2 * which + 1, half]
        theta = jnp.minimum(
            (high - mean) / (rise + limit_eps), (mean - low) / (limit_eps - fall)
        )
        theta = jnp.clip(theta, 0.0, 1.0)
        return [mean + theta * (value - mean) for value in values]

    def field_after(which, scale, put, arrived):
        from_east, from_west, from_north, from_south = arrived
        later = jnp.stack(unpack_x_high([from_east[which, 0], from_east[which, 1]]))
        earlier = jnp.stack(unpack_x_low([from_west[which, 0], from_west[which, 1]]))
        low, high = trace_x[which, 0], trace_x[which, 1]
        flux = [
            upwind(face_x[0], jnp.where(low_quad, earlier, spin(high[1], 4, 1)), low[0]),
            upwind(face_x[1], high[0], low[1]),
            upwind(face_x[2], high[1], jnp.where(low_quad, spin(low[0], 4, 1), later)),
        ]
        for half in range(2):
            chunk = pl.ds(4 * half, 4)
            low, high = trace_y[which, 0, chunk], trace_y[which, 1, chunk]
            before = jnp.where(first_zone, unpack_y(from_south[which, half], 0), spin(high, 1, 1))
            after = jnp.where(last_zone, unpack_y(from_north[which, half], 3), spin(low, 7, 1))
            lift_y = turned(
                lifts_of(
                    upwind(face_y[0, chunk], before, low), upwind(face_y[1, chunk], high, after)
                )
            )
            lift_x = lifts_of(flux[half], flux[half + 1])
            values = [
                acc_f[which, 4 * half + i] + (lift_x[i] + lift_y[i]) for i in range(4)
            ]
            if scale != 1.0:
                values = [scale * value for value in values]
            values = limited(which, half, values)
            for i in range(4):
                put(4 * half + i, values[i])

    for which in range(3):
        arrange(raw_m, work_m, which)
    for item in range(4):
        mesh_before(item)
    for which in range(2):
        field_ends(which, work_u)
    for which in range(3):
        velocity_before(which, work_v, lambda x: work_v[which, x])
    def keep_field(x, value):
        sec_f[which, x] = value

    def keep_velocity(x, value):
        sec_v[which, x] = value

    def finish_field(x, value):
        for j in range(4):
            results[which, x, pl.ds(j, 8, stride=4), :] = value[j]

    def finish_velocity(x, value):
        for j in range(4):
            results[2 + which, x, pl.ds(j, 8, stride=4), :] = 0.5 * value[j]

    for copy in first_m:
        copy.wait_recv()
    mesh_halo()
    for item in range(4):
        mesh_after(item)
    for copy in first_v:
        copy.wait_recv()
    for which in range(3):
        velocity_after(which, keep_velocity, arrived_c)
        pack_velocity(sec_v, which, leaving_d)
    second_v = send_all(leaving_d, arrived_d)
    for which in range(2):
        field_before(which, work_u, lambda x: work_u[which, x])
    for copy in first:
        copy.wait_recv()
    second = []
    for which in range(2):
        field_after(which, 1.0, keep_field, arrived_a)
        field_traces(which, sec_f)
        pack_field(which, which, leaving_b)
        second.append(
            send_all([ref.at[which] for ref in leaving_b], [ref.at[which] for ref in arrived_b])
        )

    for which in range(3):
        velocity_before(which, sec_v, lambda x: work_v[which, x] + sec_v[which, x])
    for which in range(2):
        field_ends(which, sec_f)
    for which in range(2):
        field_before(which, sec_f, lambda x: work_u[which, x] + sec_f[which, x])
    for copy in second_v:
        copy.wait_recv()
    for which in range(3):
        velocity_after(which, finish_velocity, arrived_d)
    for which in range(2):
        for copy in second[which]:
            copy.wait_recv()
        field_after(which, 0.5, finish_field, arrived_b)
    for copy in copies:
        copy.wait_send()


def unfold(results, new_density, new_energy, new_velocity, store_sem):
    copies = []
    for half in range(2):
        rows, block = pl.ds(16 * half, 16), pl.ds(8 * half, 8)
        for source, target in (
            (results.at[0, :, rows, :], new_density.at[block]),
            (results.at[1, :, rows, :], new_energy.at[block]),
            (results.at[pl.ds(2, 3), :, rows, :], new_velocity.at[:, block]),
        ):
            copy = pltpu.make_async_copy(source, target, store_sem.at[len(copies)])
            copy.start()
            copies.append(copy)
    for copy in copies:
        copy.wait()


def solution(mesh):
    counts = (mesh.shape["gx"], mesh.shape["gy"])
    matrices = lane_matrices(128)

    def on_device(*arguments):
        vmem = lambda *shape: pltpu.VMEM(shape, F32)
        scratch = [
            vmem(2, 8, 32, 128), vmem(3, 8, 32, 128), vmem(3, 8, 32, 128),
            vmem(*matrices.shape),
            pltpu.VMEM((256, 512), BF16), pltpu.VMEM((384, 256), BF16),
            pltpu.VMEM((256, 128), BF16), pltpu.VMEM((256, 256), BF16),
            vmem(4, 4, 4, 32), vmem(4, 2, 8, 128), vmem(4, 2, 8, 128),
            vmem(2, 8, 4, 8, 128), vmem(3, 8, 4, 8, 128), vmem(3, 8, 4, 8, 128),
            vmem(3, 8, 4, 8, 128), vmem(3, 8, 4, 8, 128),
            vmem(2, 8, 4, 8, 128), vmem(2, 8, 4, 8, 128),
            vmem(4, 8, 4, 8, 128), vmem(3, 4, 8, 128), vmem(2, 8, 8, 128),
            vmem(2, 2, 2, 4, 8, 128), vmem(2, 2, 8, 8, 128), vmem(2, 2, 256, 128),
            vmem(4, 32, 128), vmem(4, 2, 8, 128), vmem(4, 8, 128),
        ]
        scratch += [vmem(2, 2, 8, 128)] * 8
        scratch += [vmem(3, 2, 8, 128), vmem(3, 16, 128), vmem(3, 2, 8, 128)] + [vmem(8, 128)] * 2
        for items in (3, 2, 3):
            scratch += [vmem(items, 2, 8, 128)] * 8
        scratch += [
            pltpu.SemaphoreType.DMA((13,)),
            pltpu.SemaphoreType.DMA((23,)),
            pltpu.SemaphoreType.DMA((23,)),
        ]
        operands = [
            pltpu.with_memory_space_constraint(value, pltpu.HBM)
            for value in (*arguments, jnp.asarray(matrices))
        ]
        results = pl.pallas_call(
            functools.partial(kernel, counts),
            out_shape=pltpu.VMEM((5, 8, 32, 128), F32),
            in_specs=[pl.BlockSpec(memory_space=pltpu.HBM)] * 9,
            out_specs=pl.BlockSpec(memory_space=pltpu.VMEM),
            scratch_shapes=scratch,
            compiler_params=pltpu.CompilerParams(
                collective_id=0, has_side_effects=True, vmem_limit_bytes=32 * 1024 * 1024
            ),
        )(*operands)
        return pl.pallas_call(
            unfold,
            out_shape=[jax.ShapeDtypeStruct(value.shape, F32) for value in arguments[:3]],
            in_specs=[pl.BlockSpec(memory_space=pltpu.VMEM)],
            out_specs=[pl.BlockSpec(memory_space=pltpu.HBM)] * 3,
            scratch_shapes=[pltpu.SemaphoreType.DMA((6,))],
            compiler_params=pltpu.CompilerParams(vmem_limit_bytes=32 * 1024 * 1024),
        )(results)

    fields, vectors = P("gx", "gy", None), P(None, "gx", "gy", None)
    return jax.shard_map(
        on_device,
        mesh=mesh,
        in_specs=(fields, fields, vectors, vectors, fields, fields, fields, fields),
        out_specs=(fields, fields, vectors),
        check_vma=False,
    )
```

```python
import functools
import math

import jax
import jax.numpy as jnp
import numpy as np
from jax import lax
from jax.experimental import pallas as pl
from jax.experimental.pallas import tpu as pltpu
from jax.sharding import PartitionSpec as P

MESH = pl.DeviceIdType.MESH
F32 = jnp.float32
BF16 = jnp.bfloat16
time_step = 0.02
limit_eps = 1e-06


def lagrange_values(node_set, points):
    result = np.ones((len(points), len(node_set)))
    for column in range(len(node_set)):
        for partner in range(len(node_set)):
            if partner != column:
                result[:, column] = (
                    result[:, column]
                    * (points - node_set[partner])
                    / (node_set[column] - node_set[partner])
                )
    return result


def lagrange_slopes(node_set, points):
    node_total = len(node_set)
    result = np.zeros((len(points), node_total))
    for column in range(node_total):
        for skipped in range(node_total):
            if skipped != column:
                factor = np.ones(len(points)) / (node_set[column] - node_set[skipped])
                for partner in range(node_total):
                    if partner != column and partner != skipped:
                        factor = (
                            factor
                            * (points - node_set[partner])
                            / (node_set[column] - node_set[partner])
                        )
                result[:, column] = result[:, column] + factor
    return result


def basis_tables():
    gauss_points = np.array(
        [-0.8611363115940526, -0.3399810435848563, 0.3399810435848563, 0.8611363115940526]
    )
    gauss_weights = np.array(
        [0.3478548451374538, 0.6521451548625461, 0.6521451548625461, 0.3478548451374538]
    )
    lobatto_points = np.array([-1.0, -math.sqrt(3.0 / 7.0), 0.0, math.sqrt(3.0 / 7.0), 1.0])
    lobatto_weights = np.array([0.1, 49.0 / 90.0, 32.0 / 45.0, 49.0 / 90.0, 0.1])
    slopes = lagrange_slopes(gauss_points, gauss_points)
    volume = (2.0 / gauss_weights)[:, None] * slopes.T * gauss_weights[None, :]
    trace_low = lagrange_values(gauss_points, np.array([-1.0]))[0]
    trace_high = lagrange_values(gauss_points, np.array([1.0]))[0]
    stiffness = (
        2.0 * lobatto_weights[:, None] * lagrange_slopes(lobatto_points, lobatto_points)
    )
    lumped = np.array([0.2, lobatto_weights[1], lobatto_weights[2], lobatto_weights[3], 0.2])
    return {
        "weights": gauss_weights / 2.0,
        "volume": time_step * volume,
        "trace_low": trace_low,
        "trace_high": trace_high,
        "lift_low": time_step * 2.0 * trace_low / gauss_weights,
        "lift_high": time_step * 2.0 * trace_high / gauss_weights,
        "to_points": lagrange_values(lobatto_points, gauss_points),
        "stiffness": -time_step * stiffness / lumped[:, None],
    }


TABLES = basis_tables()
TABLE = {name: TABLES[name].tolist() for name in TABLES}


def lane_matrices(lanes):
    zones = lanes // 4
    shape = (lanes, lanes)
    volume, lift = np.zeros(shape), np.zeros(shape)
    minus, plus = np.zeros(shape), np.zeros(shape)
    stiff, interp = np.zeros(shape), np.zeros(shape)
    pick, spread = np.zeros(shape), np.zeros(shape)
    for zone in range(zones):
        at = 4 * zone
        before = 4 * ((zone - 1) % zones)
        for within in range(4):
            for source in range(4):
                volume[at + source, at + within] = TABLES["volume"][within, source]
                minus[before + source, at + within] = TABLES["trace_high"][source]
                plus[at + source, at + within] = TABLES["trace_low"][source]
            lift[at, at + within] = TABLES["lift_low"][within]
            lift[at, before + within] = -TABLES["lift_high"][within]
            pick[at, at + within] = 1.0
            spread[zone, at + within] = 1.0
            for source in range(5):
                interp[(at + source) % lanes, at + within] += TABLES["to_points"][within, source]
        for target in range(5):
            for source in range(5):
                stiff[(at + source) % lanes, (at + target) % lanes] += TABLES["stiffness"][
                    target, source
                ]
    matrices = [minus, plus, stiff, interp, pick, spread, volume, lift]
    return np.concatenate(matrices, axis=1).astype(np.float32)


def spin(values, steps, axis):
    size = values.shape[axis]
    steps = steps % size
    return values if steps == 0 else pltpu.roll(values, steps, axis)


def rows_of(shape):
    return lax.broadcasted_iota(jnp.int32, shape, len(shape) - 2)


def low_half(shape):
    return rows_of(shape) < 4


def at_zone(shape, zone):
    return rows_of(shape) % 4 == zone


def combine(coefficients, terms):
    total = None
    for factor, term in zip(coefficients, terms):
        part = factor * term
        total = part if total is None else total + part
    return total


def parted(values):
    upper = values.astype(BF16)
    return upper, (values - upper.astype(F32)).astype(BF16)


def product(left, right):
    return jnp.dot(left, right, preferred_element_type=F32)


def mirrored(matrix):
    size = len(matrix[0])
    middle = size // 2
    even = [[(row[c] + row[size - 1 - c]) / 2 for c in range(middle)] for row in matrix]
    odd = [[(row[c] - row[size - 1 - c]) / 2 for c in range(middle)] for row in matrix]
    centre = [row[middle] for row in matrix] if size % 2 else None
    return even, odd, centre


def pairs_of(values):
    size = len(values)
    sums = [values[c] + values[size - 1 - c] for c in range(size // 2)]
    gaps = [values[c] - values[size - 1 - c] for c in range(size // 2)]
    return sums, gaps


def slopes_of(matrix, values):
    even, odd, centre = mirrored(matrix)
    sums, gaps = pairs_of(values)
    size = len(matrix)
    result = [None] * size
    for a in range(size // 2):
        factors, terms = list(even[a]), list(sums)
        if centre is not None:
            factors.append(centre[a])
            terms.append(values[size // 2])
        outer, inner = combine(factors, terms), combine(odd[a], gaps)
        result[a], result[size - 1 - a] = inner + outer, inner - outer
    if size % 2:
        result[size // 2] = combine(odd[size // 2], gaps)
    return result


def points_of(matrix, values):
    even, odd, centre = mirrored(matrix)
    sums, gaps = pairs_of(values)
    result = [None] * 4
    for i in range(2):
        outer = combine(even[i] + [centre[i]], sums + [values[2]])
        inner = combine(odd[i], gaps)
        result[i], result[3 - i] = outer + inner, outer - inner
    return result


def traces_of(values):
    sums, gaps = pairs_of(values)
    even, odd, _ = mirrored([TABLE["trace_low"]])
    outer, inner = combine(even[0], sums), combine(odd[0], gaps)
    return outer + inner, outer - inner


def lifts_of(lower, upper):
    even, odd, _ = mirrored([TABLE["lift_low"]])
    gap, both = lower - upper, lower + upper
    result = [None] * 4
    for i in range(2):
        outer, inner = even[0][i] * gap, odd[0][i] * both
        result[i], result[3 - i] = outer + inner, outer - inner
    return result


def turned(pieces):
    return [jnp.stack([pieces[j][i] for j in range(4)]) for i in range(4)]


def pack_x_low(planes):
    mask = low_half((8, 128))
    return [jnp.where(mask, planes[t], spin(planes[t + 1], 4, 0)) for t in (0, 2)]


def pack_x_high(planes):
    mask = low_half((8, 128))
    return [jnp.where(mask, spin(planes[t], 4, 0), planes[t + 1]) for t in (0, 2)]


def unpack_x_high(packed):
    return [spin(packed[0], 4, 0), packed[0], spin(packed[1], 4, 0), packed[1]]


def unpack_x_low(packed):
    return [packed[0], spin(packed[0], 4, 0), packed[1], spin(packed[1], 4, 0)]


def pack_y(values, start):
    shape = (8, 128)
    packed = spin(values[3], 3 - start, 0)
    for place in (2, 1, 0):
        moved = spin(values[place], place - start, 0)
        packed = jnp.where(at_zone(shape, place), moved, packed)
    return packed


def unpack_y(packed, end):
    return jnp.stack([spin(packed, end - place, 0) for place in range(4)])


def kernel(
    counts,
    density, energy, velocity, mesh_velocity, density_low, density_high, energy_low, energy_high,
    tables_hbm,
    results,
    raw_u, raw_v, raw_m, tables, square, ends, picker, tall, bound_in, bound_rows,
    bounds, work_u, work_v, work_m,
    acc_v, sec_v, acc_f, sec_f, speed, face_x, face_y, trace_x, trace_y, ends_z,
    zoned,
    out_dx, out_ux, out_dy, out_uy, in_dx, in_ux, in_dy, in_uy,
    out_corner, in_corner,
    out_dx2, out_ux2, out_dy2, out_uy2, in_dx2, in_ux2, in_dy2, in_uy2,
    load_sem, send_sem, recv_sem,
):
    count_x, count_y = counts
    here_x, here_y = lax.axis_index("gx"), lax.axis_index("gy")
    west = lax.rem(here_x + count_x - 1, count_x)
    east = lax.rem(here_x + 1, count_x)
    south = lax.rem(here_y + count_y - 1, count_y)
    north = lax.rem(here_y + 1, count_y)
    to_west, to_east = (west, here_y), (east, here_y)
    to_south, to_north = (here_x, south), (here_x, north)
    to_corner, from_corner = (west, south), (east, north)

    barrier = pltpu.get_barrier_semaphore()
    for peer in (to_west, to_east, to_south, to_north, to_corner, from_corner):
        pl.semaphore_signal(barrier, inc=1, device_id=peer, device_id_type=MESH)

    loads = {}

    def load(name, source, target):
        copy = pltpu.make_async_copy(source, target, load_sem.at[sum(map(len, loads.values()))])
        copy.start()
        loads.setdefault(name, []).append(copy)

    def loaded(name):
        for copy in loads[name]:
            copy.wait()

    places = [(pl.ds(16 * half, 16), pl.ds(8 * half, 8)) for half in range(2)]
    for rows, block in places:
        load("mesh", mesh_velocity.at[:, block], raw_m.at[:, :, rows, :])
    load("tables", tables_hbm, tables)
    for rows, block in places:
        load("velocity", velocity.at[:, block], raw_v.at[:, :, rows, :])
        load("fields", density.at[block], raw_u.at[0, :, rows, :])
        load("fields", energy.at[block], raw_u.at[1, :, rows, :])
    for index, source in enumerate((density_low, density_high, energy_low, energy_high)):
        load("bounds", source, bound_in.at[index])

    quad, plane = (4, 8, 128), (8, 128)
    low_rows, low_quad = low_half(plane), low_half(quad)
    first_zone, last_zone = at_zone(quad, 0), at_zone(quad, 3)
    stiff, points = TABLE["stiffness"], TABLE["to_points"]
    zero = jnp.zeros(plane, F32)

    def arrange(source, target, which, half):
        chunk = pl.ds(4 * half, 4)
        for j in range(4):
            target[which, chunk, j] = source[which, chunk, pl.ds(j, 8, stride=4), :]

    def put_pair(target, item, pair):
        target[item, 0] = pair[0]
        target[item, 1] = pair[1]

    def sided(values):
        upper, lower = parted(values)
        return upper, jnp.concatenate([upper, lower], 1)

    def lanes_product(values, column):
        _, pair = sided(values)
        both = product(pair, square[:, 256 * column : 256 * (column + 1)])
        return both[:, :128] + both[:, 128:]

    def picked(values):
        return product(sided(values)[1], picker[...])

    def traces_along_x(section, which, source, half):
        low, high = traces_of([source[which, 4 * half + i] for i in range(4)])
        trace_x[section, which, 0, half], trace_x[section, which, 1, half] = low, high

    def traces_along_y(which, source, half):
        chunk = pl.ds(4 * half, 4)
        low, high = traces_of([source[which, chunk, j] for j in range(4)])
        trace_y[which, 0, chunk], trace_y[which, 1, chunk] = low, high

    def pack_east(section, fields, vectors, target):
        for which in range(3):
            closing = combine(stiff[4][:4], [vectors[which, 4 + a] for a in range(4)])
            put_pair(target, 2 + which, pack_x_high(closing))
        for which in range(2):
            traces_along_x(section, which, fields, 1)
            put_pair(target, which, pack_x_high(trace_x[section, which, 1, 1]))

    def pack_west(section, fields, vectors, target):
        for which in range(3):
            put_pair(target, 2 + which, pack_x_low(vectors[which, 0]))
        for which in range(2):
            traces_along_x(section, which, fields, 0)
            put_pair(target, which, pack_x_low(trace_x[section, which, 0, 0]))

    def pack_south_north(half, fields, vectors, south_to, north_to):
        chunk = pl.ds(4 * half, 4)
        for which in range(2):
            traces_along_y(which, fields, half)
            south_to[half, which] = pack_y(trace_y[which, 0, chunk], 0)
            north_to[half, which] = pack_y(trace_y[which, 1, chunk], 3)
        for which in range(3):
            south_to[half, 2 + which] = pack_y(vectors[which, chunk, 0], 0)
            closing = combine(stiff[4][:4], [vectors[which, chunk, j] for j in range(4)])
            north_to[half, 2 + which] = pack_y(closing, 3)

    loaded("tables")
    minus, plus, stiff_z, interp_z, pick_z, spread_z, volume_z, lift_z = (
        tables[:, 128 * column : 128 * (column + 1)] for column in range(8)
    )
    for column, table in enumerate((stiff_z, interp_z)):
        upper, lower = parted(table)
        at = 256 * column
        square[:128, at : at + 128] = upper
        square[128:, at : at + 128] = upper
        square[:128, at + 128 : at + 256] = lower
        square[128:, at + 128 : at + 256] = jnp.zeros((128, 128), BF16)
    for column, table in enumerate((minus, plus)):
        upper, lower = parted(table)
        at = 128 * column
        ends[:128, at : at + 128] = upper
        ends[128:256, at : at + 128] = upper
        ends[256:, at : at + 128] = lower
    picker[:128] = pick_z.astype(BF16)
    picker[128:] = pick_z.astype(BF16)
    for row, table in enumerate((volume_z, lift_z)):
        upper, lower = parted(table)
        tall[128 * row : 128 * (row + 1), :128] = upper
        tall[128 * row : 128 * (row + 1), 128:] = lower

    loaded("mesh")
    corner = zero
    for item in range(4):
        if item < 3:
            for half in range(2):
                arrange(raw_m, work_m, item, half)
        values = work_m[min(item, 2)].reshape(256, 128)
        values = lanes_product(values, 1) if item < 3 else picked(values)
        values = values.reshape(8, 4, 8, 128)
        zoned[item] = values
        put_pair(out_dx, 5 + item, pack_x_low(values[0]))
        for half in range(2):
            out_dy[half, 5 + item] = pack_y([values[4 * half + a, 0] for a in range(4)], 0)
        corner = jnp.where(rows_of(plane) == item, spin(values[0, 0], item, 0), corner)
    out_corner[...] = corner
    loaded("velocity")
    loaded("fields")
    for half in range(2):
        for which in range(3):
            arrange(raw_v, work_v, which, half)
        for which in range(2):
            arrange(raw_u, work_u, which, half)
    pack_east(0, work_u, work_v, out_ux)
    pack_west(0, work_u, work_v, out_dx)
    for half in range(2):
        pack_south_north(half, work_u, work_v, out_dy, out_uy)

    pl.semaphore_wait(barrier, 6)
    copies = []

    def send(source, target, peer):
        copy = pltpu.make_async_remote_copy(
            src_ref=source, dst_ref=target,
            send_sem=send_sem.at[len(copies)], recv_sem=recv_sem.at[len(copies)],
            device_id=peer, device_id_type=MESH,
        )
        copy.start()
        copies.append(copy)
        return copy

    first = [send(out_dx, in_dx, to_west)]
    first_ux = send(out_ux, in_ux, to_east)
    first += [
        send(out_dy, in_dy, to_south),
        send(out_uy, in_uy, to_north),
        send(out_corner, in_corner, to_corner),
    ]
    arrived_a, arrived_b = (in_dx, in_ux, in_dy, in_uy), (in_dx2, in_ux2, in_dy2, in_uy2)

    loaded("bounds")
    bound_rows[...] = jnp.zeros((4, 2, 8, 128), F32)
    for index in range(4):
        for zone in range(4):
            bound_rows[index, zone % 2, pl.ds(4 * (zone // 2), 4), pl.ds(0, 32)] = bound_in[
                index, zone
            ]
    values = bound_rows[...].reshape(64, 128)
    spreader = spread_z.astype(BF16)
    upper = values.astype(BF16)
    rest = values - upper.astype(F32)
    middle = rest.astype(BF16)
    lowest = (rest - middle.astype(F32)).astype(BF16)
    values = product(upper, spreader) + (product(middle, spreader) + product(lowest, spreader))
    bounds[...] = values.reshape(4, 2, 8, 128)

    def velocity_before(which, source, base):
        along_z = lanes_product(source[which].reshape(256, 128), 0).reshape(8, 4, 8, 128)
        own = stiff[4][4]
        opening = source[which, 0]
        inner = jnp.where(low_quad, spin(opening, 4, 1), 0.0)
        last_end = combine(stiff[4], [source[which, 4 + a] for a in range(4)] + [inner])
        carried = jnp.where(low_quad, own * opening, spin(last_end, 4, 1))
        for half in range(2):
            chunk = pl.ds(4 * half, 4)
            ahead = source[which, 4] if half == 0 else inner
            along_x = slopes_of(stiff, [source[which, 4 * half + a] for a in range(4)] + [ahead])
            along_x[0] = along_x[0] + carried
            carried = along_x[4]
            lines = [source[which, chunk, j] for j in range(4)]
            ahead = jnp.where(last_zone, 0.0, spin(lines[0], 7, 1))
            along_y = slopes_of(stiff, lines + [ahead])
            along_y[0] = along_y[0] + jnp.where(first_zone, own * lines[0], spin(along_y[4], 1, 1))
            along_y = turned(along_y[:4])
            for a in range(4):
                x = 4 * half + a
                acc_v[which, x] = base(x) + (
                    work_m[0, x] * along_x[a]
                    + work_m[1, x] * along_y[a]
                    + work_m[2, x] * along_z[x]
                )

    def velocity_after(which, half, put, arrived):
        from_east, from_west, from_north, from_south = arrived
        item = 2 + which
        above = jnp.where(last_zone, unpack_y(from_north[half, item], 3), 0.0)
        below = jnp.where(first_zone, unpack_y(from_south[half, item], 0), 0.0)
        extra_y = [stiff[j][4] * above for j in range(4)]
        extra_y[0] = extra_y[0] + below
        extra_y = turned(extra_y)
        if half == 1:
            later = jnp.stack(unpack_x_high([from_east[item, 0], from_east[item, 1]]))
            later = jnp.where(low_quad, 0.0, later)
        else:
            earlier = jnp.stack(unpack_x_low([from_west[item, 0], from_west[item, 1]]))
            earlier = jnp.where(low_quad, earlier, 0.0)
        for a in range(4):
            x = 4 * half + a
            value = acc_v[which, x] + work_m[1, x] * extra_y[a]
            if half == 1:
                value = value + work_m[0, x] * (stiff[a][4] * later)
            elif a == 0:
                value = value + work_m[0, x] * earlier
            put(x, value)

    def mesh_before(item):
        values = zoned[item]
        inner = jnp.where(low_quad, spin(values[0], 4, 1), 0.0)
        for half in range(2):
            chunk = pl.ds(4 * half, 4)
            ahead = values[4] if half == 0 else inner
            across = points_of(points, [values[4 * half + a] for a in range(4)] + [ahead])
            across = turned(across)
            ahead = jnp.where(last_zone, 0.0, spin(across[0], 7, 1))
            for j, result in enumerate(points_of(points, across + [ahead])):
                speed[item, chunk, j] = result
            if item == 0:
                edge = values[4 * half]
                ahead = jnp.where(at_zone(plane, 3), 0.0, spin(edge[0], 7, 0))
                edge = points_of(points, [edge[j] for j in range(4)] + [ahead])
                face_x[half] = jnp.stack(edge)
            if item == 1:
                face_y[0, chunk] = across[0]
                face_y[1, chunk] = ahead

    def mesh_after(item, half):
        rows = rows_of(plane)
        above = jnp.where(last_zone, unpack_y(in_dy[half, 5 + item], 3), 0.0)
        if half == 1:
            first_above = jnp.where(at_zone(plane, 3), spin(in_dy[0, 5 + item], 3, 0), 0.0)
            ahead = jnp.where(low_rows, spin(first_above, 4, 0), 0.0)
            later = unpack_x_high([in_dx[5 + item, 0], in_dx[5 + item, 1]])
            later = [jnp.where(low_rows, 0.0, value) for value in later]
            far = jnp.where(at_zone(plane, 3), 0.0, spin(later[0], 7, 0))
            far = jnp.where(rows == 7, spin(in_corner[...], 7 - item, 0), far)
            later.append(jnp.where(low_rows, 0.0, far))
            edge = jnp.stack(points_of(points, later))
        else:
            ahead = jnp.where(at_zone(plane, 3), spin(in_dy[1, 5 + item], 3, 0), 0.0)
        across = points_of(points, [above[a] for a in range(4)] + [ahead])
        for i in range(4):
            x = 4 * half + i
            extra = jnp.stack([points[j][4] * across[i] for j in range(4)])
            if half == 1:
                extra = extra + points[i][4] * edge
            speed[item, x] += extra
            if item == 1:
                upper = face_y[1, x] + across[i]
                if half == 1:
                    upper = upper + points[i][4] * later[4]
                    face_y[0, x] += points[i][4] * later[0]
                face_y[1, x] = upper
        if item == 0:
            face_x[half] += jnp.stack([points[j][4] * above[0] for j in range(4)])
            if half == 1:
                lowest = face_x[0] + jnp.stack([points[j][4] * first_above for j in range(4)])
                face_x[2] = jnp.where(low_quad, spin(lowest, 4, 1), edge)

    def upwind(face, minus_side, plus_side):
        return jnp.maximum(face, 0.0) * minus_side + jnp.minimum(face, 0.0) * plus_side

    def field_ends(which, source):
        upper, pair = sided(source[which].reshape(256, 128))
        sides = product(pair, ends[:256]) + product(upper, ends[256:])
        ends_z[which, 0] = sides[:, :128]
        ends_z[which, 1] = sides[:, 128:]

    def field_before(which, half, source, base):
        chunk, rows = pl.ds(4 * half, 4), pl.ds(128 * half, 128)
        values = source[which, chunk].reshape(128, 128)
        flux = upwind(
            speed[3, chunk].reshape(128, 128), ends_z[which, 0, rows], ends_z[which, 1, rows]
        )
        moved = speed[2, chunk].reshape(128, 128) * values
        upper, lower = parted(jnp.concatenate([moved, flux], 1))
        sums = product(upper, tall[...])
        along_z = sums[:, :128] + sums[:, 128:] + product(lower, tall[:, :128])
        along_z = along_z.reshape(4, 4, 8, 128)
        places = [4 * half + i for i in range(4)]
        along_x = slopes_of(TABLE["volume"], [speed[0, x] * source[which, x] for x in places])
        along_y = slopes_of(
            TABLE["volume"],
            [speed[1, chunk, j] * source[which, chunk, j] for j in range(4)],
        )
        along_y = turned(along_y)
        for i, x in enumerate(places):
            acc_f[which, x] = base(x) + ((along_x[i] + along_y[i]) + along_z[i])

    def in_group(values, join):
        lane = lax.broadcasted_iota(jnp.int32, plane, 1)
        partner = jnp.where(lane % 2 == 0, spin(values, 127, 1), spin(values, 1, 1))
        values = join(values, partner)
        partner = jnp.where(lane // 2 % 2 == 0, spin(values, 126, 1), spin(values, 2, 1))
        return join(values, partner)

    def over_zone(values, join):
        total = functools.reduce(join, values)
        return functools.reduce(join, [total[j] for j in range(4)])

    def limited(which, half, values):
        weights = TABLE["weights"]
        mean = combine(weights, values)
        mean = combine(weights, [mean[j] for j in range(4)])
        lane = lax.broadcasted_iota(jnp.int32, plane, 1) % 4
        middle = (lane == 1) | (lane == 2)
        mean = in_group(mean * jnp.where(middle, weights[1], weights[0]), jnp.add)
        rise = in_group(over_zone(values, jnp.maximum), jnp.maximum) - mean
        fall = in_group(over_zone(values, jnp.minimum), jnp.minimum) - mean
        low, high = bounds[2 * which, half], bounds[2 * which + 1, half]
        theta = jnp.minimum(
            (high - mean) / (rise + limit_eps), (mean - low) / (limit_eps - fall)
        )
        theta = jnp.clip(theta, 0.0, 1.0)
        return [mean + theta * (value - mean) for value in values]

    def field_after(section, which, half, put, arrived):
        from_east, from_west, from_north, from_south = arrived
        low, high = trace_x[section, which, 0], trace_x[section, which, 1]
        flux = [None, upwind(face_x[1], high[0], low[1]), None]
        if half == 1:
            later = jnp.stack(unpack_x_high([from_east[which, 0], from_east[which, 1]]))
            later = jnp.where(low_quad, spin(low[0], 4, 1), later)
            flux[2] = upwind(face_x[2], high[1], later)
        else:
            earlier = jnp.stack(unpack_x_low([from_west[which, 0], from_west[which, 1]]))
            earlier = jnp.where(low_quad, earlier, spin(high[1], 4, 1))
            flux[0] = upwind(face_x[0], earlier, low[0])
        chunk = pl.ds(4 * half, 4)
        low, high = trace_y[which, 0, chunk], trace_y[which, 1, chunk]
        before = jnp.where(first_zone, unpack_y(from_south[half, which], 0), spin(high, 1, 1))
        after = jnp.where(last_zone, unpack_y(from_north[half, which], 3), spin(low, 7, 1))
        lift_y = turned(
            lifts_of(upwind(face_y[0, chunk], before, low), upwind(face_y[1, chunk], high, after))
        )
        lift_x = lifts_of(flux[half], flux[half + 1])
        values = [acc_f[which, 4 * half + i] + (lift_x[i] + lift_y[i]) for i in range(4)]
        if section == 1:
            values = [0.5 * value for value in values]
        values = limited(which, half, values)
        for i in range(4):
            put(4 * half + i, values[i])

    for item in range(4):
        mesh_before(item)
    for which in range(2):
        field_ends(which, work_u)
    for which in range(3):
        velocity_before(which, work_v, lambda x: work_v[which, x])

    def keep_field(x, value):
        sec_f[which, x] = value

    def keep_velocity(x, value):
        sec_v[which, x] = value

    def finish_field(x, value):
        for j in range(4):
            results[which, x, pl.ds(j, 8, stride=4), :] = value[j]

    def finish_velocity(x, value):
        for j in range(4):
            results[2 + which, x, pl.ds(j, 8, stride=4), :] = 0.5 * value[j]

    for copy in first:
        copy.wait_recv()
    second = [None, None]
    for half in (1, 0):
        if half == 0:
            first_ux.wait_recv()
        for item in range(4):
            mesh_after(item, half)
        for which in range(2):
            field_before(which, half, work_u, lambda x: work_u[which, x])
        for which in range(3):
            velocity_after(which, half, keep_velocity, arrived_a)
        for which in range(2):
            field_after(0, which, half, keep_field, arrived_a)
        if half == 1:
            pack_east(1, sec_f, sec_v, out_ux2)
            east_copy = send(out_ux2, in_ux2, to_east)
        else:
            pack_west(1, sec_f, sec_v, out_dx2)
            west_copy = send(out_dx2, in_dx2, to_west)
        pack_south_north(half, sec_f, sec_v, out_dy2, out_uy2)
        second[half] = [
            send(out_dy2.at[half], in_dy2.at[half], to_south),
            send(out_uy2.at[half], in_uy2.at[half], to_north),
        ]

    for which in range(3):
        velocity_before(which, sec_v, lambda x: work_v[which, x] + sec_v[which, x])
    for which in range(2):
        field_ends(which, sec_f)
    for which in range(2):
        for half in range(2):
            field_before(which, half, sec_f, lambda x: work_u[which, x] + sec_f[which, x])
    for half in (1, 0):
        for copy in second[half] + [west_copy if half == 1 else east_copy]:
            copy.wait_recv()
        for which in range(3):
            velocity_after(which, half, finish_velocity, arrived_b)
        for which in range(2):
            field_after(1, which, half, finish_field, arrived_b)
    for copy in copies:
        copy.wait_send()


def unfold(results, new_density, new_energy, new_velocity, store_sem):
    copies = []
    for half in range(2):
        rows, block = pl.ds(16 * half, 16), pl.ds(8 * half, 8)
        for source, target in (
            (results.at[0, :, rows, :], new_density.at[block]),
            (results.at[1, :, rows, :], new_energy.at[block]),
            (results.at[pl.ds(2, 3), :, rows, :], new_velocity.at[:, block]),
        ):
            copy = pltpu.make_async_copy(source, target, store_sem.at[len(copies)])
            copy.start()
            copies.append(copy)
    for copy in copies:
        copy.wait()


def solution(mesh):
    counts = (mesh.shape["gx"], mesh.shape["gy"])
    matrices = lane_matrices(128)

    def on_device(*arguments):
        vmem = lambda *shape: pltpu.VMEM(shape, F32)
        scratch = [
            vmem(2, 8, 32, 128), vmem(3, 8, 32, 128), vmem(3, 8, 32, 128),
            vmem(*matrices.shape),
            pltpu.VMEM((256, 512), BF16), pltpu.VMEM((384, 256), BF16),
            pltpu.VMEM((256, 128), BF16), pltpu.VMEM((256, 256), BF16),
            vmem(4, 4, 4, 32), vmem(4, 2, 8, 128), vmem(4, 2, 8, 128),
            vmem(2, 8, 4, 8, 128), vmem(3, 8, 4, 8, 128), vmem(3, 8, 4, 8, 128),
            vmem(3, 8, 4, 8, 128), vmem(3, 8, 4, 8, 128),
            vmem(2, 8, 4, 8, 128), vmem(2, 8, 4, 8, 128),
            vmem(4, 8, 4, 8, 128), vmem(3, 4, 8, 128), vmem(2, 8, 8, 128),
            vmem(2, 2, 2, 2, 4, 8, 128), vmem(2, 2, 8, 8, 128), vmem(2, 2, 256, 128),
            vmem(4, 8, 4, 8, 128),
        ]
        for items_x, items_y in ((9, 9), (5, 5)):
            west, east = vmem(items_x, 2, 8, 128), vmem(5, 2, 8, 128)
            south, north = vmem(2, items_y, 8, 128), vmem(2, 5, 8, 128)
            scratch += [west, east, south, north] * 2
            if items_x == 9:
                scratch += [vmem(8, 128)] * 2
        scratch += [
            pltpu.SemaphoreType.DMA((13,)),
            pltpu.SemaphoreType.DMA((13,)),
            pltpu.SemaphoreType.DMA((13,)),
        ]
        operands = [
            pltpu.with_memory_space_constraint(value, pltpu.HBM)
            for value in (*arguments, jnp.asarray(matrices))
        ]
        results = pl.pallas_call(
            functools.partial(kernel, counts),
            out_shape=pltpu.VMEM((5, 8, 32, 128), F32),
            in_specs=[pl.BlockSpec(memory_space=pltpu.HBM)] * 9,
            out_specs=pl.BlockSpec(memory_space=pltpu.VMEM),
            scratch_shapes=scratch,
            compiler_params=pltpu.CompilerParams(
                collective_id=0, has_side_effects=True, vmem_limit_bytes=32 * 1024 * 1024
            ),
        )(*operands)
        return pl.pallas_call(
            unfold,
            out_shape=[jax.ShapeDtypeStruct(value.shape, F32) for value in arguments[:3]],
            in_specs=[pl.BlockSpec(memory_space=pltpu.VMEM)],
            out_specs=[pl.BlockSpec(memory_space=pltpu.HBM)] * 3,
            scratch_shapes=[pltpu.SemaphoreType.DMA((6,))],
            compiler_params=pltpu.CompilerParams(vmem_limit_bytes=32 * 1024 * 1024),
        )(results)

    fields, vectors = P("gx", "gy", None), P(None, "gx", "gy", None)
    return jax.shard_map(
        on_device,
        mesh=mesh,
        in_specs=(fields, fields, vectors, vectors, fields, fields, fields, fields),
        out_specs=(fields, fields, vectors),
        check_vma=False,
    )
```

```python
import functools
import math

import jax
import jax.numpy as jnp
import numpy as np
from jax import lax
from jax.experimental import pallas as pl
from jax.experimental.pallas import tpu as pltpu
from jax.sharding import PartitionSpec as P

MESH = pl.DeviceIdType.MESH
F32 = jnp.float32
BF16 = jnp.bfloat16
time_step = 0.02
limit_eps = 1e-06


def lagrange_values(node_set, points):
    result = np.ones((len(points), len(node_set)))
    for column in range(len(node_set)):
        for partner in range(len(node_set)):
            if partner != column:
                result[:, column] = (
                    result[:, column]
                    * (points - node_set[partner])
                    / (node_set[column] - node_set[partner])
                )
    return result


def lagrange_slopes(node_set, points):
    node_total = len(node_set)
    result = np.zeros((len(points), node_total))
    for column in range(node_total):
        for skipped in range(node_total):
            if skipped != column:
                factor = np.ones(len(points)) / (node_set[column] - node_set[skipped])
                for partner in range(node_total):
                    if partner != column and partner != skipped:
                        factor = (
                            factor
                            * (points - node_set[partner])
                            / (node_set[column] - node_set[partner])
                        )
                result[:, column] = result[:, column] + factor
    return result


def basis_tables():
    gauss_points = np.array(
        [-0.8611363115940526, -0.3399810435848563, 0.3399810435848563, 0.8611363115940526]
    )
    gauss_weights = np.array(
        [0.3478548451374538, 0.6521451548625461, 0.6521451548625461, 0.3478548451374538]
    )
    lobatto_points = np.array([-1.0, -math.sqrt(3.0 / 7.0), 0.0, math.sqrt(3.0 / 7.0), 1.0])
    lobatto_weights = np.array([0.1, 49.0 / 90.0, 32.0 / 45.0, 49.0 / 90.0, 0.1])
    slopes = lagrange_slopes(gauss_points, gauss_points)
    volume = (2.0 / gauss_weights)[:, None] * slopes.T * gauss_weights[None, :]
    trace_low = lagrange_values(gauss_points, np.array([-1.0]))[0]
    trace_high = lagrange_values(gauss_points, np.array([1.0]))[0]
    stiffness = (
        2.0 * lobatto_weights[:, None] * lagrange_slopes(lobatto_points, lobatto_points)
    )
    lumped = np.array([0.2, lobatto_weights[1], lobatto_weights[2], lobatto_weights[3], 0.2])
    return {
        "weights": gauss_weights / 2.0,
        "volume": time_step * volume,
        "trace_low": trace_low,
        "trace_high": trace_high,
        "lift_low": time_step * 2.0 * trace_low / gauss_weights,
        "lift_high": time_step * 2.0 * trace_high / gauss_weights,
        "to_points": lagrange_values(lobatto_points, gauss_points),
        "stiffness": -time_step * stiffness / lumped[:, None],
    }


TABLES = basis_tables()
TABLE = {name: TABLES[name].tolist() for name in TABLES}


def lane_matrices(lanes):
    zones = lanes // 4
    shape = (lanes, lanes)
    volume, lift = np.zeros(shape), np.zeros(shape)
    minus, plus = np.zeros(shape), np.zeros(shape)
    stiff, interp = np.zeros(shape), np.zeros(shape)
    pick, spread = np.zeros(shape), np.zeros(shape)
    for zone in range(zones):
        at = 4 * zone
        before = 4 * ((zone - 1) % zones)
        for within in range(4):
            for source in range(4):
                volume[at + source, at + within] = TABLES["volume"][within, source]
                minus[before + source, at + within] = TABLES["trace_high"][source]
                plus[at + source, at + within] = TABLES["trace_low"][source]
            lift[at, at + within] = TABLES["lift_low"][within]
            lift[at, before + within] = -TABLES["lift_high"][within]
            pick[at, at + within] = 1.0
            spread[zone, at + within] = 1.0
            for source in range(5):
                interp[(at + source) % lanes, at + within] += TABLES["to_points"][within, source]
        for target in range(5):
            for source in range(5):
                stiff[(at + source) % lanes, (at + target) % lanes] += TABLES["stiffness"][
                    target, source
                ]
    matrices = [minus, plus, stiff, interp, pick, spread, volume, lift]
    return np.concatenate(matrices, axis=1).astype(np.float32)


def spin(values, steps, axis):
    size = values.shape[axis]
    steps = steps % size
    return values if steps == 0 else pltpu.roll(values, steps, axis)


def rows_of(shape):
    return lax.broadcasted_iota(jnp.int32, shape, len(shape) - 2)


def low_half(shape):
    return rows_of(shape) < 4


def at_zone(shape, zone):
    return rows_of(shape) % 4 == zone


def combine(coefficients, terms):
    total = None
    for factor, term in zip(coefficients, terms):
        part = factor * term
        total = part if total is None else total + part
    return total


def parted(values):
    upper = values.astype(BF16)
    return upper, (values - upper.astype(F32)).astype(BF16)


def product(left, right):
    return jnp.dot(left, right, preferred_element_type=F32)


def mirrored(matrix):
    size = len(matrix[0])
    middle = size // 2
    even = [[(row[c] + row[size - 1 - c]) / 2 for c in range(middle)] for row in matrix]
    odd = [[(row[c] - row[size - 1 - c]) / 2 for c in range(middle)] for row in matrix]
    centre = [row[middle] for row in matrix] if size % 2 else None
    return even, odd, centre


def pairs_of(values):
    size = len(values)
    sums = [values[c] + values[size - 1 - c] for c in range(size // 2)]
    gaps = [values[c] - values[size - 1 - c] for c in range(size // 2)]
    return sums, gaps


def slopes_of(matrix, values):
    even, odd, centre = mirrored(matrix)
    sums, gaps = pairs_of(values)
    size = len(matrix)
    result = [None] * size
    for a in range(size // 2):
        factors, terms = list(even[a]), list(sums)
        if centre is not None:
            factors.append(centre[a])
            terms.append(values[size // 2])
        outer, inner = combine(factors, terms), combine(odd[a], gaps)
        result[a], result[size - 1 - a] = inner + outer, inner - outer
    if size % 2:
        result[size // 2] = combine(odd[size // 2], gaps)
    return result


def points_of(matrix, values):
    even, odd, centre = mirrored(matrix)
    sums, gaps = pairs_of(values)
    result = [None] * 4
    for i in range(2):
        outer = combine(even[i] + [centre[i]], sums + [values[2]])
        inner = combine(odd[i], gaps)
        result[i], result[3 - i] = outer + inner, outer - inner
    return result


def traces_of(values):
    sums, gaps = pairs_of(values)
    even, odd, _ = mirrored([TABLE["trace_low"]])
    outer, inner = combine(even[0], sums), combine(odd[0], gaps)
    return outer + inner, outer - inner


def lifts_of(lower, upper):
    even, odd, _ = mirrored([TABLE["lift_low"]])
    gap, both = lower - upper, lower + upper
    result = [None] * 4
    for i in range(2):
        outer, inner = even[0][i] * gap, odd[0][i] * both
        result[i], result[3 - i] = outer + inner, outer - inner
    return result


def turned(pieces):
    return [jnp.stack([pieces[j][i] for j in range(4)]) for i in range(4)]


def pack_x_low(planes):
    mask = low_half((8, 128))
    return [jnp.where(mask, planes[t], spin(planes[t + 1], 4, 0)) for t in (0, 2)]


def pack_x_high(planes):
    mask = low_half((8, 128))
    return [jnp.where(mask, spin(planes[t], 4, 0), planes[t + 1]) for t in (0, 2)]


def unpack_x_high(packed):
    return [spin(packed[0], 4, 0), packed[0], spin(packed[1], 4, 0), packed[1]]


def unpack_x_low(packed):
    return [packed[0], spin(packed[0], 4, 0), packed[1], spin(packed[1], 4, 0)]


def pack_y(values, start):
    shape = (8, 128)
    packed = []
    for half in range(2):
        total = spin(values[4 * half + 3], 3 - start, 0)
        for place in (2, 1, 0):
            moved = spin(values[4 * half + place], place - start, 0)
            total = jnp.where(at_zone(shape, place), moved, total)
        packed.append(total)
    return packed


def unpack_y(packed, end):
    return jnp.stack([spin(packed, end - place, 0) for place in range(4)])


def kernel(
    counts,
    density, energy, velocity, mesh_velocity, density_low, density_high, energy_low, energy_high,
    tables_hbm,
    results,
    raw_u, raw_v, raw_m, tables, square, ends, picker, tall, bound_in, bound_rows,
    bounds, work_u, work_v, work_m,
    acc_v, sec_v, acc_f, sec_f, speed, face_x, face_y, trace_x, trace_y, ends_z,
    halo_x, halo_y, halo_corner,
    out_dx, out_ux, out_dy, out_uy, in_dx, in_ux, in_dy, in_uy,
    out_my, in_mx, in_my, out_corner, in_corner,
    out_vx, out_wx, out_vy, out_wy, in_vx, in_wx, in_vy, in_wy,
    out_dx2, out_ux2, out_dy2, out_uy2, in_dx2, in_ux2, in_dy2, in_uy2,
    out_vx2, out_wx2, out_vy2, out_wy2, in_vx2, in_wx2, in_vy2, in_wy2,
    load_sem, send_sem, recv_sem,
):
    count_x, count_y = counts
    here_x, here_y = lax.axis_index("gx"), lax.axis_index("gy")
    west = lax.rem(here_x + count_x - 1, count_x)
    east = lax.rem(here_x + 1, count_x)
    south = lax.rem(here_y + count_y - 1, count_y)
    north = lax.rem(here_y + 1, count_y)
    to_west, to_east = (west, here_y), (east, here_y)
    to_south, to_north = (here_x, south), (here_x, north)
    to_corner, from_corner = (west, south), (east, north)

    barrier = pltpu.get_barrier_semaphore()
    for peer in (to_west, to_east, from_corner, to_south, to_north):
        pl.semaphore_signal(barrier, inc=1, device_id=peer, device_id_type=MESH)

    loads = {}

    def load(name, source, target):
        copy = pltpu.make_async_copy(source, target, load_sem.at[sum(map(len, loads.values()))])
        copy.start()
        loads.setdefault(name, []).append(copy)

    def loaded(name):
        for copy in loads[name]:
            copy.wait()

    places = [(pl.ds(16 * half, 16), pl.ds(8 * half, 8)) for half in range(2)]
    for rows, block in places:
        load("mesh", mesh_velocity.at[:, block], raw_m.at[:, :, rows, :])
    for rows, block in places:
        load("velocity", velocity.at[:, block], raw_v.at[:, :, rows, :])
    for rows, block in places:
        load("fields", density.at[block], raw_u.at[0, :, rows, :])
        load("fields", energy.at[block], raw_u.at[1, :, rows, :])
    load("tables", tables_hbm, tables)
    for index, source in enumerate((density_low, density_high, energy_low, energy_high)):
        load("bounds", source, bound_in.at[index])

    quad, plane = (4, 8, 128), (8, 128)
    low_rows, low_quad = low_half(plane), low_half(quad)
    first_zone, last_zone = at_zone(quad, 0), at_zone(quad, 3)
    stiff, points = TABLE["stiffness"], TABLE["to_points"]
    zero = jnp.zeros(plane, F32)

    def arrange(source, target, which):
        for j in range(4):
            target[which, :, j] = source[which, :, pl.ds(j, 8, stride=4), :]

    def put_pair(target, item, pair):
        target[item, 0] = pair[0]
        target[item, 1] = pair[1]

    def sided(values):
        upper, lower = parted(values)
        return upper, jnp.concatenate([upper, lower], 1)

    def lanes_product(values, column):
        _, pair = sided(values)
        both = product(pair, square[:, 256 * column : 256 * (column + 1)])
        return both[:, :128] + both[:, 128:]

    def picked(values):
        return product(sided(values)[1], picker[...])

    def field_traces(which, source):
        for half in range(2):
            chunk = pl.ds(4 * half, 4)
            low, high = traces_of([source[which, 4 * half + i] for i in range(4)])
            trace_x[which, 0, half], trace_x[which, 1, half] = low, high
            low, high = traces_of([source[which, chunk, j] for j in range(4)])
            trace_y[which, 0, chunk], trace_y[which, 1, chunk] = low, high

    def pack_field(which, item, buffers):
        west_to, east_to, south_to, north_to = buffers
        put_pair(west_to, item, pack_x_low(trace_x[which, 0, 0]))
        put_pair(east_to, item, pack_x_high(trace_x[which, 1, 1]))
        put_pair(south_to, item, pack_y(trace_y[which, 0], 0))
        put_pair(north_to, item, pack_y(trace_y[which, 1], 3))

    def pack_velocity(source, item, buffers):
        west_to, east_to, south_to, north_to = buffers
        put_pair(west_to, item, pack_x_low(source[item, 0]))
        closing = combine(stiff[4][:4], [source[item, 4 + a] for a in range(4)])
        put_pair(east_to, item, pack_x_high(closing))
        put_pair(south_to, item, pack_y(source[item, :, 0], 0))
        closing = combine(stiff[4][:4], [source[item, :, j] for j in range(4)])
        put_pair(north_to, item, pack_y(closing, 3))

    loaded("mesh")
    corner = zero
    for which in range(3):
        values = raw_m[which, :, pl.ds(0, 8, stride=4), :]
        put_pair(out_my, which, pack_y(values, 0))
        corner = jnp.where(rows_of(plane) == which, spin(values[0], which, 0), corner)
    out_corner[...] = corner

    pl.semaphore_wait(barrier, 5)
    copies = []
    peers = (to_west, to_east, to_south, to_north)

    def send(source, target, peer):
        copy = pltpu.make_async_remote_copy(
            src_ref=source, dst_ref=target,
            send_sem=send_sem.at[len(copies)], recv_sem=recv_sem.at[len(copies)],
            device_id=peer, device_id_type=MESH,
        )
        copy.start()
        copies.append(copy)
        return copy

    def send_all(sources, targets):
        return [send(*triple) for triple in zip(sources, targets, peers)]

    arrived_a, arrived_b = (in_dx, in_ux, in_dy, in_uy), (in_dx2, in_ux2, in_dy2, in_uy2)
    leaving_a, leaving_b = (out_dx, out_ux, out_dy, out_uy), (out_dx2, out_ux2, out_dy2, out_uy2)
    arrived_c, arrived_d = (in_vx, in_wx, in_vy, in_wy), (in_vx2, in_wx2, in_vy2, in_wy2)
    leaving_c, leaving_d = (out_vx, out_wx, out_vy, out_wy), (out_vx2, out_wx2, out_vy2, out_wy2)
    first_m = [
        send(raw_m.at[:, 0, pl.ds(0, 16), :], in_mx, to_west),
        send(out_my, in_my, to_south),
        send(out_corner, in_corner, to_corner),
    ]
    loaded("velocity")
    for which in range(3):
        arrange(raw_v, work_v, which)
        pack_velocity(work_v, which, leaving_c)
    first_v = send_all(leaving_c, arrived_c)
    loaded("fields")
    for which in range(2):
        arrange(raw_u, work_u, which)
        field_traces(which, work_u)
        pack_field(which, which, leaving_a)
    first = send_all(leaving_a, arrived_a)

    loaded("tables")
    minus, plus, stiff_z, interp_z, pick_z, spread_z, volume_z, lift_z = (
        tables[:, 128 * column : 128 * (column + 1)] for column in range(8)
    )
    for column, table in enumerate((stiff_z, interp_z)):
        upper, lower = parted(table)
        at = 256 * column
        square[:128, at : at + 128] = upper
        square[128:, at : at + 128] = upper
        square[:128, at + 128 : at + 256] = lower
        square[128:, at + 128 : at + 256] = jnp.zeros((128, 128), BF16)
    for column, table in enumerate((minus, plus)):
        upper, lower = parted(table)
        at = 128 * column
        ends[:128, at : at + 128] = upper
        ends[128:256, at : at + 128] = upper
        ends[256:, at : at + 128] = lower
    picker[:128] = pick_z.astype(BF16)
    picker[128:] = pick_z.astype(BF16)
    for row, table in enumerate((volume_z, lift_z)):
        upper, lower = parted(table)
        tall[128 * row : 128 * (row + 1), :128] = upper
        tall[128 * row : 128 * (row + 1), 128:] = lower

    loaded("bounds")
    bound_rows[...] = jnp.zeros((4, 2, 8, 128), F32)
    for index in range(4):
        for zone in range(4):
            bound_rows[index, zone % 2, pl.ds(4 * (zone // 2), 4), pl.ds(0, 32)] = bound_in[
                index, zone
            ]
    values = bound_rows[...].reshape(64, 128)
    spreader = spread_z.astype(BF16)
    upper = values.astype(BF16)
    rest = values - upper.astype(F32)
    middle = rest.astype(BF16)
    lowest = (rest - middle.astype(F32)).astype(BF16)
    values = product(upper, spreader) + (product(middle, spreader) + product(lowest, spreader))
    bounds[...] = values.reshape(4, 2, 8, 128)

    def velocity_before(which, source, base):
        along_z = lanes_product(source[which].reshape(256, 128), 0).reshape(8, 4, 8, 128)
        own = stiff[4][4]
        opening = source[which, 0]
        inner = jnp.where(low_quad, spin(opening, 4, 1), 0.0)
        last_end = combine(stiff[4], [source[which, 4 + a] for a in range(4)] + [inner])
        carried = jnp.where(low_quad, own * opening, spin(last_end, 4, 1))
        for half in range(2):
            chunk = pl.ds(4 * half, 4)
            ahead = source[which, 4] if half == 0 else inner
            along_x = slopes_of(stiff, [source[which, 4 * half + a] for a in range(4)] + [ahead])
            along_x[0] = along_x[0] + carried
            carried = along_x[4]
            lines = [source[which, chunk, j] for j in range(4)]
            ahead = jnp.where(last_zone, 0.0, spin(lines[0], 7, 1))
            along_y = slopes_of(stiff, lines + [ahead])
            along_y[0] = along_y[0] + jnp.where(first_zone, own * lines[0], spin(along_y[4], 1, 1))
            along_y = turned(along_y[:4])
            for a in range(4):
                x = 4 * half + a
                acc_v[which, x] = base(x) + (
                    work_m[0, x] * along_x[a]
                    + work_m[1, x] * along_y[a]
                    + work_m[2, x] * along_z[x]
                )

    def velocity_after(which, put, arrived):
        from_east, from_west, from_north, from_south = arrived
        later = jnp.stack(unpack_x_high([from_east[which, 0], from_east[which, 1]]))
        earlier = jnp.stack(unpack_x_low([from_west[which, 0], from_west[which, 1]]))
        later = jnp.where(low_quad, 0.0, later)
        earlier = jnp.where(low_quad, earlier, 0.0)
        for half in range(2):
            above = jnp.where(last_zone, unpack_y(from_north[which, half], 3), 0.0)
            below = jnp.where(first_zone, unpack_y(from_south[which, half], 0), 0.0)
            extra_y = [stiff[j][4] * above for j in range(4)]
            extra_y[0] = extra_y[0] + below
            extra_y = turned(extra_y)
            for a in range(4):
                x = 4 * half + a
                value = acc_v[which, x] + work_m[1, x] * extra_y[a]
                if half == 1:
                    value = value + work_m[0, x] * (stiff[a][4] * later)
                elif a == 0:
                    value = value + work_m[0, x] * earlier
                put(x, value)

    def mesh_before(item):
        values = work_m[min(item, 2)].reshape(256, 128)
        values = lanes_product(values, 1) if item < 3 else picked(values)
        values = values.reshape(8, 4, 8, 128)
        inner = jnp.where(low_quad, spin(values[0], 4, 1), 0.0)
        for half in range(2):
            chunk = pl.ds(4 * half, 4)
            ahead = values[4] if half == 0 else inner
            across = points_of(points, [values[4 * half + a] for a in range(4)] + [ahead])
            across = turned(across)
            ahead = jnp.where(last_zone, 0.0, spin(across[0], 7, 1))
            for j, result in enumerate(points_of(points, across + [ahead])):
                speed[item, chunk, j] = result
            if item == 0:
                edge = values[4 * half]
                ahead = jnp.where(at_zone(plane, 3), 0.0, spin(edge[0], 7, 0))
                edge = points_of(points, [edge[j] for j in range(4)] + [ahead])
                face_x[half] = jnp.stack(edge)
            if item == 1:
                face_y[0, chunk] = across[0]
                face_y[1, chunk] = ahead

    def mesh_halo():
        values = jnp.concatenate(
            [in_mx[...].reshape(48, 128), in_my[...].reshape(48, 128), in_corner[...], zero], 0
        )
        both, extra = lanes_product(values, 1), picked(values)
        for item in range(4):
            which, source = min(item, 2), both if item < 3 else extra
            rows = source[16 * which : 16 * (which + 1)]
            halo_x[item, pl.ds(0, 16)] = rows
            halo_x[item, pl.ds(16, 16)] = rows
            halo_y[item] = source[48 + 16 * which : 64 + 16 * which].reshape(2, 8, 128)
            halo_corner[item] = spin(source[96:104], 7 - which, 0)

    def mesh_after(item):
        rows = rows_of(plane)
        later = [
            jnp.where(low_rows, 0.0, halo_x[item, pl.ds(j, 8, stride=4), :]) for j in range(4)
        ]
        far = jnp.where(at_zone(plane, 3), 0.0, spin(later[0], 7, 0))
        far = jnp.where(rows == 7, halo_corner[item], far)
        later.append(jnp.where(low_rows, 0.0, far))
        edge = jnp.stack(points_of(points, later))
        above = [
            jnp.where(last_zone, unpack_y(halo_y[item, half], 3), 0.0) for half in range(2)
        ]
        inner = jnp.where(low_rows, spin(above[0][0], 4, 0), 0.0)
        for half in range(2):
            ahead = above[1][0] if half == 0 else inner
            across = points_of(points, [above[half][a] for a in range(4)] + [ahead])
            for i in range(4):
                x = 4 * half + i
                extra = jnp.stack([points[j][4] * across[i] for j in range(4)])
                if half == 1:
                    extra = extra + points[i][4] * edge
                speed[item, x] += extra
                if item == 1:
                    upper = face_y[1, x] + across[i]
                    if half == 1:
                        upper = upper + points[i][4] * later[4]
                        face_y[0, x] += points[i][4] * later[0]
                    face_y[1, x] = upper
            if item == 0:
                face_x[half] += jnp.stack([points[j][4] * above[half][0] for j in range(4)])
        if item == 0:
            face_x[2] = jnp.where(low_quad, spin(face_x[0], 4, 1), edge)

    def upwind(face, minus_side, plus_side):
        return jnp.maximum(face, 0.0) * minus_side + jnp.minimum(face, 0.0) * plus_side

    def field_ends(which, source):
        upper, pair = sided(source[which].reshape(256, 128))
        sides = product(pair, ends[:256]) + product(upper, ends[256:])
        ends_z[which, 0] = sides[:, :128]
        ends_z[which, 1] = sides[:, 128:]

    def field_before(which, source, base):
        values = source[which].reshape(256, 128)
        flux = upwind(speed[3].reshape(256, 128), ends_z[which, 0], ends_z[which, 1])
        moved = speed[2].reshape(256, 128) * values
        upper, lower = parted(jnp.concatenate([moved, flux], 1))
        sums = product(upper, tall[...])
        along_z = sums[:, :128] + sums[:, 128:] + product(lower, tall[:, :128])
        along_z = along_z.reshape(8, 4, 8, 128)
        for half in range(2):
            chunk = pl.ds(4 * half, 4)
            places = [4 * half + i for i in range(4)]
            along_x = slopes_of(TABLE["volume"], [speed[0, x] * source[which, x] for x in places])
            along_y = slopes_of(
                TABLE["volume"],
                [speed[1, chunk, j] * source[which, chunk, j] for j in range(4)],
            )
            along_y = turned(along_y)
            for i, x in enumerate(places):
                acc_f[which, x] = base(x) + ((along_x[i] + along_y[i]) + along_z[x])

    def in_group(values, join):
        lane = lax.broadcasted_iota(jnp.int32, plane, 1)
        partner = jnp.where(lane % 2 == 0, spin(values, 127, 1), spin(values, 1, 1))
        values = join(values, partner)
        partner = jnp.where(lane // 2 % 2 == 0, spin(values, 126, 1), spin(values, 2, 1))
        return join(values, partner)

    def over_zone(values, join):
        total = functools.reduce(join, values)
        return functools.reduce(join, [total[j] for j in range(4)])

    def limited(which, half, values):
        weights = TABLE["weights"]
        mean = combine(weights, values)
        mean = combine(weights, [mean[j] for j in range(4)])
        lane = lax.broadcasted_iota(jnp.int32, plane, 1) % 4
        middle = (lane == 1) | (lane == 2)
        mean = in_group(mean * jnp.where(middle, weights[1], weights[0]), jnp.add)
        rise = in_group(over_zone(values, jnp.maximum), jnp.maximum) - mean
        fall = in_group(over_zone(values, jnp.minimum), jnp.minimum) - mean
        low, high = bounds[2 * which, half], bounds[2 * which + 1, half]
        theta = jnp.minimum(
            (high - mean) / (rise + limit_eps), (mean - low) / (limit_eps - fall)
        )
        theta = jnp.clip(theta, 0.0, 1.0)
        return [mean + theta * (value - mean) for value in values]

    def field_after(which, scale, put, arrived):
        from_east, from_west, from_north, from_south = arrived
        later = jnp.stack(unpack_x_high([from_east[which, 0], from_east[which, 1]]))
        earlier = jnp.stack(unpack_x_low([from_west[which, 0], from_west[which, 1]]))
        low, high = trace_x[which, 0], trace_x[which, 1]
        flux = [
            upwind(face_x[0], jnp.where(low_quad, earlier, spin(high[1], 4, 1)), low[0]),
            upwind(face_x[1], high[0], low[1]),
            upwind(face_x[2], high[1], jnp.where(low_quad, spin(low[0], 4, 1), later)),
        ]
        for half in range(2):
            chunk = pl.ds(4 * half, 4)
            low, high = trace_y[which, 0, chunk], trace_y[which, 1, chunk]
            before = jnp.where(first_zone, unpack_y(from_south[which, half], 0), spin(high, 1, 1))
            after = jnp.where(last_zone, unpack_y(from_north[which, half], 3), spin(low, 7, 1))
            lift_y = turned(
                lifts_of(
                    upwind(face_y[0, chunk], before, low), upwind(face_y[1, chunk], high, after)
                )
            )
            lift_x = lifts_of(flux[half], flux[half + 1])
            values = [
                acc_f[which, 4 * half + i] + (lift_x[i] + lift_y[i]) for i in range(4)
            ]
            if scale != 1.0:
                values = [scale * value for value in values]
            values = limited(which, half, values)
            for i in range(4):
                put(4 * half + i, values[i])

    for which in range(3):
        arrange(raw_m, work_m, which)
    for item in range(4):
        mesh_before(item)
    for which in range(2):
        field_ends(which, work_u)
    for which in range(3):
        velocity_before(which, work_v, lambda x: work_v[which, x])
    def keep_field(x, value):
        sec_f[which, x] = value

    def keep_velocity(x, value):
        sec_v[which, x] = value

    def finish_field(x, value):
        for j in range(4):
            results[which, x, pl.ds(j, 8, stride=4), :] = value[j]

    def finish_velocity(x, value):
        for j in range(4):
            results[2 + which, x, pl.ds(j, 8, stride=4), :] = 0.5 * value[j]

    for copy in first_m:
        copy.wait_recv()
    mesh_halo()
    for item in range(4):
        mesh_after(item)
    for copy in first_v:
        copy.wait_recv()
    for which in range(3):
        velocity_after(which, keep_velocity, arrived_c)
        pack_velocity(sec_v, which, leaving_d)
    second_v = send_all(leaving_d, arrived_d)
    for which in range(2):
        field_before(which, work_u, lambda x: work_u[which, x])
    for copy in first:
        copy.wait_recv()
    second = []
    for which in range(2):
        field_after(which, 1.0, keep_field, arrived_a)
        field_traces(which, sec_f)
        pack_field(which, which, leaving_b)
        second.append(
            send_all([ref.at[which] for ref in leaving_b], [ref.at[which] for ref in arrived_b])
        )

    for which in range(3):
        velocity_before(which, sec_v, lambda x: work_v[which, x] + sec_v[which, x])
    for which in range(2):
        field_ends(which, sec_f)
    for which in range(2):
        field_before(which, sec_f, lambda x: work_u[which, x] + sec_f[which, x])
    for copy in second_v:
        copy.wait_recv()
    for which in range(3):
        velocity_after(which, finish_velocity, arrived_d)
    for which in range(2):
        for copy in second[which]:
            copy.wait_recv()
        field_after(which, 0.5, finish_field, arrived_b)
    for copy in copies:
        copy.wait_send()


def unfold(results, new_density, new_energy, new_velocity, store_sem):
    copies = []
    for half in range(2):
        rows, block = pl.ds(16 * half, 16), pl.ds(8 * half, 8)
        for source, target in (
            (results.at[0, :, rows, :], new_density.at[block]),
            (results.at[1, :, rows, :], new_energy.at[block]),
            (results.at[pl.ds(2, 3), :, rows, :], new_velocity.at[:, block]),
        ):
            copy = pltpu.make_async_copy(source, target, store_sem.at[len(copies)])
            copy.start()
            copies.append(copy)
    for copy in copies:
        copy.wait()


def solution(mesh):
    counts = (mesh.shape["gx"], mesh.shape["gy"])
    matrices = lane_matrices(128)

    def on_device(*arguments):
        vmem = lambda *shape: pltpu.VMEM(shape, F32)
        scratch = [
            vmem(2, 8, 32, 128), vmem(3, 8, 32, 128), vmem(3, 8, 32, 128),
            vmem(*matrices.shape),
            pltpu.VMEM((256, 512), BF16), pltpu.VMEM((384, 256), BF16),
            pltpu.VMEM((256, 128), BF16), pltpu.VMEM((256, 256), BF16),
            vmem(4, 4, 4, 32), vmem(4, 2, 8, 128), vmem(4, 2, 8, 128),
            vmem(2, 8, 4, 8, 128), vmem(3, 8, 4, 8, 128), vmem(3, 8, 4, 8, 128),
            vmem(3, 8, 4, 8, 128), vmem(3, 8, 4, 8, 128),
            vmem(2, 8, 4, 8, 128), vmem(2, 8, 4, 8, 128),
            vmem(4, 8, 4, 8, 128), vmem(3, 4, 8, 128), vmem(2, 8, 8, 128),
            vmem(2, 2, 2, 4, 8, 128), vmem(2, 2, 8, 8, 128), vmem(2, 2, 256, 128),
            vmem(4, 32, 128), vmem(4, 2, 8, 128), vmem(4, 8, 128),
        ]
        scratch += [vmem(2, 2, 8, 128)] * 8
        scratch += [vmem(3, 2, 8, 128), vmem(3, 16, 128), vmem(3, 2, 8, 128)] + [vmem(8, 128)] * 2
        for items in (3, 2, 3):
            scratch += [vmem(items, 2, 8, 128)] * 8
        scratch += [
            pltpu.SemaphoreType.DMA((13,)),
            pltpu.SemaphoreType.DMA((23,)),
            pltpu.SemaphoreType.DMA((23,)),
        ]
        operands = [
            pltpu.with_memory_space_constraint(value, pltpu.HBM)
            for value in (*arguments, jnp.asarray(matrices))
        ]
        results = pl.pallas_call(
            functools.partial(kernel, counts),
            out_shape=pltpu.VMEM((5, 8, 32, 128), F32),
            in_specs=[pl.BlockSpec(memory_space=pltpu.HBM)] * 9,
            out_specs=pl.BlockSpec(memory_space=pltpu.VMEM),
            scratch_shapes=scratch,
            compiler_params=pltpu.CompilerParams(
                collective_id=0, has_side_effects=True, vmem_limit_bytes=32 * 1024 * 1024
            ),
        )(*operands)
        return pl.pallas_call(
            unfold,
            out_shape=[jax.ShapeDtypeStruct(value.shape, F32) for value in arguments[:3]],
            in_specs=[pl.BlockSpec(memory_space=pltpu.VMEM)],
            out_specs=[pl.BlockSpec(memory_space=pltpu.HBM)] * 3,
            scratch_shapes=[pltpu.SemaphoreType.DMA((6,))],
            compiler_params=pltpu.CompilerParams(vmem_limit_bytes=32 * 1024 * 1024),
        )(results)

    fields, vectors = P("gx", "gy", None), P(None, "gx", "gy", None)
    return jax.shard_map(
        on_device,
        mesh=mesh,
        in_specs=(fields, fields, vectors, vectors, fields, fields, fields, fields),
        out_specs=(fields, fields, vectors),
        check_vma=False,
    )
```

```python
import functools
import math

import jax
import jax.numpy as jnp
import numpy as np
from jax import lax
from jax.experimental import pallas as pl
from jax.experimental.pallas import tpu as pltpu
from jax.sharding import PartitionSpec as P

MESH = pl.DeviceIdType.MESH
F32 = jnp.float32
BF16 = jnp.bfloat16
time_step = 0.02
limit_eps = 1e-06


def lagrange_values(node_set, points):
    result = np.ones((len(points), len(node_set)))
    for column in range(len(node_set)):
        for partner in range(len(node_set)):
            if partner != column:
                result[:, column] = (
                    result[:, column]
                    * (points - node_set[partner])
                    / (node_set[column] - node_set[partner])
                )
    return result


def lagrange_slopes(node_set, points):
    node_total = len(node_set)
    result = np.zeros((len(points), node_total))
    for column in range(node_total):
        for skipped in range(node_total):
            if skipped != column:
                factor = np.ones(len(points)) / (node_set[column] - node_set[skipped])
                for partner in range(node_total):
                    if partner != column and partner != skipped:
                        factor = (
                            factor
                            * (points - node_set[partner])
                            / (node_set[column] - node_set[partner])
                        )
                result[:, column] = result[:, column] + factor
    return result


def basis_tables():
    gauss_points = np.array(
        [-0.8611363115940526, -0.3399810435848563, 0.3399810435848563, 0.8611363115940526]
    )
    gauss_weights = np.array(
        [0.3478548451374538, 0.6521451548625461, 0.6521451548625461, 0.3478548451374538]
    )
    lobatto_points = np.array([-1.0, -math.sqrt(3.0 / 7.0), 0.0, math.sqrt(3.0 / 7.0), 1.0])
    lobatto_weights = np.array([0.1, 49.0 / 90.0, 32.0 / 45.0, 49.0 / 90.0, 0.1])
    slopes = lagrange_slopes(gauss_points, gauss_points)
    volume = (2.0 / gauss_weights)[:, None] * slopes.T * gauss_weights[None, :]
    trace_low = lagrange_values(gauss_points, np.array([-1.0]))[0]
    trace_high = lagrange_values(gauss_points, np.array([1.0]))[0]
    stiffness = (
        2.0 * lobatto_weights[:, None] * lagrange_slopes(lobatto_points, lobatto_points)
    )
    lumped = np.array([0.2, lobatto_weights[1], lobatto_weights[2], lobatto_weights[3], 0.2])
    return {
        "weights": gauss_weights / 2.0,
        "volume": time_step * volume,
        "trace_low": trace_low,
        "trace_high": trace_high,
        "lift_low": time_step * 2.0 * trace_low / gauss_weights,
        "lift_high": time_step * 2.0 * trace_high / gauss_weights,
        "to_points": lagrange_values(lobatto_points, gauss_points),
        "stiffness": -time_step * stiffness / lumped[:, None],
    }


TABLES = basis_tables()
TABLE = {name: TABLES[name].tolist() for name in TABLES}


def lane_matrices(lanes):
    zones = lanes // 4
    shape = (lanes, lanes)
    volume, lift = np.zeros(shape), np.zeros(shape)
    minus, plus = np.zeros(shape), np.zeros(shape)
    stiff, interp = np.zeros(shape), np.zeros(shape)
    pick, spread = np.zeros(shape), np.zeros(shape)
    for zone in range(zones):
        at = 4 * zone
        before = 4 * ((zone - 1) % zones)
        for within in range(4):
            for source in range(4):
                volume[at + source, at + within] = TABLES["volume"][within, source]
                minus[before + source, at + within] = TABLES["trace_high"][source]
                plus[at + source, at + within] = TABLES["trace_low"][source]
            lift[at, at + within] = TABLES["lift_low"][within]
            lift[at, before + within] = -TABLES["lift_high"][within]
            pick[at, at + within] = 1.0
            spread[zone, at + within] = 1.0
            for source in range(5):
                interp[(at + source) % lanes, at + within] += TABLES["to_points"][within, source]
        for target in range(5):
            for source in range(5):
                stiff[(at + source) % lanes, (at + target) % lanes] += TABLES["stiffness"][
                    target, source
                ]
    matrices = [minus, plus, stiff, interp, pick, spread, volume, lift]
    return np.concatenate(matrices, axis=1).astype(np.float32)


def spin(values, steps, axis):
    size = values.shape[axis]
    steps = steps % size
    return values if steps == 0 else pltpu.roll(values, steps, axis)


def rows_of(shape):
    return lax.broadcasted_iota(jnp.int32, shape, len(shape) - 2)


def low_half(shape):
    return rows_of(shape) < 4


def at_zone(shape, zone):
    return rows_of(shape) % 4 == zone


def combine(coefficients, terms):
    total = None
    for factor, term in zip(coefficients, terms):
        part = factor * term
        total = part if total is None else total + part
    return total


def parted(values):
    upper = values.astype(BF16)
    return upper, (values - upper.astype(F32)).astype(BF16)


def product(left, right):
    return jnp.dot(left, right, preferred_element_type=F32)


def mirrored(matrix):
    size = len(matrix[0])
    middle = size // 2
    even = [[(row[c] + row[size - 1 - c]) / 2 for c in range(middle)] for row in matrix]
    odd = [[(row[c] - row[size - 1 - c]) / 2 for c in range(middle)] for row in matrix]
    centre = [row[middle] for row in matrix] if size % 2 else None
    return even, odd, centre


def pairs_of(values):
    size = len(values)
    sums = [values[c] + values[size - 1 - c] for c in range(size // 2)]
    gaps = [values[c] - values[size - 1 - c] for c in range(size // 2)]
    return sums, gaps


def slopes_of(matrix, values):
    even, odd, centre = mirrored(matrix)
    sums, gaps = pairs_of(values)
    size = len(matrix)
    result = [None] * size
    for a in range(size // 2):
        factors, terms = list(even[a]), list(sums)
        if centre is not None:
            factors.append(centre[a])
            terms.append(values[size // 2])
        outer, inner = combine(factors, terms), combine(odd[a], gaps)
        result[a], result[size - 1 - a] = inner + outer, inner - outer
    if size % 2:
        result[size // 2] = combine(odd[size // 2], gaps)
    return result


def points_of(matrix, values):
    even, odd, centre = mirrored(matrix)
    sums, gaps = pairs_of(values)
    result = [None] * 4
    for i in range(2):
        outer = combine(even[i] + [centre[i]], sums + [values[2]])
        inner = combine(odd[i], gaps)
        result[i], result[3 - i] = outer + inner, outer - inner
    return result


def traces_of(values):
    sums, gaps = pairs_of(values)
    even, odd, _ = mirrored([TABLE["trace_low"]])
    outer, inner = combine(even[0], sums), combine(odd[0], gaps)
    return outer + inner, outer - inner


def lifts_of(lower, upper):
    even, odd, _ = mirrored([TABLE["lift_low"]])
    gap, both = lower - upper, lower + upper
    result = [None] * 4
    for i in range(2):
        outer, inner = even[0][i] * gap, odd[0][i] * both
        result[i], result[3 - i] = outer + inner, outer - inner
    return result


def turned(pieces):
    return [jnp.stack([pieces[j][i] for j in range(4)]) for i in range(4)]


def pack_x_low(planes):
    mask = low_half((8, 128))
    return [jnp.where(mask, planes[t], spin(planes[t + 1], 4, 0)) for t in (0, 2)]


def pack_x_high(planes):
    mask = low_half((8, 128))
    return [jnp.where(mask, spin(planes[t], 4, 0), planes[t + 1]) for t in (0, 2)]


def unpack_x_high(packed):
    return [spin(packed[0], 4, 0), packed[0], spin(packed[1], 4, 0), packed[1]]


def unpack_x_low(packed):
    return [packed[0], spin(packed[0], 4, 0), packed[1], spin(packed[1], 4, 0)]


def pack_y(values, start):
    shape = (8, 128)
    packed = []
    for half in range(2):
        total = spin(values[4 * half + 3], 3 - start, 0)
        for place in (2, 1, 0):
            moved = spin(values[4 * half + place], place - start, 0)
            total = jnp.where(at_zone(shape, place), moved, total)
        packed.append(total)
    return packed


def unpack_y(packed, end):
    return jnp.stack([spin(packed, end - place, 0) for place in range(4)])


def kernel(
    counts,
    density, energy, velocity, mesh_velocity, density_low, density_high, energy_low, energy_high,
    tables_hbm,
    results,
    raw_u, raw_v, raw_m, tables, square, ends, picker, tall, bound_in, bound_rows,
    bounds, work_u, work_v, work_m,
    acc_v, sec_v, acc_f, sec_f, speed, face_x, face_y, trace_x, trace_y, ends_z,
    halo_x, halo_y, halo_corner,
    out_dx, out_ux, out_dy, out_uy, in_dx, in_ux, in_dy, in_uy,
    out_my, in_mx, in_my, out_corner, in_corner,
    out_vx, out_wx, out_vy, out_wy, in_vx, in_wx, in_vy, in_wy,
    out_dx2, out_ux2, out_dy2, out_uy2, in_dx2, in_ux2, in_dy2, in_uy2,
    out_vx2, out_wx2, out_vy2, out_wy2, in_vx2, in_wx2, in_vy2, in_wy2,
    load_sem, send_sem, recv_sem,
):
    count_x, count_y = counts
    here_x, here_y = lax.axis_index("gx"), lax.axis_index("gy")
    west = lax.rem(here_x + count_x - 1, count_x)
    east = lax.rem(here_x + 1, count_x)
    south = lax.rem(here_y + count_y - 1, count_y)
    north = lax.rem(here_y + 1, count_y)
    to_west, to_east = (west, here_y), (east, here_y)
    to_south, to_north = (here_x, south), (here_x, north)
    to_corner, from_corner = (west, south), (east, north)

    barrier = pltpu.get_barrier_semaphore()
    for peer in (to_west, to_east, from_corner, to_south, to_north):
        pl.semaphore_signal(barrier, inc=1, device_id=peer, device_id_type=MESH)

    loads = {}

    def load(name, source, target):
        copy = pltpu.make_async_copy(source, target, load_sem.at[sum(map(len, loads.values()))])
        copy.start()
        loads.setdefault(name, []).append(copy)

    def loaded(name):
        for copy in loads[name]:
            copy.wait()

    places = [(pl.ds(16 * half, 16), pl.ds(8 * half, 8)) for half in range(2)]
    for rows, block in places:
        load("mesh", mesh_velocity.at[:, block], raw_m.at[:, :, rows, :])
    for rows, block in places:
        load("velocity", velocity.at[:, block], raw_v.at[:, :, rows, :])
    for rows, block in places:
        load("fields", density.at[block], raw_u.at[0, :, rows, :])
        load("fields", energy.at[block], raw_u.at[1, :, rows, :])
    load("tables", tables_hbm, tables)
    for index, source in enumerate((density_low, density_high, energy_low, energy_high)):
        load("bounds", source, bound_in.at[index])

    quad, plane = (4, 8, 128), (8, 128)
    low_rows, low_quad = low_half(plane), low_half(quad)
    first_zone, last_zone = at_zone(quad, 0), at_zone(quad, 3)
    stiff, points = TABLE["stiffness"], TABLE["to_points"]
    zero = jnp.zeros(plane, F32)

    def arrange(source, target, which):
        for j in range(4):
            target[which, :, j] = source[which, :, pl.ds(j, 8, stride=4), :]

    def put_pair(target, item, pair):
        target[item, 0] = pair[0]
        target[item, 1] = pair[1]

    def sided(values):
        upper, lower = parted(values)
        return upper, jnp.concatenate([upper, lower], 1)

    def lanes_product(values, column):
        _, pair = sided(values)
        both = product(pair, square[:, 256 * column : 256 * (column + 1)])
        return both[:, :128] + both[:, 128:]

    def picked(values):
        return product(sided(values)[1], picker[...])

    def field_traces(which, source):
        for half in range(2):
            chunk = pl.ds(4 * half, 4)
            low, high = traces_of([source[which, 4 * half + i] for i in range(4)])
            trace_x[which, 0, half], trace_x[which, 1, half] = low, high
            low, high = traces_of([source[which, chunk, j] for j in range(4)])
            trace_y[which, 0, chunk], trace_y[which, 1, chunk] = low, high

    def pack_field(which, item, buffers):
        west_to, east_to, south_to, north_to = buffers
        put_pair(west_to, item, pack_x_low(trace_x[which, 0, 0]))
        put_pair(east_to, item, pack_x_high(trace_x[which, 1, 1]))
        put_pair(south_to, item, pack_y(trace_y[which, 0], 0))
        put_pair(north_to, item, pack_y(trace_y[which, 1], 3))

    def pack_velocity(source, item, buffers):
        west_to, east_to, south_to, north_to = buffers
        put_pair(west_to, item, pack_x_low(source[item, 0]))
        closing = combine(stiff[4][:4], [source[item, 4 + a] for a in range(4)])
        put_pair(east_to, item, pack_x_high(closing))
        put_pair(south_to, item, pack_y(source[item, :, 0], 0))
        closing = combine(stiff[4][:4], [source[item, :, j] for j in range(4)])
        put_pair(north_to, item, pack_y(closing, 3))

    loaded("mesh")
    corner = zero
    for which in range(3):
        values = raw_m[which, :, pl.ds(0, 8, stride=4), :]
        put_pair(out_my, which, pack_y(values, 0))
        corner = jnp.where(rows_of(plane) == which, spin(values[0], which, 0), corner)
    out_corner[...] = corner

    arrived_a, arrived_b = (in_dx, in_ux, in_dy, in_uy), (in_dx2, in_ux2, in_dy2, in_uy2)
    leaving_a, leaving_b = (out_dx, out_ux, out_dy, out_uy), (out_dx2, out_ux2, out_dy2, out_uy2)
    arrived_c, arrived_d = (in_vx, in_wx, in_vy, in_wy), (in_vx2, in_wx2, in_vy2, in_wy2)
    leaving_c, leaving_d = (out_vx, out_wx, out_vy, out_wy), (out_vx2, out_wx2, out_vy2, out_wy2)
    loaded("velocity")
    for which in range(3):
        arrange(raw_v, work_v, which)
        pack_velocity(work_v, which, leaving_c)
    loaded("fields")
    for which in range(2):
        arrange(raw_u, work_u, which)
        field_traces(which, work_u)
        pack_field(which, which, leaving_a)

    pl.semaphore_wait(barrier, 5)
    copies = []
    peers = (to_west, to_east, to_south, to_north)

    def send(source, target, peer):
        copy = pltpu.make_async_remote_copy(
            src_ref=source, dst_ref=target,
            send_sem=send_sem.at[len(copies)], recv_sem=recv_sem.at[len(copies)],
            device_id=peer, device_id_type=MESH,
        )
        copy.start()
        copies.append(copy)
        return copy

    def send_all(sources, targets):
        return [send(*triple) for triple in zip(sources, targets, peers)]

    first_m = [
        send(raw_m.at[:, 0, pl.ds(0, 16), :], in_mx, to_west),
        send(out_my, in_my, to_south),
        send(out_corner, in_corner, to_corner),
    ]
    first_v = send_all(leaving_c, arrived_c)
    first = send_all(leaving_a, arrived_a)

    loaded("tables")
    minus, plus, stiff_z, interp_z, pick_z, spread_z, volume_z, lift_z = (
        tables[:, 128 * column : 128 * (column + 1)] for column in range(8)
    )
    for column, table in enumerate((stiff_z, interp_z)):
        upper, lower = parted(table)
        at = 256 * column
        square[:128, at : at + 128] = upper
        square[128:, at : at + 128] = upper
        square[:128, at + 128 : at + 256] = lower
        square[128:, at + 128 : at + 256] = jnp.zeros((128, 128), BF16)
    for column, table in enumerate((minus, plus)):
        upper, lower = parted(table)
        at = 128 * column
        ends[:128, at : at + 128] = upper
        ends[128:256, at : at + 128] = upper
        ends[256:, at : at + 128] = lower
    picker[:128] = pick_z.astype(BF16)
    picker[128:] = pick_z.astype(BF16)
    for row, table in enumerate((volume_z, lift_z)):
        upper, lower = parted(table)
        tall[128 * row : 128 * (row + 1), :128] = upper
        tall[128 * row : 128 * (row + 1), 128:] = lower

    loaded("bounds")
    bound_rows[...] = jnp.zeros((4, 2, 8, 128), F32)
    for index in range(4):
        for zone in range(4):
            bound_rows[index, zone % 2, pl.ds(4 * (zone // 2), 4), pl.ds(0, 32)] = bound_in[
                index, zone
            ]
    values = bound_rows[...].reshape(64, 128)
    spreader = spread_z.astype(BF16)
    upper = values.astype(BF16)
    rest = values - upper.astype(F32)
    middle = rest.astype(BF16)
    lowest = (rest - middle.astype(F32)).astype(BF16)
    values = product(upper, spreader) + (product(middle, spreader) + product(lowest, spreader))
    bounds[...] = values.reshape(4, 2, 8, 128)

    def velocity_before(which, source, base):
        along_z = lanes_product(source[which].reshape(256, 128), 0).reshape(8, 4, 8, 128)
        own = stiff[4][4]
        opening = source[which, 0]
        inner = jnp.where(low_quad, spin(opening, 4, 1), 0.0)
        last_end = combine(stiff[4], [source[which, 4 + a] for a in range(4)] + [inner])
        carried = jnp.where(low_quad, own * opening, spin(last_end, 4, 1))
        for half in range(2):
            chunk = pl.ds(4 * half, 4)
            ahead = source[which, 4] if half == 0 else inner
            along_x = slopes_of(stiff, [source[which, 4 * half + a] for a in range(4)] + [ahead])
            along_x[0] = along_x[0] + carried
            carried = along_x[4]
            lines = [source[which, chunk, j] for j in range(4)]
            ahead = jnp.where(last_zone, 0.0, spin(lines[0], 7, 1))
            along_y = slopes_of(stiff, lines + [ahead])
            along_y[0] = along_y[0] + jnp.where(first_zone, own * lines[0], spin(along_y[4], 1, 1))
            along_y = turned(along_y[:4])
            for a in range(4):
                x = 4 * half + a
                acc_v[which, x] = base(x) + (
                    work_m[0, x] * along_x[a]
                    + work_m[1, x] * along_y[a]
                    + work_m[2, x] * along_z[x]
                )

    def velocity_after(which, put, arrived):
        from_east, from_west, from_north, from_south = arrived
        later = jnp.stack(unpack_x_high([from_east[which, 0], from_east[which, 1]]))
        earlier = jnp.stack(unpack_x_low([from_west[which, 0], from_west[which, 1]]))
        later = jnp.where(low_quad, 0.0, later)
        earlier = jnp.where(low_quad, earlier, 0.0)
        for half in range(2):
            above = jnp.where(last_zone, unpack_y(from_north[which, half], 3), 0.0)
            below = jnp.where(first_zone, unpack_y(from_south[which, half], 0), 0.0)
            extra_y = [stiff[j][4] * above for j in range(4)]
            extra_y[0] = extra_y[0] + below
            extra_y = turned(extra_y)
            for a in range(4):
                x = 4 * half + a
                value = acc_v[which, x] + work_m[1, x] * extra_y[a]
                if half == 1:
                    value = value + work_m[0, x] * (stiff[a][4] * later)
                elif a == 0:
                    value = value + work_m[0, x] * earlier
                put(x, value)

    def mesh_before(item):
        values = work_m[min(item, 2)].reshape(256, 128)
        values = lanes_product(values, 1) if item < 3 else picked(values)
        values = values.reshape(8, 4, 8, 128)
        inner = jnp.where(low_quad, spin(values[0], 4, 1), 0.0)
        for half in range(2):
            chunk = pl.ds(4 * half, 4)
            ahead = values[4] if half == 0 else inner
            across = points_of(points, [values[4 * half + a] for a in range(4)] + [ahead])
            across = turned(across)
            ahead = jnp.where(last_zone, 0.0, spin(across[0], 7, 1))
            for j, result in enumerate(points_of(points, across + [ahead])):
                speed[item, chunk, j] = result
            if item == 0:
                edge = values[4 * half]
                ahead = jnp.where(at_zone(plane, 3), 0.0, spin(edge[0], 7, 0))
                edge = points_of(points, [edge[j] for j in range(4)] + [ahead])
                face_x[half] = jnp.stack(edge)
            if item == 1:
                face_y[0, chunk] = across[0]
                face_y[1, chunk] = ahead

    def mesh_halo():
        values = jnp.concatenate(
            [in_mx[...].reshape(48, 128), in_my[...].reshape(48, 128), in_corner[...], zero], 0
        )
        both, extra = lanes_product(values, 1), picked(values)
        for item in range(4):
            which, source = min(item, 2), both if item < 3 else extra
            rows = source[16 * which : 16 * (which + 1)]
            halo_x[item, pl.ds(0, 16)] = rows
            halo_x[item, pl.ds(16, 16)] = rows
            halo_y[item] = source[48 + 16 * which : 64 + 16 * which].reshape(2, 8, 128)
            halo_corner[item] = spin(source[96:104], 7 - which, 0)

    def mesh_after(item):
        rows = rows_of(plane)
        later = [
            jnp.where(low_rows, 0.0, halo_x[item, pl.ds(j, 8, stride=4), :]) for j in range(4)
        ]
        far = jnp.where(at_zone(plane, 3), 0.0, spin(later[0], 7, 0))
        far = jnp.where(rows == 7, halo_corner[item], far)
        later.append(jnp.where(low_rows, 0.0, far))
        edge = jnp.stack(points_of(points, later))
        above = [
            jnp.where(last_zone, unpack_y(halo_y[item, half], 3), 0.0) for half in range(2)
        ]
        inner = jnp.where(low_rows, spin(above[0][0], 4, 0), 0.0)
        for half in range(2):
            ahead = above[1][0] if half == 0 else inner
            across = points_of(points, [above[half][a] for a in range(4)] + [ahead])
            for i in range(4):
                x = 4 * half + i
                extra = jnp.stack([points[j][4] * across[i] for j in range(4)])
                if half == 1:
                    extra = extra + points[i][4] * edge
                speed[item, x] += extra
                if item == 1:
                    upper = face_y[1, x] + across[i]
                    if half == 1:
                        upper = upper + points[i][4] * later[4]
                        face_y[0, x] += points[i][4] * later[0]
                    face_y[1, x] = upper
            if item == 0:
                face_x[half] += jnp.stack([points[j][4] * above[half][0] for j in range(4)])
        if item == 0:
            face_x[2] = jnp.where(low_quad, spin(face_x[0], 4, 1), edge)

    def upwind(face, minus_side, plus_side):
        return jnp.maximum(face, 0.0) * minus_side + jnp.minimum(face, 0.0) * plus_side

    def field_ends(which, source):
        upper, pair = sided(source[which].reshape(256, 128))
        sides = product(pair, ends[:256]) + product(upper, ends[256:])
        ends_z[which, 0] = sides[:, :128]
        ends_z[which, 1] = sides[:, 128:]

    def field_before(which, source, base):
        values = source[which].reshape(256, 128)
        flux = upwind(speed[3].reshape(256, 128), ends_z[which, 0], ends_z[which, 1])
        moved = speed[2].reshape(256, 128) * values
        upper, lower = parted(jnp.concatenate([moved, flux], 1))
        sums = product(upper, tall[...])
        along_z = sums[:, :128] + sums[:, 128:] + product(lower, tall[:, :128])
        along_z = along_z.reshape(8, 4, 8, 128)
        for half in range(2):
            chunk = pl.ds(4 * half, 4)
            places = [4 * half + i for i in range(4)]
            along_x = slopes_of(TABLE["volume"], [speed[0, x] * source[which, x] for x in places])
            along_y = slopes_of(
                TABLE["volume"],
                [speed[1, chunk, j] * source[which, chunk, j] for j in range(4)],
            )
            along_y = turned(along_y)
            for i, x in enumerate(places):
                acc_f[which, x] = base(x) + ((along_x[i] + along_y[i]) + along_z[x])

    def in_group(values, join):
        lane = lax.broadcasted_iota(jnp.int32, plane, 1)
        partner = jnp.where(lane % 2 == 0, spin(values, 127, 1), spin(values, 1, 1))
        values = join(values, partner)
        partner = jnp.where(lane // 2 % 2 == 0, spin(values, 126, 1), spin(values, 2, 1))
        return join(values, partner)

    def over_zone(values, join):
        total = functools.reduce(join, values)
        return functools.reduce(join, [total[j] for j in range(4)])

    def limited(which, half, values):
        weights = TABLE["weights"]
        mean = combine(weights, values)
        mean = combine(weights, [mean[j] for j in range(4)])
        lane = lax.broadcasted_iota(jnp.int32, plane, 1) % 4
        middle = (lane == 1) | (lane == 2)
        mean = in_group(mean * jnp.where(middle, weights[1], weights[0]), jnp.add)
        rise = in_group(over_zone(values, jnp.maximum), jnp.maximum) - mean
        fall = in_group(over_zone(values, jnp.minimum), jnp.minimum) - mean
        low, high = bounds[2 * which, half], bounds[2 * which + 1, half]
        theta = jnp.minimum(
            (high - mean) / (rise + limit_eps), (mean - low) / (limit_eps - fall)
        )
        theta = jnp.clip(theta, 0.0, 1.0)
        return [mean + theta * (value - mean) for value in values]

    def field_after(which, scale, put, arrived):
        from_east, from_west, from_north, from_south = arrived
        later = jnp.stack(unpack_x_high([from_east[which, 0], from_east[which, 1]]))
        earlier = jnp.stack(unpack_x_low([from_west[which, 0], from_west[which, 1]]))
        low, high = trace_x[which, 0], trace_x[which, 1]
        flux = [
            upwind(face_x[0], jnp.where(low_quad, earlier, spin(high[1], 4, 1)), low[0]),
            upwind(face_x[1], high[0], low[1]),
            upwind(face_x[2], high[1], jnp.where(low_quad, spin(low[0], 4, 1), later)),
        ]
        for half in range(2):
            chunk = pl.ds(4 * half, 4)
            low, high = trace_y[which, 0, chunk], trace_y[which, 1, chunk]
            before = jnp.where(first_zone, unpack_y(from_south[which, half], 0), spin(high, 1, 1))
            after = jnp.where(last_zone, unpack_y(from_north[which, half], 3), spin(low, 7, 1))
            lift_y = turned(
                lifts_of(
                    upwind(face_y[0, chunk], before, low), upwind(face_y[1, chunk], high, after)
                )
            )
            lift_x = lifts_of(flux[half], flux[half + 1])
            values = [
                acc_f[which, 4 * half + i] + (lift_x[i] + lift_y[i]) for i in range(4)
            ]
            if scale != 1.0:
                values = [scale * value for value in values]
            values = limited(which, half, values)
            for i in range(4):
                put(4 * half + i, values[i])

    for which in range(3):
        arrange(raw_m, work_m, which)
    for item in range(4):
        mesh_before(item)
    for which in range(2):
        field_ends(which, work_u)
    for which in range(3):
        velocity_before(which, work_v, lambda x: work_v[which, x])
    def keep_field(x, value):
        sec_f[which, x] = value

    def keep_velocity(x, value):
        sec_v[which, x] = value

    def finish_field(x, value):
        for j in range(4):
            results[which, x, pl.ds(j, 8, stride=4), :] = value[j]

    def finish_velocity(x, value):
        for j in range(4):
            results[2 + which, x, pl.ds(j, 8, stride=4), :] = 0.5 * value[j]

    for copy in first_m:
        copy.wait_recv()
    mesh_halo()
    for item in range(4):
        mesh_after(item)
    for copy in first_v:
        copy.wait_recv()
    for which in range(3):
        velocity_after(which, keep_velocity, arrived_c)
        pack_velocity(sec_v, which, leaving_d)
    second_v = send_all(leaving_d, arrived_d)
    for which in range(2):
        field_before(which, work_u, lambda x: work_u[which, x])
    for copy in first:
        copy.wait_recv()
    second = []
    for which in range(2):
        field_after(which, 1.0, keep_field, arrived_a)
        field_traces(which, sec_f)
        pack_field(which, which, leaving_b)
        second.append(
            send_all([ref.at[which] for ref in leaving_b], [ref.at[which] for ref in arrived_b])
        )

    for which in range(3):
        velocity_before(which, sec_v, lambda x: work_v[which, x] + sec_v[which, x])
    for which in range(2):
        field_ends(which, sec_f)
    for which in range(2):
        field_before(which, sec_f, lambda x: work_u[which, x] + sec_f[which, x])
    for copy in second_v:
        copy.wait_recv()
    for which in range(3):
        velocity_after(which, finish_velocity, arrived_d)
    for which in range(2):
        for copy in second[which]:
            copy.wait_recv()
        field_after(which, 0.5, finish_field, arrived_b)
    for copy in copies:
        copy.wait_send()


def unfold(results, new_density, new_energy, new_velocity, store_sem):
    copies = []
    for half in range(2):
        rows, block = pl.ds(16 * half, 16), pl.ds(8 * half, 8)
        for source, target in (
            (results.at[0, :, rows, :], new_density.at[block]),
            (results.at[1, :, rows, :], new_energy.at[block]),
            (results.at[pl.ds(2, 3), :, rows, :], new_velocity.at[:, block]),
        ):
            copy = pltpu.make_async_copy(source, target, store_sem.at[len(copies)])
            copy.start()
            copies.append(copy)
    for copy in copies:
        copy.wait()


def solution(mesh):
    counts = (mesh.shape["gx"], mesh.shape["gy"])
    matrices = lane_matrices(128)

    def on_device(*arguments):
        vmem = lambda *shape: pltpu.VMEM(shape, F32)
        scratch = [
            vmem(2, 8, 32, 128), vmem(3, 8, 32, 128), vmem(3, 8, 32, 128),
            vmem(*matrices.shape),
            pltpu.VMEM((256, 512), BF16), pltpu.VMEM((384, 256), BF16),
            pltpu.VMEM((256, 128), BF16), pltpu.VMEM((256, 256), BF16),
            vmem(4, 4, 4, 32), vmem(4, 2, 8, 128), vmem(4, 2, 8, 128),
            vmem(2, 8, 4, 8, 128), vmem(3, 8, 4, 8, 128), vmem(3, 8, 4, 8, 128),
            vmem(3, 8, 4, 8, 128), vmem(3, 8, 4, 8, 128),
            vmem(2, 8, 4, 8, 128), vmem(2, 8, 4, 8, 128),
            vmem(4, 8, 4, 8, 128), vmem(3, 4, 8, 128), vmem(2, 8, 8, 128),
            vmem(2, 2, 2, 4, 8, 128), vmem(2, 2, 8, 8, 128), vmem(2, 2, 256, 128),
            vmem(4, 32, 128), vmem(4, 2, 8, 128), vmem(4, 8, 128),
        ]
        scratch += [vmem(2, 2, 8, 128)] * 8
        scratch += [vmem(3, 2, 8, 128), vmem(3, 16, 128), vmem(3, 2, 8, 128)] + [vmem(8, 128)] * 2
        for items in (3, 2, 3):
            scratch += [vmem(items, 2, 8, 128)] * 8
        scratch += [
            pltpu.SemaphoreType.DMA((13,)),
            pltpu.SemaphoreType.DMA((23,)),
            pltpu.SemaphoreType.DMA((23,)),
        ]
        operands = [
            pltpu.with_memory_space_constraint(value, pltpu.HBM)
            for value in (*arguments, jnp.asarray(matrices))
        ]
        results = pl.pallas_call(
            functools.partial(kernel, counts),
            out_shape=pltpu.VMEM((5, 8, 32, 128), F32),
            in_specs=[pl.BlockSpec(memory_space=pltpu.HBM)] * 9,
            out_specs=pl.BlockSpec(memory_space=pltpu.VMEM),
            scratch_shapes=scratch,
            compiler_params=pltpu.CompilerParams(
                collective_id=0, has_side_effects=True, vmem_limit_bytes=32 * 1024 * 1024
            ),
        )(*operands)
        return pl.pallas_call(
            unfold,
            out_shape=[jax.ShapeDtypeStruct(value.shape, F32) for value in arguments[:3]],
            in_specs=[pl.BlockSpec(memory_space=pltpu.VMEM)],
            out_specs=[pl.BlockSpec(memory_space=pltpu.HBM)] * 3,
            scratch_shapes=[pltpu.SemaphoreType.DMA((6,))],
            compiler_params=pltpu.CompilerParams(vmem_limit_bytes=32 * 1024 * 1024),
        )(results)

    fields, vectors = P("gx", "gy", None), P(None, "gx", "gy", None)
    return jax.shard_map(
        on_device,
        mesh=mesh,
        in_specs=(fields, fields, vectors, vectors, fields, fields, fields, fields),
        out_specs=(fields, fields, vectors),
        check_vma=False,
    )
```

```python
import functools
import math

import jax
import jax.numpy as jnp
import numpy as np
from jax import lax
from jax.experimental import pallas as pl
from jax.experimental.pallas import tpu as pltpu
from jax.sharding import PartitionSpec as P

MESH = pl.DeviceIdType.MESH
F32 = jnp.float32
BF16 = jnp.bfloat16
time_step = 0.02
limit_eps = 1e-06


def lagrange_values(node_set, points):
    result = np.ones((len(points), len(node_set)))
    for column in range(len(node_set)):
        for partner in range(len(node_set)):
            if partner != column:
                result[:, column] = (
                    result[:, column]
                    * (points - node_set[partner])
                    / (node_set[column] - node_set[partner])
                )
    return result


def lagrange_slopes(node_set, points):
    node_total = len(node_set)
    result = np.zeros((len(points), node_total))
    for column in range(node_total):
        for skipped in range(node_total):
            if skipped != column:
                factor = np.ones(len(points)) / (node_set[column] - node_set[skipped])
                for partner in range(node_total):
                    if partner != column and partner != skipped:
                        factor = (
                            factor
                            * (points - node_set[partner])
                            / (node_set[column] - node_set[partner])
                        )
                result[:, column] = result[:, column] + factor
    return result


def basis_tables():
    gauss_points = np.array(
        [-0.8611363115940526, -0.3399810435848563, 0.3399810435848563, 0.8611363115940526]
    )
    gauss_weights = np.array(
        [0.3478548451374538, 0.6521451548625461, 0.6521451548625461, 0.3478548451374538]
    )
    lobatto_points = np.array([-1.0, -math.sqrt(3.0 / 7.0), 0.0, math.sqrt(3.0 / 7.0), 1.0])
    lobatto_weights = np.array([0.1, 49.0 / 90.0, 32.0 / 45.0, 49.0 / 90.0, 0.1])
    slopes = lagrange_slopes(gauss_points, gauss_points)
    volume = (2.0 / gauss_weights)[:, None] * slopes.T * gauss_weights[None, :]
    trace_low = lagrange_values(gauss_points, np.array([-1.0]))[0]
    trace_high = lagrange_values(gauss_points, np.array([1.0]))[0]
    stiffness = (
        2.0 * lobatto_weights[:, None] * lagrange_slopes(lobatto_points, lobatto_points)
    )
    lumped = np.array([0.2, lobatto_weights[1], lobatto_weights[2], lobatto_weights[3], 0.2])
    return {
        "weights": gauss_weights / 2.0,
        "volume": time_step * volume,
        "trace_low": trace_low,
        "trace_high": trace_high,
        "lift_low": time_step * 2.0 * trace_low / gauss_weights,
        "lift_high": time_step * 2.0 * trace_high / gauss_weights,
        "to_points": lagrange_values(lobatto_points, gauss_points),
        "stiffness": -time_step * stiffness / lumped[:, None],
    }


TABLES = basis_tables()
TABLE = {name: TABLES[name].tolist() for name in TABLES}


def lane_matrices(lanes):
    zones = lanes // 4
    shape = (lanes, lanes)
    volume, lift = np.zeros(shape), np.zeros(shape)
    minus, plus = np.zeros(shape), np.zeros(shape)
    stiff, interp = np.zeros(shape), np.zeros(shape)
    pick, spread = np.zeros(shape), np.zeros(shape)
    for zone in range(zones):
        at = 4 * zone
        before = 4 * ((zone - 1) % zones)
        for within in range(4):
            for source in range(4):
                volume[at + source, at + within] = TABLES["volume"][within, source]
                minus[before + source, at + within] = TABLES["trace_high"][source]
                plus[at + source, at + within] = TABLES["trace_low"][source]
            lift[at, at + within] = TABLES["lift_low"][within]
            lift[at, before + within] = -TABLES["lift_high"][within]
            pick[at, at + within] = 1.0
            spread[zone, at + within] = 1.0
            for source in range(5):
                interp[(at + source) % lanes, at + within] += TABLES["to_points"][within, source]
        for target in range(5):
            for source in range(5):
                stiff[(at + source) % lanes, (at + target) % lanes] += TABLES["stiffness"][
                    target, source
                ]
    matrices = [minus, plus, stiff, interp, pick, spread, volume, lift]
    return np.concatenate(matrices, axis=1).astype(np.float32)


def spin(values, steps, axis):
    size = values.shape[axis]
    steps = steps % size
    return values if steps == 0 else pltpu.roll(values, steps, axis)


def rows_of(shape):
    return lax.broadcasted_iota(jnp.int32, shape, len(shape) - 2)


def low_half(shape):
    return rows_of(shape) < 4


def at_zone(shape, zone):
    return rows_of(shape) % 4 == zone


def combine(coefficients, terms):
    total = None
    for factor, term in zip(coefficients, terms):
        part = factor * term
        total = part if total is None else total + part
    return total


def parted(values):
    upper = values.astype(BF16)
    return upper, (values - upper.astype(F32)).astype(BF16)


def product(left, right):
    return jnp.dot(left, right, preferred_element_type=F32)


def mirrored(matrix):
    size = len(matrix[0])
    middle = size // 2
    even = [[(row[c] + row[size - 1 - c]) / 2 for c in range(middle)] for row in matrix]
    odd = [[(row[c] - row[size - 1 - c]) / 2 for c in range(middle)] for row in matrix]
    centre = [row[middle] for row in matrix] if size % 2 else None
    return even, odd, centre


def pairs_of(values):
    size = len(values)
    sums = [values[c] + values[size - 1 - c] for c in range(size // 2)]
    gaps = [values[c] - values[size - 1 - c] for c in range(size // 2)]
    return sums, gaps


def slopes_of(matrix, values):
    even, odd, centre = mirrored(matrix)
    sums, gaps = pairs_of(values)
    size = len(matrix)
    result = [None] * size
    for a in range(size // 2):
        factors, terms = list(even[a]), list(sums)
        if centre is not None:
            factors.append(centre[a])
            terms.append(values[size // 2])
        outer, inner = combine(factors, terms), combine(odd[a], gaps)
        result[a], result[size - 1 - a] = inner + outer, inner - outer
    if size % 2:
        result[size // 2] = combine(odd[size // 2], gaps)
    return result


def points_of(matrix, values):
    even, odd, centre = mirrored(matrix)
    sums, gaps = pairs_of(values)
    result = [None] * 4
    for i in range(2):
        outer = combine(even[i] + [centre[i]], sums + [values[2]])
        inner = combine(odd[i], gaps)
        result[i], result[3 - i] = outer + inner, outer - inner
    return result


def traces_of(values):
    sums, gaps = pairs_of(values)
    even, odd, _ = mirrored([TABLE["trace_low"]])
    outer, inner = combine(even[0], sums), combine(odd[0], gaps)
    return outer + inner, outer - inner


def lifts_of(lower, upper):
    even, odd, _ = mirrored([TABLE["lift_low"]])
    gap, both = lower - upper, lower + upper
    result = [None] * 4
    for i in range(2):
        outer, inner = even[0][i] * gap, odd[0][i] * both
        result[i], result[3 - i] = outer + inner, outer - inner
    return result


def turned(pieces):
    return [jnp.stack([pieces[j][i] for j in range(4)]) for i in range(4)]


def pack_x_low(planes):
    mask = low_half((8, 128))
    return [jnp.where(mask, planes[t], spin(planes[t + 1], 4, 0)) for t in (0, 2)]


def pack_x_high(planes):
    mask = low_half((8, 128))
    return [jnp.where(mask, spin(planes[t], 4, 0), planes[t + 1]) for t in (0, 2)]


def unpack_x_high(packed):
    return [spin(packed[0], 4, 0), packed[0], spin(packed[1], 4, 0), packed[1]]


def unpack_x_low(packed):
    return [packed[0], spin(packed[0], 4, 0), packed[1], spin(packed[1], 4, 0)]


def pack_y(values, start):
    shape = (8, 128)
    packed = []
    for half in range(2):
        total = spin(values[4 * half + 3], 3 - start, 0)
        for place in (2, 1, 0):
            moved = spin(values[4 * half + place], place - start, 0)
            total = jnp.where(at_zone(shape, place), moved, total)
        packed.append(total)
    return packed


def unpack_y(packed, end):
    return jnp.stack([spin(packed, end - place, 0) for place in range(4)])


def kernel(
    counts,
    density, energy, velocity, mesh_velocity, density_low, density_high, energy_low, energy_high,
    tables_hbm,
    results,
    raw_u, raw_v, raw_m, tables, square, ends, picker, tall, bound_in, bound_rows,
    bounds, work_u, work_v, work_m,
    acc_v, sec_v, acc_f, sec_f, speed, face_x, face_y, trace_x, trace_y, ends_z,
    halo_x, halo_y, halo_corner,
    out_dx, out_ux, out_dy, out_uy, in_dx, in_ux, in_dy, in_uy,
    out_my, in_mx, in_my, out_corner, in_corner,
    out_vx, out_wx, out_vy, out_wy, in_vx, in_wx, in_vy, in_wy,
    out_dx2, out_ux2, out_dy2, out_uy2, in_dx2, in_ux2, in_dy2, in_uy2,
    out_vx2, out_wx2, out_vy2, out_wy2, in_vx2, in_wx2, in_vy2, in_wy2,
    load_sem, send_sem, recv_sem,
):
    count_x, count_y = counts
    here_x, here_y = lax.axis_index("gx"), lax.axis_index("gy")
    west = lax.rem(here_x + count_x - 1, count_x)
    east = lax.rem(here_x + 1, count_x)
    south = lax.rem(here_y + count_y - 1, count_y)
    north = lax.rem(here_y + 1, count_y)
    to_west, to_east = (west, here_y), (east, here_y)
    to_south, to_north = (here_x, south), (here_x, north)
    to_corner, from_corner = (west, south), (east, north)

    barrier = pltpu.get_barrier_semaphore()
    for peer in (to_west, to_east, from_corner, to_south, to_north):
        pl.semaphore_signal(barrier, inc=1, device_id=peer, device_id_type=MESH)

    loads = {}

    def load(name, source, target):
        copy = pltpu.make_async_copy(source, target, load_sem.at[sum(map(len, loads.values()))])
        copy.start()
        loads.setdefault(name, []).append(copy)

    def loaded(name):
        for copy in loads[name]:
            copy.wait()

    places = [(pl.ds(16 * half, 16), pl.ds(8 * half, 8)) for half in range(2)]
    for rows, block in places:
        load("mesh", mesh_velocity.at[:, block], raw_m.at[:, :, rows, :])
    for rows, block in places:
        load("velocity", velocity.at[:, block], raw_v.at[:, :, rows, :])
    for rows, block in places:
        load("fields", density.at[block], raw_u.at[0, :, rows, :])
        load("fields", energy.at[block], raw_u.at[1, :, rows, :])
    load("tables", tables_hbm, tables)
    for index, source in enumerate((density_low, density_high, energy_low, energy_high)):
        load("bounds", source, bound_in.at[index])

    quad, plane = (4, 8, 128), (8, 128)
    low_rows, low_quad = low_half(plane), low_half(quad)
    first_zone, last_zone = at_zone(quad, 0), at_zone(quad, 3)
    stiff, points = TABLE["stiffness"], TABLE["to_points"]
    zero = jnp.zeros(plane, F32)

    def arrange(source, target, which):
        for j in range(4):
            target[which, :, j] = source[which, :, pl.ds(j, 8, stride=4), :]

    def put_pair(target, item, pair):
        target[item, 0] = pair[0]
        target[item, 1] = pair[1]

    def sided(values):
        upper, lower = parted(values)
        return upper, jnp.concatenate([upper, lower], 1)

    def lanes_product(values, column):
        _, pair = sided(values)
        both = product(pair, square[:, 256 * column : 256 * (column + 1)])
        return both[:, :128] + both[:, 128:]

    def picked(values):
        return product(sided(values)[1], picker[...])

    def field_traces(which, source):
        for half in range(2):
            chunk = pl.ds(4 * half, 4)
            low, high = traces_of([source[which, 4 * half + i] for i in range(4)])
            trace_x[which, 0, half], trace_x[which, 1, half] = low, high
            low, high = traces_of([source[which, chunk, j] for j in range(4)])
            trace_y[which, 0, chunk], trace_y[which, 1, chunk] = low, high

    def pack_field(which, item, buffers):
        west_to, east_to, south_to, north_to = buffers
        put_pair(west_to, item, pack_x_low(trace_x[which, 0, 0]))
        put_pair(east_to, item, pack_x_high(trace_x[which, 1, 1]))
        put_pair(south_to, item, pack_y(trace_y[which, 0], 0))
        put_pair(north_to, item, pack_y(trace_y[which, 1], 3))

    def pack_velocity(source, item, buffers):
        west_to, east_to, south_to, north_to = buffers
        put_pair(west_to, item, pack_x_low(source[item, 0]))
        closing = combine(stiff[4][:4], [source[item, 4 + a] for a in range(4)])
        put_pair(east_to, item, pack_x_high(closing))
        put_pair(south_to, item, pack_y(source[item, :, 0], 0))
        closing = combine(stiff[4][:4], [source[item, :, j] for j in range(4)])
        put_pair(north_to, item, pack_y(closing, 3))

    loaded("mesh")
    corner = zero
    for which in range(3):
        values = raw_m[which, :, pl.ds(0, 8, stride=4), :]
        put_pair(out_my, which, pack_y(values, 0))
        corner = jnp.where(rows_of(plane) == which, spin(values[0], which, 0), corner)
    out_corner[...] = corner

    arrived_a, arrived_b = (in_dx, in_ux, in_dy, in_uy), (in_dx2, in_ux2, in_dy2, in_uy2)
    leaving_a, leaving_b = (out_dx, out_ux, out_dy, out_uy), (out_dx2, out_ux2, out_dy2, out_uy2)
    arrived_c, arrived_d = (in_vx, in_wx, in_vy, in_wy), (in_vx2, in_wx2, in_vy2, in_wy2)
    leaving_c, leaving_d = (out_vx, out_wx, out_vy, out_wy), (out_vx2, out_wx2, out_vy2, out_wy2)
    loaded("velocity")
    for which in range(3):
        arrange(raw_v, work_v, which)
        pack_velocity(work_v, which, leaving_c)
    loaded("fields")
    for which in range(2):
        arrange(raw_u, work_u, which)
        field_traces(which, work_u)
        pack_field(which, which, leaving_a)

    pl.semaphore_wait(barrier, 5)
    copies = []
    peers = (to_west, to_east, to_south, to_north)

    def send(source, target, peer):
        copy = pltpu.make_async_remote_copy(
            src_ref=source, dst_ref=target,
            send_sem=send_sem.at[len(copies)], recv_sem=recv_sem.at[len(copies)],
            device_id=peer, device_id_type=MESH,
        )
        copy.start()
        copies.append(copy)
        return copy

    def send_all(sources, targets):
        return [send(*triple) for triple in zip(sources, targets, peers)]

    first_m = [
        send(raw_m.at[:, 0, pl.ds(0, 16), :], in_mx, to_west),
        send(out_my, in_my, to_south),
        send(out_corner, in_corner, to_corner),
    ]
    first_v = send_all(leaving_c, arrived_c)
    first = send_all(leaving_a, arrived_a)

    loaded("tables")
    minus, plus, stiff_z, interp_z, pick_z, spread_z, volume_z, lift_z = (
        tables[:, 128 * column : 128 * (column + 1)] for column in range(8)
    )
    for column, table in enumerate((stiff_z, interp_z)):
        upper, lower = parted(table)
        at = 256 * column
        square[:128, at : at + 128] = upper
        square[128:, at : at + 128] = upper
        square[:128, at + 128 : at + 256] = lower
        square[128:, at + 128 : at + 256] = jnp.zeros((128, 128), BF16)
    for column, table in enumerate((minus, plus)):
        upper, lower = parted(table)
        at = 128 * column
        ends[:128, at : at + 128] = upper
        ends[128:256, at : at + 128] = upper
        ends[256:, at : at + 128] = lower
    picker[:128] = pick_z.astype(BF16)
    picker[128:] = pick_z.astype(BF16)
    for row, table in enumerate((volume_z, lift_z)):
        upper, lower = parted(table)
        tall[128 * row : 128 * (row + 1), :128] = upper
        tall[128 * row : 128 * (row + 1), 128:] = lower

    loaded("bounds")
    bound_rows[...] = jnp.zeros((4, 2, 8, 128), F32)
    for index in range(4):
        for zone in range(4):
            bound_rows[index, zone % 2, pl.ds(4 * (zone // 2), 4), pl.ds(0, 32)] = bound_in[
                index, zone
            ]
    values = bound_rows[...].reshape(64, 128)
    spreader = spread_z.astype(BF16)
    upper = values.astype(BF16)
    rest = values - upper.astype(F32)
    middle = rest.astype(BF16)
    lowest = (rest - middle.astype(F32)).astype(BF16)
    values = product(upper, spreader) + (product(middle, spreader) + product(lowest, spreader))
    bounds[...] = values.reshape(4, 2, 8, 128)

    def velocity_before(which, source, base):
        along_z = lanes_product(source[which].reshape(256, 128), 0).reshape(8, 4, 8, 128)
        own = stiff[4][4]
        opening = source[which, 0]
        inner = jnp.where(low_quad, spin(opening, 4, 1), 0.0)
        last_end = combine(stiff[4], [source[which, 4 + a] for a in range(4)] + [inner])
        carried = jnp.where(low_quad, own * opening, spin(last_end, 4, 1))
        for half in range(2):
            chunk = pl.ds(4 * half, 4)
            ahead = source[which, 4] if half == 0 else inner
            along_x = slopes_of(stiff, [source[which, 4 * half + a] for a in range(4)] + [ahead])
            along_x[0] = along_x[0] + carried
            carried = along_x[4]
            lines = [source[which, chunk, j] for j in range(4)]
            ahead = jnp.where(last_zone, 0.0, spin(lines[0], 7, 1))
            along_y = slopes_of(stiff, lines + [ahead])
            along_y[0] = along_y[0] + jnp.where(first_zone, own * lines[0], spin(along_y[4], 1, 1))
            along_y = turned(along_y[:4])
            for a in range(4):
                x = 4 * half + a
                acc_v[which, x] = base(x) + (
                    work_m[0, x] * along_x[a]
                    + work_m[1, x] * along_y[a]
                    + work_m[2, x] * along_z[x]
                )

    def velocity_after(which, put, arrived):
        from_east, from_west, from_north, from_south = arrived
        later = jnp.stack(unpack_x_high([from_east[which, 0], from_east[which, 1]]))
        earlier = jnp.stack(unpack_x_low([from_west[which, 0], from_west[which, 1]]))
        later = jnp.where(low_quad, 0.0, later)
        earlier = jnp.where(low_quad, earlier, 0.0)
        for half in range(2):
            above = jnp.where(last_zone, unpack_y(from_north[which, half], 3), 0.0)
            below = jnp.where(first_zone, unpack_y(from_south[which, half], 0), 0.0)
            extra_y = [stiff[j][4] * above for j in range(4)]
            extra_y[0] = extra_y[0] + below
            extra_y = turned(extra_y)
            for a in range(4):
                x = 4 * half + a
                value = acc_v[which, x] + work_m[1, x] * extra_y[a]
                if half == 1:
                    value = value + work_m[0, x] * (stiff[a][4] * later)
                elif a == 0:
                    value = value + work_m[0, x] * earlier
                put(x, value)

    def mesh_before(item):
        values = work_m[min(item, 2)].reshape(256, 128)
        values = lanes_product(values, 1) if item < 3 else picked(values)
        values = values.reshape(8, 4, 8, 128)
        inner = jnp.where(low_quad, spin(values[0], 4, 1), 0.0)
        for half in range(2):
            chunk = pl.ds(4 * half, 4)
            ahead = values[4] if half == 0 else inner
            across = points_of(points, [values[4 * half + a] for a in range(4)] + [ahead])
            across = turned(across)
            ahead = jnp.where(last_zone, 0.0, spin(across[0], 7, 1))
            for j, result in enumerate(points_of(points, across + [ahead])):
                speed[item, chunk, j] = result
            if item == 0:
                edge = values[4 * half]
                ahead = jnp.where(at_zone(plane, 3), 0.0, spin(edge[0], 7, 0))
                edge = points_of(points, [edge[j] for j in range(4)] + [ahead])
                face_x[half] = jnp.stack(edge)
            if item == 1:
                face_y[0, chunk] = across[0]
                face_y[1, chunk] = ahead

    def mesh_halo():
        values = jnp.concatenate(
            [in_mx[...].reshape(48, 128), in_my[...].reshape(48, 128), in_corner[...], zero], 0
        )
        both, extra = lanes_product(values, 1), picked(values)
        for item in range(4):
            which, source = min(item, 2), both if item < 3 else extra
            rows = source[16 * which : 16 * (which + 1)]
            halo_x[item, pl.ds(0, 16)] = rows
            halo_x[item, pl.ds(16, 16)] = rows
            halo_y[item] = source[48 + 16 * which : 64 + 16 * which].reshape(2, 8, 128)
            halo_corner[item] = spin(source[96:104], 7 - which, 0)

    def mesh_after(item):
        rows = rows_of(plane)
        later = [
            jnp.where(low_rows, 0.0, halo_x[item, pl.ds(j, 8, stride=4), :]) for j in range(4)
        ]
        far = jnp.where(at_zone(plane, 3), 0.0, spin(later[0], 7, 0))
        far = jnp.where(rows == 7, halo_corner[item], far)
        later.append(jnp.where(low_rows, 0.0, far))
        edge = jnp.stack(points_of(points, later))
        above = [
            jnp.where(last_zone, unpack_y(halo_y[item, half], 3), 0.0) for half in range(2)
        ]
        inner = jnp.where(low_rows, spin(above[0][0], 4, 0), 0.0)
        for half in range(2):
            ahead = above[1][0] if half == 0 else inner
            across = points_of(points, [above[half][a] for a in range(4)] + [ahead])
            for i in range(4):
                x = 4 * half + i
                extra = jnp.stack([points[j][4] * across[i] for j in range(4)])
                if half == 1:
                    extra = extra + points[i][4] * edge
                speed[item, x] += extra
                if item == 1:
                    upper = face_y[1, x] + across[i]
                    if half == 1:
                        upper = upper + points[i][4] * later[4]
                        face_y[0, x] += points[i][4] * later[0]
                    face_y[1, x] = upper
            if item == 0:
                face_x[half] += jnp.stack([points[j][4] * above[half][0] for j in range(4)])
        if item == 0:
            face_x[2] = jnp.where(low_quad, spin(face_x[0], 4, 1), edge)

    def upwind(face, minus_side, plus_side):
        return jnp.maximum(face, 0.0) * minus_side + jnp.minimum(face, 0.0) * plus_side

    def field_ends(which, source):
        upper, pair = sided(source[which].reshape(256, 128))
        sides = product(pair, ends[:256]) + product(upper, ends[256:])
        ends_z[which, 0] = sides[:, :128]
        ends_z[which, 1] = sides[:, 128:]

    def field_before(which, source, base):
        values = source[which].reshape(256, 128)
        flux = upwind(speed[3].reshape(256, 128), ends_z[which, 0], ends_z[which, 1])
        moved = speed[2].reshape(256, 128) * values
        upper, lower = parted(jnp.concatenate([moved, flux], 1))
        sums = product(upper, tall[...])
        along_z = sums[:, :128] + sums[:, 128:] + product(lower, tall[:, :128])
        along_z = along_z.reshape(8, 4, 8, 128)
        for half in range(2):
            chunk = pl.ds(4 * half, 4)
            places = [4 * half + i for i in range(4)]
            along_x = slopes_of(TABLE["volume"], [speed[0, x] * source[which, x] for x in places])
            along_y = slopes_of(
                TABLE["volume"],
                [speed[1, chunk, j] * source[which, chunk, j] for j in range(4)],
            )
            along_y = turned(along_y)
            for i, x in enumerate(places):
                acc_f[which, x] = base(x) + ((along_x[i] + along_y[i]) + along_z[x])

    def in_group(values, join):
        lane = lax.broadcasted_iota(jnp.int32, plane, 1)
        partner = jnp.where(lane % 2 == 0, spin(values, 127, 1), spin(values, 1, 1))
        values = join(values, partner)
        partner = jnp.where(lane // 2 % 2 == 0, spin(values, 126, 1), spin(values, 2, 1))
        return join(values, partner)

    def over_zone(values, join):
        total = functools.reduce(join, values)
        return functools.reduce(join, [total[j] for j in range(4)])

    def limited(which, half, values):
        weights = TABLE["weights"]
        mean = combine(weights, values)
        mean = combine(weights, [mean[j] for j in range(4)])
        lane = lax.broadcasted_iota(jnp.int32, plane, 1) % 4
        middle = (lane == 1) | (lane == 2)
        mean = in_group(mean * jnp.where(middle, weights[1], weights[0]), jnp.add)
        rise = in_group(over_zone(values, jnp.maximum), jnp.maximum) - mean
        fall = in_group(over_zone(values, jnp.minimum), jnp.minimum) - mean
        low, high = bounds[2 * which, half], bounds[2 * which + 1, half]
        theta = jnp.minimum(
            (high - mean) / (rise + limit_eps), (mean - low) / (limit_eps - fall)
        )
        theta = jnp.clip(theta, 0.0, 1.0)
        return [mean + theta * (value - mean) for value in values]

    def field_after(which, scale, put, arrived):
        from_east, from_west, from_north, from_south = arrived
        later = jnp.stack(unpack_x_high([from_east[which, 0], from_east[which, 1]]))
        earlier = jnp.stack(unpack_x_low([from_west[which, 0], from_west[which, 1]]))
        low, high = trace_x[which, 0], trace_x[which, 1]
        flux = [
            upwind(face_x[0], jnp.where(low_quad, earlier, spin(high[1], 4, 1)), low[0]),
            upwind(face_x[1], high[0], low[1]),
            upwind(face_x[2], high[1], jnp.where(low_quad, spin(low[0], 4, 1), later)),
        ]
        for half in range(2):
            chunk = pl.ds(4 * half, 4)
            low, high = trace_y[which, 0, chunk], trace_y[which, 1, chunk]
            before = jnp.where(first_zone, unpack_y(from_south[which, half], 0), spin(high, 1, 1))
            after = jnp.where(last_zone, unpack_y(from_north[which, half], 3), spin(low, 7, 1))
            lift_y = turned(
                lifts_of(
                    upwind(face_y[0, chunk], before, low), upwind(face_y[1, chunk], high, after)
                )
            )
            lift_x = lifts_of(flux[half], flux[half + 1])
            values = [
                acc_f[which, 4 * half + i] + (lift_x[i] + lift_y[i]) for i in range(4)
            ]
            if scale != 1.0:
                values = [scale * value for value in values]
            values = limited(which, half, values)
            for i in range(4):
                put(4 * half + i, values[i])

    for which in range(3):
        arrange(raw_m, work_m, which)
    for item in range(4):
        mesh_before(item)
    for which in range(2):
        field_ends(which, work_u)
    for which in range(3):
        velocity_before(which, work_v, lambda x: work_v[which, x])
    def keep_field(x, value):
        sec_f[which, x] = value

    def keep_velocity(x, value):
        sec_v[which, x] = value

    def finish_field(x, value):
        for j in range(4):
            results[which, x, pl.ds(j, 8, stride=4), :] = value[j]

    def finish_velocity(x, value):
        for j in range(4):
            results[2 + which, x, pl.ds(j, 8, stride=4), :] = 0.5 * value[j]

    for copy in first_m:
        copy.wait_recv()
    mesh_halo()
    for item in range(4):
        mesh_after(item)
    for copy in first_v:
        copy.wait_recv()
    for which in range(3):
        velocity_after(which, keep_velocity, arrived_c)
        pack_velocity(sec_v, which, leaving_d)
    second_v = send_all(leaving_d, arrived_d)
    for which in range(2):
        field_before(which, work_u, lambda x: work_u[which, x])
    for copy in first:
        copy.wait_recv()
    second = []
    for which in range(2):
        field_after(which, 1.0, keep_field, arrived_a)
        field_traces(which, sec_f)
        pack_field(which, which, leaving_b)
        second.append(
            send_all([ref.at[which] for ref in leaving_b], [ref.at[which] for ref in arrived_b])
        )

    for which in range(3):
        velocity_before(which, sec_v, lambda x: work_v[which, x] + sec_v[which, x])
    for which in range(2):
        field_ends(which, sec_f)
    for which in range(2):
        field_before(which, sec_f, lambda x: work_u[which, x] + sec_f[which, x])
    for copy in copies:
        copy.wait_send()
    for copy in second_v:
        copy.wait_recv()
    for which in range(3):
        velocity_after(which, finish_velocity, arrived_d)
    for which in range(2):
        for copy in second[which]:
            copy.wait_recv()
        field_after(which, 0.5, finish_field, arrived_b)


def unfold(results, new_density, new_energy, new_velocity, store_sem):
    copies = []
    for half in range(2):
        rows, block = pl.ds(16 * half, 16), pl.ds(8 * half, 8)
        for source, target in (
            (results.at[pl.ds(2, 3), :, rows, :], new_velocity.at[:, block]),
            (results.at[0, :, rows, :], new_density.at[block]),
            (results.at[1, :, rows, :], new_energy.at[block]),
        ):
            copy = pltpu.make_async_copy(source, target, store_sem.at[len(copies)])
            copy.start()
            copies.append(copy)
    for copy in copies:
        copy.wait()


def solution(mesh):
    counts = (mesh.shape["gx"], mesh.shape["gy"])
    matrices = lane_matrices(128)

    def on_device(*arguments):
        vmem = lambda *shape: pltpu.VMEM(shape, F32)
        scratch = [
            vmem(2, 8, 32, 128), vmem(3, 8, 32, 128), vmem(3, 8, 32, 128),
            vmem(*matrices.shape),
            pltpu.VMEM((256, 512), BF16), pltpu.VMEM((384, 256), BF16),
            pltpu.VMEM((256, 128), BF16), pltpu.VMEM((256, 256), BF16),
            vmem(4, 4, 4, 32), vmem(4, 2, 8, 128), vmem(4, 2, 8, 128),
            vmem(2, 8, 4, 8, 128), vmem(3, 8, 4, 8, 128), vmem(3, 8, 4, 8, 128),
            vmem(3, 8, 4, 8, 128), vmem(3, 8, 4, 8, 128),
            vmem(2, 8, 4, 8, 128), vmem(2, 8, 4, 8, 128),
            vmem(4, 8, 4, 8, 128), vmem(3, 4, 8, 128), vmem(2, 8, 8, 128),
            vmem(2, 2, 2, 4, 8, 128), vmem(2, 2, 8, 8, 128), vmem(2, 2, 256, 128),
            vmem(4, 32, 128), vmem(4, 2, 8, 128), vmem(4, 8, 128),
        ]
        scratch += [vmem(2, 2, 8, 128)] * 8
        scratch += [vmem(3, 2, 8, 128), vmem(3, 16, 128), vmem(3, 2, 8, 128)] + [vmem(8, 128)] * 2
        for items in (3, 2, 3):
            scratch += [vmem(items, 2, 8, 128)] * 8
        scratch += [
            pltpu.SemaphoreType.DMA((13,)),
            pltpu.SemaphoreType.DMA((23,)),
            pltpu.SemaphoreType.DMA((23,)),
        ]
        operands = [
            pltpu.with_memory_space_constraint(value, pltpu.HBM)
            for value in (*arguments, jnp.asarray(matrices))
        ]
        results = pl.pallas_call(
            functools.partial(kernel, counts),
            out_shape=pltpu.VMEM((5, 8, 32, 128), F32),
            in_specs=[pl.BlockSpec(memory_space=pltpu.HBM)] * 9,
            out_specs=pl.BlockSpec(memory_space=pltpu.VMEM),
            scratch_shapes=scratch,
            compiler_params=pltpu.CompilerParams(
                collective_id=0, has_side_effects=True, vmem_limit_bytes=32 * 1024 * 1024
            ),
        )(*operands)
        return pl.pallas_call(
            unfold,
            out_shape=[jax.ShapeDtypeStruct(value.shape, F32) for value in arguments[:3]],
            in_specs=[pl.BlockSpec(memory_space=pltpu.VMEM)],
            out_specs=[pl.BlockSpec(memory_space=pltpu.HBM)] * 3,
            scratch_shapes=[pltpu.SemaphoreType.DMA((6,))],
            compiler_params=pltpu.CompilerParams(vmem_limit_bytes=32 * 1024 * 1024),
        )(results)

    fields, vectors = P("gx", "gy", None), P(None, "gx", "gy", None)
    return jax.shard_map(
        on_device,
        mesh=mesh,
        in_specs=(fields, fields, vectors, vectors, fields, fields, fields, fields),
        out_specs=(fields, fields, vectors),
        check_vma=False,
    )
```

```python
import functools
import math

import jax
import jax.numpy as jnp
import numpy as np
from jax import lax
from jax.experimental import pallas as pl
from jax.experimental.pallas import tpu as pltpu
from jax.sharding import PartitionSpec as P

MESH = pl.DeviceIdType.MESH
F32 = jnp.float32
BF16 = jnp.bfloat16
time_step = 0.02
limit_eps = 1e-06


def lagrange_values(node_set, points):
    result = np.ones((len(points), len(node_set)))
    for column in range(len(node_set)):
        for partner in range(len(node_set)):
            if partner != column:
                result[:, column] = (
                    result[:, column]
                    * (points - node_set[partner])
                    / (node_set[column] - node_set[partner])
                )
    return result


def lagrange_slopes(node_set, points):
    node_total = len(node_set)
    result = np.zeros((len(points), node_total))
    for column in range(node_total):
        for skipped in range(node_total):
            if skipped != column:
                factor = np.ones(len(points)) / (node_set[column] - node_set[skipped])
                for partner in range(node_total):
                    if partner != column and partner != skipped:
                        factor = (
                            factor
                            * (points - node_set[partner])
                            / (node_set[column] - node_set[partner])
                        )
                result[:, column] = result[:, column] + factor
    return result


def basis_tables():
    gauss_points = np.array(
        [-0.8611363115940526, -0.3399810435848563, 0.3399810435848563, 0.8611363115940526]
    )
    gauss_weights = np.array(
        [0.3478548451374538, 0.6521451548625461, 0.6521451548625461, 0.3478548451374538]
    )
    lobatto_points = np.array([-1.0, -math.sqrt(3.0 / 7.0), 0.0, math.sqrt(3.0 / 7.0), 1.0])
    lobatto_weights = np.array([0.1, 49.0 / 90.0, 32.0 / 45.0, 49.0 / 90.0, 0.1])
    slopes = lagrange_slopes(gauss_points, gauss_points)
    volume = (2.0 / gauss_weights)[:, None] * slopes.T * gauss_weights[None, :]
    trace_low = lagrange_values(gauss_points, np.array([-1.0]))[0]
    trace_high = lagrange_values(gauss_points, np.array([1.0]))[0]
    stiffness = (
        2.0 * lobatto_weights[:, None] * lagrange_slopes(lobatto_points, lobatto_points)
    )
    lumped = np.array([0.2, lobatto_weights[1], lobatto_weights[2], lobatto_weights[3], 0.2])
    return {
        "weights": gauss_weights / 2.0,
        "volume": time_step * volume,
        "trace_low": trace_low,
        "trace_high": trace_high,
        "lift_low": time_step * 2.0 * trace_low / gauss_weights,
        "lift_high": time_step * 2.0 * trace_high / gauss_weights,
        "to_points": lagrange_values(lobatto_points, gauss_points),
        "stiffness": -time_step * stiffness / lumped[:, None],
    }


TABLES = basis_tables()
TABLE = {name: TABLES[name].tolist() for name in TABLES}


def lane_matrices(lanes):
    zones = lanes // 4
    shape = (lanes, lanes)
    volume, lift = np.zeros(shape), np.zeros(shape)
    minus, plus = np.zeros(shape), np.zeros(shape)
    stiff, interp = np.zeros(shape), np.zeros(shape)
    pick, spread = np.zeros(shape), np.zeros(shape)
    for zone in range(zones):
        at = 4 * zone
        before = 4 * ((zone - 1) % zones)
        for within in range(4):
            for source in range(4):
                volume[at + source, at + within] = TABLES["volume"][within, source]
                minus[before + source, at + within] = TABLES["trace_high"][source]
                plus[at + source, at + within] = TABLES["trace_low"][source]
            lift[at, at + within] = TABLES["lift_low"][within]
            lift[at, before + within] = -TABLES["lift_high"][within]
            pick[at, at + within] = 1.0
            spread[zone, at + within] = 1.0
            for source in range(5):
                interp[(at + source) % lanes, at + within] += TABLES["to_points"][within, source]
        for target in range(5):
            for source in range(5):
                stiff[(at + source) % lanes, (at + target) % lanes] += TABLES["stiffness"][
                    target, source
                ]
    matrices = [minus, plus, stiff, interp, pick, spread, volume, lift]
    return np.concatenate(matrices, axis=1).astype(np.float32)


def spin(values, steps, axis):
    size = values.shape[axis]
    steps = steps % size
    return values if steps == 0 else pltpu.roll(values, steps, axis)


def rows_of(shape):
    return lax.broadcasted_iota(jnp.int32, shape, len(shape) - 2)


def low_half(shape):
    return rows_of(shape) < 4


def at_zone(shape, zone):
    return rows_of(shape) % 4 == zone


def combine(coefficients, terms):
    total = None
    for factor, term in zip(coefficients, terms):
        part = factor * term
        total = part if total is None else total + part
    return total


def parted(values):
    upper = values.astype(BF16)
    return upper, (values - upper.astype(F32)).astype(BF16)


def product(left, right):
    return jnp.dot(left, right, preferred_element_type=F32)


def mirrored(matrix):
    size = len(matrix[0])
    middle = size // 2
    even = [[(row[c] + row[size - 1 - c]) / 2 for c in range(middle)] for row in matrix]
    odd = [[(row[c] - row[size - 1 - c]) / 2 for c in range(middle)] for row in matrix]
    centre = [row[middle] for row in matrix] if size % 2 else None
    return even, odd, centre


def pairs_of(values):
    size = len(values)
    sums = [values[c] + values[size - 1 - c] for c in range(size // 2)]
    gaps = [values[c] - values[size - 1 - c] for c in range(size // 2)]
    return sums, gaps


def slopes_of(matrix, values):
    even, odd, centre = mirrored(matrix)
    sums, gaps = pairs_of(values)
    size = len(matrix)
    result = [None] * size
    for a in range(size // 2):
        factors, terms = list(even[a]), list(sums)
        if centre is not None:
            factors.append(centre[a])
            terms.append(values[size // 2])
        outer, inner = combine(factors, terms), combine(odd[a], gaps)
        result[a], result[size - 1 - a] = inner + outer, inner - outer
    if size % 2:
        result[size // 2] = combine(odd[size // 2], gaps)
    return result


def points_of(matrix, values):
    even, odd, centre = mirrored(matrix)
    sums, gaps = pairs_of(values)
    result = [None] * 4
    for i in range(2):
        outer = combine(even[i] + [centre[i]], sums + [values[2]])
        inner = combine(odd[i], gaps)
        result[i], result[3 - i] = outer + inner, outer - inner
    return result


def traces_of(values):
    sums, gaps = pairs_of(values)
    even, odd, _ = mirrored([TABLE["trace_low"]])
    outer, inner = combine(even[0], sums), combine(odd[0], gaps)
    return outer + inner, outer - inner


def lifts_of(lower, upper):
    even, odd, _ = mirrored([TABLE["lift_low"]])
    gap, both = lower - upper, lower + upper
    result = [None] * 4
    for i in range(2):
        outer, inner = even[0][i] * gap, odd[0][i] * both
        result[i], result[3 - i] = outer + inner, outer - inner
    return result


def turned(pieces):
    return [jnp.stack([pieces[j][i] for j in range(4)]) for i in range(4)]


def pack_x_low(planes):
    mask = low_half((8, 128))
    return [jnp.where(mask, planes[t], spin(planes[t + 1], 4, 0)) for t in (0, 2)]


def pack_x_high(planes):
    mask = low_half((8, 128))
    return [jnp.where(mask, spin(planes[t], 4, 0), planes[t + 1]) for t in (0, 2)]


def unpack_x_high(packed):
    return [spin(packed[0], 4, 0), packed[0], spin(packed[1], 4, 0), packed[1]]


def unpack_x_low(packed):
    return [packed[0], spin(packed[0], 4, 0), packed[1], spin(packed[1], 4, 0)]


def pack_y(values, start):
    shape = (8, 128)
    packed = []
    for half in range(2):
        total = spin(values[4 * half + 3], 3 - start, 0)
        for place in (2, 1, 0):
            moved = spin(values[4 * half + place], place - start, 0)
            total = jnp.where(at_zone(shape, place), moved, total)
        packed.append(total)
    return packed


def unpack_y(packed, end):
    return jnp.stack([spin(packed, end - place, 0) for place in range(4)])


def kernel(
    counts,
    density, energy, velocity, mesh_velocity, density_low, density_high, energy_low, energy_high,
    tables_hbm,
    results,
    raw_u, raw_v, raw_m, tables, square, ends, picker, tall, bound_in, bound_rows,
    bounds, work_u, work_v, work_m,
    acc_v, sec_v, acc_f, sec_f, speed, face_x, face_y, trace_x, trace_y, ends_z,
    halo_x, halo_y, halo_corner,
    out_dx, out_ux, out_dy, out_uy, in_dx, in_ux, in_dy, in_uy,
    out_my, in_mx, in_my, out_corner, in_corner,
    out_vx, out_wx, out_vy, out_wy, in_vx, in_wx, in_vy, in_wy,
    out_dx2, out_ux2, out_dy2, out_uy2, in_dx2, in_ux2, in_dy2, in_uy2,
    out_vx2, out_wx2, out_vy2, out_wy2, in_vx2, in_wx2, in_vy2, in_wy2,
    load_sem, send_sem, recv_sem,
):
    count_x, count_y = counts
    here_x, here_y = lax.axis_index("gx"), lax.axis_index("gy")
    west = lax.rem(here_x + count_x - 1, count_x)
    east = lax.rem(here_x + 1, count_x)
    south = lax.rem(here_y + count_y - 1, count_y)
    north = lax.rem(here_y + 1, count_y)
    to_west, to_east = (west, here_y), (east, here_y)
    to_south, to_north = (here_x, south), (here_x, north)
    to_corner, from_corner = (west, south), (east, north)

    barrier = pltpu.get_barrier_semaphore()
    for peer in (to_west, to_east, from_corner, to_south, to_north):
        pl.semaphore_signal(barrier, inc=1, device_id=peer, device_id_type=MESH)

    loads = {}

    def load(name, source, target):
        copy = pltpu.make_async_copy(source, target, load_sem.at[sum(map(len, loads.values()))])
        copy.start()
        loads.setdefault(name, []).append(copy)

    def loaded(name):
        for copy in loads[name]:
            copy.wait()

    places = [(pl.ds(16 * half, 16), pl.ds(8 * half, 8)) for half in range(2)]
    for rows, block in places:
        load("mesh", mesh_velocity.at[:, block], raw_m.at[:, :, rows, :])
    for rows, block in places:
        load("velocity", velocity.at[:, block], raw_v.at[:, :, rows, :])
    for rows, block in places:
        load("fields", density.at[block], raw_u.at[0, :, rows, :])
        load("fields", energy.at[block], raw_u.at[1, :, rows, :])
    load("tables", tables_hbm, tables)
    for index, source in enumerate((density_low, density_high, energy_low, energy_high)):
        load("bounds", source, bound_in.at[index])

    quad, plane = (4, 8, 128), (8, 128)
    low_rows, low_quad = low_half(plane), low_half(quad)
    first_zone, last_zone = at_zone(quad, 0), at_zone(quad, 3)
    stiff, points = TABLE["stiffness"], TABLE["to_points"]
    zero = jnp.zeros(plane, F32)

    def arrange(source, target, which):
        for j in range(4):
            target[which, :, j] = source[which, :, pl.ds(j, 8, stride=4), :]

    def put_pair(target, item, pair):
        target[item, 0] = pair[0]
        target[item, 1] = pair[1]

    def sided(values):
        upper, lower = parted(values)
        return upper, jnp.concatenate([upper, lower], 1)

    def lanes_product(values, column):
        _, pair = sided(values)
        both = product(pair, square[:, 256 * column : 256 * (column + 1)])
        return both[:, :128] + both[:, 128:]

    def picked(values):
        return product(sided(values)[1], picker[...])

    def field_traces(which, source):
        for half in range(2):
            chunk = pl.ds(4 * half, 4)
            low, high = traces_of([source[which, 4 * half + i] for i in range(4)])
            trace_x[which, 0, half], trace_x[which, 1, half] = low, high
            low, high = traces_of([source[which, chunk, j] for j in range(4)])
            trace_y[which, 0, chunk], trace_y[which, 1, chunk] = low, high

    def pack_field(which, item, buffers):
        west_to, east_to, south_to, north_to = buffers
        put_pair(west_to, item, pack_x_low(trace_x[which, 0, 0]))
        put_pair(east_to, item, pack_x_high(trace_x[which, 1, 1]))
        put_pair(south_to, item, pack_y(trace_y[which, 0], 0))
        put_pair(north_to, item, pack_y(trace_y[which, 1], 3))

    def pack_velocity(source, item, buffers):
        west_to, east_to, south_to, north_to = buffers
        put_pair(west_to, item, pack_x_low(source[item, 0]))
        closing = combine(stiff[4][:4], [source[item, 4 + a] for a in range(4)])
        put_pair(east_to, item, pack_x_high(closing))
        put_pair(south_to, item, pack_y(source[item, :, 0], 0))
        closing = combine(stiff[4][:4], [source[item, :, j] for j in range(4)])
        put_pair(north_to, item, pack_y(closing, 3))

    loaded("mesh")
    corner = zero
    for which in range(3):
        values = raw_m[which, :, pl.ds(0, 8, stride=4), :]
        put_pair(out_my, which, pack_y(values, 0))
        corner = jnp.where(rows_of(plane) == which, spin(values[0], which, 0), corner)
    out_corner[...] = corner

    arrived_a, arrived_b = (in_dx, in_ux, in_dy, in_uy), (in_dx2, in_ux2, in_dy2, in_uy2)
    leaving_a, leaving_b = (out_dx, out_ux, out_dy, out_uy), (out_dx2, out_ux2, out_dy2, out_uy2)
    arrived_c, arrived_d = (in_vx, in_wx, in_vy, in_wy), (in_vx2, in_wx2, in_vy2, in_wy2)
    leaving_c, leaving_d = (out_vx, out_wx, out_vy, out_wy), (out_vx2, out_wx2, out_vy2, out_wy2)
    loaded("velocity")
    for which in range(3):
        arrange(raw_v, work_v, which)
        pack_velocity(work_v, which, leaving_c)
    loaded("fields")
    for which in range(2):
        arrange(raw_u, work_u, which)
        field_traces(which, work_u)
        pack_field(which, which, leaving_a)

    pl.semaphore_wait(barrier, 5)
    copies = []
    peers = (to_west, to_east, to_south, to_north)

    def send(source, target, peer):
        copy = pltpu.make_async_remote_copy(
            src_ref=source, dst_ref=target,
            send_sem=send_sem.at[len(copies)], recv_sem=recv_sem.at[len(copies)],
            device_id=peer, device_id_type=MESH,
        )
        copy.start()
        copies.append(copy)
        return copy

    def send_all(sources, targets):
        return [send(*triple) for triple in zip(sources, targets, peers)]

    def send_some(sources, targets, sides):
        return [send(sources[side], targets[side], peers[side]) for side in sides]

    first_m = [send(raw_m.at[:, 0, pl.ds(0, 16), :], in_mx, to_west)]
    first_v = send_some(leaving_c, arrived_c, (0, 1))
    first = send_some(leaving_a, arrived_a, (0, 1))
    first_m += [send(out_corner, in_corner, to_corner), send(out_my, in_my, to_south)]
    first_v += send_some(leaving_c, arrived_c, (2, 3))
    first += send_some(leaving_a, arrived_a, (2, 3))

    loaded("tables")
    minus, plus, stiff_z, interp_z, pick_z, spread_z, volume_z, lift_z = (
        tables[:, 128 * column : 128 * (column + 1)] for column in range(8)
    )
    for column, table in enumerate((stiff_z, interp_z)):
        upper, lower = parted(table)
        at = 256 * column
        square[:128, at : at + 128] = upper
        square[128:, at : at + 128] = upper
        square[:128, at + 128 : at + 256] = lower
        square[128:, at + 128 : at + 256] = jnp.zeros((128, 128), BF16)
    for column, table in enumerate((minus, plus)):
        upper, lower = parted(table)
        at = 128 * column
        ends[:128, at : at + 128] = upper
        ends[128:256, at : at + 128] = upper
        ends[256:, at : at + 128] = lower
    picker[:128] = pick_z.astype(BF16)
    picker[128:] = pick_z.astype(BF16)
    for row, table in enumerate((volume_z, lift_z)):
        upper, lower = parted(table)
        tall[128 * row : 128 * (row + 1), :128] = upper
        tall[128 * row : 128 * (row + 1), 128:] = lower

    loaded("bounds")
    bound_rows[...] = jnp.zeros((4, 2, 8, 128), F32)
    for index in range(4):
        for zone in range(4):
            bound_rows[index, zone % 2, pl.ds(4 * (zone // 2), 4), pl.ds(0, 32)] = bound_in[
                index, zone
            ]
    values = bound_rows[...].reshape(64, 128)
    spreader = spread_z.astype(BF16)
    upper = values.astype(BF16)
    rest = values - upper.astype(F32)
    middle = rest.astype(BF16)
    lowest = (rest - middle.astype(F32)).astype(BF16)
    values = product(upper, spreader) + (product(middle, spreader) + product(lowest, spreader))
    bounds[...] = values.reshape(4, 2, 8, 128)

    def velocity_before(which, source, base):
        along_z = lanes_product(source[which].reshape(256, 128), 0).reshape(8, 4, 8, 128)
        own = stiff[4][4]
        opening = source[which, 0]
        inner = jnp.where(low_quad, spin(opening, 4, 1), 0.0)
        last_end = combine(stiff[4], [source[which, 4 + a] for a in range(4)] + [inner])
        carried = jnp.where(low_quad, own * opening, spin(last_end, 4, 1))
        for half in range(2):
            chunk = pl.ds(4 * half, 4)
            ahead = source[which, 4] if half == 0 else inner
            along_x = slopes_of(stiff, [source[which, 4 * half + a] for a in range(4)] + [ahead])
            along_x[0] = along_x[0] + carried
            carried = along_x[4]
            lines = [source[which, chunk, j] for j in range(4)]
            ahead = jnp.where(last_zone, 0.0, spin(lines[0], 7, 1))
            along_y = slopes_of(stiff, lines + [ahead])
            along_y[0] = along_y[0] + jnp.where(first_zone, own * lines[0], spin(along_y[4], 1, 1))
            along_y = turned(along_y[:4])
            for a in range(4):
                x = 4 * half + a
                acc_v[which, x] = base(x) + (
                    work_m[0, x] * along_x[a]
                    + work_m[1, x] * along_y[a]
                    + work_m[2, x] * along_z[x]
                )

    def velocity_after(which, put, arrived):
        from_east, from_west, from_north, from_south = arrived
        later = jnp.stack(unpack_x_high([from_east[which, 0], from_east[which, 1]]))
        earlier = jnp.stack(unpack_x_low([from_west[which, 0], from_west[which, 1]]))
        later = jnp.where(low_quad, 0.0, later)
        earlier = jnp.where(low_quad, earlier, 0.0)
        for half in range(2):
            above = jnp.where(last_zone, unpack_y(from_north[which, half], 3), 0.0)
            below = jnp.where(first_zone, unpack_y(from_south[which, half], 0), 0.0)
            extra_y = [stiff[j][4] * above for j in range(4)]
            extra_y[0] = extra_y[0] + below
            extra_y = turned(extra_y)
            for a in range(4):
                x = 4 * half + a
                value = acc_v[which, x] + work_m[1, x] * extra_y[a]
                if half == 1:
                    value = value + work_m[0, x] * (stiff[a][4] * later)
                elif a == 0:
                    value = value + work_m[0, x] * earlier
                put(x, value)

    def mesh_before(item):
        values = work_m[min(item, 2)].reshape(256, 128)
        values = lanes_product(values, 1) if item < 3 else picked(values)
        values = values.reshape(8, 4, 8, 128)
        inner = jnp.where(low_quad, spin(values[0], 4, 1), 0.0)
        for half in range(2):
            chunk = pl.ds(4 * half, 4)
            ahead = values[4] if half == 0 else inner
            across = points_of(points, [values[4 * half + a] for a in range(4)] + [ahead])
            across = turned(across)
            ahead = jnp.where(last_zone, 0.0, spin(across[0], 7, 1))
            for j, result in enumerate(points_of(points, across + [ahead])):
                speed[item, chunk, j] = result
            if item == 0:
                edge = values[4 * half]
                ahead = jnp.where(at_zone(plane, 3), 0.0, spin(edge[0], 7, 0))
                edge = points_of(points, [edge[j] for j in range(4)] + [ahead])
                face_x[half] = jnp.stack(edge)
            if item == 1:
                face_y[0, chunk] = across[0]
                face_y[1, chunk] = ahead

    def mesh_halo():
        values = jnp.concatenate(
            [in_mx[...].reshape(48, 128), in_my[...].reshape(48, 128), in_corner[...], zero], 0
        )
        both, extra = lanes_product(values, 1), picked(values)
        for item in range(4):
            which, source = min(item, 2), both if item < 3 else extra
            rows = source[16 * which : 16 * (which + 1)]
            halo_x[item, pl.ds(0, 16)] = rows
            halo_x[item, pl.ds(16, 16)] = rows
            halo_y[item] = source[48 + 16 * which : 64 + 16 * which].reshape(2, 8, 128)
            halo_corner[item] = spin(source[96:104], 7 - which, 0)

    def mesh_after(item):
        rows = rows_of(plane)
        later = [
            jnp.where(low_rows, 0.0, halo_x[item, pl.ds(j, 8, stride=4), :]) for j in range(4)
        ]
        far = jnp.where(at_zone(plane, 3), 0.0, spin(later[0], 7, 0))
        far = jnp.where(rows == 7, halo_corner[item], far)
        later.append(jnp.where(low_rows, 0.0, far))
        edge = jnp.stack(points_of(points, later))
        above = [
            jnp.where(last_zone, unpack_y(halo_y[item, half], 3), 0.0) for half in range(2)
        ]
        inner = jnp.where(low_rows, spin(above[0][0], 4, 0), 0.0)
        for half in range(2):
            ahead = above[1][0] if half == 0 else inner
            across = points_of(points, [above[half][a] for a in range(4)] + [ahead])
            for i in range(4):
                x = 4 * half + i
                extra = jnp.stack([points[j][4] * across[i] for j in range(4)])
                if half == 1:
                    extra = extra + points[i][4] * edge
                speed[item, x] += extra
                if item == 1:
                    upper = face_y[1, x] + across[i]
                    if half == 1:
                        upper = upper + points[i][4] * later[4]
                        face_y[0, x] += points[i][4] * later[0]
                    face_y[1, x] = upper
            if item == 0:
                face_x[half] += jnp.stack([points[j][4] * above[half][0] for j in range(4)])
        if item == 0:
            face_x[2] = jnp.where(low_quad, spin(face_x[0], 4, 1), edge)

    def upwind(face, minus_side, plus_side):
        return jnp.maximum(face, 0.0) * minus_side + jnp.minimum(face, 0.0) * plus_side

    def field_ends(which, source):
        upper, pair = sided(source[which].reshape(256, 128))
        sides = product(pair, ends[:256]) + product(upper, ends[256:])
        ends_z[which, 0] = sides[:, :128]
        ends_z[which, 1] = sides[:, 128:]

    def field_before(which, source, base):
        values = source[which].reshape(256, 128)
        flux = upwind(speed[3].reshape(256, 128), ends_z[which, 0], ends_z[which, 1])
        moved = speed[2].reshape(256, 128) * values
        upper, lower = parted(jnp.concatenate([moved, flux], 1))
        sums = product(upper, tall[...])
        along_z = sums[:, :128] + sums[:, 128:] + product(lower, tall[:, :128])
        along_z = along_z.reshape(8, 4, 8, 128)
        for half in range(2):
            chunk = pl.ds(4 * half, 4)
            places = [4 * half + i for i in range(4)]
            along_x = slopes_of(TABLE["volume"], [speed[0, x] * source[which, x] for x in places])
            along_y = slopes_of(
                TABLE["volume"],
                [speed[1, chunk, j] * source[which, chunk, j] for j in range(4)],
            )
            along_y = turned(along_y)
            for i, x in enumerate(places):
                acc_f[which, x] = base(x) + ((along_x[i] + along_y[i]) + along_z[x])

    def in_group(values, join):
        lane = lax.broadcasted_iota(jnp.int32, plane, 1)
        partner = jnp.where(lane % 2 == 0, spin(values, 127, 1), spin(values, 1, 1))
        values = join(values, partner)
        partner = jnp.where(lane // 2 % 2 == 0, spin(values, 126, 1), spin(values, 2, 1))
        return join(values, partner)

    def over_zone(values, join):
        total = functools.reduce(join, values)
        return functools.reduce(join, [total[j] for j in range(4)])

    def limited(which, half, values):
        weights = TABLE["weights"]
        mean = combine(weights, values)
        mean = combine(weights, [mean[j] for j in range(4)])
        lane = lax.broadcasted_iota(jnp.int32, plane, 1) % 4
        middle = (lane == 1) | (lane == 2)
        mean = in_group(mean * jnp.where(middle, weights[1], weights[0]), jnp.add)
        rise = in_group(over_zone(values, jnp.maximum), jnp.maximum) - mean
        fall = in_group(over_zone(values, jnp.minimum), jnp.minimum) - mean
        low, high = bounds[2 * which, half], bounds[2 * which + 1, half]
        theta = jnp.minimum(
            (high - mean) / (rise + limit_eps), (mean - low) / (limit_eps - fall)
        )
        theta = jnp.clip(theta, 0.0, 1.0)
        return [mean + theta * (value - mean) for value in values]

    def field_after(which, scale, put, arrived):
        from_east, from_west, from_north, from_south = arrived
        later = jnp.stack(unpack_x_high([from_east[which, 0], from_east[which, 1]]))
        earlier = jnp.stack(unpack_x_low([from_west[which, 0], from_west[which, 1]]))
        low, high = trace_x[which, 0], trace_x[which, 1]
        flux = [
            upwind(face_x[0], jnp.where(low_quad, earlier, spin(high[1], 4, 1)), low[0]),
            upwind(face_x[1], high[0], low[1]),
            upwind(face_x[2], high[1], jnp.where(low_quad, spin(low[0], 4, 1), later)),
        ]
        for half in range(2):
            chunk = pl.ds(4 * half, 4)
            low, high = trace_y[which, 0, chunk], trace_y[which, 1, chunk]
            before = jnp.where(first_zone, unpack_y(from_south[which, half], 0), spin(high, 1, 1))
            after = jnp.where(last_zone, unpack_y(from_north[which, half], 3), spin(low, 7, 1))
            lift_y = turned(
                lifts_of(
                    upwind(face_y[0, chunk], before, low), upwind(face_y[1, chunk], high, after)
                )
            )
            lift_x = lifts_of(flux[half], flux[half + 1])
            values = [
                acc_f[which, 4 * half + i] + (lift_x[i] + lift_y[i]) for i in range(4)
            ]
            if scale != 1.0:
                values = [scale * value for value in values]
            values = limited(which, half, values)
            for i in range(4):
                put(4 * half + i, values[i])

    for which in range(3):
        arrange(raw_m, work_m, which)
    for item in range(4):
        mesh_before(item)
    for which in range(2):
        field_ends(which, work_u)
    for which in range(3):
        velocity_before(which, work_v, lambda x: work_v[which, x])
    def keep_field(x, value):
        sec_f[which, x] = value

    def keep_velocity(x, value):
        sec_v[which, x] = value

    def finish_field(x, value):
        for j in range(4):
            results[which, x, pl.ds(j, 8, stride=4), :] = value[j]

    def finish_velocity(x, value):
        for j in range(4):
            results[2 + which, x, pl.ds(j, 8, stride=4), :] = 0.5 * value[j]

    for copy in first_m:
        copy.wait_recv()
    mesh_halo()
    for item in range(4):
        mesh_after(item)
    for copy in first_v:
        copy.wait_recv()
    for which in range(3):
        velocity_after(which, keep_velocity, arrived_c)
        pack_velocity(sec_v, which, leaving_d)
    second_v = send_all(leaving_d, arrived_d)
    for which in range(2):
        field_before(which, work_u, lambda x: work_u[which, x])
    for copy in first:
        copy.wait_recv()
    second = []
    for which in range(2):
        field_after(which, 1.0, keep_field, arrived_a)
        field_traces(which, sec_f)
        pack_field(which, which, leaving_b)
        second.append(
            send_all([ref.at[which] for ref in leaving_b], [ref.at[which] for ref in arrived_b])
        )

    for which in range(3):
        velocity_before(which, sec_v, lambda x: work_v[which, x] + sec_v[which, x])
    for which in range(2):
        field_ends(which, sec_f)
    for which in range(2):
        field_before(which, sec_f, lambda x: work_u[which, x] + sec_f[which, x])
    for copy in copies:
        copy.wait_send()
    for copy in second_v:
        copy.wait_recv()
    for which in range(3):
        velocity_after(which, finish_velocity, arrived_d)
    for which in range(2):
        for copy in second[which]:
            copy.wait_recv()
        field_after(which, 0.5, finish_field, arrived_b)


def unfold(results, new_density, new_energy, new_velocity, store_sem):
    copies = []
    for half in range(2):
        rows, block = pl.ds(16 * half, 16), pl.ds(8 * half, 8)
        for source, target in (
            (results.at[pl.ds(2, 3), :, rows, :], new_velocity.at[:, block]),
            (results.at[0, :, rows, :], new_density.at[block]),
            (results.at[1, :, rows, :], new_energy.at[block]),
        ):
            copy = pltpu.make_async_copy(source, target, store_sem.at[len(copies)])
            copy.start()
            copies.append(copy)
    for copy in copies:
        copy.wait()


def solution(mesh):
    counts = (mesh.shape["gx"], mesh.shape["gy"])
    matrices = lane_matrices(128)

    def on_device(*arguments):
        vmem = lambda *shape: pltpu.VMEM(shape, F32)
        scratch = [
            vmem(2, 8, 32, 128), vmem(3, 8, 32, 128), vmem(3, 8, 32, 128),
            vmem(*matrices.shape),
            pltpu.VMEM((256, 512), BF16), pltpu.VMEM((384, 256), BF16),
            pltpu.VMEM((256, 128), BF16), pltpu.VMEM((256, 256), BF16),
            vmem(4, 4, 4, 32), vmem(4, 2, 8, 128), vmem(4, 2, 8, 128),
            vmem(2, 8, 4, 8, 128), vmem(3, 8, 4, 8, 128), vmem(3, 8, 4, 8, 128),
            vmem(3, 8, 4, 8, 128), vmem(3, 8, 4, 8, 128),
            vmem(2, 8, 4, 8, 128), vmem(2, 8, 4, 8, 128),
            vmem(4, 8, 4, 8, 128), vmem(3, 4, 8, 128), vmem(2, 8, 8, 128),
            vmem(2, 2, 2, 4, 8, 128), vmem(2, 2, 8, 8, 128), vmem(2, 2, 256, 128),
            vmem(4, 32, 128), vmem(4, 2, 8, 128), vmem(4, 8, 128),
        ]
        scratch += [vmem(2, 2, 8, 128)] * 8
        scratch += [vmem(3, 2, 8, 128), vmem(3, 16, 128), vmem(3, 2, 8, 128)] + [vmem(8, 128)] * 2
        for items in (3, 2, 3):
            scratch += [vmem(items, 2, 8, 128)] * 8
        scratch += [
            pltpu.SemaphoreType.DMA((13,)),
            pltpu.SemaphoreType.DMA((23,)),
            pltpu.SemaphoreType.DMA((23,)),
        ]
        operands = [
            pltpu.with_memory_space_constraint(value, pltpu.HBM)
            for value in (*arguments, jnp.asarray(matrices))
        ]
        results = pl.pallas_call(
            functools.partial(kernel, counts),
            out_shape=pltpu.VMEM((5, 8, 32, 128), F32),
            in_specs=[pl.BlockSpec(memory_space=pltpu.HBM)] * 9,
            out_specs=pl.BlockSpec(memory_space=pltpu.VMEM),
            scratch_shapes=scratch,
            compiler_params=pltpu.CompilerParams(
                collective_id=0, has_side_effects=True, vmem_limit_bytes=32 * 1024 * 1024
            ),
        )(*operands)
        return pl.pallas_call(
            unfold,
            out_shape=[jax.ShapeDtypeStruct(value.shape, F32) for value in arguments[:3]],
            in_specs=[pl.BlockSpec(memory_space=pltpu.VMEM)],
            out_specs=[pl.BlockSpec(memory_space=pltpu.HBM)] * 3,
            scratch_shapes=[pltpu.SemaphoreType.DMA((6,))],
            compiler_params=pltpu.CompilerParams(vmem_limit_bytes=32 * 1024 * 1024),
        )(results)

    fields, vectors = P("gx", "gy", None), P(None, "gx", "gy", None)
    return jax.shard_map(
        on_device,
        mesh=mesh,
        in_specs=(fields, fields, vectors, vectors, fields, fields, fields, fields),
        out_specs=(fields, fields, vectors),
        check_vma=False,
    )
```

```python
import functools
import math

import jax
import jax.numpy as jnp
import numpy as np
from jax import lax
from jax.experimental import pallas as pl
from jax.experimental.pallas import tpu as pltpu
from jax.sharding import PartitionSpec as P

MESH = pl.DeviceIdType.MESH
F32 = jnp.float32
BF16 = jnp.bfloat16
time_step = 0.02
limit_eps = 1e-06


def lagrange_values(node_set, points):
    result = np.ones((len(points), len(node_set)))
    for column in range(len(node_set)):
        for partner in range(len(node_set)):
            if partner != column:
                result[:, column] = (
                    result[:, column]
                    * (points - node_set[partner])
                    / (node_set[column] - node_set[partner])
                )
    return result


def lagrange_slopes(node_set, points):
    node_total = len(node_set)
    result = np.zeros((len(points), node_total))
    for column in range(node_total):
        for skipped in range(node_total):
            if skipped != column:
                factor = np.ones(len(points)) / (node_set[column] - node_set[skipped])
                for partner in range(node_total):
                    if partner != column and partner != skipped:
                        factor = (
                            factor
                            * (points - node_set[partner])
                            / (node_set[column] - node_set[partner])
                        )
                result[:, column] = result[:, column] + factor
    return result


def basis_tables():
    gauss_points = np.array(
        [-0.8611363115940526, -0.3399810435848563, 0.3399810435848563, 0.8611363115940526]
    )
    gauss_weights = np.array(
        [0.3478548451374538, 0.6521451548625461, 0.6521451548625461, 0.3478548451374538]
    )
    lobatto_points = np.array([-1.0, -math.sqrt(3.0 / 7.0), 0.0, math.sqrt(3.0 / 7.0), 1.0])
    lobatto_weights = np.array([0.1, 49.0 / 90.0, 32.0 / 45.0, 49.0 / 90.0, 0.1])
    slopes = lagrange_slopes(gauss_points, gauss_points)
    volume = (2.0 / gauss_weights)[:, None] * slopes.T * gauss_weights[None, :]
    trace_low = lagrange_values(gauss_points, np.array([-1.0]))[0]
    trace_high = lagrange_values(gauss_points, np.array([1.0]))[0]
    stiffness = (
        2.0 * lobatto_weights[:, None] * lagrange_slopes(lobatto_points, lobatto_points)
    )
    lumped = np.array([0.2, lobatto_weights[1], lobatto_weights[2], lobatto_weights[3], 0.2])
    return {
        "weights": gauss_weights / 2.0,
        "volume": time_step * volume,
        "trace_low": trace_low,
        "trace_high": trace_high,
        "lift_low": time_step * 2.0 * trace_low / gauss_weights,
        "lift_high": time_step * 2.0 * trace_high / gauss_weights,
        "to_points": lagrange_values(lobatto_points, gauss_points),
        "stiffness": -time_step * stiffness / lumped[:, None],
    }


TABLES = basis_tables()
TABLE = {name: TABLES[name].tolist() for name in TABLES}


def lane_matrices(lanes):
    zones = lanes // 4
    shape = (lanes, lanes)
    volume, lift = np.zeros(shape), np.zeros(shape)
    minus, plus = np.zeros(shape), np.zeros(shape)
    stiff, interp = np.zeros(shape), np.zeros(shape)
    pick, spread = np.zeros(shape), np.zeros(shape)
    for zone in range(zones):
        at = 4 * zone
        before = 4 * ((zone - 1) % zones)
        for within in range(4):
            for source in range(4):
                volume[at + source, at + within] = TABLES["volume"][within, source]
                minus[before + source, at + within] = TABLES["trace_high"][source]
                plus[at + source, at + within] = TABLES["trace_low"][source]
            lift[at, at + within] = TABLES["lift_low"][within]
            lift[at, before + within] = -TABLES["lift_high"][within]
            pick[at, at + within] = 1.0
            spread[zone, at + within] = 1.0
            for source in range(5):
                interp[(at + source) % lanes, at + within] += TABLES["to_points"][within, source]
        for target in range(5):
            for source in range(5):
                stiff[(at + source) % lanes, (at + target) % lanes] += TABLES["stiffness"][
                    target, source
                ]
    matrices = [minus, plus, stiff, interp, pick, spread, volume, lift]
    return np.concatenate(matrices, axis=1).astype(np.float32)


def spin(values, steps, axis):
    size = values.shape[axis]
    steps = steps % size
    return values if steps == 0 else pltpu.roll(values, steps, axis)


def rows_of(shape):
    return lax.broadcasted_iota(jnp.int32, shape, len(shape) - 2)


def low_half(shape):
    return rows_of(shape) < 4


def at_zone(shape, zone):
    return rows_of(shape) % 4 == zone


def combine(coefficients, terms):
    total = None
    for factor, term in zip(coefficients, terms):
        part = factor * term
        total = part if total is None else total + part
    return total


def parted(values):
    upper = values.astype(BF16)
    return upper, (values - upper.astype(F32)).astype(BF16)


def product(left, right):
    return jnp.dot(left, right, preferred_element_type=F32)


def mirrored(matrix):
    size = len(matrix[0])
    middle = size // 2
    even = [[(row[c] + row[size - 1 - c]) / 2 for c in range(middle)] for row in matrix]
    odd = [[(row[c] - row[size - 1 - c]) / 2 for c in range(middle)] for row in matrix]
    centre = [row[middle] for row in matrix] if size % 2 else None
    return even, odd, centre


def pairs_of(values):
    size = len(values)
    sums = [values[c] + values[size - 1 - c] for c in range(size // 2)]
    gaps = [values[c] - values[size - 1 - c] for c in range(size // 2)]
    return sums, gaps


def slopes_of(matrix, values):
    even, odd, centre = mirrored(matrix)
    sums, gaps = pairs_of(values)
    size = len(matrix)
    result = [None] * size
    for a in range(size // 2):
        factors, terms = list(even[a]), list(sums)
        if centre is not None:
            factors.append(centre[a])
            terms.append(values[size // 2])
        outer, inner = combine(factors, terms), combine(odd[a], gaps)
        result[a], result[size - 1 - a] = inner + outer, inner - outer
    if size % 2:
        result[size // 2] = combine(odd[size // 2], gaps)
    return result


def points_of(matrix, values):
    even, odd, centre = mirrored(matrix)
    sums, gaps = pairs_of(values)
    result = [None] * 4
    for i in range(2):
        outer = combine(even[i] + [centre[i]], sums + [values[2]])
        inner = combine(odd[i], gaps)
        result[i], result[3 - i] = outer + inner, outer - inner
    return result


def traces_of(values):
    sums, gaps = pairs_of(values)
    even, odd, _ = mirrored([TABLE["trace_low"]])
    outer, inner = combine(even[0], sums), combine(odd[0], gaps)
    return outer + inner, outer - inner


def lifts_of(lower, upper):
    even, odd, _ = mirrored([TABLE["lift_low"]])
    gap, both = lower - upper, lower + upper
    result = [None] * 4
    for i in range(2):
        outer, inner = even[0][i] * gap, odd[0][i] * both
        result[i], result[3 - i] = outer + inner, outer - inner
    return result


def turned(pieces):
    return [jnp.stack([pieces[j][i] for j in range(4)]) for i in range(4)]


def pack_x_low(planes):
    mask = low_half((8, 128))
    return [jnp.where(mask, planes[t], spin(planes[t + 1], 4, 0)) for t in (0, 2)]


def pack_x_high(planes):
    mask = low_half((8, 128))
    return [jnp.where(mask, spin(planes[t], 4, 0), planes[t + 1]) for t in (0, 2)]


def unpack_x_high(packed):
    return [spin(packed[0], 4, 0), packed[0], spin(packed[1], 4, 0), packed[1]]


def unpack_x_low(packed):
    return [packed[0], spin(packed[0], 4, 0), packed[1], spin(packed[1], 4, 0)]


def pack_y(values, start):
    shape = (8, 128)
    packed = []
    for half in range(2):
        total = spin(values[4 * half + 3], 3 - start, 0)
        for place in (2, 1, 0):
            moved = spin(values[4 * half + place], place - start, 0)
            total = jnp.where(at_zone(shape, place), moved, total)
        packed.append(total)
    return packed


def unpack_y(packed, end):
    return jnp.stack([spin(packed, end - place, 0) for place in range(4)])


def kernel(
    counts,
    density, energy, velocity, mesh_velocity, density_low, density_high, energy_low, energy_high,
    tables_hbm,
    results,
    raw_u, raw_v, raw_m, tables, square, ends, picker, tall, bound_in, bound_rows,
    bounds, work_u, work_v, work_m,
    acc_v, sec_v, acc_f, sec_f, speed, face_x, face_y, trace_x, trace_y, ends_z,
    halo_x, halo_y, halo_corner,
    out_dx, out_ux, out_dy, out_uy, in_dx, in_ux, in_dy, in_uy,
    out_my, in_mx, in_my, out_corner, in_corner,
    out_vx, out_wx, out_vy, out_wy, in_vx, in_wx, in_vy, in_wy,
    out_dx2, out_ux2, out_dy2, out_uy2, in_dx2, in_ux2, in_dy2, in_uy2,
    out_vx2, out_wx2, out_vy2, out_wy2, in_vx2, in_wx2, in_vy2, in_wy2,
    load_sem, send_sem, recv_sem,
):
    count_x, count_y = counts
    here_x, here_y = lax.axis_index("gx"), lax.axis_index("gy")
    west = lax.rem(here_x + count_x - 1, count_x)
    east = lax.rem(here_x + 1, count_x)
    south = lax.rem(here_y + count_y - 1, count_y)
    north = lax.rem(here_y + 1, count_y)
    to_west, to_east = (west, here_y), (east, here_y)
    to_south, to_north = (here_x, south), (here_x, north)
    to_corner, from_corner = (west, south), (east, north)

    barrier = pltpu.get_barrier_semaphore()
    for peer in (to_west, to_east, from_corner, to_south, to_north):
        pl.semaphore_signal(barrier, inc=1, device_id=peer, device_id_type=MESH)

    loads = {}

    def load(name, source, target):
        copy = pltpu.make_async_copy(source, target, load_sem.at[sum(map(len, loads.values()))])
        copy.start()
        loads.setdefault(name, []).append(copy)

    def loaded(name):
        for copy in loads[name]:
            copy.wait()

    places = [(pl.ds(16 * half, 16), pl.ds(8 * half, 8)) for half in range(2)]
    for rows, block in places:
        load("mesh", mesh_velocity.at[:, block], raw_m.at[:, :, rows, :])
    for rows, block in places:
        load("velocity", velocity.at[:, block], raw_v.at[:, :, rows, :])
    for rows, block in places:
        load("fields", density.at[block], raw_u.at[0, :, rows, :])
        load("fields", energy.at[block], raw_u.at[1, :, rows, :])
    load("tables", tables_hbm, tables)
    for index, source in enumerate((density_low, density_high, energy_low, energy_high)):
        load("bounds", source, bound_in.at[index])

    quad, plane = (4, 8, 128), (8, 128)
    low_rows, low_quad = low_half(plane), low_half(quad)
    first_zone, last_zone = at_zone(quad, 0), at_zone(quad, 3)
    stiff, points = TABLE["stiffness"], TABLE["to_points"]
    zero = jnp.zeros(plane, F32)

    def arrange(source, target, which):
        for j in range(4):
            target[which, :, j] = source[which, :, pl.ds(j, 8, stride=4), :]

    def put_pair(target, item, pair):
        target[item, 0] = pair[0]
        target[item, 1] = pair[1]

    def sided(values):
        upper, lower = parted(values)
        return upper, jnp.concatenate([upper, lower], 1)

    def lanes_product(values, column):
        _, pair = sided(values)
        both = product(pair, square[:, 256 * column : 256 * (column + 1)])
        return both[:, :128] + both[:, 128:]

    def picked(values):
        return product(sided(values)[1], picker[...])

    def field_traces(which, source):
        for half in range(2):
            chunk = pl.ds(4 * half, 4)
            low, high = traces_of([source[which, 4 * half + i] for i in range(4)])
            trace_x[which, 0, half], trace_x[which, 1, half] = low, high
            low, high = traces_of([source[which, chunk, j] for j in range(4)])
            trace_y[which, 0, chunk], trace_y[which, 1, chunk] = low, high

    def pack_field(which, item, buffers):
        west_to, east_to, south_to, north_to = buffers
        put_pair(west_to, item, pack_x_low(trace_x[which, 0, 0]))
        put_pair(east_to, item, pack_x_high(trace_x[which, 1, 1]))
        put_pair(south_to, item, pack_y(trace_y[which, 0], 0))
        put_pair(north_to, item, pack_y(trace_y[which, 1], 3))

    def pack_velocity(source, item, buffers):
        west_to, east_to, south_to, north_to = buffers
        put_pair(west_to, item, pack_x_low(source[item, 0]))
        closing = combine(stiff[4][:4], [source[item, 4 + a] for a in range(4)])
        put_pair(east_to, item, pack_x_high(closing))
        put_pair(south_to, item, pack_y(source[item, :, 0], 0))
        closing = combine(stiff[4][:4], [source[item, :, j] for j in range(4)])
        put_pair(north_to, item, pack_y(closing, 3))

    loaded("mesh")
    corner = zero
    for which in range(3):
        values = raw_m[which, :, pl.ds(0, 8, stride=4), :]
        put_pair(out_my, which, pack_y(values, 0))
        corner = jnp.where(rows_of(plane) == which, spin(values[0], which, 0), corner)
    out_corner[...] = corner

    arrived_a, arrived_b = (in_dx, in_ux, in_dy, in_uy), (in_dx2, in_ux2, in_dy2, in_uy2)
    leaving_a, leaving_b = (out_dx, out_ux, out_dy, out_uy), (out_dx2, out_ux2, out_dy2, out_uy2)
    arrived_c, arrived_d = (in_vx, in_wx, in_vy, in_wy), (in_vx2, in_wx2, in_vy2, in_wy2)
    leaving_c, leaving_d = (out_vx, out_wx, out_vy, out_wy), (out_vx2, out_wx2, out_vy2, out_wy2)
    loaded("velocity")
    for which in range(3):
        arrange(raw_v, work_v, which)
        pack_velocity(work_v, which, leaving_c)
    loaded("fields")
    for which in range(2):
        arrange(raw_u, work_u, which)
        field_traces(which, work_u)
        pack_field(which, which, leaving_a)

    pl.semaphore_wait(barrier, 5)
    copies = []
    peers = (to_west, to_east, to_south, to_north)

    def send(source, target, peer):
        copy = pltpu.make_async_remote_copy(
            src_ref=source, dst_ref=target,
            send_sem=send_sem.at[len(copies)], recv_sem=recv_sem.at[len(copies)],
            device_id=peer, device_id_type=MESH,
        )
        copy.start()
        copies.append(copy)
        return copy

    def send_all(sources, targets):
        return [send(*triple) for triple in zip(sources, targets, peers)]

    def send_some(sources, targets, sides):
        return [send(sources[side], targets[side], peers[side]) for side in sides]

    first_m = [send(raw_m.at[:, 0, pl.ds(0, 16), :], in_mx, to_west)]
    first_v = send_some(leaving_c, arrived_c, (0, 1))
    first = send_some(leaving_a, arrived_a, (0, 1))
    first_m += [send(out_corner, in_corner, to_corner), send(out_my, in_my, to_south)]
    first_v += send_some(leaving_c, arrived_c, (2, 3))
    first += send_some(leaving_a, arrived_a, (2, 3))

    loaded("tables")
    minus, plus, stiff_z, interp_z, pick_z, spread_z, volume_z, lift_z = (
        tables[:, 128 * column : 128 * (column + 1)] for column in range(8)
    )
    for column, table in enumerate((stiff_z, interp_z)):
        upper, lower = parted(table)
        at = 256 * column
        square[:128, at : at + 128] = upper
        square[128:, at : at + 128] = upper
        square[:128, at + 128 : at + 256] = lower
        square[128:, at + 128 : at + 256] = jnp.zeros((128, 128), BF16)
    for column, table in enumerate((minus, plus)):
        upper, lower = parted(table)
        at = 128 * column
        ends[:128, at : at + 128] = upper
        ends[128:256, at : at + 128] = upper
        ends[256:, at : at + 128] = lower
    picker[:128] = pick_z.astype(BF16)
    picker[128:] = pick_z.astype(BF16)
    for row, table in enumerate((volume_z, lift_z)):
        upper, lower = parted(table)
        tall[128 * row : 128 * (row + 1), :128] = upper
        tall[128 * row : 128 * (row + 1), 128:] = lower

    loaded("bounds")
    bound_rows[...] = jnp.zeros((4, 2, 8, 128), F32)
    for index in range(4):
        for zone in range(4):
            bound_rows[index, zone % 2, pl.ds(4 * (zone // 2), 4), pl.ds(0, 32)] = bound_in[
                index, zone
            ]
    values = bound_rows[...].reshape(64, 128)
    spreader = spread_z.astype(BF16)
    upper = values.astype(BF16)
    rest = values - upper.astype(F32)
    middle = rest.astype(BF16)
    lowest = (rest - middle.astype(F32)).astype(BF16)
    values = product(upper, spreader) + (product(middle, spreader) + product(lowest, spreader))
    bounds[...] = values.reshape(4, 2, 8, 128)

    def velocity_before(which, source, base):
        along_z = lanes_product(source[which].reshape(256, 128), 0).reshape(8, 4, 8, 128)
        own = stiff[4][4]
        opening = source[which, 0]
        inner = jnp.where(low_quad, spin(opening, 4, 1), 0.0)
        last_end = combine(stiff[4], [source[which, 4 + a] for a in range(4)] + [inner])
        carried = jnp.where(low_quad, own * opening, spin(last_end, 4, 1))
        for half in range(2):
            chunk = pl.ds(4 * half, 4)
            ahead = source[which, 4] if half == 0 else inner
            along_x = slopes_of(stiff, [source[which, 4 * half + a] for a in range(4)] + [ahead])
            along_x[0] = along_x[0] + carried
            carried = along_x[4]
            lines = [source[which, chunk, j] for j in range(4)]
            ahead = jnp.where(last_zone, 0.0, spin(lines[0], 7, 1))
            along_y = slopes_of(stiff, lines + [ahead])
            along_y[0] = along_y[0] + jnp.where(first_zone, own * lines[0], spin(along_y[4], 1, 1))
            along_y = turned(along_y[:4])
            for a in range(4):
                x = 4 * half + a
                acc_v[which, x] = base(x) + (
                    work_m[0, x] * along_x[a]
                    + work_m[1, x] * along_y[a]
                    + work_m[2, x] * along_z[x]
                )

    def velocity_after(which, put, arrived):
        from_east, from_west, from_north, from_south = arrived
        later = jnp.stack(unpack_x_high([from_east[which, 0], from_east[which, 1]]))
        earlier = jnp.stack(unpack_x_low([from_west[which, 0], from_west[which, 1]]))
        later = jnp.where(low_quad, 0.0, later)
        earlier = jnp.where(low_quad, earlier, 0.0)
        for half in range(2):
            above = jnp.where(last_zone, unpack_y(from_north[which, half], 3), 0.0)
            below = jnp.where(first_zone, unpack_y(from_south[which, half], 0), 0.0)
            extra_y = [stiff[j][4] * above for j in range(4)]
            extra_y[0] = extra_y[0] + below
            extra_y = turned(extra_y)
            for a in range(4):
                x = 4 * half + a
                value = acc_v[which, x] + work_m[1, x] * extra_y[a]
                if half == 1:
                    value = value + work_m[0, x] * (stiff[a][4] * later)
                elif a == 0:
                    value = value + work_m[0, x] * earlier
                put(x, value)

    def mesh_before(item):
        values = work_m[min(item, 2)].reshape(256, 128)
        values = lanes_product(values, 1) if item < 3 else picked(values)
        values = values.reshape(8, 4, 8, 128)
        inner = jnp.where(low_quad, spin(values[0], 4, 1), 0.0)
        for half in range(2):
            chunk = pl.ds(4 * half, 4)
            ahead = values[4] if half == 0 else inner
            across = points_of(points, [values[4 * half + a] for a in range(4)] + [ahead])
            across = turned(across)
            ahead = jnp.where(last_zone, 0.0, spin(across[0], 7, 1))
            for j, result in enumerate(points_of(points, across + [ahead])):
                speed[item, chunk, j] = result
            if item == 0:
                edge = values[4 * half]
                ahead = jnp.where(at_zone(plane, 3), 0.0, spin(edge[0], 7, 0))
                edge = points_of(points, [edge[j] for j in range(4)] + [ahead])
                face_x[half] = jnp.stack(edge)
            if item == 1:
                face_y[0, chunk] = across[0]
                face_y[1, chunk] = ahead

    def mesh_halo():
        values = jnp.concatenate(
            [in_mx[...].reshape(48, 128), in_my[...].reshape(48, 128), in_corner[...], zero], 0
        )
        both, extra = lanes_product(values, 1), picked(values)
        for item in range(4):
            which, source = min(item, 2), both if item < 3 else extra
            rows = source[16 * which : 16 * (which + 1)]
            halo_x[item, pl.ds(0, 16)] = rows
            halo_x[item, pl.ds(16, 16)] = rows
            halo_y[item] = source[48 + 16 * which : 64 + 16 * which].reshape(2, 8, 128)
            halo_corner[item] = spin(source[96:104], 7 - which, 0)

    def mesh_after(item):
        rows = rows_of(plane)
        later = [
            jnp.where(low_rows, 0.0, halo_x[item, pl.ds(j, 8, stride=4), :]) for j in range(4)
        ]
        far = jnp.where(at_zone(plane, 3), 0.0, spin(later[0], 7, 0))
        far = jnp.where(rows == 7, halo_corner[item], far)
        later.append(jnp.where(low_rows, 0.0, far))
        edge = jnp.stack(points_of(points, later))
        above = [
            jnp.where(last_zone, unpack_y(halo_y[item, half], 3), 0.0) for half in range(2)
        ]
        inner = jnp.where(low_rows, spin(above[0][0], 4, 0), 0.0)
        for half in range(2):
            ahead = above[1][0] if half == 0 else inner
            across = points_of(points, [above[half][a] for a in range(4)] + [ahead])
            for i in range(4):
                x = 4 * half + i
                extra = jnp.stack([points[j][4] * across[i] for j in range(4)])
                if half == 1:
                    extra = extra + points[i][4] * edge
                speed[item, x] += extra
                if item == 1:
                    upper = face_y[1, x] + across[i]
                    if half == 1:
                        upper = upper + points[i][4] * later[4]
                        face_y[0, x] += points[i][4] * later[0]
                    face_y[1, x] = upper
            if item == 0:
                face_x[half] += jnp.stack([points[j][4] * above[half][0] for j in range(4)])
        if item == 0:
            face_x[2] = jnp.where(low_quad, spin(face_x[0], 4, 1), edge)

    def upwind(face, minus_side, plus_side):
        return jnp.maximum(face, 0.0) * minus_side + jnp.minimum(face, 0.0) * plus_side

    def field_ends(which, source):
        upper, pair = sided(source[which].reshape(256, 128))
        sides = product(pair, ends[:256]) + product(upper, ends[256:])
        ends_z[which, 0] = sides[:, :128]
        ends_z[which, 1] = sides[:, 128:]

    def field_before(which, source, base):
        values = source[which].reshape(256, 128)
        flux = upwind(speed[3].reshape(256, 128), ends_z[which, 0], ends_z[which, 1])
        moved = speed[2].reshape(256, 128) * values
        upper, lower = parted(jnp.concatenate([moved, flux], 1))
        sums = product(upper, tall[...])
        along_z = sums[:, :128] + sums[:, 128:] + product(lower, tall[:, :128])
        along_z = along_z.reshape(8, 4, 8, 128)
        for half in range(2):
            chunk = pl.ds(4 * half, 4)
            places = [4 * half + i for i in range(4)]
            along_x = slopes_of(TABLE["volume"], [speed[0, x] * source[which, x] for x in places])
            along_y = slopes_of(
                TABLE["volume"],
                [speed[1, chunk, j] * source[which, chunk, j] for j in range(4)],
            )
            along_y = turned(along_y)
            for i, x in enumerate(places):
                acc_f[which, x] = base(x) + ((along_x[i] + along_y[i]) + along_z[x])

    def in_group(values, join):
        lane = lax.broadcasted_iota(jnp.int32, plane, 1)
        partner = jnp.where(lane % 2 == 0, spin(values, 127, 1), spin(values, 1, 1))
        values = join(values, partner)
        partner = jnp.where(lane // 2 % 2 == 0, spin(values, 126, 1), spin(values, 2, 1))
        return join(values, partner)

    def over_zone(values, join):
        total = functools.reduce(join, values)
        return functools.reduce(join, [total[j] for j in range(4)])

    def limited(which, half, values):
        weights = TABLE["weights"]
        mean = combine(weights, values)
        mean = combine(weights, [mean[j] for j in range(4)])
        lane = lax.broadcasted_iota(jnp.int32, plane, 1) % 4
        middle = (lane == 1) | (lane == 2)
        mean = in_group(mean * jnp.where(middle, weights[1], weights[0]), jnp.add)
        rise = in_group(over_zone(values, jnp.maximum), jnp.maximum) - mean
        fall = in_group(over_zone(values, jnp.minimum), jnp.minimum) - mean
        low, high = bounds[2 * which, half], bounds[2 * which + 1, half]
        theta = jnp.minimum(
            (high - mean) / (rise + limit_eps), (mean - low) / (limit_eps - fall)
        )
        theta = jnp.clip(theta, 0.0, 1.0)
        return [mean + theta * (value - mean) for value in values]

    def field_after(which, scale, put, arrived):
        from_east, from_west, from_north, from_south = arrived
        later = jnp.stack(unpack_x_high([from_east[which, 0], from_east[which, 1]]))
        earlier = jnp.stack(unpack_x_low([from_west[which, 0], from_west[which, 1]]))
        low, high = trace_x[which, 0], trace_x[which, 1]
        flux = [
            upwind(face_x[0], jnp.where(low_quad, earlier, spin(high[1], 4, 1)), low[0]),
            upwind(face_x[1], high[0], low[1]),
            upwind(face_x[2], high[1], jnp.where(low_quad, spin(low[0], 4, 1), later)),
        ]
        for half in range(2):
            chunk = pl.ds(4 * half, 4)
            low, high = trace_y[which, 0, chunk], trace_y[which, 1, chunk]
            before = jnp.where(first_zone, unpack_y(from_south[which, half], 0), spin(high, 1, 1))
            after = jnp.where(last_zone, unpack_y(from_north[which, half], 3), spin(low, 7, 1))
            lift_y = turned(
                lifts_of(
                    upwind(face_y[0, chunk], before, low), upwind(face_y[1, chunk], high, after)
                )
            )
            lift_x = lifts_of(flux[half], flux[half + 1])
            values = [
                acc_f[which, 4 * half + i] + (lift_x[i] + lift_y[i]) for i in range(4)
            ]
            if scale != 1.0:
                values = [scale * value for value in values]
            values = limited(which, half, values)
            for i in range(4):
                put(4 * half + i, values[i])

    for which in range(3):
        arrange(raw_m, work_m, which)
    for item in range(4):
        mesh_before(item)
    for which in range(2):
        field_ends(which, work_u)
    for which in range(3):
        velocity_before(which, work_v, lambda x: work_v[which, x])
    def keep_field(x, value):
        sec_f[which, x] = value

    def keep_velocity(x, value):
        sec_v[which, x] = value

    def finish_field(x, value):
        for j in range(4):
            results[which, x, pl.ds(j, 8, stride=4), :] = value[j]

    def finish_velocity(x, value):
        for j in range(4):
            results[2 + which, x, pl.ds(j, 8, stride=4), :] = 0.5 * value[j]

    for copy in first_m:
        copy.wait_recv()
    mesh_halo()
    for item in range(4):
        mesh_after(item)
    for which in range(2):
        field_before(which, work_u, lambda x: work_u[which, x])
    for copy in first_v:
        copy.wait_recv()
    for which in range(3):
        velocity_after(which, keep_velocity, arrived_c)
        pack_velocity(sec_v, which, leaving_d)
    second_v = send_all(leaving_d, arrived_d)
    for copy in first:
        copy.wait_recv()
    second = []
    for which in range(2):
        field_after(which, 1.0, keep_field, arrived_a)
        field_traces(which, sec_f)
        pack_field(which, which, leaving_b)
        second.append(
            send_all([ref.at[which] for ref in leaving_b], [ref.at[which] for ref in arrived_b])
        )

    for which in range(3):
        velocity_before(which, sec_v, lambda x: work_v[which, x] + sec_v[which, x])
    for which in range(2):
        field_ends(which, sec_f)
    for which in range(2):
        field_before(which, sec_f, lambda x: work_u[which, x] + sec_f[which, x])
    for copy in copies:
        copy.wait_send()
    for copy in second_v:
        copy.wait_recv()
    for which in range(3):
        velocity_after(which, finish_velocity, arrived_d)
    for which in range(2):
        for copy in second[which]:
            copy.wait_recv()
        field_after(which, 0.5, finish_field, arrived_b)


def unfold(results, new_density, new_energy, new_velocity, store_sem):
    copies = []
    for half in range(2):
        rows, block = pl.ds(16 * half, 16), pl.ds(8 * half, 8)
        for source, target in (
            (results.at[pl.ds(2, 3), :, rows, :], new_velocity.at[:, block]),
            (results.at[0, :, rows, :], new_density.at[block]),
            (results.at[1, :, rows, :], new_energy.at[block]),
        ):
            copy = pltpu.make_async_copy(source, target, store_sem.at[len(copies)])
            copy.start()
            copies.append(copy)
    for copy in copies:
        copy.wait()


def solution(mesh):
    counts = (mesh.shape["gx"], mesh.shape["gy"])
    matrices = lane_matrices(128)

    def on_device(*arguments):
        vmem = lambda *shape: pltpu.VMEM(shape, F32)
        scratch = [
            vmem(2, 8, 32, 128), vmem(3, 8, 32, 128), vmem(3, 8, 32, 128),
            vmem(*matrices.shape),
            pltpu.VMEM((256, 512), BF16), pltpu.VMEM((384, 256), BF16),
            pltpu.VMEM((256, 128), BF16), pltpu.VMEM((256, 256), BF16),
            vmem(4, 4, 4, 32), vmem(4, 2, 8, 128), vmem(4, 2, 8, 128),
            vmem(2, 8, 4, 8, 128), vmem(3, 8, 4, 8, 128), vmem(3, 8, 4, 8, 128),
            vmem(3, 8, 4, 8, 128), vmem(3, 8, 4, 8, 128),
            vmem(2, 8, 4, 8, 128), vmem(2, 8, 4, 8, 128),
            vmem(4, 8, 4, 8, 128), vmem(3, 4, 8, 128), vmem(2, 8, 8, 128),
            vmem(2, 2, 2, 4, 8, 128), vmem(2, 2, 8, 8, 128), vmem(2, 2, 256, 128),
            vmem(4, 32, 128), vmem(4, 2, 8, 128), vmem(4, 8, 128),
        ]
        scratch += [vmem(2, 2, 8, 128)] * 8
        scratch += [vmem(3, 2, 8, 128), vmem(3, 16, 128), vmem(3, 2, 8, 128)] + [vmem(8, 128)] * 2
        for items in (3, 2, 3):
            scratch += [vmem(items, 2, 8, 128)] * 8
        scratch += [
            pltpu.SemaphoreType.DMA((13,)),
            pltpu.SemaphoreType.DMA((23,)),
            pltpu.SemaphoreType.DMA((23,)),
        ]
        operands = [
            pltpu.with_memory_space_constraint(value, pltpu.HBM)
            for value in (*arguments, jnp.asarray(matrices))
        ]
        results = pl.pallas_call(
            functools.partial(kernel, counts),
            out_shape=pltpu.VMEM((5, 8, 32, 128), F32),
            in_specs=[pl.BlockSpec(memory_space=pltpu.HBM)] * 9,
            out_specs=pl.BlockSpec(memory_space=pltpu.VMEM),
            scratch_shapes=scratch,
            compiler_params=pltpu.CompilerParams(
                collective_id=0, has_side_effects=True, vmem_limit_bytes=32 * 1024 * 1024
            ),
        )(*operands)
        return pl.pallas_call(
            unfold,
            out_shape=[jax.ShapeDtypeStruct(value.shape, F32) for value in arguments[:3]],
            in_specs=[pl.BlockSpec(memory_space=pltpu.VMEM)],
            out_specs=[pl.BlockSpec(memory_space=pltpu.HBM)] * 3,
            scratch_shapes=[pltpu.SemaphoreType.DMA((6,))],
            compiler_params=pltpu.CompilerParams(vmem_limit_bytes=32 * 1024 * 1024),
        )(results)

    fields, vectors = P("gx", "gy", None), P(None, "gx", "gy", None)
    return jax.shard_map(
        on_device,
        mesh=mesh,
        in_specs=(fields, fields, vectors, vectors, fields, fields, fields, fields),
        out_specs=(fields, fields, vectors),
        check_vma=False,
    )
```

```python
import functools
import math

import jax
import jax.numpy as jnp
import numpy as np
from jax import lax
from jax.experimental import pallas as pl
from jax.experimental.pallas import tpu as pltpu
from jax.sharding import PartitionSpec as P

MESH = pl.DeviceIdType.MESH
F32 = jnp.float32
BF16 = jnp.bfloat16
time_step = 0.02
limit_eps = 1e-06


def lagrange_values(node_set, points):
    result = np.ones((len(points), len(node_set)))
    for column in range(len(node_set)):
        for partner in range(len(node_set)):
            if partner != column:
                result[:, column] = (
                    result[:, column]
                    * (points - node_set[partner])
                    / (node_set[column] - node_set[partner])
                )
    return result


def lagrange_slopes(node_set, points):
    node_total = len(node_set)
    result = np.zeros((len(points), node_total))
    for column in range(node_total):
        for skipped in range(node_total):
            if skipped != column:
                factor = np.ones(len(points)) / (node_set[column] - node_set[skipped])
                for partner in range(node_total):
                    if partner != column and partner != skipped:
                        factor = (
                            factor
                            * (points - node_set[partner])
                            / (node_set[column] - node_set[partner])
                        )
                result[:, column] = result[:, column] + factor
    return result


def basis_tables():
    gauss_points = np.array(
        [-0.8611363115940526, -0.3399810435848563, 0.3399810435848563, 0.8611363115940526]
    )
    gauss_weights = np.array(
        [0.3478548451374538, 0.6521451548625461, 0.6521451548625461, 0.3478548451374538]
    )
    lobatto_points = np.array([-1.0, -math.sqrt(3.0 / 7.0), 0.0, math.sqrt(3.0 / 7.0), 1.0])
    lobatto_weights = np.array([0.1, 49.0 / 90.0, 32.0 / 45.0, 49.0 / 90.0, 0.1])
    slopes = lagrange_slopes(gauss_points, gauss_points)
    volume = (2.0 / gauss_weights)[:, None] * slopes.T * gauss_weights[None, :]
    trace_low = lagrange_values(gauss_points, np.array([-1.0]))[0]
    trace_high = lagrange_values(gauss_points, np.array([1.0]))[0]
    stiffness = (
        2.0 * lobatto_weights[:, None] * lagrange_slopes(lobatto_points, lobatto_points)
    )
    lumped = np.array([0.2, lobatto_weights[1], lobatto_weights[2], lobatto_weights[3], 0.2])
    return {
        "weights": gauss_weights / 2.0,
        "volume": time_step * volume,
        "trace_low": trace_low,
        "trace_high": trace_high,
        "lift_low": time_step * 2.0 * trace_low / gauss_weights,
        "lift_high": time_step * 2.0 * trace_high / gauss_weights,
        "to_points": lagrange_values(lobatto_points, gauss_points),
        "stiffness": -time_step * stiffness / lumped[:, None],
    }


TABLES = basis_tables()
TABLE = {name: TABLES[name].tolist() for name in TABLES}


def lane_matrices(lanes):
    zones = lanes // 4
    shape = (lanes, lanes)
    volume, lift = np.zeros(shape), np.zeros(shape)
    minus, plus = np.zeros(shape), np.zeros(shape)
    stiff, interp = np.zeros(shape), np.zeros(shape)
    pick, spread = np.zeros(shape), np.zeros(shape)
    for zone in range(zones):
        at = 4 * zone
        before = 4 * ((zone - 1) % zones)
        for within in range(4):
            for source in range(4):
                volume[at + source, at + within] = TABLES["volume"][within, source]
                minus[before + source, at + within] = TABLES["trace_high"][source]
                plus[at + source, at + within] = TABLES["trace_low"][source]
            lift[at, at + within] = TABLES["lift_low"][within]
            lift[at, before + within] = -TABLES["lift_high"][within]
            pick[at, at + within] = 1.0
            spread[zone, at + within] = 1.0
            for source in range(5):
                interp[(at + source) % lanes, at + within] += TABLES["to_points"][within, source]
        for target in range(5):
            for source in range(5):
                stiff[(at + source) % lanes, (at + target) % lanes] += TABLES["stiffness"][
                    target, source
                ]
    matrices = [minus, plus, stiff, interp, pick, spread, volume, lift]
    return np.concatenate(matrices, axis=1).astype(np.float32)


def spin(values, steps, axis):
    size = values.shape[axis]
    steps = steps % size
    return values if steps == 0 else pltpu.roll(values, steps, axis)


def rows_of(shape):
    return lax.broadcasted_iota(jnp.int32, shape, len(shape) - 2)


def low_half(shape):
    return rows_of(shape) < 4


def at_zone(shape, zone):
    return rows_of(shape) % 4 == zone


def combine(coefficients, terms):
    total = None
    for factor, term in zip(coefficients, terms):
        part = factor * term
        total = part if total is None else total + part
    return total


def parted(values):
    upper = values.astype(BF16)
    return upper, (values - upper.astype(F32)).astype(BF16)


def product(left, right):
    return jnp.dot(left, right, preferred_element_type=F32)


def mirrored(matrix):
    size = len(matrix[0])
    middle = size // 2
    even = [[(row[c] + row[size - 1 - c]) / 2 for c in range(middle)] for row in matrix]
    odd = [[(row[c] - row[size - 1 - c]) / 2 for c in range(middle)] for row in matrix]
    centre = [row[middle] for row in matrix] if size % 2 else None
    return even, odd, centre


def pairs_of(values):
    size = len(values)
    sums = [values[c] + values[size - 1 - c] for c in range(size // 2)]
    gaps = [values[c] - values[size - 1 - c] for c in range(size // 2)]
    return sums, gaps


def slopes_of(matrix, values):
    even, odd, centre = mirrored(matrix)
    sums, gaps = pairs_of(values)
    size = len(matrix)
    result = [None] * size
    for a in range(size // 2):
        factors, terms = list(even[a]), list(sums)
        if centre is not None:
            factors.append(centre[a])
            terms.append(values[size // 2])
        outer, inner = combine(factors, terms), combine(odd[a], gaps)
        result[a], result[size - 1 - a] = inner + outer, inner - outer
    if size % 2:
        result[size // 2] = combine(odd[size // 2], gaps)
    return result


def points_of(matrix, values):
    even, odd, centre = mirrored(matrix)
    sums, gaps = pairs_of(values)
    result = [None] * 4
    for i in range(2):
        outer = combine(even[i] + [centre[i]], sums + [values[2]])
        inner = combine(odd[i], gaps)
        result[i], result[3 - i] = outer + inner, outer - inner
    return result


def traces_of(values):
    sums, gaps = pairs_of(values)
    even, odd, _ = mirrored([TABLE["trace_low"]])
    outer, inner = combine(even[0], sums), combine(odd[0], gaps)
    return outer + inner, outer - inner


def lifts_of(lower, upper):
    even, odd, _ = mirrored([TABLE["lift_low"]])
    gap, both = lower - upper, lower + upper
    result = [None] * 4
    for i in range(2):
        outer, inner = even[0][i] * gap, odd[0][i] * both
        result[i], result[3 - i] = outer + inner, outer - inner
    return result


def turned(pieces):
    return [jnp.stack([pieces[j][i] for j in range(4)]) for i in range(4)]


def pack_x_low(planes):
    mask = low_half((8, 128))
    return [jnp.where(mask, planes[t], spin(planes[t + 1], 4, 0)) for t in (0, 2)]


def pack_x_high(planes):
    mask = low_half((8, 128))
    return [jnp.where(mask, spin(planes[t], 4, 0), planes[t + 1]) for t in (0, 2)]


def unpack_x_high(packed):
    return [spin(packed[0], 4, 0), packed[0], spin(packed[1], 4, 0), packed[1]]


def unpack_x_low(packed):
    return [packed[0], spin(packed[0], 4, 0), packed[1], spin(packed[1], 4, 0)]


def pack_y(values, start):
    shape = (8, 128)
    packed = []
    for half in range(2):
        total = spin(values[4 * half + 3], 3 - start, 0)
        for place in (2, 1, 0):
            moved = spin(values[4 * half + place], place - start, 0)
            total = jnp.where(at_zone(shape, place), moved, total)
        packed.append(total)
    return packed


def unpack_y(packed, end):
    return jnp.stack([spin(packed, end - place, 0) for place in range(4)])


def kernel(
    counts,
    density, energy, velocity, mesh_velocity, density_low, density_high, energy_low, energy_high,
    tables_hbm,
    results,
    raw_u, raw_v, raw_m, tables, square, ends, picker, tall, bound_in, bound_rows,
    bounds, work_u, work_v, work_m,
    acc_v, sec_v, acc_f, sec_f, speed, face_x, face_y, trace_x, trace_y, ends_z,
    halo_x, halo_y, halo_corner,
    out_dx, out_ux, out_dy, out_uy, in_dx, in_ux, in_dy, in_uy,
    out_my, in_mx, in_my, out_corner, in_corner,
    out_vx, out_wx, out_vy, out_wy, in_vx, in_wx, in_vy, in_wy,
    out_dx2, out_ux2, out_dy2, out_uy2, in_dx2, in_ux2, in_dy2, in_uy2,
    out_vx2, out_wx2, out_vy2, out_wy2, in_vx2, in_wx2, in_vy2, in_wy2,
    load_sem, send_sem, recv_sem,
):
    count_x, count_y = counts
    here_x, here_y = lax.axis_index("gx"), lax.axis_index("gy")
    west = lax.rem(here_x + count_x - 1, count_x)
    east = lax.rem(here_x + 1, count_x)
    south = lax.rem(here_y + count_y - 1, count_y)
    north = lax.rem(here_y + 1, count_y)
    to_west, to_east = (west, here_y), (east, here_y)
    to_south, to_north = (here_x, south), (here_x, north)
    to_corner, from_corner = (west, south), (east, north)

    barrier = pltpu.get_barrier_semaphore()
    for peer in (to_west, to_east, from_corner, to_south, to_north):
        pl.semaphore_signal(barrier, inc=1, device_id=peer, device_id_type=MESH)

    loads = {}

    def load(name, source, target):
        copy = pltpu.make_async_copy(source, target, load_sem.at[sum(map(len, loads.values()))])
        copy.start()
        loads.setdefault(name, []).append(copy)

    def loaded(name):
        for copy in loads[name]:
            copy.wait()

    places = [(pl.ds(16 * half, 16), pl.ds(8 * half, 8)) for half in range(2)]
    for rows, block in places:
        load("mesh", mesh_velocity.at[:, block], raw_m.at[:, :, rows, :])
    for rows, block in places:
        load("velocity", velocity.at[:, block], raw_v.at[:, :, rows, :])
    for rows, block in places:
        load("fields", density.at[block], raw_u.at[0, :, rows, :])
        load("fields", energy.at[block], raw_u.at[1, :, rows, :])
    load("tables", tables_hbm, tables)
    for index, source in enumerate((density_low, density_high, energy_low, energy_high)):
        load("bounds", source, bound_in.at[index])

    quad, plane = (4, 8, 128), (8, 128)
    low_rows, low_quad = low_half(plane), low_half(quad)
    first_zone, last_zone = at_zone(quad, 0), at_zone(quad, 3)
    stiff, points = TABLE["stiffness"], TABLE["to_points"]
    zero = jnp.zeros(plane, F32)

    def arrange(source, target, which):
        for j in range(4):
            target[which, :, j] = source[which, :, pl.ds(j, 8, stride=4), :]

    def put_pair(target, item, pair):
        target[item, 0] = pair[0]
        target[item, 1] = pair[1]

    def sided(values):
        upper, lower = parted(values)
        return upper, jnp.concatenate([upper, lower], 1)

    def lanes_product(values, column):
        _, pair = sided(values)
        both = product(pair, square[:, 256 * column : 256 * (column + 1)])
        return both[:, :128] + both[:, 128:]

    def picked(values):
        return product(sided(values)[1], picker[...])

    def field_traces(which, source):
        for half in range(2):
            chunk = pl.ds(4 * half, 4)
            low, high = traces_of([source[which, 4 * half + i] for i in range(4)])
            trace_x[which, 0, half], trace_x[which, 1, half] = low, high
            low, high = traces_of([source[which, chunk, j] for j in range(4)])
            trace_y[which, 0, chunk], trace_y[which, 1, chunk] = low, high

    def pack_field(which, item, buffers):
        west_to, east_to, south_to, north_to = buffers
        put_pair(west_to, item, pack_x_low(trace_x[which, 0, 0]))
        put_pair(east_to, item, pack_x_high(trace_x[which, 1, 1]))
        put_pair(south_to, item, pack_y(trace_y[which, 0], 0))
        put_pair(north_to, item, pack_y(trace_y[which, 1], 3))

    def pack_velocity(source, item, buffers):
        west_to, east_to, south_to, north_to = buffers
        put_pair(west_to, item, pack_x_low(source[item, 0]))
        closing = combine(stiff[4][:4], [source[item, 4 + a] for a in range(4)])
        put_pair(east_to, item, pack_x_high(closing))
        put_pair(south_to, item, pack_y(source[item, :, 0], 0))
        closing = combine(stiff[4][:4], [source[item, :, j] for j in range(4)])
        put_pair(north_to, item, pack_y(closing, 3))

    loaded("mesh")
    corner = zero
    for which in range(3):
        values = raw_m[which, :, pl.ds(0, 8, stride=4), :]
        put_pair(out_my, which, pack_y(values, 0))
        corner = jnp.where(rows_of(plane) == which, spin(values[0], which, 0), corner)
    out_corner[...] = corner

    arrived_a, arrived_b = (in_dx, in_ux, in_dy, in_uy), (in_dx2, in_ux2, in_dy2, in_uy2)
    leaving_a, leaving_b = (out_dx, out_ux, out_dy, out_uy), (out_dx2, out_ux2, out_dy2, out_uy2)
    arrived_c, arrived_d = (in_vx, in_wx, in_vy, in_wy), (in_vx2, in_wx2, in_vy2, in_wy2)
    leaving_c, leaving_d = (out_vx, out_wx, out_vy, out_wy), (out_vx2, out_wx2, out_vy2, out_wy2)
    loaded("velocity")
    for which in range(3):
        arrange(raw_v, work_v, which)
        pack_velocity(work_v, which, leaving_c)
    loaded("fields")
    for which in range(2):
        arrange(raw_u, work_u, which)
        field_traces(which, work_u)
        pack_field(which, which, leaving_a)

    pl.semaphore_wait(barrier, 5)
    copies = []
    peers = (to_west, to_east, to_south, to_north)

    def send(source, target, peer):
        copy = pltpu.make_async_remote_copy(
            src_ref=source, dst_ref=target,
            send_sem=send_sem.at[len(copies)], recv_sem=recv_sem.at[len(copies)],
            device_id=peer, device_id_type=MESH,
        )
        copy.start()
        copies.append(copy)
        return copy

    def send_all(sources, targets):
        return [send(*triple) for triple in zip(sources, targets, peers)]

    def send_some(sources, targets, sides):
        return [send(sources[side], targets[side], peers[side]) for side in sides]

    first_m = [send(raw_m.at[:, 0, pl.ds(0, 16), :], in_mx, to_west)]
    first_v = send_some(leaving_c, arrived_c, (0, 1))
    first = send_some(leaving_a, arrived_a, (0, 1))
    first_m += [send(out_corner, in_corner, to_corner), send(out_my, in_my, to_south)]
    first_v += send_some(leaving_c, arrived_c, (2, 3))
    first += send_some(leaving_a, arrived_a, (2, 3))

    loaded("tables")
    minus, plus, stiff_z, interp_z, pick_z, spread_z, volume_z, lift_z = (
        tables[:, 128 * column : 128 * (column + 1)] for column in range(8)
    )
    for column, table in enumerate((stiff_z, interp_z)):
        upper, lower = parted(table)
        at = 256 * column
        square[:128, at : at + 128] = upper
        square[128:, at : at + 128] = upper
        square[:128, at + 128 : at + 256] = lower
        square[128:, at + 128 : at + 256] = jnp.zeros((128, 128), BF16)
    for column, table in enumerate((minus, plus)):
        upper, lower = parted(table)
        at = 128 * column
        ends[:128, at : at + 128] = upper
        ends[128:256, at : at + 128] = upper
        ends[256:, at : at + 128] = lower
    picker[:128] = pick_z.astype(BF16)
    picker[128:] = pick_z.astype(BF16)
    for row, table in enumerate((volume_z, lift_z)):
        upper, lower = parted(table)
        tall[128 * row : 128 * (row + 1), :128] = upper
        tall[128 * row : 128 * (row + 1), 128:] = lower

    loaded("bounds")
    bound_rows[...] = jnp.zeros((4, 2, 8, 128), F32)
    for index in range(4):
        for zone in range(4):
            bound_rows[index, zone % 2, pl.ds(4 * (zone // 2), 4), pl.ds(0, 32)] = bound_in[
                index, zone
            ]
    values = bound_rows[...].reshape(64, 128)
    spreader = spread_z.astype(BF16)
    upper = values.astype(BF16)
    rest = values - upper.astype(F32)
    middle = rest.astype(BF16)
    lowest = (rest - middle.astype(F32)).astype(BF16)
    values = product(upper, spreader) + (product(middle, spreader) + product(lowest, spreader))
    bounds[...] = values.reshape(4, 2, 8, 128)

    def velocity_before(which, source, base):
        along_z = lanes_product(source[which].reshape(256, 128), 0).reshape(8, 4, 8, 128)
        own = stiff[4][4]
        opening = source[which, 0]
        inner = jnp.where(low_quad, spin(opening, 4, 1), 0.0)
        last_end = combine(stiff[4], [source[which, 4 + a] for a in range(4)] + [inner])
        carried = jnp.where(low_quad, own * opening, spin(last_end, 4, 1))
        for half in range(2):
            chunk = pl.ds(4 * half, 4)
            ahead = source[which, 4] if half == 0 else inner
            along_x = slopes_of(stiff, [source[which, 4 * half + a] for a in range(4)] + [ahead])
            along_x[0] = along_x[0] + carried
            carried = along_x[4]
            lines = [source[which, chunk, j] for j in range(4)]
            ahead = jnp.where(last_zone, 0.0, spin(lines[0], 7, 1))
            along_y = slopes_of(stiff, lines + [ahead])
            along_y[0] = along_y[0] + jnp.where(first_zone, own * lines[0], spin(along_y[4], 1, 1))
            along_y = turned(along_y[:4])
            for a in range(4):
                x = 4 * half + a
                acc_v[which, x] = base(x) + (
                    work_m[0, x] * along_x[a]
                    + work_m[1, x] * along_y[a]
                    + work_m[2, x] * along_z[x]
                )

    def velocity_after(which, put, arrived):
        from_east, from_west, from_north, from_south = arrived
        later = jnp.stack(unpack_x_high([from_east[which, 0], from_east[which, 1]]))
        earlier = jnp.stack(unpack_x_low([from_west[which, 0], from_west[which, 1]]))
        later = jnp.where(low_quad, 0.0, later)
        earlier = jnp.where(low_quad, earlier, 0.0)
        for half in range(2):
            above = jnp.where(last_zone, unpack_y(from_north[which, half], 3), 0.0)
            below = jnp.where(first_zone, unpack_y(from_south[which, half], 0), 0.0)
            extra_y = [stiff[j][4] * above for j in range(4)]
            extra_y[0] = extra_y[0] + below
            extra_y = turned(extra_y)
            for a in range(4):
                x = 4 * half + a
                value = acc_v[which, x] + work_m[1, x] * extra_y[a]
                if half == 1:
                    value = value + work_m[0, x] * (stiff[a][4] * later)
                elif a == 0:
                    value = value + work_m[0, x] * earlier
                put(x, value)

    def mesh_before(item):
        values = work_m[min(item, 2)].reshape(256, 128)
        values = lanes_product(values, 1) if item < 3 else picked(values)
        values = values.reshape(8, 4, 8, 128)
        inner = jnp.where(low_quad, spin(values[0], 4, 1), 0.0)
        for half in range(2):
            chunk = pl.ds(4 * half, 4)
            ahead = values[4] if half == 0 else inner
            across = points_of(points, [values[4 * half + a] for a in range(4)] + [ahead])
            across = turned(across)
            ahead = jnp.where(last_zone, 0.0, spin(across[0], 7, 1))
            for j, result in enumerate(points_of(points, across + [ahead])):
                speed[item, chunk, j] = result
            if item == 0:
                edge = values[4 * half]
                ahead = jnp.where(at_zone(plane, 3), 0.0, spin(edge[0], 7, 0))
                edge = points_of(points, [edge[j] for j in range(4)] + [ahead])
                face_x[half] = jnp.stack(edge)
            if item == 1:
                face_y[0, chunk] = across[0]
                face_y[1, chunk] = ahead

    def mesh_halo():
        values = jnp.concatenate(
            [in_mx[...].reshape(48, 128), in_my[...].reshape(48, 128), in_corner[...], zero], 0
        )
        both, extra = lanes_product(values, 1), picked(values)
        for item in range(4):
            which, source = min(item, 2), both if item < 3 else extra
            rows = source[16 * which : 16 * (which + 1)]
            halo_x[item, pl.ds(0, 16)] = rows
            halo_x[item, pl.ds(16, 16)] = rows
            halo_y[item] = source[48 + 16 * which : 64 + 16 * which].reshape(2, 8, 128)
            halo_corner[item] = spin(source[96:104], 7 - which, 0)

    def mesh_after(item):
        rows = rows_of(plane)
        later = [
            jnp.where(low_rows, 0.0, halo_x[item, pl.ds(j, 8, stride=4), :]) for j in range(4)
        ]
        far = jnp.where(at_zone(plane, 3), 0.0, spin(later[0], 7, 0))
        far = jnp.where(rows == 7, halo_corner[item], far)
        later.append(jnp.where(low_rows, 0.0, far))
        edge = jnp.stack(points_of(points, later))
        above = [
            jnp.where(last_zone, unpack_y(halo_y[item, half], 3), 0.0) for half in range(2)
        ]
        inner = jnp.where(low_rows, spin(above[0][0], 4, 0), 0.0)
        for half in range(2):
            ahead = above[1][0] if half == 0 else inner
            across = points_of(points, [above[half][a] for a in range(4)] + [ahead])
            for i in range(4):
                x = 4 * half + i
                extra = jnp.stack([points[j][4] * across[i] for j in range(4)])
                if half == 1:
                    extra = extra + points[i][4] * edge
                speed[item, x] += extra
                if item == 1:
                    upper = face_y[1, x] + across[i]
                    if half == 1:
                        upper = upper + points[i][4] * later[4]
                        face_y[0, x] += points[i][4] * later[0]
                    face_y[1, x] = upper
            if item == 0:
                face_x[half] += jnp.stack([points[j][4] * above[half][0] for j in range(4)])
        if item == 0:
            face_x[2] = jnp.where(low_quad, spin(face_x[0], 4, 1), edge)

    def upwind(face, minus_side, plus_side):
        return jnp.maximum(face, 0.0) * minus_side + jnp.minimum(face, 0.0) * plus_side

    def field_ends(which, source):
        upper, pair = sided(source[which].reshape(256, 128))
        sides = product(pair, ends[:256]) + product(upper, ends[256:])
        ends_z[which, 0] = sides[:, :128]
        ends_z[which, 1] = sides[:, 128:]

    def field_before(which, source, base):
        values = source[which].reshape(256, 128)
        flux = upwind(speed[3].reshape(256, 128), ends_z[which, 0], ends_z[which, 1])
        moved = speed[2].reshape(256, 128) * values
        upper, lower = parted(jnp.concatenate([moved, flux], 1))
        sums = product(upper, tall[...])
        along_z = sums[:, :128] + sums[:, 128:] + product(lower, tall[:, :128])
        along_z = along_z.reshape(8, 4, 8, 128)
        for half in range(2):
            chunk = pl.ds(4 * half, 4)
            places = [4 * half + i for i in range(4)]
            along_x = slopes_of(TABLE["volume"], [speed[0, x] * source[which, x] for x in places])
            along_y = slopes_of(
                TABLE["volume"],
                [speed[1, chunk, j] * source[which, chunk, j] for j in range(4)],
            )
            along_y = turned(along_y)
            for i, x in enumerate(places):
                acc_f[which, x] = base(x) + ((along_x[i] + along_y[i]) + along_z[x])

    def in_group(values, join):
        lane = lax.broadcasted_iota(jnp.int32, plane, 1)
        partner = jnp.where(lane % 2 == 0, spin(values, 127, 1), spin(values, 1, 1))
        values = join(values, partner)
        partner = jnp.where(lane // 2 % 2 == 0, spin(values, 126, 1), spin(values, 2, 1))
        return join(values, partner)

    def over_zone(values, join):
        total = functools.reduce(join, values)
        return functools.reduce(join, [total[j] for j in range(4)])

    def limited(which, half, values):
        weights = TABLE["weights"]
        mean = combine(weights, values)
        mean = combine(weights, [mean[j] for j in range(4)])
        lane = lax.broadcasted_iota(jnp.int32, plane, 1) % 4
        middle = (lane == 1) | (lane == 2)
        mean = in_group(mean * jnp.where(middle, weights[1], weights[0]), jnp.add)
        rise = in_group(over_zone(values, jnp.maximum), jnp.maximum) - mean
        fall = in_group(over_zone(values, jnp.minimum), jnp.minimum) - mean
        low, high = bounds[2 * which, half], bounds[2 * which + 1, half]
        theta = jnp.minimum(
            (high - mean) / (rise + limit_eps), (mean - low) / (limit_eps - fall)
        )
        theta = jnp.clip(theta, 0.0, 1.0)
        return [mean + theta * (value - mean) for value in values]

    def field_after(which, scale, put, arrived):
        from_east, from_west, from_north, from_south = arrived
        later = jnp.stack(unpack_x_high([from_east[which, 0], from_east[which, 1]]))
        earlier = jnp.stack(unpack_x_low([from_west[which, 0], from_west[which, 1]]))
        low, high = trace_x[which, 0], trace_x[which, 1]
        flux = [
            upwind(face_x[0], jnp.where(low_quad, earlier, spin(high[1], 4, 1)), low[0]),
            upwind(face_x[1], high[0], low[1]),
            upwind(face_x[2], high[1], jnp.where(low_quad, spin(low[0], 4, 1), later)),
        ]
        for half in range(2):
            chunk = pl.ds(4 * half, 4)
            low, high = trace_y[which, 0, chunk], trace_y[which, 1, chunk]
            before = jnp.where(first_zone, unpack_y(from_south[which, half], 0), spin(high, 1, 1))
            after = jnp.where(last_zone, unpack_y(from_north[which, half], 3), spin(low, 7, 1))
            lift_y = turned(
                lifts_of(
                    upwind(face_y[0, chunk], before, low), upwind(face_y[1, chunk], high, after)
                )
            )
            lift_x = lifts_of(flux[half], flux[half + 1])
            values = [
                acc_f[which, 4 * half + i] + (lift_x[i] + lift_y[i]) for i in range(4)
            ]
            if scale != 1.0:
                values = [scale * value for value in values]
            values = limited(which, half, values)
            for i in range(4):
                put(4 * half + i, values[i])

    for which in range(3):
        arrange(raw_m, work_m, which)
    for item in range(4):
        mesh_before(item)
    for which in range(2):
        field_ends(which, work_u)
    for which in range(3):
        velocity_before(which, work_v, lambda x: work_v[which, x])
    def keep_field(x, value):
        sec_f[which, x] = value

    def keep_velocity(x, value):
        sec_v[which, x] = value

    def finish_field(x, value):
        for j in range(4):
            results[which, x, pl.ds(j, 8, stride=4), :] = value[j]

    def finish_velocity(x, value):
        for j in range(4):
            results[2 + which, x, pl.ds(j, 8, stride=4), :] = 0.5 * value[j]

    for copy in first_m:
        copy.wait_recv()
    mesh_halo()
    for item in range(4):
        mesh_after(item)
    for which in range(2):
        field_before(which, work_u, lambda x: work_u[which, x])
    for copy in first_v:
        copy.wait_recv()
    for which in range(3):
        velocity_after(which, keep_velocity, arrived_c)
        pack_velocity(sec_v, which, leaving_d)
    second_v = send_all(leaving_d, arrived_d)
    for copy in first:
        copy.wait_recv()
    second = []
    for which in range(2):
        field_after(which, 1.0, keep_field, arrived_a)
        field_traces(which, sec_f)
        pack_field(which, which, leaving_b)
        second.append(
            send_all([ref.at[which] for ref in leaving_b], [ref.at[which] for ref in arrived_b])
        )

    for which in range(3):
        velocity_before(which, sec_v, lambda x: work_v[which, x] + sec_v[which, x])
    for which in range(2):
        field_ends(which, sec_f)
    for which in range(2):
        field_before(which, sec_f, lambda x: work_u[which, x] + sec_f[which, x])
    for copy in copies:
        copy.wait_send()
    for copy in second_v:
        copy.wait_recv()
    for which in range(3):
        velocity_after(which, finish_velocity, arrived_d)
    for which in range(2):
        for copy in second[which]:
            copy.wait_recv()
        field_after(which, 0.5, finish_field, arrived_b)


def unfold(results, new_density, new_energy, new_velocity, store_sem):
    copies = []
    for half in range(2):
        rows, block = pl.ds(16 * half, 16), pl.ds(8 * half, 8)
        for source, target in (
            (results.at[pl.ds(2, 3), :, rows, :], new_velocity.at[:, block]),
            (results.at[0, :, rows, :], new_density.at[block]),
            (results.at[1, :, rows, :], new_energy.at[block]),
        ):
            copy = pltpu.make_async_copy(source, target, store_sem.at[len(copies)])
            copy.start()
            copies.append(copy)
    for copy in copies:
        copy.wait()


def solution(mesh):
    counts = (mesh.shape["gx"], mesh.shape["gy"])
    matrices = lane_matrices(128)

    def on_device(*arguments):
        vmem = lambda *shape: pltpu.VMEM(shape, F32)
        scratch = [
            vmem(2, 8, 40, 128), vmem(3, 8, 40, 128), vmem(3, 8, 40, 128),
            vmem(*matrices.shape),
            pltpu.VMEM((256, 512), BF16), pltpu.VMEM((384, 256), BF16),
            pltpu.VMEM((256, 128), BF16), pltpu.VMEM((256, 256), BF16),
            vmem(4, 4, 4, 32), vmem(4, 2, 8, 128), vmem(4, 2, 8, 128),
            vmem(2, 8, 4, 8, 128), vmem(3, 8, 4, 8, 128), vmem(3, 8, 4, 8, 128),
            vmem(3, 8, 4, 8, 128), vmem(3, 8, 4, 8, 128),
            vmem(2, 8, 4, 8, 128), vmem(2, 8, 4, 8, 128),
            vmem(4, 8, 4, 8, 128), vmem(3, 4, 8, 128), vmem(2, 8, 8, 128),
            vmem(2, 2, 2, 4, 8, 128), vmem(2, 2, 8, 8, 128), vmem(2, 2, 256, 128),
            vmem(4, 32, 128), vmem(4, 2, 8, 128), vmem(4, 8, 128),
        ]
        scratch += [vmem(2, 2, 8, 128)] * 8
        scratch += [vmem(3, 2, 8, 128), vmem(3, 16, 128), vmem(3, 2, 8, 128)] + [vmem(8, 128)] * 2
        for items in (3, 2, 3):
            scratch += [vmem(items, 2, 8, 128)] * 8
        scratch += [
            pltpu.SemaphoreType.DMA((13,)),
            pltpu.SemaphoreType.DMA((23,)),
            pltpu.SemaphoreType.DMA((23,)),
        ]
        operands = [
            pltpu.with_memory_space_constraint(value, pltpu.HBM)
            for value in (*arguments, jnp.asarray(matrices))
        ]
        results = pl.pallas_call(
            functools.partial(kernel, counts),
            out_shape=pltpu.VMEM((5, 8, 40, 128), F32),
            in_specs=[pl.BlockSpec(memory_space=pltpu.HBM)] * 9,
            out_specs=pl.BlockSpec(memory_space=pltpu.VMEM),
            scratch_shapes=scratch,
            compiler_params=pltpu.CompilerParams(
                collective_id=0, has_side_effects=True, vmem_limit_bytes=32 * 1024 * 1024
            ),
        )(*operands)
        return pl.pallas_call(
            unfold,
            out_shape=[jax.ShapeDtypeStruct(value.shape, F32) for value in arguments[:3]],
            in_specs=[pl.BlockSpec(memory_space=pltpu.VMEM)],
            out_specs=[pl.BlockSpec(memory_space=pltpu.HBM)] * 3,
            scratch_shapes=[pltpu.SemaphoreType.DMA((6,))],
            compiler_params=pltpu.CompilerParams(vmem_limit_bytes=32 * 1024 * 1024),
        )(results)

    fields, vectors = P("gx", "gy", None), P(None, "gx", "gy", None)
    return jax.shard_map(
        on_device,
        mesh=mesh,
        in_specs=(fields, fields, vectors, vectors, fields, fields, fields, fields),
        out_specs=(fields, fields, vectors),
        check_vma=False,
    )
```
